32 devices in a mesh: dp: 16 (over z, x, core), band: 2 (over y).
Axes of the slice: x: 2, y: 2, z: 4, core: 2. Of those that a mesh axis runs over, the one named last changes fastest.
Arguments:
- pixels: bfloat16 [384, 10, 256, 64], P('dp', 'band'), may hold values from -6 to 6
- visible: int32 [384, 64], P('dp'), may hold values from 0 to 255, as said below
- kernels: bfloat16 [10, 64, 768], P('band'), may hold values from -0.25 to 0.25
- class_token: float32 [768], replicated, may hold values from -5 to 5
- norm1_gain: float32 [768], replicated, may hold values from 0.1 to 1.9
- norm1_bias: float32 [768], replicated, may hold values from -3 to 3
- norm2_gain: float32 [768], replicated, may hold values from 0.1 to 1.9
- norm2_bias: float32 [768], replicated, may hold values from -3 to 3
- attn_qkv: bfloat16 [768, 2304], replicated, may hold values from -0.21875 to 0.21875
- attn_out: bfloat16 [768, 768], replicated, may hold values from -0.4375 to 0.4375
- mlp_up: bfloat16 [768, 3072], replicated, may hold values from -0.21875 to 0.21875
- mlp_down: bfloat16 [3072, 768], replicated, may hold values from -0.109375 to 0.109375
- cotangent: bfloat16 [384, 65, 768], P(('dp', 'band')), may hold values from -6 to 6
Outputs:
- block_output: bfloat16 [384, 65, 768], P(('dp', 'band'))
- pixel_grads: float32 [384, 10, 256, 64], P('dp', 'band')
- kernel_grads: float32 [10, 64, 768], P('band')
- class_grad: float32 [768], replicated
- norm1_gain_grad: float32 [768], replicated
- norm1_bias_grad: float32 [768], replicated
- norm2_gain_grad: float32 [768], replicated
- norm2_bias_grad: float32 [768], replicated
- qkv_grad: float32 [768, 2304], P('band', 'dp')
- outproj_grad: float32 [768, 768], P('band', 'dp')
- up_grad: float32 [768, 3072], P('band', 'dp')
- down_grad: float32 [3072, 768], P('band', 'dp')
The draws below stay inside these ranges and needn't reach their ends.
Inputs may be any that keep to these rules, and one draw needn't show every extreme that they name: `visible`: each row holds 64 different patch numbers, in no particular order.
All inputs are finite; a program needn't handle non-finite values.
Results may differ from the reference program's by a relative error of at most 0.015.
Values may be sent and summed in bfloat16 or wider, within the bound.
No kernel may reach another device: no remote copies, remote signals or barrier semaphores. Data moves between devices by JAX's collectives and lax.ppermute only.
A program may use at most 192 MiB of HBM per device.

```python
import jax
import jax.numpy as jnp
from jax import lax

D = 768
HEADS = 12
HEAD = 64
FF = 3072
BANDS = 10
PIX = 64
PATCHES = 256
VISIBLE = 64
SEQ = 65
CHIPS = 384
N_DP = 16


def draw_visible(key, part):
    key = jax.random.fold_in(key, 7)
    scores = jax.random.randint(key, (CHIPS, PATCHES), 0, 1 << 20, dtype=jnp.int32) * PATCHES
    scores = scores + jnp.arange(PATCHES, dtype=jnp.int32)[None, :]
    order = jnp.argsort(scores, axis=1, stable=True)
    return order[:, :VISIBLE].astype(jnp.int32)


def shard_levels(rng, dims, split, smallest, top_value):
    def one(axis_at, shards_of):
        steps = jax.random.uniform(jax.random.fold_in(jax.random.fold_in(rng, 6), axis_at), (shards_of,), jnp.float32, smallest / len(split), top_value / len(split))
        return jnp.repeat(jnp.exp(steps), dims[axis_at] // shards_of).reshape((-1,) + (1,) * (len(dims) - axis_at - 1))

    factor_of = one(*split[0])
    for cut in split[1:]:
        factor_of = factor_of * one(*cut)
    return factor_of


def normal_values(stream_key, shape, deviation, reach, cuts=(), kind=jnp.bfloat16):
    values = jax.random.normal(stream_key, shape, jnp.float32) * deviation
    if len(cuts) > 0:
        values = shard_levels(stream_key, shape, cuts, -0.22, 0.18) * values
    return jnp.clip(values, min=-reach, max=reach).astype(kind)


def setup_inputs(seed: int = 0) -> dict:
    key_of = jax.random.split(jax.random.key(seed), 14)
    return {
        "pixels": normal_values(key_of[0], (CHIPS, BANDS, PATCHES, PIX), 1.0, 6.0, ((0, 16), (1, 2))),
        "visible": draw_visible(jax.random.fold_in(key_of[13], 71), 0),
        "kernels": normal_values(key_of[2], (BANDS, PIX, D), (BANDS * PIX) ** -0.5, 0.25, ((0, 2),)),
        "class_token": normal_values(key_of[3], (D,), 1.0, 5.0, (), jnp.float32),
        "norm1_gain": jnp.clip(1.0 + 0.18 * jax.random.normal(key_of[4], (D,), jnp.float32), 0.1, 1.9),
        "norm1_bias": normal_values(key_of[5], (D,), 0.5, 3.0, (), jnp.float32),
        "norm2_gain": jnp.clip(1.0 + 0.18 * jax.random.normal(key_of[6], (D,), jnp.float32), 0.1, 1.9),
        "norm2_bias": normal_values(key_of[7], (D,), 0.5, 3.0, (), jnp.float32),
        "attn_qkv": normal_values(key_of[8], (D, 3 * D), D ** -0.5, 0.21875),
        "attn_out": normal_values(key_of[9], (D, D), (D // 4) ** -0.5, 0.4375),
        "mlp_up": normal_values(key_of[10], (D, FF), D ** -0.5, 0.21875),
        "mlp_down": normal_values(key_of[11], (FF, D), FF ** -0.5, 0.109375),
        "cotangent": normal_values(key_of[12], (CHIPS, SEQ, D), 1.0, 6.0, ((0, 32),)),
    }


@jax.custom_vjp
def low(v):
    return lax.optimization_barrier(v.astype(jnp.bfloat16)).astype(jnp.float32)

@jax.custom_vjp
def low_back(v):
    return v

def low_keep(v):
    return (low(v), None)

def low_pass(kept, grad):
    return (grad,)

def back_keep(v):
    return (v, None)

def back_low(kept, grad):
    return (low(grad),)
low.defvjp(low_keep, low_pass)
low_back.defvjp(back_keep, back_low)

def layer_norm(values, norm_gain, norm_bias):
    average = lax.optimization_barrier(jnp.mean(values, axis=-1, keepdims=True))
    centred = values - average
    spread = lax.optimization_barrier(jnp.mean(centred * centred, axis=-1, keepdims=True))
    return centred * lax.rsqrt(spread + 1e-06) * norm_gain + norm_bias

def gelu_exact(values):
    return jax.nn.gelu(values, approximate=False)

def group_forward(pixels, visible, kernels, class_token, norm1_gain, norm1_bias, norm2_gain, norm2_bias, attn_qkv, attn_out, mlp_up, mlp_down):
    highest = lax.Precision.HIGHEST
    chip_count = pixels.shape[0]
    picked = jnp.take_along_axis(pixels, visible[:, None, :, None], axis=2)
    embedded = low_back(jnp.einsum('cbvp,bpd->cvd', picked, kernels, precision=highest))
    leading = jnp.broadcast_to(class_token[None, None, :], (chip_count, 1, D))
    stream = jnp.concatenate([leading, embedded], axis=1)
    normed1 = low(layer_norm(stream, norm1_gain, norm1_bias))
    packed = jnp.einsum('csd,de->cse', normed1, attn_qkv, precision=highest)
    packed = low_back(low(packed)).reshape(chip_count, SEQ, 3, HEADS, HEAD)
    queries = packed[:, :, 0]
    keys_all = packed[:, :, 1]
    values_all = packed[:, :, 2]
    raw_scores = low_back(jnp.einsum('cqhe,ckhe->chqk', queries, keys_all, precision=highest))
    scores = raw_scores * HEAD ** (-0.5)
    row_max = lax.optimization_barrier(jnp.max(scores, axis=-1, keepdims=True))
    raised = jnp.exp(scores - row_max)
    probs = low(raised / lax.optimization_barrier(jnp.sum(raised, axis=-1, keepdims=True)))
    attended = jnp.einsum('chqk,ckhe->cqhe', probs, values_all, precision=highest)
    attended = low_back(low(attended)).reshape(chip_count, SEQ, D)
    branch = low_back(jnp.einsum('csd,de->cse', attended, attn_out, precision=highest))
    mid_stream = stream + branch
    normed2 = low(layer_norm(mid_stream, norm2_gain, norm2_bias))
    hidden_pre = low_back(jnp.einsum('csd,df->csf', normed2, mlp_up, precision=highest))
    activated = low(gelu_exact(hidden_pre))
    return mid_stream + jnp.einsum('csf,fd->csd', activated, mlp_down, precision=highest)

def reference(pixels, visible, kernels, class_token, norm1_gain, norm1_bias, norm2_gain, norm2_bias, attn_qkv, attn_out, mlp_up, mlp_down, cotangent):
    group_size = CHIPS // N_DP
    stacked_visible = visible.reshape(N_DP, group_size, VISIBLE)
    step_forward = jax.checkpoint(group_forward)

    def forward(pixel_values, kernel_values, class_value, gain_one, bias_one, gain_two, bias_two, qkv_weight, out_weight, up_weight, down_weight):
        stacked_pixels = pixel_values.reshape(N_DP, group_size, BANDS, PATCHES, PIX)

        def scan_step(carry, pieces):
            result = step_forward(pieces[0], pieces[1], kernel_values, class_value, gain_one, bias_one, gain_two, bias_two, qkv_weight, out_weight, up_weight, down_weight)
            return (carry, result)
        unused, results = lax.scan(scan_step, jnp.zeros((), jnp.float32), (stacked_pixels, stacked_visible))
        return results.reshape(CHIPS, SEQ, D)
    outputs, pullback = jax.vjp(forward, pixels.astype(jnp.float32), kernels.astype(jnp.float32), class_token, norm1_gain, norm1_bias, norm2_gain, norm2_bias, attn_qkv.astype(jnp.float32), attn_out.astype(jnp.float32), mlp_up.astype(jnp.float32), mlp_down.astype(jnp.float32))
    grads = pullback(cotangent.astype(jnp.float32))
    return (outputs.astype(jnp.bfloat16), grads[0], grads[1], grads[2], grads[3], grads[4], grads[5], grads[6], grads[7], grads[8], grads[9], grads[10])
```

```python
import functools

import jax
import jax.numpy as jnp
from jax import lax
from jax.experimental import pallas as pl
from jax.experimental.pallas import tpu as pltpu
from jax.sharding import PartitionSpec as P

HEADS = 12
HEAD = 64
BF = jnp.bfloat16
F32 = jnp.float32
TAIL = 16
BLOCK = 112
KEYS = 80
LIMIT = 56 * 1024 * 1024
SCALE = HEAD ** (-0.5)


def dot(a, b):
    return jnp.dot(a, b, preferred_element_type=F32)


def dot_nt(a, b):
    return lax.dot_general(a, b, (((1,), (1,)), ((), ())), preferred_element_type=F32)


def dot_tn(a, b):
    return lax.dot_general(a, b, (((0,), (0,)), ((), ())), preferred_element_type=F32)


def params(*semantics):
    return pltpu.CompilerParams(
        vmem_limit_bytes=LIMIT, dimension_semantics=semantics if semantics else None
    )


def cost(flops, moved):
    return pl.CostEstimate(flops=int(flops), bytes_accessed=int(moved), transcendentals=0)


def pick_kernel(base_ref, seen_ref, pixel_ref, out_ref):
    patches = pixel_ref.shape[2]
    slots = seen_ref.shape[2] // 2
    ids = lax.broadcasted_iota(jnp.int32, (patches, 2 * slots), 0)
    lane = lax.broadcasted_iota(jnp.int32, (patches, 2 * slots), 1)
    hit = ids == seen_ref[0]
    first = jnp.where(hit & (lane < slots), 1.0, 0.0).astype(BF)
    second = jnp.where(hit & (lane >= slots), 1.0, 0.0).astype(BF)
    out_ref[...] = (dot(pixel_ref[0], first) + dot(pixel_ref[1], second)).astype(BF)


def pick(pixel_rows, seen_pairs, pair_base, pairs):
    chips, depth, patches = pixel_rows.shape
    wide = seen_pairs.shape[2]
    return pl.pallas_call(
        pick_kernel,
        out_shape=jax.ShapeDtypeStruct((depth, pairs * wide), BF),
        grid_spec=pltpu.PrefetchScalarGridSpec(
            num_scalar_prefetch=1,
            grid=(pairs,),
            in_specs=[
                pl.BlockSpec((1, 1, wide), lambda i, base: (base[0] + i, 0, 0)),
                pl.BlockSpec((2, depth, patches), lambda i, base: (base[0] + i, 0, 0)),
            ],
            out_specs=pl.BlockSpec((depth, wide), lambda i, base: (0, i)),
        ),
        compiler_params=params("arbitrary"),
        cost_estimate=cost(
            2 * pairs * 2 * depth * patches * 256, pairs * 2 * depth * patches * 2
        ),
        name="pick",
    )(pair_base, seen_pairs, pixel_rows)


def row_stats(values):
    average = jnp.mean(values, axis=-1, keepdims=True)
    centred = values - average
    spread = jnp.mean(centred * centred, axis=-1, keepdims=True)
    root = lax.rsqrt(spread + 1e-06)
    return centred * root, root


def norm_back(xhat, root, grad_out, gain):
    scaled = grad_out * gain
    mean_scaled = jnp.mean(scaled, axis=-1, keepdims=True)
    mean_along = jnp.mean(scaled * xhat, axis=-1, keepdims=True)
    return root * (scaled - mean_scaled - xhat * mean_along)


def head_rows(width):
    row = lax.broadcasted_iota(jnp.int32, (TAIL, width), 0)
    lane = lax.broadcasted_iota(jnp.int32, (TAIL, width), 1)
    return (lane // HEAD) == row


def two_heads(pair):
    low = lax.broadcasted_iota(jnp.int32, pair.shape, 1) < HEAD
    zero = jnp.zeros_like(pair)
    return jnp.concatenate([jnp.where(low, pair, zero), jnp.where(low, zero, pair)], axis=0)


def own_heads(stacked):
    rows = stacked.shape[0] // 2
    low = lax.broadcasted_iota(jnp.int32, (rows, stacked.shape[1]), 1) < HEAD
    return jnp.where(low, stacked[:rows], stacked[rows:])


def softmax_keys(scores, count):
    key = lax.broadcasted_iota(jnp.int32, scores.shape, 0)
    scores = jnp.where(key < count, scores * SCALE, -1e30)
    raised = jnp.exp(scores - jnp.max(scores, axis=0, keepdims=True))
    return raised * (1.0 / jnp.sum(raised, axis=0, keepdims=True))


def forward_kernel(
    chips,
    xo_ref,
    xr_ref,
    ko_ref,
    kr_ref,
    token_ref,
    gain1_ref,
    bias1_ref,
    gain2_ref,
    bias2_ref,
    wqkv_ref,
    wout_ref,
    stream_ref,
    n1_ref,
    packed_ref,
    probs_ref,
    tprobs_ref,
    att_ref,
    mid_ref,
    n2_ref,
    tatt_ref,
):
    rows, width = n1_ref.shape
    body = rows - TAIL
    slots = body // chips
    stream_ref[0:body, :] = dot_tn(xo_ref[...], ko_ref[...]) + dot_tn(xr_ref[...], kr_ref[...])
    tail_row = lax.broadcasted_iota(jnp.int32, (TAIL, width), 0)
    stream_ref[body:rows, :] = jnp.where(tail_row < chips, token_ref[...], 0.0)

    def first_norm(i, carry):
        at = pl.ds(pl.multiple_of(i * BLOCK, BLOCK), BLOCK)
        xhat, unused = row_stats(stream_ref[at, :])
        n1_ref[at, :] = (xhat * gain1_ref[...] + bias1_ref[...]).astype(BF)
        return carry

    lax.fori_loop(0, rows // BLOCK, first_norm, 0)

    def project(j, carry):
        at = pl.ds(pl.multiple_of(j * 256, 256), 256)
        packed_ref[:, at] = dot(n1_ref[...], wqkv_ref[:, at]).astype(BF)
        return carry

    lax.fori_loop(0, 3 * width // 256, project, 0)
    tail = packed_ref[body:rows, :]
    heads = head_rows(width)
    tquery = jnp.where(heads, jnp.broadcast_to(tail[0:1, 0:width], (TAIL, width)), 0).astype(BF)
    tatt_ref[...] = jnp.zeros_like(tatt_ref)

    def chip(c, carry):
        at = pl.ds(pl.multiple_of(c * slots, slots), slots)
        for p in range(width // 128):
            here = slice(128 * p, 128 * p + 128)
            there = slice(width + 128 * p, width + 128 * p + 128)
            yonder = slice(2 * width + 128 * p, 2 * width + 128 * p + 128)
            query = two_heads(packed_ref[at, here])
            key = jnp.concatenate([packed_ref[at, there], tail[:, there]], axis=0)
            val = jnp.concatenate([packed_ref[at, yonder], tail[:, yonder]], axis=0)
            probs = softmax_keys(dot_nt(key, query), slots + 1).astype(BF)
            probs_ref[c, p] = probs
            att_ref[at, here] = own_heads(dot_tn(probs, val)).astype(BF)
        key = jnp.concatenate(
            [packed_ref[at, width : 2 * width], tail[:, width : 2 * width]], axis=0
        )
        val = jnp.concatenate([packed_ref[at, 2 * width :], tail[:, 2 * width :]], axis=0)
        tprobs = softmax_keys(dot_nt(key, tquery), slots + 1).astype(BF)
        tprobs_ref[c] = tprobs
        mixed = jnp.where(heads, dot_tn(tprobs, val), 0.0)
        tatt_ref[pl.ds(c, 1), :] = jnp.sum(mixed, axis=0, keepdims=True)
        return carry

    lax.fori_loop(0, chips, chip, 0)
    att_ref[body:rows, :] = tatt_ref[...].astype(BF)

    def out_project(j, carry):
        at = pl.ds(pl.multiple_of(j * 256, 256), 256)
        mid_ref[:, at] = stream_ref[:, at] + dot(att_ref[...], wout_ref[:, at])
        return carry

    lax.fori_loop(0, width // 256, out_project, 0)

    def second_norm(i, carry):
        at = pl.ds(pl.multiple_of(i * BLOCK, BLOCK), BLOCK)
        xhat, unused = row_stats(mid_ref[at, :])
        n2_ref[at, :] = (xhat * gain2_ref[...] + bias2_ref[...]).astype(BF)
        return carry

    lax.fori_loop(0, rows // BLOCK, second_norm, 0)


def forward(chips, xo, xr, ko, kr, token, gain1, bias1, gain2, bias2, wqkv, wout):
    width = wout.shape[0]
    body = xo.shape[1]
    rows = body + TAIL
    shape = jax.ShapeDtypeStruct
    return pl.pallas_call(
        functools.partial(forward_kernel, chips),
        out_shape=(
            shape((rows, width), F32),
            shape((rows, width), BF),
            shape((rows, 3 * width), BF),
            shape((chips, width // 128, KEYS, 128), BF),
            shape((chips, KEYS, TAIL), BF),
            shape((rows, width), BF),
            shape((rows, width), F32),
            shape((rows, width), BF),
        ),
        scratch_shapes=[pltpu.VMEM((TAIL, width), F32)],
        compiler_params=params(),
        cost_estimate=cost(2 * rows * width * width * 8, 20e6),
        name="encoder_forward",
    )(xo, xr, ko, kr, token, gain1, bias1, gain2, bias2, wqkv, wout)


def mlp_kernel(
    split,
    core_ref,
    n2_ref,
    cot_ref,
    cot_t_ref,
    up_ref,
    down_ref,
    out_in_ref,
    back_in_ref,
    down_send_ref,
    down_keep_ref,
    up_send_ref,
    up_keep_ref,
    out_ref,
    back_ref,
    act_ref,
    gpre_ref,
    grad_ref,
):
    step = pl.program_id(0)

    @pl.when(step == 0)
    def _():
        out_ref[...] = out_in_ref[...]
        back_ref[...] = back_in_ref[...]

    rows = n2_ref.shape[0]
    width = n2_ref.shape[1]
    for low, high in ((0, split), (split, rows)):
        pre = dot(n2_ref[low:high, :], up_ref[...])
        gact = dot_nt(cot_ref[low:high, :], down_ref[...])
        half = 0.5 + 0.5 * lax.erf(pre * (0.5**0.5))
        bell = jnp.exp(-0.5 * pre * pre) * 0.3989422804014327
        act_ref[low:high, :] = (pre * half).astype(BF)
        gpre_ref[low:high, :] = (gact * (half + pre * bell)).astype(BF)
    down_grad = dot(cot_t_ref[...], act_ref[...]).astype(BF)
    half_rows = width // 2
    down_send_ref[...] = down_grad[:half_rows].reshape(down_send_ref.shape)
    down_keep_ref[...] = down_grad[half_rows:].reshape(down_keep_ref.shape)
    grad_ref[...] = dot_tn(gpre_ref[...], n2_ref[...]).astype(BF)
    part = grad_ref.shape[0] // 2
    core = core_ref[0]
    sent = grad_ref[pl.ds(pl.multiple_of((1 - core) * part, part), part), :]
    kept = grad_ref[pl.ds(pl.multiple_of(core * part, part), part), :]
    for b in range(2):
        cols = slice(b * half_rows, (b + 1) * half_rows)
        up_send_ref[0, 0, b] = sent[:, cols]
        up_keep_ref[0, 0, b] = kept[:, cols]
    out_ref[...] += dot(act_ref[...], down_ref[...])
    back_ref[...] += dot_nt(gpre_ref[...], up_ref[...])


def mlp(third, core, n2, cot, cot_t, up, down, out_in, back_in):
    rows, width = n2.shape
    hidden = up.shape[1]
    chunk = hidden // 8
    part = chunk // 2
    band_cols = width // 2
    shape = jax.ShapeDtypeStruct
    whole = lambda i, core: (0, 0)
    block_at = lambda i: (i // 2) * 4 + third * 2 + i % 2
    down_shape = shape((2, 2, width // 4, 2 * chunk), BF)
    down_spec = pl.BlockSpec((2, 1, width // 4, chunk), lambda i, core: (0, i // 2, 0, i % 2))
    up_shape = shape((2, 2, 2, part, band_cols), BF)
    up_spec = pl.BlockSpec(
        (1, 1, 2, part, band_cols), lambda i, core: (i // 2, i % 2, 0, 0, 0)
    )
    return pl.pallas_call(
        functools.partial(mlp_kernel, rows // 32 * 16),
        out_shape=(
            down_shape,
            down_shape,
            up_shape,
            up_shape,
            shape((rows, width), F32),
            shape((rows, width), F32),
        ),
        grid_spec=pltpu.PrefetchScalarGridSpec(
            num_scalar_prefetch=1,
            grid=(4,),
            in_specs=[
                pl.BlockSpec((rows, width), whole),
                pl.BlockSpec((rows, width), whole),
                pl.BlockSpec((width, rows), whole),
                pl.BlockSpec((width, chunk), lambda i, core: (0, block_at(i))),
                pl.BlockSpec((chunk, width), lambda i, core: (block_at(i), 0)),
                pl.BlockSpec((rows, width), whole),
                pl.BlockSpec((rows, width), whole),
            ],
            out_specs=(
                down_spec,
                down_spec,
                up_spec,
                up_spec,
                pl.BlockSpec((rows, width), whole),
                pl.BlockSpec((rows, width), whole),
            ),
            scratch_shapes=[
                pltpu.VMEM((rows, chunk), BF),
                pltpu.VMEM((rows, chunk), BF),
                pltpu.VMEM((chunk, width), BF),
            ],
        ),
        compiler_params=params("arbitrary"),
        cost_estimate=cost(2 * rows * width * hidden * 3, 25e6),
        name="mlp_both_ways",
    )(core, n2, cot, cot_t, up, down, out_in, back_in)


def spread_blocks(full_ref, send_ref, keep_ref, core, block):
    cols = full_ref.shape[1] // 2
    for z in range(4):
        for x in range(2):
            base = (z * 2 + x) * 2
            sent = full_ref[pl.ds(pl.multiple_of((base + 1 - core) * block, 16), block), :]
            kept = full_ref[pl.ds(pl.multiple_of((base + core) * block, 16), block), :]
            for b in range(2):
                send_ref[x, b, z] = sent[:, b * cols : (b + 1) * cols]
                keep_ref[x, b, z] = kept[:, b * cols : (b + 1) * cols]


def attention_back_kernel(
    chips,
    core_ref,
    back_ref,
    mid_ref,
    cot_ref,
    gain2_ref,
    wout_ref,
    att_ref,
    packed_ref,
    probs_ref,
    tprobs_ref,
    gmid_ref,
    gpacked_ref,
    out_send_ref,
    out_keep_ref,
    vec_ref,
    branch_ref,
    gatt_ref,
    full_ref,
    tgrad_ref,
    tout_ref,
):
    rows, width = mid_ref.shape
    body = rows - TAIL
    slots = body // chips

    def norm(i, carry):
        at = pl.ds(pl.multiple_of(i * BLOCK, BLOCK), BLOCK)
        xhat, root = row_stats(mid_ref[at, :])
        grad = back_ref[at, :]
        back = norm_back(xhat, root, grad, gain2_ref[...])
        total = cot_ref[at, :].astype(F32) + back
        gmid_ref[at, :] = total
        branch_ref[at, :] = total.astype(BF)
        return (
            carry[0] + jnp.sum(grad * xhat, axis=0, keepdims=True),
            carry[1] + jnp.sum(grad, axis=0, keepdims=True),
        )

    zero = jnp.zeros((1, width), F32)
    gain_sum, bias_sum = lax.fori_loop(0, rows // BLOCK, norm, (zero, zero))
    vec_ref[0:1, :] = gain_sum
    vec_ref[1:2, :] = bias_sum

    full_ref[...] = dot_tn(branch_ref[...], att_ref[...]).astype(BF)
    spread_blocks(full_ref, out_send_ref, out_keep_ref, core_ref[0], width // 16)

    gatt = dot_nt(branch_ref[...], wout_ref[...])
    gatt_ref[...] = gatt[:body].astype(BF)
    tgrad_ref[...] = gatt[body:].astype(BF).astype(F32)
    tout_ref[...] = jnp.zeros_like(tout_ref)
    tail = packed_ref[body:rows, :]
    heads = head_rows(width)
    tquery = jnp.where(heads, jnp.broadcast_to(tail[0:1, 0:width], (TAIL, width)), 0).astype(BF)

    def chip(c, carry):
        at = pl.ds(pl.multiple_of(c * slots, slots), slots)
        key_all = jnp.concatenate(
            [packed_ref[at, width : 2 * width], tail[:, width : 2 * width]], axis=0
        )
        val_all = jnp.concatenate([packed_ref[at, 2 * width :], tail[:, 2 * width :]], axis=0)
        tgrad = jnp.where(
            heads, jnp.broadcast_to(tgrad_ref[pl.ds(c, 1), :], (TAIL, width)), 0.0
        ).astype(BF)
        tprobs = tprobs_ref[c]
        wide = tprobs.astype(F32)
        gprobs = dot_nt(val_all, tgrad)
        inner = jnp.sum(gprobs * wide, axis=0, keepdims=True)
        tscores = (wide * (gprobs - inner) * SCALE).astype(BF)
        gval_tail = dot(tprobs, tgrad)
        gkey_tail = dot(tscores, tquery)
        tq = jnp.sum(jnp.where(heads, dot_tn(tscores, key_all), 0.0), axis=0, keepdims=True)
        tkeys, tvals = [], []
        for p in range(width // 128):
            here = slice(128 * p, 128 * p + 128)
            there = slice(width + 128 * p, width + 128 * p + 128)
            yonder = slice(2 * width + 128 * p, 2 * width + 128 * p + 128)
            query = two_heads(packed_ref[at, here])
            gout = two_heads(gatt_ref[at, here])
            key = key_all[:, here]
            val = val_all[:, here]
            probs = probs_ref[c, p]
            wide = probs.astype(F32)
            gval = dot(probs, gout) + gval_tail[:, here]
            gprobs = dot_nt(val, gout)
            inner = jnp.sum(gprobs * wide, axis=0, keepdims=True)
            gscores = (wide * (gprobs - inner) * SCALE).astype(BF)
            gkey = dot(gscores, query) + gkey_tail[:, here]
            gpacked_ref[at, here] = own_heads(dot_tn(gscores, key)).astype(BF)
            gpacked_ref[at, there] = gkey[:slots].astype(BF)
            gpacked_ref[at, yonder] = gval[:slots].astype(BF)
            tkeys.append(gkey[slots : slots + 1])
            tvals.append(gval[slots : slots + 1])
        tout_ref[pl.ds(c, 1), :] = jnp.concatenate([tq] + tkeys + tvals, axis=1)
        return carry

    lax.fori_loop(0, chips, chip, 0)
    gpacked_ref[body:rows, :] = tout_ref[...].astype(BF)


def attention_back(chips, core, back, mid, cot, gain2, wout, att, packed, probs, tprobs):
    rows, width = mid.shape
    shape = jax.ShapeDtypeStruct
    block = width // 16
    vmem = pl.BlockSpec(memory_space=pltpu.VMEM)
    return pl.pallas_call(
        functools.partial(attention_back_kernel, chips),
        out_shape=(
            shape((rows, width), F32),
            shape((rows, 3 * width), BF),
            shape((2, 2, 4, block, width // 2), BF),
            shape((2, 2, 4, block, width // 2), BF),
            shape((2, width), F32),
        ),
        in_specs=[pl.BlockSpec(memory_space=pltpu.SMEM)] + [vmem] * 9,
        out_specs=(vmem,) * 5,
        scratch_shapes=[
            pltpu.VMEM((rows, width), BF),
            pltpu.VMEM((rows - TAIL, width), BF),
            pltpu.VMEM((width, width), BF),
            pltpu.VMEM((TAIL, width), F32),
            pltpu.VMEM((TAIL, 3 * width), F32),
        ],
        compiler_params=params(),
        cost_estimate=cost(2 * rows * width * width * 6, 20e6),
        name="attention_back",
    )(core, back, mid, cot, gain2, wout, att, packed, probs, tprobs)


def embed_back_kernel(
    chips,
    gpacked_ref,
    wqkv_ref,
    stream_ref,
    gmid_ref,
    gain1_ref,
    xo_ref,
    xr_ref,
    ko_ref,
    kr_ref,
    kgrad_own_ref,
    kgrad_far_ref,
    pgrad_own_ref,
    pgrad_far_ref,
    vec_ref,
    back_ref,
    embed_ref,
):
    rows, width = stream_ref.shape
    body = rows - TAIL

    back_ref[...] = dot_nt(gpacked_ref[...], wqkv_ref[...])

    def norm(i, carry):
        at = pl.ds(pl.multiple_of(i * BLOCK, BLOCK), BLOCK)
        xhat, root = row_stats(stream_ref[at, :])
        grad = back_ref[at, :]
        total = gmid_ref[at, :] + norm_back(xhat, root, grad, gain1_ref[...])
        back_ref[at, :] = total
        embed_ref[at, :] = total.astype(BF)
        return (
            carry[0] + jnp.sum(grad * xhat, axis=0, keepdims=True),
            carry[1] + jnp.sum(grad, axis=0, keepdims=True),
        )

    zero = jnp.zeros((1, width), F32)
    gain_sum, bias_sum = lax.fori_loop(0, rows // BLOCK, norm, (zero, zero))
    vec_ref[0:1, :] = gain_sum
    vec_ref[1:2, :] = bias_sum
    vec_ref[2:3, :] = jnp.sum(back_ref[body:rows, :], axis=0, keepdims=True)
    grad = embed_ref[0:body, :]
    kgrad_far_ref[...] = dot(xr_ref[...], grad).astype(BF)
    kgrad_own_ref[...] = dot(xo_ref[...], grad).astype(BF)
    pgrad_far_ref[...] = dot_nt(kr_ref[...], grad).astype(BF)
    pgrad_own_ref[...] = dot_nt(ko_ref[...], grad).astype(BF)


def embed_back(chips, gpacked, wqkv, stream, gmid, gain1, xo, xr, ko, kr):
    rows, width = stream.shape
    depth, body = xo.shape
    shape = jax.ShapeDtypeStruct
    return pl.pallas_call(
        functools.partial(embed_back_kernel, chips),
        out_shape=(
            shape((depth, width), BF),
            shape((depth, width), BF),
            shape((depth, body), BF),
            shape((depth, body), BF),
            shape((3, width), F32),
        ),
        scratch_shapes=[pltpu.VMEM((rows, width), F32), pltpu.VMEM((rows, width), BF)],
        compiler_params=params(),
        cost_estimate=cost(2 * rows * width * width * 5, 15e6),
        name="embed_back",
    )(gpacked, wqkv, stream, gmid, gain1, xo, xr, ko, kr)


def qkv_grad_kernel(core_ref, gpacked_ref, n1_ref, send_ref, keep_ref, full_ref):
    tile = 384

    def step(j, carry):
        at = pl.ds(pl.multiple_of(j * tile, tile), tile)
        full_ref[at, :] = dot_tn(gpacked_ref[:, at], n1_ref[...]).astype(BF)
        return carry

    lax.fori_loop(0, full_ref.shape[0] // tile, step, 0)
    spread_blocks(full_ref, send_ref, keep_ref, core_ref[0], full_ref.shape[0] // 16)


def qkv_grad(core, gpacked, n1):
    rows, width = n1.shape
    shape = jax.ShapeDtypeStruct
    vmem = pl.BlockSpec(memory_space=pltpu.VMEM)
    block = 3 * width // 16
    return pl.pallas_call(
        qkv_grad_kernel,
        out_shape=(shape((2, 2, 4, block, width // 2), BF),) * 2,
        in_specs=[pl.BlockSpec(memory_space=pltpu.SMEM), vmem, vmem],
        out_specs=(vmem, vmem),
        scratch_shapes=[pltpu.VMEM((3 * width, width), BF)],
        compiler_params=params(),
        cost_estimate=cost(2 * rows * width * width * 3, 8e6),
        name="qkv_grad",
    )(core, gpacked, n1)


def scatter_kernel(base_ref, seen_ref, grad_ref, *rest):
    out_ref = rest[-1]
    patches = out_ref.shape[2]
    wide = seen_ref.shape[2]
    slots = wide // 2
    ids = lax.broadcasted_iota(jnp.int32, (patches, wide), 0)
    lane = lax.broadcasted_iota(jnp.int32, (patches, wide), 1)
    hit = ids == seen_ref[0]
    first = jnp.where(hit & (lane < slots), 1.0, 0.0).astype(BF)
    second = jnp.where(hit & (lane >= slots), 1.0, 0.0).astype(BF)
    out_ref[0] = dot_nt(grad_ref[...], first)
    out_ref[1] = dot_nt(grad_ref[...], second)


def scatter(grads, seen_pairs, pair_base, patches, earlier=None):
    depth = grads.shape[0]
    wide = seen_pairs.shape[2]
    pairs = grads.shape[1] // wide
    chips = 2 * seen_pairs.shape[0]
    in_specs = [
        pl.BlockSpec((1, 1, wide), lambda i, base: (base[0] + i, 0, 0)),
        pl.BlockSpec((depth, wide), lambda i, base: (0, i)),
    ]
    operands = (pair_base, seen_pairs, grads)
    alias = {}
    if earlier is not None:
        in_specs.append(pl.BlockSpec(memory_space=pl.ANY))
        operands = operands + (earlier,)
        alias = {3: 0}
    return pl.pallas_call(
        scatter_kernel,
        out_shape=jax.ShapeDtypeStruct((chips, depth, patches), F32),
        grid_spec=pltpu.PrefetchScalarGridSpec(
            num_scalar_prefetch=1,
            grid=(pairs,),
            in_specs=in_specs,
            out_specs=pl.BlockSpec((2, depth, patches), lambda i, base: (base[0] + i, 0, 0)),
        ),
        input_output_aliases=alias,
        compiler_params=params("arbitrary"),
        cost_estimate=cost(2 * pairs * 2 * depth * patches * wide, pairs * 2 * depth * patches * 4),
        name="scatter",
    )(*operands)


class Links:
    def __init__(self, mesh):
        self.count = mesh.shape["dp"]
        self.extra = self.count // 16

    def swap(self, array, where):
        if where == "band":
            return lax.ppermute(array, "band", [(0, 1), (1, 0)])
        flip = (1 << where) * self.extra
        return lax.ppermute(array, "dp", [(d, d ^ flip) for d in range(self.count)])

    def bit(self, where):
        if where == "band":
            return lax.axis_index("band")
        return (lax.axis_index("dp") // self.extra // (1 << where)) % 2

    def halve(self, array, dim, where):
        mine = self.bit(where)
        sent = lax.dynamic_index_in_dim(array, 1 - mine, dim, keepdims=False)
        kept = lax.dynamic_index_in_dim(array, mine, dim, keepdims=False)
        return self.add(kept, self.swap(sent, where))

    def add(self, a, b):
        return (a.astype(F32) + b.astype(F32)).astype(BF)

    def reduce(self, array, names, order):
        names = list(names)
        for where in order:
            dim = names.index(where)
            array = self.halve(array, dim, where)
            names.pop(dim)
        return array.astype(F32)

    def last(self, array, rows_dim):
        if self.extra == 1:
            return array
        groups = [
            [block * self.extra + i for i in range(self.extra)] for block in range(16)
        ]
        return lax.psum_scatter(
            array, "dp", scatter_dimension=rows_dim, tiled=True, axis_index_groups=groups
        )

    def total(self, array):
        if self.extra == 1:
            return array
        groups = [
            [block * self.extra + i for i in range(self.extra)] for block in range(16)
        ]
        return lax.psum(array, "dp", axis_index_groups=groups)


def shards(
    links,
    pixels,
    visible,
    kernels,
    class_token,
    norm1_gain,
    norm1_bias,
    norm2_gain,
    norm2_bias,
    attn_qkv,
    attn_out,
    mlp_up,
    mlp_down,
    cotangent,
):
    width = attn_out.shape[0]
    chips, seq = cotangent.shape[0], cotangent.shape[1]
    group_chips, bands, patches, pix = pixels.shape
    slots = visible.shape[1]
    body = chips * slots
    rows = body + TAIL
    depth = bands * pix
    pairs = chips // 2
    band = lax.axis_index("band")
    core = links.bit(0)
    core_arg = core.reshape(1).astype(jnp.int32)

    flat_kernels = kernels.reshape(depth, width)
    kernel_halves = flat_kernels.reshape(2, depth // 2, width)
    my_half = lax.dynamic_index_in_dim(kernel_halves, core, 0, keepdims=False)
    far_half = links.swap(my_half, "band")
    far_other = links.swap(far_half, 0)
    kernels_far = jnp.where(
        core == 0,
        jnp.concatenate([far_half, far_other], axis=0),
        jnp.concatenate([far_other, far_half], axis=0),
    )

    pixel_rows = jnp.swapaxes(pixels, 2, 3).reshape(group_chips, depth, patches)
    seen_pairs = visible.reshape(group_chips // 2, 1, 2 * slots)
    own_base = (band * pairs).reshape(1).astype(jnp.int32)
    far_base = ((1 - band) * pairs).reshape(1).astype(jnp.int32)
    picked_far = pick(pixel_rows, seen_pairs, far_base, pairs)
    picked_in = links.swap(picked_far, "band")
    picked_own = pick(pixel_rows, seen_pairs, own_base, pairs)

    cot_rows = jnp.concatenate(
        [
            cotangent[:, 1:, :].reshape(body, width),
            cotangent[:, 0, :],
            jnp.zeros((TAIL - chips, width), BF),
        ],
        axis=0,
    )
    cot_t = cot_rows.T.reshape(4, 2, 2, width // 16, rows)
    cot_t = jnp.swapaxes(cot_t, 0, 1)
    cot_t = jnp.concatenate(
        [
            lax.dynamic_index_in_dim(cot_t, 1 - core, 2, keepdims=False).reshape(width // 2, rows),
            lax.dynamic_index_in_dim(cot_t, core, 2, keepdims=False).reshape(width // 2, rows),
        ],
        axis=0,
    )

    row = lambda v: v.reshape(1, width)
    stream, n1, packed, probs, tprobs, att, mid, n2 = forward(
        chips,
        picked_own,
        picked_in,
        flat_kernels,
        kernels_far,
        row(class_token),
        row(norm1_gain),
        row(norm1_bias),
        row(norm2_gain),
        row(norm2_bias),
        attn_qkv,
        attn_out,
    )

    out_rows, back = mid, jnp.zeros((rows, width), F32)
    down_parts, up_parts = [], []
    for third in range(2):
        down_send, down_keep, up_send, up_keep, out_rows, back = mlp(
            third, core_arg, n2, cot_rows, cot_t, mlp_up, mlp_down, out_rows, back
        )
        down_sum = links.add(down_keep, links.swap(down_send, 0))
        up_sum = links.add(up_keep, links.swap(up_send, 0))
        down_sum = down_sum.reshape(2, 2, 2, 2, width // 16, down_sum.shape[-1])
        down_parts.append(links.reduce(down_sum, (1, "band", 3, 2), (1, "band", 2, 3)))
        up_parts.append((third, up_sum))

    block_output = jnp.concatenate(
        [
            out_rows[body : body + chips].astype(BF)[:, None, :],
            out_rows[:body].astype(BF).reshape(chips, slots, width),
        ],
        axis=1,
    )

    up_all = jnp.stack([up_parts[0][1], up_parts[1][1]], axis=1)
    up_final = links.reduce(up_all, (3, 2, 1, "band"), ("band", 1, 2, 3))

    gmid, gpacked, out_send, out_keep, vec2 = attention_back(
        chips,
        core_arg,
        back,
        mid,
        cot_rows,
        row(norm2_gain),
        attn_out,
        att,
        packed,
        probs,
        tprobs,
    )
    names = (1, "band", 3, 2)
    out_sum = links.add(out_keep, links.swap(out_send, 0))
    out_sum = out_sum.reshape((2, 2, 2, 2) + out_sum.shape[3:])
    out_final = links.reduce(out_sum, names, (1, "band", 2, 3))

    kgrad_own, kgrad_far, pgrad_own, pgrad_far, vec1 = embed_back(
        chips,
        gpacked,
        attn_qkv,
        stream,
        gmid,
        row(norm1_gain),
        picked_own,
        picked_in,
        flat_kernels,
        kernels_far,
    )
    pgrad_in = links.swap(pgrad_far, "band")
    qkv_send, qkv_keep = qkv_grad(core_arg, gpacked, n1)
    qkv_sum = links.add(qkv_keep, links.swap(qkv_send, 0))
    qkv_sum = qkv_sum.reshape((2, 2, 2, 2) + qkv_sum.shape[3:])
    qkv_final = links.reduce(qkv_sum, names, ("band", 1, 2, 3))

    partly = scatter(pgrad_own, seen_pairs, own_base, patches)
    pixel_grads = scatter(pgrad_in, seen_pairs, far_base, patches, partly)
    pixel_grads = jnp.swapaxes(
        pixel_grads.reshape(group_chips, bands, pix, patches), 2, 3
    )

    kgrad = links.add(kgrad_own, links.swap(kgrad_far, "band"))
    for where in range(4):
        kgrad = links.halve(kgrad.reshape(2, -1, width), 0, where)
    kgrad = links.total(kgrad)
    for where in (3, 2, 1, 0):
        other = links.swap(kgrad, where)
        kgrad = jnp.where(
            links.bit(where) == 0,
            jnp.concatenate([kgrad, other], axis=0),
            jnp.concatenate([other, kgrad], axis=0),
        )
    kernel_grads = kgrad.astype(F32).reshape(bands, pix, width)

    vecs = jnp.concatenate([vec1, vec2], axis=0)
    for where in (0, "band", 1, 2, 3):
        vecs = vecs + links.swap(vecs, where)
    vecs = links.total(vecs)

    down_final = jnp.concatenate(down_parts, axis=-1)
    weight = lambda part: jnp.swapaxes(links.last(part, 0), 0, 1)
    return (
        block_output,
        pixel_grads,
        kernel_grads,
        vecs[2],
        vecs[0],
        vecs[1],
        vecs[3],
        vecs[4],
        weight(qkv_final),
        weight(out_final),
        weight(up_final),
        weight(down_final),
    )


def solution(mesh):
    placed = (
        P("dp", "band", None, None),
        P("dp", None),
        P("band", None, None),
        P(),
        P(),
        P(),
        P(),
        P(),
        P(),
        P(),
        P(),
        P(),
        P(("dp", "band"), None, None),
    )
    return jax.shard_map(
        functools.partial(shards, Links(mesh)),
        mesh=mesh,
        in_specs=placed,
        out_specs=(
            P(("dp", "band"), None, None),
            P("dp", "band", None, None),
            P("band", None, None),
            P(),
            P(),
            P(),
            P(),
            P(),
            P("band", "dp"),
            P("band", "dp"),
            P("band", "dp"),
            P("band", "dp"),
        ),
        check_vma=False,
    )
```

```python
import functools

import jax
import jax.numpy as jnp
from jax import lax
from jax.experimental import pallas as pl
from jax.experimental.pallas import tpu as pltpu
from jax.sharding import PartitionSpec as P

HEADS = 12
HEAD = 64
BF = jnp.bfloat16
F32 = jnp.float32
TAIL = 16
BLOCK = 112
KEYS = 80
SCALE = HEAD ** (-0.5)


def dot(a, b):
    return jnp.dot(a, b, preferred_element_type=F32)


def dot_nt(a, b):
    return lax.dot_general(a, b, (((1,), (1,)), ((), ())), preferred_element_type=F32)


def dot_tn(a, b):
    return lax.dot_general(a, b, (((0,), (0,)), ((), ())), preferred_element_type=F32)


def params(mib, *semantics):
    return pltpu.CompilerParams(
        vmem_limit_bytes=mib * 1024 * 1024,
        dimension_semantics=semantics if semantics else None,
    )


def cost(flops, moved):
    return pl.CostEstimate(flops=int(flops), bytes_accessed=int(moved), transcendentals=0)


def chosen(seen_ref, patches):
    slots = seen_ref.shape[2] // 2
    ids = lax.broadcasted_iota(jnp.int32, (patches, 2 * slots), 0)
    lane = lax.broadcasted_iota(jnp.int32, (patches, 2 * slots), 1)
    hit = ids == seen_ref[0]
    first = jnp.where(hit & (lane < slots), 1.0, 0.0).astype(BF)
    second = jnp.where(hit & (lane >= slots), 1.0, 0.0).astype(BF)
    return first, second


def pick_kernel(where_ref, seen_ref, pixel_ref, half_ref, out_ref, half_out_ref):
    first, second = chosen(seen_ref, pixel_ref.shape[2])
    out_ref[...] = (dot(pixel_ref[0], first) + dot(pixel_ref[1], second)).astype(BF)

    @pl.when(pl.program_id(0) == 0)
    def _():
        half_out_ref[...] = half_ref[...]


def pick(where, pixel_rows, seen_pairs, halves, pairs):
    chips, depth, patches = pixel_rows.shape
    wide = seen_pairs.shape[2]
    half, width = halves.shape[1:]
    return pl.pallas_call(
        pick_kernel,
        out_shape=(
            jax.ShapeDtypeStruct((depth, pairs * wide), BF),
            jax.ShapeDtypeStruct((half, width), BF),
        ),
        grid_spec=pltpu.PrefetchScalarGridSpec(
            num_scalar_prefetch=1,
            grid=(pairs,),
            in_specs=[
                pl.BlockSpec((1, 1, wide), lambda i, w: (w[0] + i, 0, 0)),
                pl.BlockSpec((2, depth, patches), lambda i, w: (w[0] + i, 0, 0)),
                pl.BlockSpec((None, half, width), lambda i, w: (w[1], 0, 0)),
            ],
            out_specs=(
                pl.BlockSpec((depth, wide), lambda i, w: (0, i)),
                pl.BlockSpec((half, width), lambda i, w: (0, 0)),
            ),
        ),
        compiler_params=params(12, "arbitrary"),
        cost_estimate=cost(
            2 * pairs * 2 * depth * patches * 256, pairs * 2 * depth * patches * 2
        ),
        name="pick",
    )(where, seen_pairs, pixel_rows, halves)


def row_stats(values):
    average = jnp.mean(values, axis=-1, keepdims=True)
    centred = values - average
    spread = jnp.mean(centred * centred, axis=-1, keepdims=True)
    root = lax.rsqrt(spread + 1e-06)
    return centred * root, root


def norm_back(xhat, root, grad_out, gain):
    scaled = grad_out * gain
    mean_scaled = jnp.mean(scaled, axis=-1, keepdims=True)
    mean_along = jnp.mean(scaled * xhat, axis=-1, keepdims=True)
    return root * (scaled - mean_scaled - xhat * mean_along)


def head_rows(width):
    row = lax.broadcasted_iota(jnp.int32, (TAIL, width), 0)
    lane = lax.broadcasted_iota(jnp.int32, (TAIL, width), 1)
    return (lane // HEAD) == row


def two_heads(pair):
    low = lax.broadcasted_iota(jnp.int32, pair.shape, 1) < HEAD
    zero = jnp.zeros_like(pair)
    return jnp.concatenate([jnp.where(low, pair, zero), jnp.where(low, zero, pair)], axis=0)


def own_heads(stacked):
    rows = stacked.shape[0] // 2
    low = lax.broadcasted_iota(jnp.int32, (rows, stacked.shape[1]), 1) < HEAD
    return jnp.where(low, stacked[:rows], stacked[rows:])


def softmax_keys(scores, count):
    key = lax.broadcasted_iota(jnp.int32, scores.shape, 0)
    scores = jnp.where(key < count, scores * SCALE, -1e30)
    raised = jnp.exp(scores - jnp.max(scores, axis=0, keepdims=True))
    return raised * (1.0 / jnp.sum(raised, axis=0, keepdims=True))


def forward_kernel(
    chips,
    xo_ref,
    xr_ref,
    ko_ref,
    kr_ref,
    token_ref,
    gain1_ref,
    bias1_ref,
    gain2_ref,
    bias2_ref,
    wqkv_ref,
    wout_ref,
    after_ref,
    stream_ref,
    n1_ref,
    packed_ref,
    probs_ref,
    tprobs_ref,
    att_ref,
    mid_ref,
    n2_ref,
    tatt_ref,
):
    rows, width = n1_ref.shape
    body = rows - TAIL
    slots = body // chips
    stream_ref[0:body, :] = dot_tn(xo_ref[...], ko_ref[...]) + dot_tn(xr_ref[...], kr_ref[...])
    tail_row = lax.broadcasted_iota(jnp.int32, (TAIL, width), 0)
    stream_ref[body:rows, :] = jnp.where(tail_row < chips, token_ref[...], 0.0)

    def first_norm(i, carry):
        at = pl.ds(pl.multiple_of(i * BLOCK, BLOCK), BLOCK)
        xhat, unused = row_stats(stream_ref[at, :])
        n1_ref[at, :] = (xhat * gain1_ref[...] + bias1_ref[...]).astype(BF)
        return carry

    lax.fori_loop(0, rows // BLOCK, first_norm, 0)

    def project(j, carry):
        at = pl.ds(pl.multiple_of(j * 256, 256), 256)
        packed_ref[:, at] = dot(n1_ref[...], wqkv_ref[:, at]).astype(BF)
        return carry

    lax.fori_loop(0, 3 * width // 256, project, 0)
    tail = packed_ref[body:rows, :]
    heads = head_rows(width)
    tquery = jnp.where(heads, jnp.broadcast_to(tail[0:1, 0:width], (TAIL, width)), 0).astype(BF)
    tatt_ref[...] = jnp.zeros_like(tatt_ref)

    def chip(c, carry):
        at = pl.ds(pl.multiple_of(c * slots, slots), slots)
        key = jnp.concatenate(
            [packed_ref[at, width : 2 * width], tail[:, width : 2 * width]], axis=0
        )
        val = jnp.concatenate([packed_ref[at, 2 * width :], tail[:, 2 * width :]], axis=0)
        tiles = [slice(128 * p, 128 * p + 128) for p in range(width // 128)]
        scores = [dot_nt(key[:, here], two_heads(packed_ref[at, here])) for here in tiles]
        scores.append(dot_nt(key, tquery))
        probs = [softmax_keys(s, slots + 1).astype(BF) for s in scores]
        mixed = [dot_tn(probs[p], val[:, tiles[p]]) for p in range(len(tiles))]
        mixed.append(dot_tn(probs[-1], val))
        for p in range(len(tiles)):
            probs_ref[c, p] = probs[p]
            att_ref[at, tiles[p]] = own_heads(mixed[p]).astype(BF)
        tprobs_ref[c] = probs[-1]
        tatt_ref[pl.ds(c, 1), :] = jnp.sum(jnp.where(heads, mixed[-1], 0.0), axis=0, keepdims=True)
        return carry

    lax.fori_loop(0, chips, chip, 0)
    att_ref[body:rows, :] = tatt_ref[...].astype(BF)

    def out_project(j, carry):
        at = pl.ds(pl.multiple_of(j * 256, 256), 256)
        mid_ref[:, at] = stream_ref[:, at] + dot(att_ref[...], wout_ref[:, at])
        return carry

    lax.fori_loop(0, width // 256, out_project, 0)

    def second_norm(i, carry):
        at = pl.ds(pl.multiple_of(i * BLOCK, BLOCK), BLOCK)
        xhat, unused = row_stats(mid_ref[at, :])
        n2_ref[at, :] = (xhat * gain2_ref[...] + bias2_ref[...]).astype(BF)
        return carry

    lax.fori_loop(0, rows // BLOCK, second_norm, 0)


def forward(chips, xo, xr, ko, kr, token, gain1, bias1, gain2, bias2, wqkv, wout, after):
    width = wout.shape[0]
    body = xo.shape[1]
    rows = body + TAIL
    shape = jax.ShapeDtypeStruct
    return pl.pallas_call(
        functools.partial(forward_kernel, chips),
        out_shape=(
            shape((rows, width), F32),
            shape((rows, width), BF),
            shape((rows, 3 * width), BF),
            shape((chips, width // 128, KEYS, 128), BF),
            shape((chips, KEYS, TAIL), BF),
            shape((rows, width), BF),
            shape((rows, width), F32),
            shape((rows, width), BF),
        ),
        in_specs=[pl.BlockSpec(memory_space=pltpu.VMEM)] * 11
        + [pl.BlockSpec(memory_space=pl.ANY)],
        scratch_shapes=[pltpu.VMEM((TAIL, width), F32)],
        compiler_params=params(32),
        cost_estimate=cost(2 * rows * width * width * 8, 20e6),
        name="encoder_forward",
    )(xo, xr, ko, kr, token, gain1, bias1, gain2, bias2, wqkv, wout, after)


def act_grad_kernel(cot_ref, down_ref, out_ref):
    out_ref[...] = dot_nt(cot_ref[...], down_ref[...]).astype(BF)


def act_grad(cot, down):
    rows, width = cot.shape
    hidden = down.shape[0]
    chunk = hidden // 4
    return pl.pallas_call(
        act_grad_kernel,
        out_shape=jax.ShapeDtypeStruct((rows, hidden), BF),
        grid=(4,),
        in_specs=[
            pl.BlockSpec(memory_space=pltpu.VMEM),
            pl.BlockSpec((chunk, width), lambda i: (i, 0)),
        ],
        out_specs=pl.BlockSpec((rows, chunk), lambda i: (0, i)),
        compiler_params=params(12, "arbitrary"),
        cost_estimate=cost(2 * rows * width * hidden, 10e6),
        name="act_grad",
    )(cot, down)


def mlp_kernel(
    split,
    after,
    core_ref,
    n2_ref,
    cot_t_ref,
    gact_ref,
    up_ref,
    down_ref,
    out_in_ref,
    back_in_ref,
    *rest,
):
    down_send_ref, down_keep_ref, up_send_ref, up_keep_ref, out_ref, back_ref = rest[after : after + 6]
    act_ref, gpre_ref, grad_ref = rest[after + 6 :]
    step = pl.program_id(0)

    @pl.when(step == 0)
    def _():
        out_ref[...] = out_in_ref[...]
        back_ref[...] = back_in_ref[...]

    rows, width = n2_ref.shape
    half_rows = width // 2
    for low, high in ((0, split), (split, rows)):
        pre = dot(n2_ref[low:high, :], up_ref[...])
        half = 0.5 + 0.5 * lax.erf(pre * (0.5**0.5))
        bell = jnp.exp(-0.5 * pre * pre) * 0.3989422804014327
        act_ref[low:high, :] = (pre * half).astype(BF)
        gact = gact_ref[low:high, :].astype(F32)
        gpre_ref[low:high, :] = (gact * (half + pre * bell)).astype(BF)
    down_grad = dot(cot_t_ref[...], act_ref[...]).astype(BF)
    for c, ref in ((0, down_send_ref), (1, down_keep_ref)):
        for x in range(2):
            base = (c * 2 + x) * (half_rows // 2)
            for h in range(2):
                ref[x, 0, h] = down_grad[
                    base : base + half_rows // 2, h * half_rows : (h + 1) * half_rows
                ]
    grad_ref[...] = dot_tn(gpre_ref[...], n2_ref[...]).astype(BF)
    part = grad_ref.shape[0] // 4
    core = core_ref[0]
    for x in range(2):
        sent = grad_ref[pl.ds(pl.multiple_of((2 * x + 1 - core) * part, 16), part), :]
        kept = grad_ref[pl.ds(pl.multiple_of((2 * x + core) * part, 16), part), :]
        for b in range(2):
            cols = slice(b * half_rows, (b + 1) * half_rows)
            up_send_ref[0, x, b] = sent[:, cols]
            up_keep_ref[0, x, b] = kept[:, cols]
    out_ref[...] += dot(act_ref[...], down_ref[...])
    back_ref[...] += dot_nt(gpre_ref[...], up_ref[...])


def mlp(third, core, n2, cot_t, gact, up, down, out_in, back_in, after=()):
    rows, width = n2.shape
    hidden = up.shape[1]
    chunk = hidden // 4
    part = chunk // 4
    half = width // 2
    shape = jax.ShapeDtypeStruct
    vmem = pl.BlockSpec(memory_space=pltpu.VMEM)
    at = lambda i: i * 2 + third
    down_shape = shape((2, 2, 2, width // 4, half), BF)
    down_spec = pl.BlockSpec((2, 1, 2, width // 4, half), lambda i, core: (0, i, 0, 0, 0))
    up_shape = shape((2, 2, 2, part, half), BF)
    up_spec = pl.BlockSpec((1, 2, 2, part, half), lambda i, core: (i, 0, 0, 0, 0))
    return pl.pallas_call(
        functools.partial(mlp_kernel, rows // 32 * 16, len(after)),
        out_shape=(
            down_shape,
            down_shape,
            up_shape,
            up_shape,
            shape((rows, width), F32),
            shape((rows, width), F32),
        ),
        grid_spec=pltpu.PrefetchScalarGridSpec(
            num_scalar_prefetch=1,
            grid=(2,),
            in_specs=[
                vmem,
                vmem,
                pl.BlockSpec((rows, chunk), lambda i, core: (0, at(i))),
                pl.BlockSpec((width, chunk), lambda i, core: (0, at(i))),
                pl.BlockSpec((chunk, width), lambda i, core: (at(i), 0)),
                vmem,
                vmem,
            ]
            + [pl.BlockSpec(memory_space=pl.ANY)] * len(after),
            out_specs=(down_spec, down_spec, up_spec, up_spec, vmem, vmem),
            scratch_shapes=[
                pltpu.VMEM((rows, chunk), BF),
                pltpu.VMEM((rows, chunk), BF),
                pltpu.VMEM((chunk, width), BF),
            ],
        ),
        compiler_params=params(30, "arbitrary"),
        cost_estimate=cost(2 * rows * width * hidden * 3, 25e6),
        name="mlp_both_ways",
    )(core, n2, cot_t, gact, up, down, out_in, back_in, *after)


def spread_blocks(full_ref, send_refs, keep_refs, core):
    cols = full_ref.shape[1] // 2
    parts = len(send_refs)
    block = full_ref.shape[0] // 16
    piece = block // parts
    for z in range(4):
        for x in range(2):
            base = (z * 2 + x) * 2
            for refs, c in ((send_refs, 1 - core), (keep_refs, core)):
                for k in range(parts):
                    start = pl.multiple_of((base + c) * block + k * piece, 16)
                    rows = full_ref[pl.ds(start, piece), :]
                    for b in range(2):
                        refs[k][x, b, z] = rows[:, b * cols : (b + 1) * cols]


def attention_back_kernel(
    chips,
    core_ref,
    back_ref,
    mid_ref,
    cot_ref,
    gain2_ref,
    wout_ref,
    att_ref,
    packed_ref,
    probs_ref,
    tprobs_ref,
    *rest,
):
    gmid_ref, gpacked_ref, out_send_ref, out_keep_ref, vec_ref = rest[-10:-5]
    branch_ref, gatt_ref, full_ref, tgrad_ref, tout_ref = rest[-5:]
    rows, width = mid_ref.shape
    body = rows - TAIL
    slots = body // chips

    def norm(i, carry):
        at = pl.ds(pl.multiple_of(i * BLOCK, BLOCK), BLOCK)
        xhat, root = row_stats(mid_ref[at, :])
        grad = back_ref[at, :]
        back = norm_back(xhat, root, grad, gain2_ref[...])
        total = cot_ref[at, :].astype(F32) + back
        gmid_ref[at, :] = total
        branch_ref[at, :] = total.astype(BF)
        return (
            carry[0] + jnp.sum(grad * xhat, axis=0, keepdims=True),
            carry[1] + jnp.sum(grad, axis=0, keepdims=True),
        )

    zero = jnp.zeros((1, width), F32)
    gain_sum, bias_sum = lax.fori_loop(0, rows // BLOCK, norm, (zero, zero))
    vec_ref[0:1, :] = gain_sum
    vec_ref[1:2, :] = bias_sum

    full_ref[...] = dot_tn(branch_ref[...], att_ref[...]).astype(BF)
    spread_blocks(full_ref, [out_send_ref], [out_keep_ref], core_ref[0])

    gatt = dot_nt(branch_ref[...], wout_ref[...])
    gatt_ref[...] = gatt[:body].astype(BF)
    tgrad_ref[...] = gatt[body:].astype(BF).astype(F32)
    tout_ref[...] = jnp.zeros_like(tout_ref)
    tail = packed_ref[body:rows, :]
    heads = head_rows(width)
    tquery = jnp.where(heads, jnp.broadcast_to(tail[0:1, 0:width], (TAIL, width)), 0).astype(BF)

    def chip(c, carry):
        at = pl.ds(pl.multiple_of(c * slots, slots), slots)
        key_all = jnp.concatenate(
            [packed_ref[at, width : 2 * width], tail[:, width : 2 * width]], axis=0
        )
        val_all = jnp.concatenate([packed_ref[at, 2 * width :], tail[:, 2 * width :]], axis=0)
        tgrad = jnp.where(
            heads, jnp.broadcast_to(tgrad_ref[pl.ds(c, 1), :], (TAIL, width)), 0.0
        ).astype(BF)
        tprobs = tprobs_ref[c]
        tiles = [slice(128 * p, 128 * p + 128) for p in range(width // 128)]
        probs = [probs_ref[c, p] for p in range(len(tiles))] + [tprobs]
        gouts = [two_heads(gatt_ref[at, here]) for here in tiles]
        queries = [two_heads(packed_ref[at, here]) for here in tiles]
        gprobs = [dot_nt(val_all[:, tiles[p]], gouts[p]) for p in range(len(tiles))]
        gprobs.append(dot_nt(val_all, tgrad))
        gscores = []
        for prob, gprob in zip(probs, gprobs):
            wide = prob.astype(F32)
            inner = jnp.sum(gprob * wide, axis=0, keepdims=True)
            gscores.append((wide * (gprob - inner) * SCALE).astype(BF))
        gval_tail = dot(tprobs, tgrad)
        gkey_tail = dot(gscores[-1], tquery)
        mixed = jnp.where(heads, dot_tn(gscores[-1], key_all), 0.0)
        gvals = [dot(probs[p], gouts[p]) + gval_tail[:, tiles[p]] for p in range(len(tiles))]
        gkeys = [dot(gscores[p], queries[p]) + gkey_tail[:, tiles[p]] for p in range(len(tiles))]
        gqueries = [own_heads(dot_tn(gscores[p], key_all[:, tiles[p]])) for p in range(len(tiles))]
        for p in range(len(tiles)):
            gpacked_ref[at, 128 * p : 128 * p + 128] = gqueries[p].astype(BF)
            base = width + 128 * p
            gpacked_ref[at, base : base + 128] = gkeys[p][:slots].astype(BF)
            gpacked_ref[at, width + base : width + base + 128] = gvals[p][:slots].astype(BF)
        tout_ref[pl.ds(c, 1), :] = jnp.concatenate(
            [jnp.sum(mixed, axis=0, keepdims=True)]
            + [g[slots : slots + 1] for g in gkeys + gvals],
            axis=1,
        )
        return carry

    lax.fori_loop(0, chips, chip, 0)
    gpacked_ref[body:rows, :] = tout_ref[...].astype(BF)


def attention_back(chips, core, back, mid, cot, gain2, wout, att, packed, probs, tprobs, after):
    rows, width = mid.shape
    shape = jax.ShapeDtypeStruct
    block = width // 16
    vmem = pl.BlockSpec(memory_space=pltpu.VMEM)
    return pl.pallas_call(
        functools.partial(attention_back_kernel, chips),
        out_shape=(
            shape((rows, width), F32),
            shape((rows, 3 * width), BF),
            shape((2, 2, 4, block, width // 2), BF),
            shape((2, 2, 4, block, width // 2), BF),
            shape((2, width), F32),
        ),
        in_specs=[pl.BlockSpec(memory_space=pltpu.SMEM)]
        + [vmem] * 9
        + [pl.BlockSpec(memory_space=pl.ANY)] * len(after),
        out_specs=(vmem,) * 5,
        scratch_shapes=[
            pltpu.VMEM((rows, width), BF),
            pltpu.VMEM((rows - TAIL, width), BF),
            pltpu.VMEM((width, width), BF),
            pltpu.VMEM((TAIL, width), F32),
            pltpu.VMEM((TAIL, 3 * width), F32),
        ],
        compiler_params=params(32),
        cost_estimate=cost(2 * rows * width * width * 6, 20e6),
        name="attention_back",
    )(core, back, mid, cot, gain2, wout, att, packed, probs, tprobs, *after)


def embed_back_kernel(
    chips,
    bits_ref,
    gpacked_ref,
    wqkv_ref,
    stream_ref,
    gmid_ref,
    gain1_ref,
    vec2_ref,
    xo_ref,
    xr_ref,
    ko_ref,
    kr_ref,
    *rest,
):
    (
        kgrad_send_ref,
        kgrad_keep_ref,
        vec_ref,
        pgrad_own_ref,
        pgrad_far_ref,
        back_ref,
        embed_ref,
        full_ref,
    ) = rest[-8:]
    rows, width = stream_ref.shape
    body = rows - TAIL
    half = width // 2

    back_ref[...] = dot_nt(gpacked_ref[...], wqkv_ref[...])

    def norm(i, carry):
        at = pl.ds(pl.multiple_of(i * BLOCK, BLOCK), BLOCK)
        xhat, root = row_stats(stream_ref[at, :])
        grad = back_ref[at, :]
        total = gmid_ref[at, :] + norm_back(xhat, root, grad, gain1_ref[...])
        back_ref[at, :] = total
        embed_ref[at, :] = total.astype(BF)
        return (
            carry[0] + jnp.sum(grad * xhat, axis=0, keepdims=True),
            carry[1] + jnp.sum(grad, axis=0, keepdims=True),
        )

    zero = jnp.zeros((1, width), F32)
    gain_sum, bias_sum = lax.fori_loop(0, rows // BLOCK, norm, (zero, zero))
    token_sum = jnp.sum(back_ref[body:rows, :], axis=0, keepdims=True)
    vec_ref[...] = jnp.zeros_like(vec_ref)
    for i, v in enumerate((gain_sum, bias_sum, token_sum, vec2_ref[0:1, :], vec2_ref[1:2, :])):
        vec_ref[2 * i : 2 * i + 1, :] = v[:, :half]
        vec_ref[2 * i + 1 : 2 * i + 2, :] = v[:, half:]
    grad = embed_ref[0:body, :]
    depth = xo_ref.shape[0]
    core, band = bits_ref[0], bits_ref[4]
    full_ref[0] = dot(xo_ref[...], grad).astype(BF)
    full_ref[1] = dot(xr_ref[...], grad).astype(BF)
    piece = depth // 4
    for where, c, ref in ((0, 1 - core, kgrad_send_ref), (1, core, kgrad_keep_ref)):
        for far in range(2):
            for x in range(2):
                start = pl.multiple_of(c * (depth // 2) + x * piece, 16)
                block = full_ref[far, pl.ds(start, piece), :]
                for h in range(2):
                    slot = ((far + band - 2 * far * band) * 2 + x) * 2 + h
                    to = pl.ds(pl.multiple_of(slot * piece, 16), piece)
                    ref[to, :] = block[:, h * half : (h + 1) * half]
    put_vec(vec_ref[...], kgrad_send_ref, 2 * depth)
    pgrad_far_ref[...] = dot_nt(kr_ref[...], grad).astype(BF)
    pgrad_own_ref[...] = dot_nt(ko_ref[...], grad).astype(BF)


def put_vec(vec, ref, at):
    high = vec.astype(BF)
    ref[at : at + 16, :] = high
    ref[at + 16 : at + 32, :] = (vec - high.astype(F32)).astype(BF)


def get_vec(ref, at):
    return ref[at : at + 16, :].astype(F32) + ref[at + 16 : at + 32, :].astype(F32)


def embed_back(chips, bits, gpacked, wqkv, stream, gmid, gain1, vec2, xo, xr, ko, kr, after):
    rows, width = stream.shape
    depth, body = xo.shape
    shape = jax.ShapeDtypeStruct
    vmem = pl.BlockSpec(memory_space=pltpu.VMEM)
    return pl.pallas_call(
        functools.partial(embed_back_kernel, chips),
        out_shape=(
            shape((2 * depth + 32, width // 2), BF),
            shape((2 * depth, width // 2), BF),
            shape((16, width // 2), F32),
            shape((depth, body), BF),
            shape((depth, body), BF),
        ),
        in_specs=[pl.BlockSpec(memory_space=pltpu.SMEM)]
        + [vmem] * 10
        + [pl.BlockSpec(memory_space=pl.ANY)] * len(after),
        scratch_shapes=[
            pltpu.VMEM((rows, width), F32),
            pltpu.VMEM((rows, width), BF),
            pltpu.VMEM((2, depth, width), BF),
        ],
        compiler_params=params(30),
        cost_estimate=cost(2 * rows * width * width * 5, 15e6),
        name="embed_back",
    )(bits, gpacked, wqkv, stream, gmid, gain1, vec2, xo, xr, ko, kr, *after)


def qkv_grad_kernel(core_ref, gpacked_ref, n1_ref, *rest):
    sends, keeps, full_ref = rest[-7:-4], rest[-4:-1], rest[-1]
    tile = n1_ref.shape[1] // 2

    def step(j, carry):
        at = pl.ds(pl.multiple_of(j * tile, tile), tile)
        full_ref[at, :] = dot_tn(gpacked_ref[:, at], n1_ref[...]).astype(BF)
        return carry

    lax.fori_loop(0, full_ref.shape[0] // tile, step, 0)
    spread_blocks(full_ref, sends, keeps, core_ref[0])


def qkv_grad(core, gpacked, n1, after):
    rows, width = n1.shape
    shape = jax.ShapeDtypeStruct
    vmem = pl.BlockSpec(memory_space=pltpu.VMEM)
    block = width // 16
    return pl.pallas_call(
        qkv_grad_kernel,
        out_shape=(shape((2, 2, 4, block, width // 2), BF),) * 6,
        in_specs=[pl.BlockSpec(memory_space=pltpu.SMEM), vmem, vmem]
        + [pl.BlockSpec(memory_space=pl.ANY)] * len(after),
        out_specs=(vmem,) * 6,
        scratch_shapes=[pltpu.VMEM((3 * width, width), BF)],
        compiler_params=params(24),
        cost_estimate=cost(2 * rows * width * width * 3, 8e6),
        name="qkv_grad",
    )(core, gpacked, n1, *after)


def scatter_kernel(base_ref, seen_ref, grad_ref, *rest):
    out_ref = rest[-1]
    first, second = chosen(seen_ref, out_ref.shape[2])
    out_ref[0] = dot_nt(grad_ref[...], first)
    out_ref[1] = dot_nt(grad_ref[...], second)


def scatter(base, grads, seen_pairs, patches, earlier=None):
    depth = grads.shape[0]
    wide = seen_pairs.shape[2]
    pairs = grads.shape[1] // wide
    chips = 2 * seen_pairs.shape[0]
    in_specs = [
        pl.BlockSpec((1, 1, wide), lambda i, base: (base[0] + i, 0, 0)),
        pl.BlockSpec((depth, wide), lambda i, base: (0, i)),
    ]
    operands = (base, seen_pairs, grads)
    alias = {}
    if earlier is not None:
        in_specs.append(pl.BlockSpec(memory_space=pl.ANY))
        operands = operands + (earlier,)
        alias = {3: 0}
    return pl.pallas_call(
        scatter_kernel,
        out_shape=jax.ShapeDtypeStruct((chips, depth, patches), F32),
        grid_spec=pltpu.PrefetchScalarGridSpec(
            num_scalar_prefetch=1,
            grid=(pairs,),
            in_specs=in_specs,
            out_specs=pl.BlockSpec((2, depth, patches), lambda i, base: (base[0] + i, 0, 0)),
        ),
        input_output_aliases=alias,
        compiler_params=params(12, "arbitrary"),
        cost_estimate=cost(2 * pairs * 2 * depth * patches * wide, pairs * 2 * depth * patches * 4),
        name="scatter",
    )(*operands)


class Links:
    def __init__(self, mesh):
        self.count = mesh.shape["dp"]
        self.extra = self.count // 16

    def swap(self, array, where):
        if where == "band":
            return lax.ppermute(array, "band", [(0, 1), (1, 0)])
        flip = (1 << where) * self.extra
        return lax.ppermute(array, "dp", [(d, d ^ flip) for d in range(self.count)])

    def bit(self, where):
        if where == "band":
            return lax.axis_index("band")
        return (lax.axis_index("dp") // self.extra // (1 << where)) % 2

    def groups(self):
        return [[block * self.extra + i for i in range(self.extra)] for block in range(16)]

    def last(self, array):
        if self.extra == 1:
            return array
        return lax.psum_scatter(
            array, "dp", scatter_dimension=0, tiled=True, axis_index_groups=self.groups()
        )

    def total(self, array):
        if self.extra == 1:
            return array
        return lax.psum(array, "dp", axis_index_groups=self.groups())


SLOT = {0: 0, 1: 1, 2: 2, 3: 3, "band": 4}


class Piece:
    def __init__(self, names, sizes, unit, kept, recv=None, at=0, vec=False):
        self.names, self.sizes, self.unit = list(names), list(sizes), unit
        self.kept = kept if vec else kept.reshape(-1, kept.shape[-1])
        self.recv, self.at, self.vec = recv, at, vec

    def rows(self):
        count = self.unit
        for size in self.sizes:
            count = count * size
        return count

    def value(self):
        if self.vec:
            part = self.recv[self.at : self.at + 32].astype(F32)
            return self.kept + part[:16] + part[16:]
        total = self.kept.astype(F32)
        if self.recv is not None:
            total = total + self.recv[self.at : self.at + self.rows()].astype(F32)
        return total.reshape(tuple(self.sizes) + (self.unit, total.shape[-1]))


def combine_kernel(jobs, recvs, sends, bits_ref, *refs):
    kept_in = refs[: len(jobs)]
    recv_in = refs[len(jobs) : len(jobs) + recvs]
    send_out = refs[len(jobs) + recvs : len(jobs) + recvs + sends]
    kept_out = refs[len(jobs) + recvs + sends :]
    for job, kept, new in zip(jobs, kept_in, kept_out):
        recv = None if job["recv"] is None else recv_in[job["recv"]]
        send = send_out[job["send"]]
        at, to = job["at"], job["to"]
        if job["vec"]:
            total = kept[...] + get_vec(recv, at)
            new[...] = total
            put_vec(total, send, to)
            continue
        pre, post = job["pre"], job["post"]
        if pre is None:
            total = kept[...] + recv[at : at + post, :]
            new[...] = total
            send[to : to + post, :] = total
            continue
        bit = bits_ref[job["slot"]]
        for p in range(pre):
            for side, ref, start in ((1 - bit, send, to), (bit, new, 0)):
                source = (2 * p + side) * post
                total = kept[pl.ds(pl.multiple_of(source, 16), post), :]
                if recv is not None:
                    total = total + recv[pl.ds(pl.multiple_of(source + at, 16), post), :]
                ref[start + p * post : start + (p + 1) * post, :] = total


def combine(links, bits, steps):
    jobs, recv_list, kept_shapes, where_list, sizes = [], [], [], [], {}
    width = steps[0][0].kept.shape[-1]
    for piece, where, split in steps:
        if where not in where_list:
            where_list.append(where)
            sizes[where] = 0
        job = {"vec": piece.vec, "at": piece.at, "recv": None, "pre": None, "post": piece.rows()}
        if piece.recv is not None:
            found = [i for i, r in enumerate(recv_list) if r is piece.recv]
            if not found:
                recv_list.append(piece.recv)
                found = [len(recv_list) - 1]
            job["recv"] = found[0]
        job["send"], job["to"] = where_list.index(where), sizes[where]
        if piece.vec:
            sent, shape = 32, jax.ShapeDtypeStruct((16, width), F32)
        elif split:
            dim = piece.names.index(where)
            pre = 1
            for size in piece.sizes[:dim]:
                pre = pre * size
            sent = piece.rows() // 2
            job.update(pre=pre, post=sent // pre, slot=SLOT[where])
            shape = jax.ShapeDtypeStruct((sent, width), BF)
        else:
            sent = piece.rows()
            shape = jax.ShapeDtypeStruct((sent, width), BF)
        sizes[where] += sent
        kept_shapes.append(shape)
        jobs.append(job)
    vmem = pl.BlockSpec(memory_space=pltpu.VMEM)
    outs = pl.pallas_call(
        functools.partial(combine_kernel, jobs, len(recv_list), len(where_list)),
        out_shape=tuple(jax.ShapeDtypeStruct((sizes[w], width), BF) for w in where_list)
        + tuple(kept_shapes),
        in_specs=[pl.BlockSpec(memory_space=pltpu.SMEM)] + [vmem] * (len(jobs) + len(recv_list)),
        out_specs=(vmem,) * (len(where_list) + len(jobs)),
        compiler_params=params(28),
        cost_estimate=cost(1e6, 6e6),
        name="combine",
    )(bits, *[piece.kept for piece, unused, also in steps], *recv_list)
    sends = outs[: len(where_list)]
    came = [links.swap(send, where) for send, where in zip(sends, where_list)]
    for (piece, where, split), job, kept in zip(steps, jobs, outs[len(where_list) :]):
        piece.kept, piece.recv, piece.at = kept, came[job["send"]], job["to"]
        if split and not piece.vec:
            dim = piece.names.index(where)
            piece.names.pop(dim)
            piece.sizes.pop(dim)
    return sends


def shards(
    links,
    pixels,
    visible,
    kernels,
    class_token,
    norm1_gain,
    norm1_bias,
    norm2_gain,
    norm2_bias,
    attn_qkv,
    attn_out,
    mlp_up,
    mlp_down,
    cotangent,
):
    width = attn_out.shape[0]
    half = width // 2
    chips, seq = cotangent.shape[0], cotangent.shape[1]
    group_chips, bands, patches, pix = pixels.shape
    slots = visible.shape[1]
    body = chips * slots
    rows = body + TAIL
    depth = bands * pix
    pairs = chips // 2
    block = width // 16
    band = lax.axis_index("band")
    core = links.bit(0)
    core_arg = core.reshape(1).astype(jnp.int32)
    bits = jnp.stack([links.bit(w) for w in (0, 1, 2, 3, "band")]).astype(jnp.int32)

    pixel_rows = jnp.swapaxes(pixels, 2, 3).reshape(group_chips, depth, patches)
    seen_pairs = visible.reshape(group_chips // 2, 1, 2 * slots)
    own_base = (band * pairs).reshape(1).astype(jnp.int32)
    far_base = ((1 - band) * pairs).reshape(1).astype(jnp.int32)
    flat_kernels = kernels.reshape(depth, width)
    halves = flat_kernels.reshape(2, depth // 2, width)
    picked_far, my_half = pick(
        jnp.concatenate([far_base, core_arg]), pixel_rows, seen_pairs, halves, pairs
    )
    picked_in = links.swap(picked_far, "band")
    far_half = links.swap(my_half, "band")
    far_other = links.swap(far_half, 0)
    kernels_far = jnp.where(
        core == 0,
        jnp.concatenate([far_half, far_other], axis=0),
        jnp.concatenate([far_other, far_half], axis=0),
    )
    picked_own, unused_half = pick(
        jnp.concatenate([own_base, core_arg]), pixel_rows, seen_pairs, halves, pairs
    )

    cot_rows = jnp.concatenate(
        [
            cotangent[:, 1:, :].reshape(body, width),
            cotangent[:, 0, :],
            jnp.zeros((TAIL - chips, width), BF),
        ],
        axis=0,
    )
    cot_t = jnp.swapaxes(cot_rows.T.reshape(4, 2, 2, block, rows), 0, 1)
    cot_t = jnp.concatenate(
        [
            lax.dynamic_index_in_dim(cot_t, 1 - core, 2, keepdims=False).reshape(half, rows),
            lax.dynamic_index_in_dim(cot_t, core, 2, keepdims=False).reshape(half, rows),
        ],
        axis=0,
    )
    gact = act_grad(cot_rows, mlp_down)

    row = lambda v: v.reshape(1, width)
    stream, n1, packed, probs, tprobs, att, mid, n2 = forward(
        chips,
        picked_own,
        picked_in,
        flat_kernels,
        kernels_far,
        row(class_token),
        row(norm1_gain),
        row(norm1_bias),
        row(norm2_gain),
        row(norm2_bias),
        attn_qkv,
        attn_out,
        gact,
    )

    def mlp_pieces(third, out_in, back_in, after=()):
        down_send, down_keep, up_send, up_keep, out_rows, back = mlp(
            third, core_arg, n2, cot_t, gact, mlp_up, mlp_down, out_in, back_in, after
        )
        flat = lambda a: a.reshape(-1, half)
        down = Piece(
            (1, "band", "h", 3, 2), (2, 2, 2, 2, 2), block, down_keep, links.swap(flat(down_send), 0)
        )
        up = Piece((3, 1, "band"), (2, 2, 2), 4 * block, up_keep, links.swap(flat(up_send), 0))
        return down, up, out_rows, back

    down1, up1, out_rows, back = mlp_pieces(0, mid, jnp.zeros((rows, width), F32))
    down2, up2, out_rows, back = mlp_pieces(1, out_rows, back)
    tie = combine(links, bits, [(down1, 1, True), (up1, "band", True)])

    block_output = jnp.concatenate(
        [
            out_rows[body : body + chips].astype(BF)[:, None, :],
            out_rows[:body].astype(BF).reshape(chips, slots, width),
        ],
        axis=1,
    )

    gmid, gpacked, out_send, out_keep, vec2 = attention_back(
        chips,
        core_arg,
        back,
        mid,
        cot_rows,
        row(norm2_gain),
        attn_out,
        att,
        packed,
        probs,
        tprobs,
        tie,
    )
    names, sizes = (1, "band", 3, 2), (2, 2, 2, 2)
    outp = Piece(names, sizes, block, out_keep, links.swap(out_send.reshape(-1, half), 0))
    tie = combine(
        links,
        bits,
        [(down1, "band", True), (up1, 1, True), (down2, 1, True), (up2, "band", True)],
    )

    sent = qkv_grad(core_arg, gpacked, n1, tie)
    qkv = [
        Piece(names, sizes, block, keep, links.swap(send.reshape(-1, half), 0))
        for send, keep in zip(sent[:3], sent[3:])
    ]
    kg_send, kg_keep, vec_keep, pgrad_own, pgrad_far = embed_back(
        chips,
        bits,
        gpacked,
        attn_qkv,
        stream,
        gmid,
        row(norm1_gain),
        vec2,
        picked_own,
        picked_in,
        flat_kernels,
        kernels_far,
        (),
    )
    kg_in = links.swap(kg_send, 0)
    kg = Piece(("band", 1, "h"), (2, 2, 2), depth // 4, kg_keep, kg_in)
    vec = Piece((), (), 16, vec_keep, kg_in, 2 * depth, True)
    pgrad_in = links.swap(pgrad_far, "band")

    combine(
        links,
        bits,
        [
            (down1, 2, True),
            (down2, "band", True),
            (up2, 1, True),
            (outp, 1, True),
            (qkv[0], 1, True),
            (qkv[1], "band", True),
            (qkv[2], 2, True),
        ],
    )
    partly = scatter(own_base, pgrad_own, seen_pairs, patches)

    stacked = jnp.stack(
        [piece.value().astype(BF).reshape(2, 4 * block, half) for piece in (up1, up2)], axis=1
    )
    up = Piece((3, 2), (2, 2), 4 * block, stacked)
    combine(
        links,
        bits,
        [
            (kg, "band", True),
            (vec, "band", False),
            (down1, 3, True),
            (down2, 2, True),
            (up, 2, True),
            (outp, "band", True),
            (qkv[0], "band", True),
            (qkv[1], 1, True),
            (qkv[2], 3, True),
        ],
    )
    pixel_grads = scatter(far_base, pgrad_in, seen_pairs, patches, partly)
    pixel_grads = jnp.swapaxes(pixel_grads.reshape(group_chips, bands, pix, patches), 2, 3)

    combine(
        links,
        bits,
        [
            (kg, 1, True),
            (vec, 1, False),
            (down2, 3, True),
            (up, 3, True),
            (outp, 2, True),
            (qkv[0], 2, True),
            (qkv[1], 2, True),
            (qkv[2], 1, True),
        ],
    )
    combine(
        links,
        bits,
        [
            (kg, 2, False),
            (vec, 2, False),
            (outp, 3, True),
            (qkv[0], 3, True),
            (qkv[1], 3, True),
            (qkv[2], "band", True),
        ],
    )
    combine(links, bits, [(kg, 3, False), (vec, 3, False)])
    vecs = links.total(vec.value()).reshape(8, width)
    kgrad = links.total(kg.value()).astype(BF)
    for where in (1, 0):
        other = links.swap(kgrad, where)
        kgrad = jnp.where(
            links.bit(where) == 0, jnp.stack([kgrad, other]), jnp.stack([other, kgrad])
        )
    kernel_grads = jnp.transpose(kgrad.astype(F32), (0, 1, 3, 2, 4)).reshape(bands, pix, width)

    weight = lambda part: jnp.swapaxes(links.last(part), 0, 1)
    down_final = jnp.concatenate([down1.value(), down2.value()], axis=0)
    return (
        block_output,
        pixel_grads,
        kernel_grads,
        vecs[2],
        vecs[0],
        vecs[1],
        vecs[3],
        vecs[4],
        weight(jnp.concatenate([piece.value() for piece in qkv], axis=0)),
        weight(outp.value()),
        weight(up.value()),
        weight(jnp.swapaxes(down_final, 0, 1).reshape(block, 4 * half)),
    )


def solution(mesh):
    placed = (
        P("dp", "band", None, None),
        P("dp", None),
        P("band", None, None),
        P(),
        P(),
        P(),
        P(),
        P(),
        P(),
        P(),
        P(),
        P(),
        P(("dp", "band"), None, None),
    )
    return jax.shard_map(
        functools.partial(shards, Links(mesh)),
        mesh=mesh,
        in_specs=placed,
        out_specs=(
            P(("dp", "band"), None, None),
            P("dp", "band", None, None),
            P("band", None, None),
            P(),
            P(),
            P(),
            P(),
            P(),
            P("band", "dp"),
            P("band", "dp"),
            P("band", "dp"),
            P("band", "dp"),
        ),
        check_vma=False,
    )
```

```python
import functools

import jax
import jax.numpy as jnp
from jax import lax
from jax.experimental import pallas as pl
from jax.experimental.pallas import tpu as pltpu
from jax.sharding import PartitionSpec as P

HEADS = 12
HEAD = 64
BF = jnp.bfloat16
F32 = jnp.float32
TAIL = 16
BLOCK = 112
KEYS = 80
SCALE = HEAD ** (-0.5)
VMEM = pl.BlockSpec(memory_space=pltpu.VMEM)
HBM = pl.BlockSpec(memory_space=pl.ANY)
shape = jax.ShapeDtypeStruct


def dot(a, b):
    return jnp.dot(a, b, preferred_element_type=F32)


def dot_nt(a, b):
    return lax.dot_general(a, b, (((1,), (1,)), ((), ())), preferred_element_type=F32)


def dot_tn(a, b):
    return lax.dot_general(a, b, (((0,), (0,)), ((), ())), preferred_element_type=F32)


def kernel_call(body, name, outs, scratch, copies, vmem_in=0, vmem_out=0, **more):
    def call(*operands):
        return pl.pallas_call(
            body,
            out_shape=tuple(outs),
            in_specs=[VMEM] * vmem_in + [HBM] * (len(operands) - vmem_in),
            out_specs=(HBM,) * (len(outs) - vmem_out) + (VMEM,) * vmem_out,
            scratch_shapes=[pltpu.VMEM(a.shape, a.dtype) for a in scratch]
            + [pltpu.SemaphoreType.DMA((copies,))],
            compiler_params=pltpu.CompilerParams(vmem_limit_bytes=58 * 1024 * 1024),
            cost_estimate=pl.CostEstimate(flops=1, bytes_accessed=1, transcendentals=0),
            name=name,
            **more,
        )(*operands)

    return call


class Copies:
    def __init__(self, sems):
        self.sems, self.count, self.open = sems, 0, []

    def start(self, source, target):
        copy = pltpu.make_async_copy(source, target, self.sems.at[self.count])
        self.count += 1
        copy.start()
        return copy

    def out(self, source, target):
        self.open.append(self.start(source, target))

    def finish(self):
        for copy in self.open:
            copy.wait()


def chosen(seen_ref, chip, patches):
    first = seen_ref[pl.ds(chip, 1), :]
    second = seen_ref[pl.ds(chip + 1, 1), :]
    slots = first.shape[1]
    seen = jnp.concatenate([first, second], axis=1)
    ids = lax.broadcasted_iota(jnp.int32, (patches, 2 * slots), 0)
    lane = lax.broadcasted_iota(jnp.int32, (patches, 2 * slots), 1)
    hit = ids == seen
    return (
        jnp.where(hit & (lane < slots), 1.0, 0.0).astype(BF),
        jnp.where(hit & (lane >= slots), 1.0, 0.0).astype(BF),
    )


def load_pixels(copies, pixel_hbm, pixel_ref, base, pairs):
    return [
        copies.start(pixel_hbm.at[pl.ds(base + 2 * i, 2)], pixel_ref.at[2 * i : 2 * i + 2])
        for i in range(pairs)
    ]


def pick_pixels(arrive, seen_ref, pixel_ref, out_ref, base):
    for i, copy in enumerate(arrive):
        first, second = chosen(seen_ref, base + 2 * i, pixel_ref.shape[2])
        wide = first.shape[1]
        copy.wait()
        out_ref[:, i * wide : (i + 1) * wide] = (
            dot(pixel_ref[2 * i], first) + dot(pixel_ref[2 * i + 1], second)
        ).astype(BF)


def pick_far_kernel(
    links, pairs, seen_ref, pixel_hbm, halves_hbm, half_hbm, out_hbm, pixel_ref, out_ref, half_ref, sems
):
    copies = Copies(sems)
    base = (1 - links.bit("band")) * 2 * pairs
    half_in = copies.start(halves_hbm.at[links.bit(0)], half_ref)
    arrive = load_pixels(copies, pixel_hbm, pixel_ref, base, pairs)
    half_in.wait()
    copies.out(half_ref, half_hbm)
    pick_pixels(arrive, seen_ref, pixel_ref, out_ref, base)
    copies.out(out_ref, out_hbm)
    copies.finish()


def pick_far(links, seen, pixel_rows, halves):
    chips, depth, patches = pixel_rows.shape
    pairs = chips // 4
    outs = (shape(halves.shape[1:], BF), shape((depth, chips // 2 * seen.shape[1]), BF))
    return kernel_call(
        functools.partial(pick_far_kernel, links, pairs),
        "pick_far",
        outs,
        (shape((2 * pairs, depth, patches), BF), outs[1], outs[0]),
        pairs + 4,
        vmem_in=1,
    )(seen, pixel_rows, halves)


def prepare_kernel(
    links,
    pairs,
    seen_ref,
    pixel_hbm,
    cot_hbm,
    down_hbm,
    picked_hbm,
    rows_hbm,
    gact_hbm,
    pixel_ref,
    cot_ref,
    down_ref,
    picked_ref,
    rows_ref,
    gact_ref,
    tail_ref,
    sems,
):
    copies = Copies(sems)
    chips = cot_ref.shape[0]
    slots = cot_ref.shape[1] - 1
    rows, width = rows_ref.shape
    base = links.bit("band") * 2 * pairs
    cot_in = copies.start(cot_hbm, cot_ref)
    arrive = load_pixels(copies, pixel_hbm, pixel_ref, base, pairs)
    chunk = down_hbm.shape[0] // 4
    parts = [slice(i * chunk, (i + 1) * chunk) for i in range(4)]
    downs = [copies.start(down_hbm.at[part, :], down_ref.at[part, :]) for part in parts]
    cot_in.wait()
    tail_ref[...] = jnp.zeros_like(tail_ref)
    for c in range(chips):
        chip = cot_ref[c].astype(F32)
        rows_ref[c * slots : (c + 1) * slots, :] = chip[1:, :].astype(BF)
        tail_ref[c : c + 1, :] = chip[0:1, :]
    rows_ref[rows - TAIL : rows, :] = tail_ref[...].astype(BF)
    copies.out(rows_ref, rows_hbm)
    pick_pixels(arrive, seen_ref, pixel_ref, picked_ref, base)
    copies.out(picked_ref, picked_hbm)
    for part, copy in zip(parts, downs):
        copy.wait()
        gact_ref[:, part] = dot_nt(rows_ref[...], down_ref[part, :]).astype(BF)
        copies.out(gact_ref.at[:, part], gact_hbm.at[:, part])
    copies.finish()


def prepare(links, seen, pixel_rows, cot, down):
    group, depth, patches = pixel_rows.shape
    pairs = group // 4
    hidden, width = down.shape
    body = cot.shape[0] * seen.shape[1]
    rows = body + TAIL
    outs = (shape((depth, body), BF), shape((rows, width), BF), shape((rows, hidden), BF))
    return kernel_call(
        functools.partial(prepare_kernel, links, pairs),
        "prepare",
        outs,
        (shape((2 * pairs, depth, patches), BF), cot, down) + outs + (shape((TAIL, width), F32),),
        pairs + 12,
        vmem_in=1,
    )(seen, pixel_rows, cot, down)


def row_stats(values):
    average = jnp.mean(values, axis=-1, keepdims=True)
    centred = values - average
    spread = jnp.mean(centred * centred, axis=-1, keepdims=True)
    root = lax.rsqrt(spread + 1e-06)
    return centred * root, root


def norm_back(xhat, root, grad_out, gain):
    scaled = grad_out * gain
    mean_scaled = jnp.mean(scaled, axis=-1, keepdims=True)
    mean_along = jnp.mean(scaled * xhat, axis=-1, keepdims=True)
    return root * (scaled - mean_scaled - xhat * mean_along)


def head_rows(width):
    row = lax.broadcasted_iota(jnp.int32, (TAIL, width), 0)
    lane = lax.broadcasted_iota(jnp.int32, (TAIL, width), 1)
    return (lane // HEAD) == row


def two_heads(pair):
    low = lax.broadcasted_iota(jnp.int32, pair.shape, 1) < HEAD
    zero = jnp.zeros_like(pair)
    return jnp.concatenate([jnp.where(low, pair, zero), jnp.where(low, zero, pair)], axis=0)


def own_heads(stacked):
    rows = stacked.shape[0] // 2
    low = lax.broadcasted_iota(jnp.int32, (rows, stacked.shape[1]), 1) < HEAD
    return jnp.where(low, stacked[:rows], stacked[rows:])


def softmax_keys(scores, count):
    key = lax.broadcasted_iota(jnp.int32, scores.shape, 0)
    scores = jnp.where(key < count, scores * SCALE, -1e30)
    raised = jnp.exp(scores - jnp.max(scores, axis=0, keepdims=True))
    return raised * (1.0 / jnp.sum(raised, axis=0, keepdims=True))


def load_far(links, copies, half_hbm, other_hbm, target):
    count = half_hbm.shape[0]
    core = links.bit(0)
    return [
        copies.start(half_hbm, target.at[pl.ds(pl.multiple_of(core * count, 16), count), :]),
        copies.start(other_hbm, target.at[pl.ds(pl.multiple_of((1 - core) * count, 16), count), :]),
    ]


def forward_kernel(
    links,
    chips,
    vecs_ref,
    xo_hbm,
    xr_hbm,
    ko_hbm,
    half_hbm,
    other_hbm,
    wqkv_hbm,
    wout_hbm,
    cot_hbm,
    gact_hbm,
    up_hbm,
    stream_hbm,
    n1_hbm,
    packed_hbm,
    probs_hbm,
    tprobs_hbm,
    att_hbm,
    mid_hbm,
    n2_hbm,
    act_hbm,
    gpre_hbm,
    down_send_hbm,
    down_keep_hbm,
    up_send_hbm,
    up_keep_hbm,
    stream_ref,
    n1_ref,
    packed_ref,
    probs_ref,
    tprobs_ref,
    att_ref,
    mid_ref,
    n2_ref,
    xo_ref,
    xr_ref,
    ko_ref,
    kr_ref,
    tatt_ref,
    wqkv_ref,
    wout_ref,
    *half_refs,
):
    copies = Copies(half_refs[-1])
    rows, width = n1_ref.shape
    body = rows - TAIL
    slots = body // chips
    token, gain1, bias1, gain2, bias2 = (vecs_ref[i : i + 1, :] for i in range(5))
    first = [
        copies.start(source, target)
        for source, target in ((xo_hbm, xo_ref), (ko_hbm, ko_ref), (xr_hbm, xr_ref))
    ] + load_far(links, copies, half_hbm, other_hbm, kr_ref)
    for copy in first:
        copy.wait()
    wqkv_in = copies.start(wqkv_hbm, wqkv_ref)
    wout_in = copies.start(wout_hbm, wout_ref)
    half = MlpHalf(links, 0, copies, half_refs[:-1])
    for m in range(0, body, 256):
        stream_ref[m : m + 256, :] = dot_tn(xo_ref[:, m : m + 256], ko_ref[...]) + dot_tn(
            xr_ref[:, m : m + 256], kr_ref[...]
        )
    tail_row = lax.broadcasted_iota(jnp.int32, (TAIL, width), 0)
    stream_ref[body:rows, :] = jnp.where(tail_row < chips, token, 0.0)

    def first_norm(i, carry):
        at = pl.ds(pl.multiple_of(i * BLOCK, BLOCK), BLOCK)
        xhat, unused = row_stats(stream_ref[at, :])
        n1_ref[at, :] = (xhat * gain1 + bias1).astype(BF)
        return carry

    lax.fori_loop(0, rows // BLOCK, first_norm, 0)
    wqkv_in.wait()
    half.load(cot_hbm, gact_hbm, up_hbm)
    copies.out(stream_ref, stream_hbm)
    copies.out(n1_ref, n1_hbm)

    def project(j, carry):
        at = pl.ds(pl.multiple_of(j * 256, 256), 256)
        packed_ref[:, at] = dot(n1_ref[...], wqkv_ref[:, at]).astype(BF)
        return carry

    lax.fori_loop(0, 3 * width // 256, project, 0)
    copies.out(packed_ref, packed_hbm)
    tail = packed_ref[body:rows, :]
    heads = head_rows(width)
    tquery = jnp.where(heads, jnp.broadcast_to(tail[0:1, 0:width], (TAIL, width)), 0).astype(BF)
    tatt_ref[...] = jnp.zeros_like(tatt_ref)

    def chip(c, carry):
        at = pl.ds(pl.multiple_of(c * slots, slots), slots)
        key = jnp.concatenate(
            [packed_ref[at, width : 2 * width], tail[:, width : 2 * width]], axis=0
        )
        val = jnp.concatenate([packed_ref[at, 2 * width :], tail[:, 2 * width :]], axis=0)
        tiles = [slice(128 * p, 128 * p + 128) for p in range(width // 128)]
        scores = [dot_nt(key[:, here], two_heads(packed_ref[at, here])) for here in tiles]
        scores.append(dot_nt(key, tquery))
        probs = [softmax_keys(s, slots + 1).astype(BF) for s in scores]
        mixed = [dot_tn(probs[p], val[:, tiles[p]]) for p in range(len(tiles))]
        mixed.append(dot_tn(probs[-1], val))
        for p in range(len(tiles)):
            probs_ref[c, p] = probs[p]
            att_ref[at, tiles[p]] = own_heads(mixed[p]).astype(BF)
        tprobs_ref[c] = probs[-1]
        tatt_ref[pl.ds(c, 1), :] = jnp.sum(jnp.where(heads, mixed[-1], 0.0), axis=0, keepdims=True)
        return carry

    lax.fori_loop(0, chips, chip, 0, unroll=2)
    att_ref[body:rows, :] = tatt_ref[...].astype(BF)
    copies.out(probs_ref, probs_hbm)
    copies.out(tprobs_ref, tprobs_hbm)
    copies.out(att_ref, att_hbm)
    wout_in.wait()

    def out_project(j, carry):
        at = pl.ds(pl.multiple_of(j * 256, 256), 256)
        mid_ref[:, at] = stream_ref[:, at] + dot(att_ref[...], wout_ref[:, at])
        return carry

    lax.fori_loop(0, width // 256, out_project, 0)
    copies.out(mid_ref, mid_hbm)

    def second_norm(i, carry):
        at = pl.ds(pl.multiple_of(i * BLOCK, BLOCK), BLOCK)
        xhat, unused = row_stats(mid_ref[at, :])
        n2_ref[at, :] = (xhat * gain2 + bias2).astype(BF)
        return carry

    lax.fori_loop(0, rows // BLOCK, second_norm, 0)
    copies.out(n2_ref, n2_hbm)
    half.run(n2_ref, down_send_hbm, down_keep_hbm, up_send_hbm, up_keep_hbm)
    copies.out(half.act, act_hbm)
    copies.out(half.gpre, gpre_hbm)
    copies.finish()


class MlpHalf:
    def __init__(self, links, third, copies, refs):
        self.links, self.third, self.copies = links, third, copies
        self.cot, self.gact, self.up, self.act, self.gpre, self.down_out, self.up_out, self.grad = refs

    @staticmethod
    def scratch(rows, width, hidden):
        half = width // 2
        return (
            shape((rows, width), BF),
            shape((rows, hidden // 2), BF),
            shape((width, hidden // 2), BF),
            shape((rows, hidden // 2), BF),
            shape((rows, hidden // 2), BF),
            shape((2, 2, 2, 2, 4, width // 16, half), BF),
            shape((2, 2, 2, 2, hidden // 16, half), BF),
            shape((hidden // 4, width), BF),
        )

    @staticmethod
    def results(rows, width, hidden):
        down = shape((2, 2, 2, 4, width // 16, width // 2), BF)
        up = shape((2, 2, 2, hidden // 16, width // 2), BF)
        act = shape((rows, hidden // 2), BF)
        return (act, act), (down, down, up, up)

    def load(self, cot_hbm, gact_hbm, up_hbm):
        chunk = up_hbm.shape[1] // 4
        start = self.copies.start
        far = lambda i: slice((2 * i + self.third) * chunk, (2 * i + self.third + 1) * chunk)
        near = lambda i: slice(i * chunk, (i + 1) * chunk)
        self.first = [
            (
                start(up_hbm.at[:, far(i)], self.up.at[:, near(i)]),
                start(gact_hbm.at[:, far(i)], self.gact.at[:, near(i)]),
            )
            for i in range(2)
        ]
        self.cot_in = start(cot_hbm, self.cot)

    def run(self, n2_ref, down_send, down_keep, up_send, up_keep):
        copies, links = self.copies, self.links
        rows, width = n2_ref.shape
        chunk = self.up.shape[1] // 2
        half = width // 2
        block = width // 16
        tile = 256
        for i in range(2):
            for copy in self.first[i]:
                copy.wait()
            for j in range(i * chunk, (i + 1) * chunk, tile):
                cols = slice(j, j + tile)
                pre = dot(n2_ref[...], self.up[:, cols])
                phi = 0.5 + 0.5 * lax.erf(pre * (0.5**0.5))
                bell = jnp.exp(-0.5 * pre * pre) * 0.3989422804014327
                self.act[:, cols] = (pre * phi).astype(BF)
                gact = self.gact[:, cols].astype(F32)
                self.gpre[:, cols] = (gact * (phi + pre * bell)).astype(BF)
        where = (1, "band") if self.third == 0 else (0, 0)
        bits = [links.bit(w) for w in where]
        self.cot_in.wait()
        for i in range(2):
            for m in range(0, width, 256):
                self.grad[m : m + 256, :] = dot_tn(
                    self.cot[:, m : m + 256], self.act[:, i * chunk : (i + 1) * chunk]
                ).astype(BF)
            for side, bit in ((0, 1 - bits[0]), (1, bits[0])):
                for other in range(2):
                    x, c = (bit, other) if where[0] == 1 else (other, bit)
                    for z in range(4):
                        at = pl.multiple_of(((z * 2 + x) * 2 + c) * block, 16)
                        piece = self.grad[pl.ds(at, block), :]
                        for h in range(2):
                            self.down_out[side, other, i, h, z] = piece[:, h * half : (h + 1) * half]
        copies.out(self.down_out.at[0], down_send)
        copies.out(self.down_out.at[1], down_keep)
        part = chunk // 4
        for i in range(2):
            for m in range(0, chunk, 256):
                self.grad[m : m + 256, :] = dot_tn(
                    self.gpre[:, i * chunk + m : i * chunk + m + 256], n2_ref[...]
                ).astype(BF)
            for side, bit in ((0, 1 - bits[1]), (1, bits[1])):
                for x in range(2):
                    for other in range(2):
                        if where[1] == "band":
                            at = (2 * x + other) * part
                            cols = pl.ds(pl.multiple_of(bit * half, 128), half)
                        else:
                            at = pl.multiple_of((2 * x + bit) * part, 16)
                            cols = slice(other * half, (other + 1) * half)
                        self.up_out[side, i, x, other] = self.grad[pl.ds(at, part), cols]
        copies.out(self.up_out.at[0], up_send)
        copies.out(self.up_out.at[1], up_keep)


def forward(links, chips, vecs, xo, xr, ko, half, other, wqkv, wout, cot, gact, up):
    width, hidden = up.shape
    body = xo.shape[1]
    rows = body + TAIL
    saved = (
        shape((rows, width), F32),
        shape((rows, width), BF),
        shape((rows, 3 * width), BF),
        shape((chips, width // 128, KEYS, 128), BF),
        shape((chips, KEYS, TAIL), BF),
        shape((rows, width), BF),
        shape((rows, width), F32),
        shape((rows, width), BF),
    )
    return kernel_call(
        functools.partial(forward_kernel, links, chips),
        "encoder_forward",
        sum((saved,) + MlpHalf.results(rows, width, hidden), ()),
        saved
        + (xo, xr, ko, ko, shape((TAIL, width), F32), wqkv, wout)
        + MlpHalf.scratch(rows, width, hidden),
        32,
        vmem_in=1,
    )(vecs, xo, xr, ko, half, other, wqkv, wout, cot, gact, up)


def spread_blocks(links, full_ref, send_refs, keep_refs):
    core = links.bit(0)
    cols = full_ref.shape[1] // 2
    parts = len(send_refs)
    block = full_ref.shape[0] // 16
    piece = block // parts
    for z in range(4):
        for x in range(2):
            base = (z * 2 + x) * 2
            for refs, c in ((send_refs, 1 - core), (keep_refs, core)):
                for k in range(parts):
                    start = pl.multiple_of((base + c) * block + k * piece, 16)
                    rows = full_ref[pl.ds(start, piece), :]
                    for b in range(2):
                        refs[k][x, b, z] = rows[:, b * cols : (b + 1) * cols]


def mlp_back_kernel(
    links,
    after,
    vecs_ref,
    n2_hbm,
    gact_hbm,
    act1_hbm,
    gpre1_hbm,
    up_hbm,
    down_hbm,
    mid_hbm,
    cot_hbm,
    att_hbm,
    wout_hbm,
    *rest,
):
    rest = rest[after:]
    grads, rest = rest[:4], rest[4:]
    gmid_hbm, gatt_hbm, send_hbm, keep_hbm, out_hbm, vec_ref = rest[:6]
    (
        n2_ref,
        gmid_ref,
        gatt_ref,
        send_ref,
        keep_ref,
        out_ref,
        act_ref,
        gpre_ref,
        up_ref,
        down_ref,
        mid_ref,
        att_ref,
        wout_ref,
        back_ref,
        branch_ref,
        full_ref,
    ) = rest[6:22]
    half_refs, sems = rest[22:-1], rest[-1]
    copies = Copies(sems)
    rows, width = mid_ref.shape
    quarter = up_hbm.shape[1] // 4
    at = lambda i: slice(i * quarter, (i + 1) * quarter)
    n2_in = copies.start(n2_hbm, n2_ref)
    half = MlpHalf(links, 1, copies, half_refs)
    half.load(cot_hbm, gact_hbm, up_hbm)
    cot_ref = half.cot
    n2_in.wait()
    first_in = [copies.start(gpre1_hbm, gpre_ref)] + [
        copies.start(up_hbm.at[:, at(2 * i)], up_ref.at[:, at(i)]) for i in range(2)
    ]
    norm_in = copies.start(mid_hbm, mid_ref)
    att_in = copies.start(att_hbm, att_ref)
    wout_in = copies.start(wout_hbm, wout_ref)
    half.run(n2_ref, *grads)
    late = [copies.start(act1_hbm, act_ref)] + [
        copies.start(down_hbm.at[at(2 * i + third), :], down_ref.at[at(2 * third + i), :])
        for third in range(2)
        for i in range(2)
    ]
    for copy in first_in:
        copy.wait()
    for j in range(0, width, 256):
        cols = slice(j, j + 256)
        back_ref[:, cols] = dot_nt(gpre_ref[...], up_ref[cols, :]) + dot_nt(
            half.gpre[...], half.up[cols, :]
        )
    norm_in.wait()
    gain = vecs_ref[3:4, :]

    def norm(i, carry):
        at = pl.ds(pl.multiple_of(i * BLOCK, BLOCK), BLOCK)
        xhat, root = row_stats(mid_ref[at, :])
        grad = back_ref[at, :]
        total = cot_ref[at, :].astype(F32) + norm_back(xhat, root, grad, gain)
        gmid_ref[at, :] = total
        branch_ref[at, :] = total.astype(BF)
        return (
            carry[0] + jnp.sum(grad * xhat, axis=0, keepdims=True),
            carry[1] + jnp.sum(grad, axis=0, keepdims=True),
        )

    zero = jnp.zeros((1, width), F32)
    gain_sum, bias_sum = lax.fori_loop(0, rows // BLOCK, norm, (zero, zero))
    vec_ref[0:1, :] = gain_sum
    vec_ref[1:2, :] = bias_sum
    copies.out(gmid_ref, gmid_hbm)
    att_in.wait()
    for m in range(0, width, 256):
        full_ref[m : m + 256, :] = dot_tn(branch_ref[:, m : m + 256], att_ref[...]).astype(BF)
    spread_blocks(links, full_ref, [send_ref], [keep_ref])
    copies.out(send_ref, send_hbm)
    copies.out(keep_ref, keep_hbm)
    wout_in.wait()
    for j in range(0, width, 256):
        gatt_ref[:, j : j + 256] = dot_nt(branch_ref[...], wout_ref[j : j + 256, :]).astype(BF)
    copies.out(gatt_ref, gatt_hbm)
    for copy in late:
        copy.wait()
    for j in range(0, width, 256):
        cols = slice(j, j + 256)
        out_ref[:, cols] = (
            mid_ref[:, cols]
            + dot(act_ref[...], down_ref[: 2 * quarter, cols])
            + dot(half.act[...], down_ref[2 * quarter :, cols])
        ).astype(BF)
    copies.out(out_ref, out_hbm)
    copies.finish()


def mlp_back(links, vecs, n2, gact, act1, gpre1, up, down, mid, cot, att, wout, after):
    rows, width = mid.shape
    hidden = up.shape[1]
    part = shape((2, 2, 4, width // 16, width // 2), BF)
    unused, grads = MlpHalf.results(rows, width, hidden)
    return kernel_call(
        functools.partial(mlp_back_kernel, links, len(after)),
        "mlp_back",
        grads + (mid, cot, part, part, cot, shape((2, width), F32)),
        (n2, mid, cot, part, part, cot, act1, gpre1)
        + (shape((width, hidden // 2), BF), down, mid, att, wout, mid, cot, wout)
        + MlpHalf.scratch(rows, width, hidden),
        40,
        vmem_in=1,
        vmem_out=1,
    )(vecs, n2, gact, act1, gpre1, up, down, mid, cot, att, wout, *after)


def split_vec(vec):
    high = vec.astype(BF)
    return high, (vec - high.astype(F32)).astype(BF)


def stream_back_kernel(
    links,
    chips,
    after,
    vecs_ref,
    vec2_ref,
    gatt_hbm,
    packed_hbm,
    probs_hbm,
    tprobs_hbm,
    wqkv_hbm,
    stream_hbm,
    gmid_hbm,
    xo_hbm,
    xr_hbm,
    ko_hbm,
    half_hbm,
    other_hbm,
    n1_hbm,
    *rest,
):
    rest = rest[after:]
    send_hbm, keep_hbm, own_hbm, far_hbm = rest[:4]
    parts_hbm, vec_ref = rest[4:10], rest[10]
    (
        gatt_ref,
        packed_ref,
        probs_ref,
        tprobs_ref,
        wqkv_ref,
        stream_ref,
        gmid_ref,
        xo_ref,
        xr_ref,
        ko_ref,
        kr_ref,
        n1_ref,
        send_ref,
        keep_ref,
        pgrad_ref,
        parts_ref,
        gpacked_ref,
        tgrad_ref,
        tout_ref,
        back_ref,
        embed_ref,
        kfull_ref,
        full_ref,
        sems,
    ) = rest[11:]
    rows, width = stream_ref.shape
    body = rows - TAIL
    slots = body // chips
    half = width // 2
    copies = Copies(sems)
    arrive = [
        copies.start(source, target)
        for source, target in (
            (packed_hbm, packed_ref),
            (gatt_hbm, gatt_ref),
            (probs_hbm, probs_ref),
            (tprobs_hbm, tprobs_ref),
        )
    ]
    tout_ref[...] = jnp.zeros_like(tout_ref)
    heads = head_rows(width)
    for copy in arrive:
        copy.wait()
    wqkv_in = copies.start(wqkv_hbm, wqkv_ref)
    late = [copies.start(stream_hbm, stream_ref), copies.start(gmid_hbm, gmid_ref)]
    last = [
        copies.start(source, target)
        for source, target in ((xo_hbm, xo_ref), (xr_hbm, xr_ref), (ko_hbm, ko_ref))
    ] + load_far(links, copies, half_hbm, other_hbm, kr_ref)
    n1_in = copies.start(n1_hbm, n1_ref)
    tgrad_ref[...] = gatt_ref[body:rows, :].astype(F32)
    tail = packed_ref[body:rows, :]
    tquery = jnp.where(heads, jnp.broadcast_to(tail[0:1, 0:width], (TAIL, width)), 0).astype(BF)

    def chip(c, carry):
        at = pl.ds(pl.multiple_of(c * slots, slots), slots)
        key_all = jnp.concatenate(
            [packed_ref[at, width : 2 * width], tail[:, width : 2 * width]], axis=0
        )
        val_all = jnp.concatenate([packed_ref[at, 2 * width :], tail[:, 2 * width :]], axis=0)
        tgrad = jnp.where(
            heads, jnp.broadcast_to(tgrad_ref[pl.ds(c, 1), :], (TAIL, width)), 0.0
        ).astype(BF)
        tiles = [slice(128 * p, 128 * p + 128) for p in range(width // 128)]
        probs = [probs_ref[c, p] for p in range(len(tiles))] + [tprobs_ref[c]]
        gouts = [two_heads(gatt_ref[at, here]) for here in tiles]
        queries = [two_heads(packed_ref[at, here]) for here in tiles]
        gprobs = [dot_nt(val_all[:, tiles[p]], gouts[p]) for p in range(len(tiles))]
        gprobs.append(dot_nt(val_all, tgrad))
        gscores = []
        for prob, gprob in zip(probs, gprobs):
            wide = prob.astype(F32)
            inner = jnp.sum(gprob * wide, axis=0, keepdims=True)
            gscores.append((wide * (gprob - inner) * SCALE).astype(BF))
        gval_tail = dot(probs[-1], tgrad)
        gkey_tail = dot(gscores[-1], tquery)
        mixed = jnp.where(heads, dot_tn(gscores[-1], key_all), 0.0)
        gvals = [dot(probs[p], gouts[p]) + gval_tail[:, tiles[p]] for p in range(len(tiles))]
        gkeys = [dot(gscores[p], queries[p]) + gkey_tail[:, tiles[p]] for p in range(len(tiles))]
        gqueries = [own_heads(dot_tn(gscores[p], key_all[:, tiles[p]])) for p in range(len(tiles))]
        for p in range(len(tiles)):
            gpacked_ref[at, 128 * p : 128 * p + 128] = gqueries[p].astype(BF)
            base = width + 128 * p
            gpacked_ref[at, base : base + 128] = gkeys[p][:slots].astype(BF)
            gpacked_ref[at, width + base : width + base + 128] = gvals[p][:slots].astype(BF)
        tout_ref[pl.ds(c, 1), :] = jnp.concatenate(
            [jnp.sum(mixed, axis=0, keepdims=True)]
            + [g[slots : slots + 1] for g in gkeys + gvals],
            axis=1,
        )
        return carry

    lax.fori_loop(0, chips, chip, 0)
    gpacked_ref[body:rows, :] = tout_ref[...].astype(BF)
    wqkv_in.wait()
    for j in range(0, width, 256):
        back_ref[:, j : j + 256] = dot_nt(gpacked_ref[...], wqkv_ref[j : j + 256, :])
    for copy in late:
        copy.wait()
    gain = vecs_ref[1:2, :]

    def norm(i, carry):
        at = pl.ds(pl.multiple_of(i * BLOCK, BLOCK), BLOCK)
        xhat, root = row_stats(stream_ref[at, :])
        grad = back_ref[at, :]
        total = gmid_ref[at, :] + norm_back(xhat, root, grad, gain)
        back_ref[at, :] = total
        embed_ref[at, :] = total.astype(BF)
        return (
            carry[0] + jnp.sum(grad * xhat, axis=0, keepdims=True),
            carry[1] + jnp.sum(grad, axis=0, keepdims=True),
        )

    zero = jnp.zeros((1, width), F32)
    gain_sum, bias_sum = lax.fori_loop(0, rows // BLOCK, norm, (zero, zero))
    token_sum = jnp.sum(back_ref[body:rows, :], axis=0, keepdims=True)
    vec_ref[...] = jnp.zeros_like(vec_ref)
    for i, v in enumerate((gain_sum, bias_sum, token_sum, vec2_ref[0:1, :], vec2_ref[1:2, :])):
        vec_ref[2 * i : 2 * i + 1, :] = v[:, :half]
        vec_ref[2 * i + 1 : 2 * i + 2, :] = v[:, half:]
    for copy in last:
        copy.wait()
    grad = embed_ref[0:body, :]
    depth = xo_ref.shape[0]
    core, band = links.bit(0), links.bit("band")
    kfull_ref[0] = dot(xo_ref[...], grad).astype(BF)
    kfull_ref[1] = dot(xr_ref[...], grad).astype(BF)
    piece = depth // 4
    for c, ref in ((1 - core, send_ref), (core, keep_ref)):
        for far in range(2):
            for x in range(2):
                start = pl.multiple_of(c * (depth // 2) + x * piece, 16)
                block = kfull_ref[far, pl.ds(start, piece), :]
                for h in range(2):
                    slot = ((far + band - 2 * far * band) * 2 + x) * 2 + h
                    to = pl.ds(pl.multiple_of(slot * piece, 16), piece)
                    ref[to, :] = block[:, h * half : (h + 1) * half]
    high, low = split_vec(vec_ref[...])
    send_ref[2 * depth : 2 * depth + 16, :] = high
    send_ref[2 * depth + 16 : 2 * depth + 32, :] = low
    vec_ref[...] = high.astype(F32) + low.astype(F32)
    copies.out(send_ref, send_hbm)
    copies.out(keep_ref, keep_hbm)
    middle = body // 2
    for side, kernel, target in ((0, kr_ref, far_hbm), (1, ko_ref, own_hbm)):
        for h in range(2):
            part = grad[h * middle : (h + 1) * middle]
            pgrad_ref[side, h] = dot_nt(kernel[...], part).astype(BF)
        copies.out(pgrad_ref.at[side], target)
    n1_in.wait()
    for m in range(0, 3 * width, 256):
        full_ref[m : m + 256, :] = dot_tn(gpacked_ref[:, m : m + 256], n1_ref[...]).astype(BF)
    spread_blocks(
        links,
        full_ref,
        [parts_ref.at[k] for k in range(3)],
        [parts_ref.at[3 + k] for k in range(3)],
    )
    for k in range(6):
        copies.out(parts_ref.at[k], parts_hbm[k])
    copies.finish()


def stream_back(
    links, chips, vecs, vec2, gatt, packed, probs, tprobs, wqkv, stream, gmid, xo, xr, ko, half, other, n1, after
):
    rows, width = stream.shape
    depth, body = xo.shape
    cols = width // 2
    send, keep = shape((2 * depth + 32, cols), BF), shape((2 * depth, cols), BF)
    pgrad = shape((2, depth, body // 2), BF)
    part = shape((2, 2, 4, width // 16, width // 2), BF)
    return kernel_call(
        functools.partial(stream_back_kernel, links, chips, len(after)),
        "stream_back",
        (send, keep, pgrad, pgrad) + (part,) * 6 + (shape((16, cols), F32),),
        (gatt, packed, probs, tprobs, wqkv, stream, gmid, xo, xr, ko, ko, n1, send, keep)
        + (
            shape((2,) + pgrad.shape, BF),
            shape((6,) + part.shape, BF),
            packed,
            shape((TAIL, width), F32),
            shape((TAIL, 3 * width), F32),
            stream,
            shape((rows, width), BF),
            shape((2, depth, width), BF),
            shape((3 * width, width), BF),
        ),
        32,
        vmem_in=2,
        vmem_out=1,
    )(
        vecs, vec2, gatt, packed, probs, tprobs, wqkv, stream, gmid, xo, xr, ko, half, other, n1, *after
    )


def scatter_kernel(links, side, pairs, depth, seen_ref, grad_hbm, *rest):
    out_hbm, grad_ref, out_ref, sems = rest[-4:]
    patches = out_ref.shape[2]
    copies = Copies(sems)
    copies.start(grad_hbm.at[0 : 2 * depth, :], grad_ref).wait()
    band = links.bit("band")
    base = (band if side == 0 else 1 - band) * 2 * pairs
    for i in range(pairs):
        first, second = chosen(seen_ref, base + 2 * i, patches)
        wide = first.shape[1]
        h, at = divmod(i * wide, grad_ref.shape[1])
        grad = grad_ref[h * depth : (h + 1) * depth, at : at + wide]
        out_ref[2 * i] = dot_nt(grad, first)
        out_ref[2 * i + 1] = dot_nt(grad, second)
        copies.out(out_ref.at[2 * i : 2 * i + 2], out_hbm.at[pl.ds(base + 2 * i, 2)])
    copies.finish()


def scatter(links, side, grads, depth, seen, patches, *earlier):
    chips = seen.shape[0]
    pairs = chips // 4
    return kernel_call(
        functools.partial(scatter_kernel, links, side, pairs, depth),
        "scatter",
        (shape((chips, depth, patches), F32),),
        (shape((2 * depth, grads.shape[1]), BF), shape((2 * pairs, depth, patches), F32)),
        pairs + 1,
        vmem_in=1,
        input_output_aliases={2: 0} if earlier else {},
    )(seen, grads, *earlier)[0]


class Links:
    def __init__(self, mesh):
        self.count = mesh.shape["dp"]
        self.extra = self.count // 16

    def swap(self, array, *where):
        flip = sum((1 << w) * self.extra for w in where if w != "band")
        if "band" not in where:
            return lax.ppermute(array, "dp", [(d, d ^ flip) for d in range(self.count)])
        if flip == 0:
            return lax.ppermute(array, "band", [(0, 1), (1, 0)])
        pairs = [
            (2 * d + b, 2 * (d ^ flip) + 1 - b) for d in range(self.count) for b in range(2)
        ]
        return lax.ppermute(array, ("dp", "band"), pairs)

    def bit(self, where):
        if where == "band":
            return lax.axis_index("band")
        return lax.rem(lax.div(lax.axis_index("dp"), self.extra << where), 2)

    def groups(self):
        return [[block * self.extra + i for i in range(self.extra)] for block in range(16)]

    def last(self, array):
        if self.extra == 1:
            return array
        return lax.psum_scatter(
            array, "dp", scatter_dimension=0, tiled=True, axis_index_groups=self.groups()
        )

    def total(self, array):
        if self.extra == 1:
            return array
        return lax.psum(array, "dp", axis_index_groups=self.groups())


class Level:
    def __init__(self, owner, terms, gone=frozenset(), rounded=False, alt=None, choice=None):
        self.owner, self.terms, self.gone, self.rounded = owner, list(terms), frozenset(gone), rounded
        self.alt, self.choice = alt, choice

    def moving(self, gone):
        strides = self.owner.strides(self.gone)
        return [(name, strides[name]) for name in self.owner.names if name in gone and name in strides]


class Piece:
    def __init__(self, names, sizes, unit, kept, came, gone=()):
        self.names, self.sizes, self.unit = list(names), list(sizes), unit
        kept = kept.reshape(-1, kept.shape[-1])
        self.gone = frozenset(gone)
        self.levels = [Level(self, [(kept, 0), came], self.gone)]

    @staticmethod
    def join(first, second, choice):
        joined = Piece(first.names, first.sizes, first.unit, first.levels[0].terms[0][0], None, first.gone)
        joined.levels = [
            Level(a.owner, a.terms, a.gone, a.rounded, b, choice)
            for a, b in zip(first.levels, second.levels)
        ]
        return joined

    def strides(self, gone):
        found, stride = {}, self.unit
        for name, size in reversed(list(zip(self.names, self.sizes))):
            if name not in gone:
                found[name] = stride
                stride = stride * size
        return found

    def layout(self, names):
        gone = self.gone | frozenset(names)
        last = max([i for i, name in enumerate(self.names) if name in gone], default=-1)
        post = self.unit
        for size in self.sizes[last + 1 :]:
            post = post * size
        loops = [{}]
        for name, size in list(zip(self.names, self.sizes))[: last + 1]:
            if name not in gone:
                loops = [{**at, name: i} for at in loops for i in range(size)]
        return post * len(loops), post, loops


class Vec:
    def __init__(self, kept, came):
        self.kept, self.came = kept, [came]

    def value(self):
        parts = [
            buffer[at : at + 16].astype(F32) + buffer[at + 16 : at + 32].astype(F32)
            for buffer, at in self.came
        ]
        return pairwise([self.kept] + parts)


def pairwise(parts):
    while len(parts) > 1:
        parts = [
            parts[i] + parts[i + 1] if i + 1 < len(parts) else parts[i]
            for i in range(0, len(parts), 2)
        ]
    return parts[0]


def combine_kernel(links, tasks, n_in, n_out, n_load, after, *refs):
    ins, refs = refs[:n_in], refs[n_in + after :]
    out_hbm, refs = refs[:n_out], refs[n_out:]
    loads, refs = refs[:n_load], refs[n_load:]
    staged, sems = refs[:-1], refs[-1]
    copies = Copies(sems)
    bits = {where: links.bit(where) for where in (0, 1, 2, 3, "band")}
    waits = []
    for task in tasks:
        mine = []
        waits.append(mine)
        if task["kind"] == "raw":
            mine.append(copies.start(ins[task["from"]], loads[task["slot"]]))
            continue
        if task["kind"] == "vec":
            mine += [
                copies.start(ins[i].at[at : at + count, :], loads[slot])
                for i, at, count, slot in task["loads"]
            ]
            continue
        index = {
            name: (1 - bits[name]) if name in task["flip"] else bits[name] for name in bits
        }
        for load in task["loads"]:
            moving = sum((index[name] * stride for name, stride in load["moving"]), load["at"])
            alt_moving = sum(
                (index[name] * stride for name, stride in load["alt_moving"]), load["alt_at"]
            )
            for p, base in enumerate(load["bases"]):
                rows = pl.ds(pl.multiple_of(moving + base, 16), load["post"])
                target = loads[load["slot"]].at[p * load["post"] : (p + 1) * load["post"], :]
                sem = copies.sems.at[copies.count]
                copies.count += 1
                if load["alt"] is None:
                    copy = pltpu.make_async_copy(ins[load["in"]].at[rows, :], target, sem)
                    copy.start()
                else:
                    chosen_bit = index[load["choice"]]
                    copy = pltpu.make_async_copy(ins[load["in"]].at[rows, :], target, sem)
                    rows = pl.ds(pl.multiple_of(alt_moving + base, 16), load["post"])
                    other = pltpu.make_async_copy(ins[load["alt"]].at[rows, :], target, sem)
                    pl.when(chosen_bit == 0)(copy.start)
                    pl.when(chosen_bit == 1)(other.start)
                mine.append(copy)
    for task, mine in zip(tasks, waits):
        for copy in mine:
            copy.wait()
        if task["kind"] == "raw":
            copies.out(loads[task["slot"]], out_hbm[task["out"]].at[task["at"], :])
            continue
        if task["kind"] == "vec":
            parts = [loads[task["loads"][0][3]][...]]
            for unused, also, count, slot in task["loads"][1:]:
                parts.append(loads[slot][0:16, :].astype(F32) + loads[slot][16:32, :].astype(F32))
            high, low = split_vec(pairwise(parts))
            sent, kept = staged[task["stage"]], staged[task["stage"] + 1]
            sent[0:16, :] = high
            sent[16:32, :] = low
            kept[...] = high.astype(F32) + low.astype(F32)
            for out, at in task["outs"]:
                copies.out(sent, out_hbm[out].at[at, :])
            copies.out(kept, out_hbm[task["kept"]])
            continue
        total = None
        for rounded, slots in task["sum"]:
            parts = [loads[slot][...].astype(F32) for slot in slots]
            if total is not None:
                parts = [total.astype(BF).astype(F32) if rounded else total] + parts
            total = pairwise(parts)
        result = staged[task["stage"]]
        result[...] = total.astype(result.dtype)
        for out, at in task["outs"]:
            copies.out(result, out_hbm[out].at[at, :])
    copies.finish()


def combine(links, steps, after=()):
    ins, tasks, loads, stages, sends, outs = [], [], [], [], {}, []
    copies = 0
    returned = []

    def index_of(array):
        for i, other in enumerate(ins):
            if other is array:
                return i
        ins.append(array)
        return len(ins) - 1

    def send_to(where, count):
        if where not in sends:
            sends[where] = len(outs)
            outs.append([0, BF])
        at = outs[sends[where]][0]
        outs[sends[where]][0] += count
        return sends[where], slice(at, at + count)

    def places(names):
        return [
            tuple(name for k, name in enumerate(names) if mask >> k & 1)
            for mask in range(1, 1 << len(names))
        ]

    for piece, names, mode in steps:
        if mode == "raw":
            out, at = send_to(names, piece.shape[0])
            tasks.append(
                {"kind": "raw", "from": index_of(piece), "out": out, "at": at, "slot": len(loads)}
            )
            loads.append(piece)
            returned.append((out, at))
            copies += 2
            continue
        if mode == "vec":
            task = {"kind": "vec", "loads": [], "stage": len(stages)}
            width = piece.kept.shape[1]
            for array, at, count in [(piece.kept, 0, 16)] + [(b, at, 32) for b, at in piece.came]:
                task["loads"].append((index_of(array), at, count, len(loads)))
                loads.append(shape((count, width), array.dtype))
            stages += [shape((32, width), BF), shape((16, width), F32)]
            task["outs"] = [send_to(place, 32) for place in places(names)]
            task["kept"] = len(outs)
            outs.append([16, F32])
            copies += len(task["loads"]) + len(task["outs"]) + 1
            tasks.append(task)
            returned.append(task)
            continue
        split = names if mode == "split" else ()
        count, post, loops = piece.layout(split)
        width = piece.levels[0].terms[0][0].shape[1]
        if mode == "final":
            groups = [((), [(len(outs), slice(0, count))])]
            outs.append([count, names])
            returned.append(len(outs) - 1)
            kind = names
        elif mode == "all":
            groups = [((), [send_to(place, count) for place in places(names)])]
            kind = BF
        else:
            groups = [(place, [send_to(place, count)]) for place in places(names)]
            kind = BF
        if mode != "final":
            returned.append([out for unused, targets in groups for out in targets])
        gone = piece.gone | frozenset(split)
        for flip, targets in groups:
            task = {"kind": "sum", "flip": flip, "loads": [], "sum": [], "stage": len(stages)}
            stages.append(shape((count, width), kind))
            task["outs"] = targets
            copies += len(targets)
            for level in piece.levels:
                strides = level.owner.strides(level.gone)
                slots = []
                for t, (array, at) in enumerate(level.terms):
                    slots.append(len(loads))
                    alt, alt_at = None, at
                    if level.alt is not None:
                        buffer, alt_at = level.alt.terms[t]
                        alt = index_of(buffer)
                    task["loads"].append(
                        {
                            "in": index_of(array),
                            "alt": alt,
                            "alt_at": alt_at,
                            "alt_moving": level.alt.moving(gone) if level.alt is not None else (),
                            "choice": level.choice,
                            "at": at,
                            "moving": level.moving(gone),
                            "bases": [
                                sum(i * strides[name] for name, i in loop.items()) for loop in loops
                            ],
                            "post": post,
                            "slot": len(loads),
                        }
                    )
                    loads.append(shape((count, width), array.dtype))
                    copies += len(loops)
                task["sum"].append((level.rounded, slots))
            tasks.append(task)
    results = kernel_call(
        functools.partial(
            combine_kernel, links, tasks, len(ins), len(outs), len(loads), len(after)
        ),
        "combine",
        [shape((count, width), kind) for count, kind in outs],
        loads + stages,
        copies,
    )(*ins, *after)
    came = {out: links.swap(results[out], *where) for where, out in sends.items()}
    values = []
    for (piece, names, mode), back in zip(steps, returned):
        if mode == "final":
            values.append(results[back])
        elif mode == "raw":
            values.append((came[back[0]], back[1].start))
        elif mode == "vec":
            piece.kept = results[back["kept"]]
            piece.came = [(came[out], at.start) for out, at in back["outs"]]
        else:
            if mode == "split":
                piece.gone = piece.gone | frozenset(names)
            piece.levels.append(
                Level(
                    piece, [(came[out], at.start) for out, at in back], piece.gone, mode == "all"
                )
            )
    return [results[out] for out in sends.values()], values


def shards(
    links,
    pixels,
    visible,
    kernels,
    class_token,
    norm1_gain,
    norm1_bias,
    norm2_gain,
    norm2_bias,
    attn_qkv,
    attn_out,
    mlp_up,
    mlp_down,
    cotangent,
):
    width = attn_out.shape[0]
    half = width // 2
    chips = cotangent.shape[0]
    group_chips, bands, patches, pix = pixels.shape
    slots = visible.shape[1]
    body = chips * slots
    depth = bands * pix
    block = width // 16
    flat = lambda a: a.reshape(-1, half)
    core_swap = lambda a: (links.swap(flat(a), 0), 0)

    pixel_rows = jnp.swapaxes(pixels, 2, 3).reshape(group_chips, depth, patches)
    kernels_own = kernels.reshape(depth, width)
    my_half, picked_far = pick_far(
        links, visible, pixel_rows, kernels_own.reshape(2, depth // 2, width)
    )
    far_half = links.swap(my_half, "band")
    picked_in = links.swap(picked_far, "band")
    picked_own, cot, gact = prepare(links, visible, pixel_rows, cotangent, mlp_down)
    far_half, cot = lax.optimization_barrier((far_half, cot))
    far_other = links.swap(far_half, 0)
    vecs = jnp.stack(
        [class_token, norm1_gain, norm1_bias, norm2_gain, norm2_bias] + [class_token] * 3
    )

    stream, n1, packed, probs, tprobs, att, mid, n2, act1, gpre1, *parts1 = forward(
        links,
        chips,
        vecs,
        picked_own,
        picked_in,
        kernels_own,
        far_half,
        far_other,
        attn_qkv,
        attn_out,
        cot,
        gact,
        mlp_up,
    )

    x, y, tower, plane = (1,), ("band",), (2, 3), (1, "band")
    down_send, down_keep, up_send, up_keep = parts1
    down1 = Piece(
        (1, 0, "band", "h", 3, 2),
        (2,) * 6,
        block,
        down_keep,
        (links.swap(flat(down_send), 1), 0),
        x,
    )
    up1 = Piece(
        (3, 1, 0, "band"), (2,) * 4, 4 * block, up_keep, (links.swap(flat(up_send), "band"), 0), y
    )
    down_send, down_keep, up_send, up_keep, gmid, gatt, out_send, out_keep, out_rows, vec2 = mlp_back(
        links, vecs, n2, gact, act1, gpre1, mlp_up, mlp_down, mid, cot, att, attn_out, ()
    )
    core = (0,)
    down2 = Piece(
        (0, 1, "band", "h", 3, 2), (2,) * 6, block, down_keep, core_swap(down_send), core
    )
    up2 = Piece((0, 3, 1, "band"), (2,) * 4, 4 * block, up_keep, core_swap(up_send), core)
    names, sizes = (0, 1, "band", 3, 2), (2,) * 5
    outp = Piece(names, sizes, block, out_keep, core_swap(out_send), core)
    tie, unused = combine(links, [(down1, y, "split"), (up1, x, "split")], (vec2,))
    more, unused = combine(links, [(down2, x, "split"), (up2, y, "split")], tie)
    tie = tie + more

    kg_send, kg_keep, pgrad_own, pgrad_far, *sent, vec_keep = stream_back(
        links,
        chips,
        vecs,
        vec2,
        gatt,
        packed,
        probs,
        tprobs,
        attn_qkv,
        stream,
        gmid,
        picked_own,
        picked_in,
        kernels_own,
        far_half,
        far_other,
        n1,
        tie,
    )
    kg_in, unused = core_swap(kg_send)
    kg = Piece((0, "band", 1, "h"), (2,) * 4, depth // 4, kg_keep, (kg_in, 0), core)
    vec = Vec(vec_keep, (kg_in, 2 * depth))
    qkv = [
        Piece(names, sizes, block, keep, core_swap(send), core)
        for send, keep in zip(sent[:3], sent[3:])
    ]
    far_grads = links.swap(flat(pgrad_far), "band")
    tie, unused = combine(
        links,
        [
            (down2, y, "split"),
            (up2, x, "split"),
            (outp, x, "split"),
            (down1, core, "split"),
            (up1, core, "split"),
        ],
        (vec_keep,),
    )
    partly = scatter(links, 0, flat(pgrad_own), depth, visible, patches)
    tie, unused = combine(
        links,
        [
            (kg, plane, "split"),
            (vec, plane, "vec"),
            (qkv[0], x, "split"),
            (qkv[1], y, "split"),
            (qkv[2], x, "split"),
            (down1, tower, "split"),
        ],
        tie,
    )
    tie, (down1_sum,) = combine(
        links,
        [
            (kg, tower, "all"),
            (vec, tower, "vec"),
            (qkv[0], y, "split"),
            (qkv[1], x, "split"),
            (qkv[2], y, "split"),
            (outp, y, "split"),
            (down2, tower, "split"),
            (down1, F32, "final"),
        ],
    )
    pixel_grads = scatter(links, 1, far_grads, depth, visible, patches, partly)
    pixel_grads = jnp.swapaxes(pixel_grads.reshape(group_chips, bands, pix, patches), 2, 3)
    up = Piece.join(up1, up2, 2)
    tie, (kgrad, down2_sum) = combine(
        links,
        [
            (kg, BF, "final"),
            (qkv[0], tower, "split"),
            (qkv[1], tower, "split"),
            (qkv[2], tower, "split"),
            (outp, tower, "split"),
            (up, tower, "split"),
            (down2, F32, "final"),
        ],
    )
    vecs = links.total(vec.value()).reshape(8, width)
    kgrad = links.total(kgrad.astype(F32)).astype(BF)
    near = [kgrad, links.swap(kgrad, 1), links.swap(kgrad, 0), links.swap(kgrad, 0, 1)]
    turn = lambda bit, a, b: [jnp.where(bit == 0, a, b), jnp.where(bit == 0, b, a)]
    rows_of = [turn(links.bit(1), *near[:2]), turn(links.bit(1), *near[2:])]
    rows_of = [turn(links.bit(0), rows_of[0][i], rows_of[1][i]) for i in range(2)]
    kgrad = jnp.stack([rows_of[i][c] for c in range(2) for i in range(2)])
    kgrad = kgrad.reshape(4, 2, depth // 4, half).astype(F32)
    kernel_grads = jnp.transpose(kgrad, (0, 2, 1, 3)).reshape(bands, pix, width)
    tie, (up_sum, out_sum, *qkv_sums) = combine(
        links,
        [(up, F32, "final"), (outp, F32, "final")] + [(part, F32, "final") for part in qkv],
    )

    block_output = jnp.concatenate(
        [
            out_rows[body : body + chips][:, None, :],
            out_rows[:body].reshape(chips, slots, width),
        ],
        axis=1,
    )
    weight = lambda part: jnp.swapaxes(links.last(part), 0, 1)
    down_sum = jnp.concatenate(
        [down1_sum.reshape(2, block, half), down2_sum.reshape(2, block, half)], axis=0
    )
    return (
        block_output,
        pixel_grads,
        kernel_grads,
        vecs[2],
        vecs[0],
        vecs[1],
        vecs[3],
        vecs[4],
        weight(jnp.concatenate(qkv_sums, axis=0)),
        weight(out_sum),
        weight(up_sum),
        weight(jnp.swapaxes(down_sum, 0, 1).reshape(block, 4 * half)),
    )


def solution(mesh):
    placed = (
        P("dp", "band", None, None),
        P("dp", None),
        P("band", None, None),
        P(),
        P(),
        P(),
        P(),
        P(),
        P(),
        P(),
        P(),
        P(),
        P(("dp", "band"), None, None),
    )
    return jax.shard_map(
        functools.partial(shards, Links(mesh)),
        mesh=mesh,
        in_specs=placed,
        out_specs=(
            P(("dp", "band"), None, None),
            P("dp", "band", None, None),
            P("band", None, None),
            P(),
            P(),
            P(),
            P(),
            P(),
            P("band", "dp"),
            P("band", "dp"),
            P("band", "dp"),
            P("band", "dp"),
        ),
        check_vma=False,
    )
```

```python
import functools

import jax
import jax.numpy as jnp
from jax import lax
from jax.experimental import pallas as pl
from jax.experimental.pallas import tpu as pltpu
from jax.sharding import PartitionSpec as P

HEADS = 12
HEAD = 64
BF = jnp.bfloat16
F32 = jnp.float32
TAIL = 16
BLOCK = 112
KEYS = 80
SCALE = HEAD ** (-0.5)
VMEM = pl.BlockSpec(memory_space=pltpu.VMEM)
HBM = pl.BlockSpec(memory_space=pl.ANY)
shape = jax.ShapeDtypeStruct
MICROSECONDS = {
    "pick_far": 5,
    "prepare": 11,
    "encoder_forward": 31,
    "mlp_back": 32,
    "attention_back": 18,
    "embed_back": 14,
    "combine": 12,
    "touch": 20,
    "scatter": 4,
}


def dot(a, b):
    return jnp.dot(a, b, preferred_element_type=F32)


def dot_nt(a, b):
    return lax.dot_general(a, b, (((1,), (1,)), ((), ())), preferred_element_type=F32)


def dot_tn(a, b):
    return lax.dot_general(a, b, (((0,), (0,)), ((), ())), preferred_element_type=F32)


def kernel_call(body, name, outs, scratch, copies, vmem_in=0, vmem_out=0, mib=58, **more):
    def call(*operands):
        return pl.pallas_call(
            body,
            out_shape=tuple(outs),
            in_specs=[VMEM] * vmem_in + [HBM] * (len(operands) - vmem_in),
            out_specs=(HBM,) * (len(outs) - vmem_out) + (VMEM,) * vmem_out,
            scratch_shapes=[pltpu.VMEM(a.shape, a.dtype) for a in scratch]
            + [pltpu.SemaphoreType.DMA((copies,))],
            compiler_params=pltpu.CompilerParams(vmem_limit_bytes=mib * 1024 * 1024),
            cost_estimate=pl.CostEstimate(
                flops=int(MICROSECONDS[name] * 1.15e9), bytes_accessed=1, transcendentals=0
            ),
            name=name,
            **more,
        )(*operands)

    return call


class Copies:
    def __init__(self, sems):
        self.sems, self.count, self.open = sems, 0, []

    def start(self, source, target):
        copy = pltpu.make_async_copy(source, target, self.sems.at[self.count])
        self.count += 1
        copy.start()
        return copy

    def out(self, source, target):
        self.open.append(self.start(source, target))

    def finish(self):
        for copy in self.open:
            copy.wait()


def chosen(seen_ref, chip, patches):
    first = seen_ref[pl.ds(chip, 1), :]
    second = seen_ref[pl.ds(chip + 1, 1), :]
    slots = first.shape[1]
    seen = jnp.concatenate([first, second], axis=1)
    ids = lax.broadcasted_iota(jnp.int32, (patches, 2 * slots), 0)
    lane = lax.broadcasted_iota(jnp.int32, (patches, 2 * slots), 1)
    hit = ids == seen
    return (
        jnp.where(hit & (lane < slots), 1.0, 0.0).astype(BF),
        jnp.where(hit & (lane >= slots), 1.0, 0.0).astype(BF),
    )


def load_pixels(copies, pixel_hbm, pixel_ref, base, pairs):
    return [
        copies.start(pixel_hbm.at[pl.ds(base + 2 * i, 2)], pixel_ref.at[2 * i : 2 * i + 2])
        for i in range(pairs)
    ]


def pick_pixels(arrive, seen_ref, pixel_ref, out_ref, base):
    for i, copy in enumerate(arrive):
        first, second = chosen(seen_ref, base + 2 * i, pixel_ref.shape[2])
        wide = first.shape[1]
        copy.wait()
        out_ref[:, i * wide : (i + 1) * wide] = (
            dot(pixel_ref[2 * i], first) + dot(pixel_ref[2 * i + 1], second)
        ).astype(BF)


def pick_far_kernel(
    links, pairs, seen_ref, pixel_hbm, halves_hbm, half_hbm, out_hbm, pixel_ref, out_ref, half_ref, sems
):
    copies = Copies(sems)
    base = (1 - links.bit("band")) * 2 * pairs
    half_in = copies.start(halves_hbm.at[links.bit(0)], half_ref)
    arrive = load_pixels(copies, pixel_hbm, pixel_ref, base, pairs)
    half_in.wait()
    copies.out(half_ref, half_hbm)
    pick_pixels(arrive, seen_ref, pixel_ref, out_ref, base)
    copies.out(out_ref, out_hbm)
    copies.finish()


def pick_far(links, seen, pixel_rows, halves):
    chips, depth, patches = pixel_rows.shape
    pairs = chips // 4
    outs = (shape(halves.shape[1:], BF), shape((depth, chips // 2 * seen.shape[1]), BF))
    return kernel_call(
        functools.partial(pick_far_kernel, links, pairs),
        "pick_far",
        outs,
        (shape((2 * pairs, depth, patches), BF), outs[1], outs[0]),
        pairs + 4,
        vmem_in=1,
    )(seen, pixel_rows, halves)


def prepare_kernel(
    links,
    pairs,
    seen_ref,
    pixel_hbm,
    cot_hbm,
    down_hbm,
    picked_hbm,
    rows_hbm,
    gact_hbm,
    pixel_ref,
    cot_ref,
    down_ref,
    picked_ref,
    rows_ref,
    gact_ref,
    tail_ref,
    sems,
):
    copies = Copies(sems)
    chips = cot_ref.shape[0]
    slots = cot_ref.shape[1] - 1
    rows, width = rows_ref.shape
    base = links.bit("band") * 2 * pairs
    cot_in = copies.start(cot_hbm, cot_ref)
    arrive = load_pixels(copies, pixel_hbm, pixel_ref, base, pairs)
    chunk = down_hbm.shape[0] // 4
    parts = [slice(i * chunk, (i + 1) * chunk) for i in range(4)]
    downs = [copies.start(down_hbm.at[part, :], down_ref.at[part, :]) for part in parts]
    cot_in.wait()
    tail_ref[...] = jnp.zeros_like(tail_ref)
    for c in range(chips):
        chip = cot_ref[c].astype(F32)
        rows_ref[c * slots : (c + 1) * slots, :] = chip[1:, :].astype(BF)
        tail_ref[c : c + 1, :] = chip[0:1, :]
    rows_ref[rows - TAIL : rows, :] = tail_ref[...].astype(BF)
    copies.out(rows_ref, rows_hbm)
    pick_pixels(arrive, seen_ref, pixel_ref, picked_ref, base)
    copies.out(picked_ref, picked_hbm)
    for part, copy in zip(parts, downs):
        copy.wait()
        gact_ref[:, part] = dot_nt(rows_ref[...], down_ref[part, :]).astype(BF)
        copies.out(gact_ref.at[:, part], gact_hbm.at[:, part])
    copies.finish()


def prepare(links, seen, pixel_rows, cot, down):
    group, depth, patches = pixel_rows.shape
    pairs = group // 4
    hidden, width = down.shape
    body = cot.shape[0] * seen.shape[1]
    rows = body + TAIL
    outs = (shape((depth, body), BF), shape((rows, width), BF), shape((rows, hidden), BF))
    return kernel_call(
        functools.partial(prepare_kernel, links, pairs),
        "prepare",
        outs,
        (shape((2 * pairs, depth, patches), BF), cot, down) + outs + (shape((TAIL, width), F32),),
        pairs + 12,
        vmem_in=1,
    )(seen, pixel_rows, cot, down)


def row_stats(values):
    average = jnp.mean(values, axis=-1, keepdims=True)
    centred = values - average
    spread = jnp.mean(centred * centred, axis=-1, keepdims=True)
    root = lax.rsqrt(spread + 1e-06)
    return centred * root, root


def norm_back(xhat, root, grad_out, gain):
    scaled = grad_out * gain
    mean_scaled = jnp.mean(scaled, axis=-1, keepdims=True)
    mean_along = jnp.mean(scaled * xhat, axis=-1, keepdims=True)
    return root * (scaled - mean_scaled - xhat * mean_along)


def head_rows(width):
    row = lax.broadcasted_iota(jnp.int32, (TAIL, width), 0)
    lane = lax.broadcasted_iota(jnp.int32, (TAIL, width), 1)
    return (lane // HEAD) == row


def two_heads(pair):
    low = lax.broadcasted_iota(jnp.int32, pair.shape, 1) < HEAD
    zero = jnp.zeros_like(pair)
    return jnp.concatenate([jnp.where(low, pair, zero), jnp.where(low, zero, pair)], axis=0)


def own_heads(stacked):
    rows = stacked.shape[0] // 2
    low = lax.broadcasted_iota(jnp.int32, (rows, stacked.shape[1]), 1) < HEAD
    return jnp.where(low, stacked[:rows], stacked[rows:])


def softmax_keys(scores, count):
    key = lax.broadcasted_iota(jnp.int32, scores.shape, 0)
    scores = jnp.where(key < count, scores * SCALE, -1e30)
    raised = jnp.exp(scores - jnp.max(scores, axis=0, keepdims=True))
    return raised * (1.0 / jnp.sum(raised, axis=0, keepdims=True))


def load_far(links, copies, half_hbm, other_hbm, target):
    count = half_hbm.shape[0]
    core = links.bit(0)
    return [
        copies.start(half_hbm, target.at[pl.ds(pl.multiple_of(core * count, 16), count), :]),
        copies.start(other_hbm, target.at[pl.ds(pl.multiple_of((1 - core) * count, 16), count), :]),
    ]


def forward_kernel(
    links,
    chips,
    vecs_ref,
    xo_hbm,
    xr_hbm,
    ko_hbm,
    half_hbm,
    other_hbm,
    wqkv_hbm,
    wout_hbm,
    cot_hbm,
    gact_hbm,
    up_hbm,
    stream_hbm,
    n1_hbm,
    packed_hbm,
    probs_hbm,
    tprobs_hbm,
    att_hbm,
    mid_hbm,
    n2_hbm,
    act_hbm,
    gpre_hbm,
    down_send_hbm,
    down_keep_hbm,
    up_send_hbm,
    up_keep_hbm,
    stream_ref,
    n1_ref,
    packed_ref,
    probs_ref,
    tprobs_ref,
    att_ref,
    mid_ref,
    n2_ref,
    xo_ref,
    xr_ref,
    ko_ref,
    kr_ref,
    tatt_ref,
    wqkv_ref,
    wout_ref,
    *half_refs,
):
    copies = Copies(half_refs[-1])
    rows, width = n1_ref.shape
    body = rows - TAIL
    slots = body // chips
    token, gain1, bias1, gain2, bias2 = (vecs_ref[i : i + 1, :] for i in range(5))
    first = [
        copies.start(source, target)
        for source, target in ((xo_hbm, xo_ref), (ko_hbm, ko_ref), (xr_hbm, xr_ref))
    ] + load_far(links, copies, half_hbm, other_hbm, kr_ref)
    for copy in first:
        copy.wait()
    wqkv_in = copies.start(wqkv_hbm, wqkv_ref)
    wout_in = copies.start(wout_hbm, wout_ref)
    half = MlpHalf(links, 0, copies, half_refs[:-1])
    for m in range(0, body, 256):
        stream_ref[m : m + 256, :] = dot_tn(xo_ref[:, m : m + 256], ko_ref[...]) + dot_tn(
            xr_ref[:, m : m + 256], kr_ref[...]
        )
    tail_row = lax.broadcasted_iota(jnp.int32, (TAIL, width), 0)
    stream_ref[body:rows, :] = jnp.where(tail_row < chips, token, 0.0)

    def first_norm(i, carry):
        at = pl.ds(pl.multiple_of(i * BLOCK, BLOCK), BLOCK)
        xhat, unused = row_stats(stream_ref[at, :])
        n1_ref[at, :] = (xhat * gain1 + bias1).astype(BF)
        return carry

    lax.fori_loop(0, rows // BLOCK, first_norm, 0)
    wqkv_in.wait()
    half.load(cot_hbm, gact_hbm, up_hbm)
    copies.out(stream_ref, stream_hbm)
    copies.out(n1_ref, n1_hbm)

    def project(j, carry):
        at = pl.ds(pl.multiple_of(j * 256, 256), 256)
        packed_ref[:, at] = dot(n1_ref[...], wqkv_ref[:, at]).astype(BF)
        return carry

    lax.fori_loop(0, 3 * width // 256, project, 0)
    copies.out(packed_ref, packed_hbm)
    tail = packed_ref[body:rows, :]
    heads = head_rows(width)
    tquery = jnp.where(heads, jnp.broadcast_to(tail[0:1, 0:width], (TAIL, width)), 0).astype(BF)
    tatt_ref[...] = jnp.zeros_like(tatt_ref)

    def chip(c, carry):
        at = pl.ds(pl.multiple_of(c * slots, slots), slots)
        key = jnp.concatenate(
            [packed_ref[at, width : 2 * width], tail[:, width : 2 * width]], axis=0
        )
        val = jnp.concatenate([packed_ref[at, 2 * width :], tail[:, 2 * width :]], axis=0)
        tiles = [slice(128 * p, 128 * p + 128) for p in range(width // 128)]
        scores = [dot_nt(key[:, here], two_heads(packed_ref[at, here])) for here in tiles]
        scores.append(dot_nt(key, tquery))
        probs = [softmax_keys(s, slots + 1).astype(BF) for s in scores]
        mixed = [dot_tn(probs[p], val[:, tiles[p]]) for p in range(len(tiles))]
        mixed.append(dot_tn(probs[-1], val))
        for p in range(len(tiles)):
            probs_ref[c, p] = probs[p]
            att_ref[at, tiles[p]] = own_heads(mixed[p]).astype(BF)
        tprobs_ref[c] = probs[-1]
        tatt_ref[pl.ds(c, 1), :] = jnp.sum(jnp.where(heads, mixed[-1], 0.0), axis=0, keepdims=True)
        return carry

    lax.fori_loop(0, chips, chip, 0, unroll=2)
    att_ref[body:rows, :] = tatt_ref[...].astype(BF)
    copies.out(probs_ref, probs_hbm)
    copies.out(tprobs_ref, tprobs_hbm)
    copies.out(att_ref, att_hbm)
    wout_in.wait()

    def out_project(j, carry):
        at = pl.ds(pl.multiple_of(j * 256, 256), 256)
        mid_ref[:, at] = stream_ref[:, at] + dot(att_ref[...], wout_ref[:, at])
        return carry

    lax.fori_loop(0, width // 256, out_project, 0)
    copies.out(mid_ref, mid_hbm)

    def second_norm(i, carry):
        at = pl.ds(pl.multiple_of(i * BLOCK, BLOCK), BLOCK)
        xhat, unused = row_stats(mid_ref[at, :])
        n2_ref[at, :] = (xhat * gain2 + bias2).astype(BF)
        return carry

    lax.fori_loop(0, rows // BLOCK, second_norm, 0)
    copies.out(n2_ref, n2_hbm)
    half.run(n2_ref, (down_send_hbm, down_keep_hbm), (up_send_hbm, up_keep_hbm))
    copies.out(half.act, act_hbm)
    copies.out(half.gpre, gpre_hbm)
    copies.finish()


class MlpHalf:
    def __init__(self, links, third, copies, refs):
        self.links, self.third, self.copies = links, third, copies
        self.cot, self.gact, self.up, self.act, self.gpre, self.stage, self.grad = refs

    @staticmethod
    def scratch(rows, width, hidden, more=0):
        half = width // 2
        return (
            shape((rows, width), BF),
            shape((rows, hidden // 2), BF),
            shape((width, hidden // 2), BF),
            shape((rows, hidden // 2), BF),
            shape((rows, hidden // 2), BF),
            shape((2, more + 2 * width + hidden // 2, half), BF),
            shape((hidden // 4, width), BF),
        )

    def load(self, cot_hbm, gact_hbm, up_hbm):
        chunk = up_hbm.shape[1] // 4
        start = self.copies.start
        far = lambda i: slice((2 * i + self.third) * chunk, (2 * i + self.third + 1) * chunk)
        near = lambda i: slice(i * chunk, (i + 1) * chunk)
        self.first = [
            (
                start(up_hbm.at[:, far(i)], self.up.at[:, near(i)]),
                start(gact_hbm.at[:, far(i)], self.gact.at[:, near(i)]),
            )
            for i in range(2)
        ]
        self.cot_in = start(cot_hbm, self.cot)

    def run(self, n2_ref, down_out, up_out):
        copies, links = self.copies, self.links
        rows, width = n2_ref.shape
        chunk = self.up.shape[1] // 2
        half = width // 2
        block = width // 16
        tile = 256
        for i in range(2):
            for copy in self.first[i]:
                copy.wait()
            for j in range(i * chunk, (i + 1) * chunk, tile):
                cols = slice(j, j + tile)
                pre = dot(n2_ref[...], self.up[:, cols])
                phi = 0.5 + 0.5 * lax.erf(pre * (0.5**0.5))
                bell = jnp.exp(-0.5 * pre * pre) * 0.3989422804014327
                self.act[:, cols] = (pre * phi).astype(BF)
                gact = self.gact[:, cols].astype(F32)
                self.gpre[:, cols] = (gact * (phi + pre * bell)).astype(BF)
        where = (1, "band") if self.third == 0 else (0, 0)
        bits = [links.bit(w) for w in where]
        self.cot_in.wait()
        for i in range(2):
            for m in range(0, width, 256):
                self.grad[m : m + 256, :] = dot_tn(
                    self.cot[:, m : m + 256], self.act[:, i * chunk : (i + 1) * chunk]
                ).astype(BF)
            for side, bit in ((0, 1 - bits[0]), (1, bits[0])):
                for other in range(2):
                    x, c = (bit, other) if where[0] == 1 else (other, bit)
                    for z in range(4):
                        at = pl.multiple_of(((z * 2 + x) * 2 + c) * block, 16)
                        piece = self.grad[pl.ds(at, block), :]
                        for h in range(2):
                            to = (((other * 2 + i) * 2 + h) * 4 + z) * block
                            self.stage[side, to : to + block, :] = piece[:, h * half : (h + 1) * half]
        middle = 2 * width
        for side in range(2):
            copies.out(self.stage.at[side, 0:middle, :], down_out[side])
        part = chunk // 4
        for i in range(2):
            for m in range(0, chunk, 256):
                self.grad[m : m + 256, :] = dot_tn(
                    self.gpre[:, i * chunk + m : i * chunk + m + 256], n2_ref[...]
                ).astype(BF)
            for side, bit in ((0, 1 - bits[1]), (1, bits[1])):
                for x in range(2):
                    for other in range(2):
                        if where[1] == "band":
                            at = (2 * x + other) * part
                            cols = pl.ds(pl.multiple_of(bit * half, 128), half)
                        else:
                            at = pl.multiple_of((2 * x + bit) * part, 16)
                            cols = slice(other * half, (other + 1) * half)
                        to = middle + ((i * 2 + x) * 2 + other) * part
                        self.stage[side, to : to + part, :] = self.grad[pl.ds(at, part), cols]
        for side in range(2):
            copies.out(self.stage.at[side, middle : middle + 8 * part, :], up_out[side])


def forward(links, chips, vecs, xo, xr, ko, half, other, wqkv, wout, cot, gact, up):
    width, hidden = up.shape
    body = xo.shape[1]
    rows = body + TAIL
    saved = (
        shape((rows, width), F32),
        shape((rows, width), BF),
        shape((rows, 3 * width), BF),
        shape((chips, width // 128, KEYS, 128), BF),
        shape((chips, KEYS, TAIL), BF),
        shape((rows, width), BF),
        shape((rows, width), F32),
        shape((rows, width), BF),
    )
    return kernel_call(
        functools.partial(forward_kernel, links, chips),
        "encoder_forward",
        saved
        + (shape((rows, hidden // 2), BF),) * 2
        + (shape((2 * width, width // 2), BF),) * 2
        + (shape((hidden // 2, width // 2), BF),) * 2,
        saved
        + (xo, xr, ko, ko, shape((TAIL, width), F32), wqkv, wout)
        + MlpHalf.scratch(rows, width, hidden),
        32,
        vmem_in=1,
    )(vecs, xo, xr, ko, half, other, wqkv, wout, cot, gact, up)


def spread_blocks(links, full_ref, stage, parts):
    core = links.bit(0)
    cols = full_ref.shape[1] // 2
    block = full_ref.shape[0] // 16
    for z in range(4):
        for x in range(2):
            for side, c in ((0, 1 - core), (1, core)):
                start = ((z * 2 + x) * 2 + c) * block
                for first, count in parts:
                    rows = full_ref[pl.ds(pl.multiple_of(start, 16), count), :]
                    start = start + count
                    for b in range(2):
                        to = first + ((x * 2 + b) * 4 + z) * count
                        stage[side, to : to + count, :] = rows[:, b * cols : (b + 1) * cols]


def mlp_back_kernel(
    links,
    after,
    vecs_ref,
    n2_hbm,
    gact_hbm,
    act1_hbm,
    gpre1_hbm,
    up_hbm,
    down_hbm,
    mid_hbm,
    cot_hbm,
    att_hbm,
    wout_hbm,
    *rest,
):
    rest = rest[after:]
    sends, (keep_hbm, gmid_hbm, gatt_hbm, out_hbm, vec_ref) = rest[:3], rest[3:8]
    (
        n2_ref,
        gmid_ref,
        gatt_ref,
        out_ref,
        act_ref,
        gpre_ref,
        up_ref,
        down_ref,
        mid_ref,
        att_ref,
        wout_ref,
        back_ref,
        branch_ref,
        full_ref,
    ) = rest[8:22]
    half_refs, sems = rest[22:-1], rest[-1]
    copies = Copies(sems)
    rows, width = mid_ref.shape
    quarter = up_hbm.shape[1] // 4
    at = lambda i: slice(i * quarter, (i + 1) * quarter)
    n2_in = copies.start(n2_hbm, n2_ref)
    half = MlpHalf(links, 1, copies, half_refs)
    half.load(cot_hbm, gact_hbm, up_hbm)
    cot_ref = half.cot
    n2_in.wait()
    first_in = [copies.start(gpre1_hbm, gpre_ref)] + [
        copies.start(up_hbm.at[:, at(2 * i)], up_ref.at[:, at(i)]) for i in range(2)
    ]
    norm_in = copies.start(mid_hbm, mid_ref)
    att_in = copies.start(att_hbm, att_ref)
    wout_in = copies.start(wout_hbm, wout_ref)
    middle = 2 * width
    end = middle + up_hbm.shape[1] // 2
    half.run(
        n2_ref,
        (sends[0], keep_hbm.at[0:middle, :]),
        (sends[1], keep_hbm.at[middle:end, :]),
    )
    late = [copies.start(act1_hbm, act_ref)] + [
        copies.start(down_hbm.at[at(2 * i + third), :], down_ref.at[at(2 * third + i), :])
        for third in range(2)
        for i in range(2)
    ]
    for copy in first_in:
        copy.wait()
    for j in range(0, width, 256):
        cols = slice(j, j + 256)
        back_ref[:, cols] = dot_nt(gpre_ref[...], up_ref[cols, :]) + dot_nt(
            half.gpre[...], half.up[cols, :]
        )
    norm_in.wait()
    gain = vecs_ref[3:4, :]

    def norm(i, carry):
        at = pl.ds(pl.multiple_of(i * BLOCK, BLOCK), BLOCK)
        xhat, root = row_stats(mid_ref[at, :])
        grad = back_ref[at, :]
        total = cot_ref[at, :].astype(F32) + norm_back(xhat, root, grad, gain)
        gmid_ref[at, :] = total
        branch_ref[at, :] = total.astype(BF)
        return (
            carry[0] + jnp.sum(grad * xhat, axis=0, keepdims=True),
            carry[1] + jnp.sum(grad, axis=0, keepdims=True),
        )

    zero = jnp.zeros((1, width), F32)
    gain_sum, bias_sum = lax.fori_loop(0, rows // BLOCK, norm, (zero, zero))
    vec_ref[0:1, :] = gain_sum
    vec_ref[1:2, :] = bias_sum
    copies.out(gmid_ref, gmid_hbm)
    att_in.wait()
    for m in range(0, width, 256):
        full_ref[m : m + 256, :] = dot_tn(branch_ref[:, m : m + 256], att_ref[...]).astype(BF)
    spread_blocks(links, full_ref, half.stage, [(end, width // 16)])
    for side, target in ((0, sends[2]), (1, keep_hbm.at[end : end + width, :])):
        copies.out(half.stage.at[side, end : end + width, :], target)
    wout_in.wait()
    for j in range(0, width, 256):
        gatt_ref[:, j : j + 256] = dot_nt(branch_ref[...], wout_ref[j : j + 256, :]).astype(BF)
    copies.out(gatt_ref, gatt_hbm)
    for copy in late:
        copy.wait()
    for j in range(0, width, 256):
        cols = slice(j, j + 256)
        out_ref[:, cols] = (
            mid_ref[:, cols]
            + dot(act_ref[...], down_ref[: 2 * quarter, cols])
            + dot(half.act[...], down_ref[2 * quarter :, cols])
        ).astype(BF)
    copies.out(out_ref, out_hbm)
    copies.finish()


def mlp_back(links, vecs, n2, gact, act1, gpre1, up, down, mid, cot, att, wout, after):
    rows, width = mid.shape
    hidden = up.shape[1]
    sums = shape((3 * width + hidden // 2, width // 2), BF)
    return kernel_call(
        functools.partial(mlp_back_kernel, links, len(after)),
        "mlp_back",
        tuple(shape((count, width // 2), BF) for count in (2 * width, hidden // 2, width))
        + (sums, mid, cot, cot, shape((2, width), F32)),
        (n2, mid, cot, cot, act1, gpre1)
        + (shape((width, hidden // 2), BF), down, mid, att, wout, mid, cot, wout)
        + MlpHalf.scratch(rows, width, hidden, width),
        40,
        vmem_in=1,
        vmem_out=1,
    )(vecs, n2, gact, act1, gpre1, up, down, mid, cot, att, wout, *after)


def split_vec(vec):
    high = vec.astype(BF)
    return high, (vec - high.astype(F32)).astype(BF)


def attention_back_kernel(
    links, chips, after, gatt_hbm, packed_hbm, probs_hbm, tprobs_hbm, n1_hbm, *rest
):
    gpacked_hbm, send_hbm, keep_hbm = rest[after : after + 3]
    (
        gpacked_ref,
        gatt_ref,
        packed_ref,
        probs_ref,
        tprobs_ref,
        n1_ref,
        tgrad_ref,
        tout_ref,
        full_ref,
        stage_ref,
        sems,
    ) = rest[after + 3 :]
    rows, width = n1_ref.shape
    body = rows - TAIL
    slots = body // chips
    copies = Copies(sems)
    arrive = [
        copies.start(source, target)
        for source, target in (
            (packed_hbm, packed_ref),
            (gatt_hbm, gatt_ref),
            (probs_hbm, probs_ref),
            (tprobs_hbm, tprobs_ref),
        )
    ]
    tout_ref[...] = jnp.zeros_like(tout_ref)
    heads = head_rows(width)
    for copy in arrive:
        copy.wait()
    n1_in = copies.start(n1_hbm, n1_ref)
    tgrad_ref[...] = gatt_ref[body:rows, :].astype(F32)
    tail = packed_ref[body:rows, :]
    tquery = jnp.where(heads, jnp.broadcast_to(tail[0:1, 0:width], (TAIL, width)), 0).astype(BF)

    def chip(c, carry):
        at = pl.ds(pl.multiple_of(c * slots, slots), slots)
        key_all = jnp.concatenate(
            [packed_ref[at, width : 2 * width], tail[:, width : 2 * width]], axis=0
        )
        val_all = jnp.concatenate([packed_ref[at, 2 * width :], tail[:, 2 * width :]], axis=0)
        tgrad = jnp.where(
            heads, jnp.broadcast_to(tgrad_ref[pl.ds(c, 1), :], (TAIL, width)), 0.0
        ).astype(BF)
        tiles = [slice(128 * p, 128 * p + 128) for p in range(width // 128)]
        probs = [probs_ref[c, p] for p in range(len(tiles))] + [tprobs_ref[c]]
        gouts = [two_heads(gatt_ref[at, here]) for here in tiles]
        queries = [two_heads(packed_ref[at, here]) for here in tiles]
        gprobs = [dot_nt(val_all[:, tiles[p]], gouts[p]) for p in range(len(tiles))]
        gprobs.append(dot_nt(val_all, tgrad))
        gscores = []
        for prob, gprob in zip(probs, gprobs):
            wide = prob.astype(F32)
            inner = jnp.sum(gprob * wide, axis=0, keepdims=True)
            gscores.append((wide * (gprob - inner) * SCALE).astype(BF))
        gval_tail = dot(probs[-1], tgrad)
        gkey_tail = dot(gscores[-1], tquery)
        mixed = jnp.where(heads, dot_tn(gscores[-1], key_all), 0.0)
        gvals = [dot(probs[p], gouts[p]) + gval_tail[:, tiles[p]] for p in range(len(tiles))]
        gkeys = [dot(gscores[p], queries[p]) + gkey_tail[:, tiles[p]] for p in range(len(tiles))]
        gqueries = [own_heads(dot_tn(gscores[p], key_all[:, tiles[p]])) for p in range(len(tiles))]
        for p in range(len(tiles)):
            gpacked_ref[at, 128 * p : 128 * p + 128] = gqueries[p].astype(BF)
            base = width + 128 * p
            gpacked_ref[at, base : base + 128] = gkeys[p][:slots].astype(BF)
            gpacked_ref[at, width + base : width + base + 128] = gvals[p][:slots].astype(BF)
        tout_ref[pl.ds(c, 1), :] = jnp.concatenate(
            [jnp.sum(mixed, axis=0, keepdims=True)]
            + [g[slots : slots + 1] for g in gkeys + gvals],
            axis=1,
        )
        return carry

    lax.fori_loop(0, chips, chip, 0, unroll=2)
    gpacked_ref[body:rows, :] = tout_ref[...].astype(BF)
    copies.out(gpacked_ref, gpacked_hbm)
    n1_in.wait()
    for m in range(0, 3 * width, 256):
        full_ref[m : m + 256, :] = dot_tn(gpacked_ref[:, m : m + 256], n1_ref[...]).astype(BF)
    spread_blocks(links, full_ref, stage_ref, qkv_parts(width))
    copies.out(stage_ref.at[0], send_hbm)
    copies.out(stage_ref.at[1], keep_hbm)
    copies.finish()


def qkv_parts(width):
    block = 3 * width // 16
    count = -(-block // 32) * 16
    return [(0, count), (16 * count, block - count)]


def attention_back(links, chips, gatt, packed, probs, tprobs, n1, after):
    rows, width = n1.shape
    sums = shape((3 * width, width // 2), BF)
    return kernel_call(
        functools.partial(attention_back_kernel, links, chips, len(after)),
        "attention_back",
        (packed, sums, sums),
        (packed, gatt, packed, probs, tprobs, n1)
        + (
            shape((TAIL, width), F32),
            shape((TAIL, 3 * width), F32),
            shape((3 * width, width), BF),
            shape((2,) + sums.shape, BF),
        ),
        10,
    )(gatt, packed, probs, tprobs, n1, *after)


def embed_back_kernel(
    links,
    chips,
    after,
    vecs_ref,
    vec2_ref,
    gpacked_hbm,
    wqkv_hbm,
    stream_hbm,
    gmid_hbm,
    xo_hbm,
    xr_hbm,
    ko_hbm,
    half_hbm,
    other_hbm,
    *rest,
):
    send_hbm, keep_hbm, own_hbm, far_hbm, vec_ref = rest[after : after + 5]
    (
        gpacked_ref,
        wqkv_ref,
        stream_ref,
        gmid_ref,
        xo_ref,
        xr_ref,
        ko_ref,
        kr_ref,
        send_ref,
        keep_ref,
        pgrad_ref,
        back_ref,
        embed_ref,
        kfull_ref,
        sems,
    ) = rest[after + 5 :]
    rows, width = stream_ref.shape
    body = rows - TAIL
    half = width // 2
    copies = Copies(sems)
    thirds = [slice(i * width, (i + 1) * width) for i in range(3)]
    arrive = [
        (
            copies.start(gpacked_hbm.at[:, part], gpacked_ref.at[:, part]),
            copies.start(wqkv_hbm.at[:, part], wqkv_ref.at[:, part]),
        )
        for part in thirds
    ]
    late = [copies.start(stream_hbm, stream_ref), copies.start(gmid_hbm, gmid_ref)]
    for i, part in enumerate(thirds):
        for copy in arrive[i]:
            copy.wait()
        if i == 1:
            last = [
                copies.start(source, target)
                for source, target in ((xo_hbm, xo_ref), (xr_hbm, xr_ref), (ko_hbm, ko_ref))
            ] + load_far(links, copies, half_hbm, other_hbm, kr_ref)
        grad = dot_nt(gpacked_ref[:, part], wqkv_ref[:, part])
        back_ref[...] = grad if i == 0 else back_ref[...] + grad
    for copy in late:
        copy.wait()
    gain = vecs_ref[1:2, :]

    def norm(i, carry):
        at = pl.ds(pl.multiple_of(i * BLOCK, BLOCK), BLOCK)
        xhat, root = row_stats(stream_ref[at, :])
        grad = back_ref[at, :]
        total = gmid_ref[at, :] + norm_back(xhat, root, grad, gain)
        back_ref[at, :] = total
        embed_ref[at, :] = total.astype(BF)
        return (
            carry[0] + jnp.sum(grad * xhat, axis=0, keepdims=True),
            carry[1] + jnp.sum(grad, axis=0, keepdims=True),
        )

    zero = jnp.zeros((1, width), F32)
    gain_sum, bias_sum = lax.fori_loop(0, rows // BLOCK, norm, (zero, zero))
    token_sum = jnp.sum(back_ref[body:rows, :], axis=0, keepdims=True)
    vec_ref[...] = jnp.zeros_like(vec_ref)
    for i, v in enumerate((gain_sum, bias_sum, token_sum, vec2_ref[0:1, :], vec2_ref[1:2, :])):
        vec_ref[2 * i : 2 * i + 1, :] = v[:, :half]
        vec_ref[2 * i + 1 : 2 * i + 2, :] = v[:, half:]
    for copy in last:
        copy.wait()
    grad = embed_ref[0:body, :]
    depth = xo_ref.shape[0]
    core, band = links.bit(0), links.bit("band")
    kfull_ref[0] = dot(xo_ref[...], grad).astype(BF)
    kfull_ref[1] = dot(xr_ref[...], grad).astype(BF)
    piece = depth // 4
    for c, ref in ((1 - core, send_ref), (core, keep_ref)):
        for far in range(2):
            for x in range(2):
                start = pl.multiple_of(c * (depth // 2) + x * piece, 16)
                block = kfull_ref[far, pl.ds(start, piece), :]
                for h in range(2):
                    slot = ((far + band - 2 * far * band) * 2 + x) * 2 + h
                    to = pl.ds(pl.multiple_of(slot * piece, 16), piece)
                    ref[to, :] = block[:, h * half : (h + 1) * half]
    high, low = split_vec(vec_ref[...])
    send_ref[2 * depth : 2 * depth + 16, :] = high
    send_ref[2 * depth + 16 : 2 * depth + 32, :] = low
    vec_ref[...] = high.astype(F32) + low.astype(F32)
    copies.out(send_ref, send_hbm)
    copies.out(keep_ref, keep_hbm)
    middle = body // 2
    for side, kernel, target in ((0, kr_ref, far_hbm), (1, ko_ref, own_hbm)):
        for h in range(2):
            part = grad[h * middle : (h + 1) * middle]
            pgrad_ref[side, h] = dot_nt(kernel[...], part).astype(BF)
        copies.out(pgrad_ref.at[side], target)
    copies.finish()


def embed_back(
    links, chips, vecs, vec2, gpacked, wqkv, stream, gmid, xo, xr, ko, half, other, after
):
    rows, width = stream.shape
    depth, body = xo.shape
    cols = width // 2
    send, keep = shape((2 * depth + 32, cols), BF), shape((2 * depth, cols), BF)
    pgrad = shape((2, depth, body // 2), BF)
    return kernel_call(
        functools.partial(embed_back_kernel, links, chips, len(after)),
        "embed_back",
        (send, keep, pgrad, pgrad, shape((16, cols), F32)),
        (gpacked, wqkv, stream, gmid, xo, xr, ko, ko, send, keep)
        + (
            shape((2,) + pgrad.shape, BF),
            stream,
            shape((rows, width), BF),
            shape((2, depth, width), BF),
        ),
        24,
        vmem_in=2,
        vmem_out=1,
    )(vecs, vec2, gpacked, wqkv, stream, gmid, xo, xr, ko, half, other, *after)


def scatter_kernel(links, side, pairs, depth, seen_ref, grad_hbm, *rest):
    out_hbm, grad_ref, out_ref, sems = rest[-4:]
    patches = out_ref.shape[2]
    copies = Copies(sems)
    copies.start(grad_hbm.at[0 : 2 * depth, :], grad_ref).wait()
    band = links.bit("band")
    base = (band if side == 0 else 1 - band) * 2 * pairs
    for i in range(pairs):
        first, second = chosen(seen_ref, base + 2 * i, patches)
        wide = first.shape[1]
        h, at = divmod(i * wide, grad_ref.shape[1])
        grad = grad_ref[h * depth : (h + 1) * depth, at : at + wide]
        out_ref[2 * i] = dot_nt(grad, first)
        out_ref[2 * i + 1] = dot_nt(grad, second)
        copies.out(out_ref.at[2 * i : 2 * i + 2], out_hbm.at[pl.ds(base + 2 * i, 2)])
    copies.finish()


def scatter(links, side, grads, depth, seen, patches, *earlier):
    chips = seen.shape[0]
    pairs = chips // 4
    return kernel_call(
        functools.partial(scatter_kernel, links, side, pairs, depth),
        "scatter",
        (shape((chips, depth, patches), F32),),
        (shape((2 * depth, grads.shape[1]), BF), shape((2 * pairs, depth, patches), F32)),
        pairs + 1,
        vmem_in=1,
        input_output_aliases={2: 0} if earlier else {},
    )(seen, grads, *earlier)[0]


class Links:
    def __init__(self, mesh):
        self.count = mesh.shape["dp"]
        self.extra = self.count // 16

    def swap(self, array, *where):
        flip = sum((1 << w) * self.extra for w in where if w != "band")
        if "band" not in where:
            return lax.ppermute(array, "dp", [(d, d ^ flip) for d in range(self.count)])
        if flip == 0:
            return lax.ppermute(array, "band", [(0, 1), (1, 0)])
        pairs = [
            (2 * d + b, 2 * (d ^ flip) + 1 - b) for d in range(self.count) for b in range(2)
        ]
        return lax.ppermute(array, ("dp", "band"), pairs)

    def bit(self, where):
        if where == "band":
            return lax.axis_index("band")
        return lax.rem(lax.div(lax.axis_index("dp"), self.extra << where), 2)

    def groups(self):
        return [[block * self.extra + i for i in range(self.extra)] for block in range(16)]

    def last(self, array):
        if self.extra == 1:
            return array
        return lax.psum_scatter(
            array, "dp", scatter_dimension=0, tiled=True, axis_index_groups=self.groups()
        )

    def total(self, array):
        if self.extra == 1:
            return array
        return lax.psum(array, "dp", axis_index_groups=self.groups())


class Level:
    def __init__(self, owner, terms, gone=frozenset(), rounded=False, alt=None, choice=None):
        self.owner, self.terms, self.gone, self.rounded = owner, list(terms), frozenset(gone), rounded
        self.alt, self.choice = alt, choice

    def moving(self, gone):
        strides = self.owner.strides(self.gone)
        return [(name, strides[name]) for name in self.owner.names if name in gone and name in strides]


class Piece:
    def __init__(self, names, sizes, unit, terms, gone=()):
        self.names, self.sizes, self.unit = list(names), list(sizes), unit
        self.gone = frozenset(gone)
        self.levels = [Level(self, terms, self.gone)]

    @staticmethod
    def join(first, second, choice):
        joined = Piece(first.names, first.sizes, first.unit, (), first.gone)
        joined.levels = [
            Level(a.owner, a.terms, a.gone, a.rounded, b, choice)
            for a, b in zip(first.levels, second.levels)
        ]
        return joined

    def strides(self, gone):
        found, stride = {}, self.unit
        for name, size in reversed(list(zip(self.names, self.sizes))):
            if name not in gone:
                found[name] = stride
                stride = stride * size
        return found

    def layout(self, names):
        gone = self.gone | frozenset(names)
        last = max([i for i, name in enumerate(self.names) if name in gone], default=-1)
        post = self.unit
        for size in self.sizes[last + 1 :]:
            post = post * size
        loops = [{}]
        for name, size in list(zip(self.names, self.sizes))[: last + 1]:
            if name not in gone:
                loops = [{**at, name: i} for at in loops for i in range(size)]
        return post * len(loops), post, loops


class Vec:
    def __init__(self, kept, came):
        self.kept, self.came = kept, [came]

    def value(self):
        parts = [
            buffer[at : at + 16].astype(F32) + buffer[at + 16 : at + 32].astype(F32)
            for buffer, at in self.came
        ]
        return pairwise([self.kept] + parts)


def pairwise(parts):
    while len(parts) > 1:
        parts = [
            parts[i] + parts[i + 1] if i + 1 < len(parts) else parts[i]
            for i in range(0, len(parts), 2)
        ]
    return parts[0]


def combine_kernel(links, tasks, n_in, n_out, n_load, after, *refs):
    ins, refs = refs[:n_in], refs[n_in + after :]
    out_hbm, refs = refs[:n_out], refs[n_out:]
    loads, refs = refs[:n_load], refs[n_load:]
    staged, sems = refs[:-1], refs[-1]
    copies = Copies(sems)
    bits = {where: links.bit(where) for where in (0, 1, 2, 3, "band")}
    waits = []
    for task in tasks:
        mine = []
        waits.append(mine)
        if task["kind"] == "raw":
            mine.append(copies.start(ins[task["from"]], loads[task["slot"]]))
            continue
        if task["kind"] == "vec":
            mine += [
                copies.start(ins[i].at[at : at + count, :], loads[slot])
                for i, at, count, slot in task["loads"]
            ]
            continue
        index = {
            name: (1 - bits[name]) if name in task["flip"] else bits[name] for name in bits
        }
        for load in task["loads"]:
            moving = sum((index[name] * stride for name, stride in load["moving"]), load["at"])
            alt_moving = sum(
                (index[name] * stride for name, stride in load["alt_moving"]), load["alt_at"]
            )
            for p, base in enumerate(load["bases"]):
                rows = pl.ds(pl.multiple_of(moving + base, 16), load["post"])
                target = loads[load["slot"]].at[p * load["post"] : (p + 1) * load["post"], :]
                sem = copies.sems.at[copies.count]
                copies.count += 1
                if load["alt"] is None:
                    copy = pltpu.make_async_copy(ins[load["in"]].at[rows, :], target, sem)
                    copy.start()
                else:
                    chosen_bit = index[load["choice"]]
                    copy = pltpu.make_async_copy(ins[load["in"]].at[rows, :], target, sem)
                    rows = pl.ds(pl.multiple_of(alt_moving + base, 16), load["post"])
                    other = pltpu.make_async_copy(ins[load["alt"]].at[rows, :], target, sem)
                    pl.when(chosen_bit == 0)(copy.start)
                    pl.when(chosen_bit == 1)(other.start)
                mine.append(copy)
    for task, mine in zip(tasks, waits):
        for copy in mine:
            copy.wait()
        if task["kind"] == "raw":
            copies.out(loads[task["slot"]], out_hbm[task["out"]].at[task["at"], :])
            continue
        if task["kind"] == "vec":
            parts = [loads[task["loads"][0][3]][...]]
            for unused, also, count, slot in task["loads"][1:]:
                parts.append(loads[slot][0:16, :].astype(F32) + loads[slot][16:32, :].astype(F32))
            high, low = split_vec(pairwise(parts))
            sent, kept = staged[task["stage"]], staged[task["stage"] + 1]
            sent[0:16, :] = high
            sent[16:32, :] = low
            kept[...] = high.astype(F32) + low.astype(F32)
            for out, at in task["outs"]:
                copies.out(sent, out_hbm[out].at[at, :])
            copies.out(kept, out_hbm[task["kept"]])
            continue
        total = None
        for rounded, slots in task["sum"]:
            parts = [loads[slot][...].astype(F32) for slot in slots]
            if total is not None:
                parts = [total.astype(BF).astype(F32) if rounded else total] + parts
            total = pairwise(parts)
        result = staged[task["stage"]]
        result[...] = total.astype(result.dtype)
        for out, at in task["outs"]:
            copies.out(result, out_hbm[out].at[at, :])
    copies.finish()


def combine(links, steps, after=(), mib=58):
    ins, tasks, loads, stages, sends, outs = [], [], [], [], {}, []
    copies = 0
    returned = []

    def index_of(array):
        for i, other in enumerate(ins):
            if other is array:
                return i
        ins.append(array)
        return len(ins) - 1

    def send_to(where, count):
        if where not in sends:
            sends[where] = len(outs)
            outs.append([0, BF])
        at = outs[sends[where]][0]
        outs[sends[where]][0] += count
        return sends[where], slice(at, at + count)

    def places(names):
        return [
            tuple(name for k, name in enumerate(names) if mask >> k & 1)
            for mask in range(1, 1 << len(names))
        ]

    for piece, names, mode in steps:
        if mode == "raw":
            out, at = send_to(names, piece.shape[0])
            tasks.append(
                {"kind": "raw", "from": index_of(piece), "out": out, "at": at, "slot": len(loads)}
            )
            loads.append(piece)
            returned.append((out, at))
            copies += 2
            continue
        if mode == "vec":
            task = {"kind": "vec", "loads": [], "stage": len(stages)}
            width = piece.kept.shape[1]
            for array, at, count in [(piece.kept, 0, 16)] + [(b, at, 32) for b, at in piece.came]:
                task["loads"].append((index_of(array), at, count, len(loads)))
                loads.append(shape((count, width), array.dtype))
            stages += [shape((32, width), BF), shape((16, width), F32)]
            task["outs"] = [send_to(place, 32) for place in places(names)]
            task["kept"] = len(outs)
            outs.append([16, F32])
            copies += len(task["loads"]) + len(task["outs"]) + 1
            tasks.append(task)
            returned.append(task)
            continue
        split = names if mode == "split" else ()
        count, post, loops = piece.layout(split)
        width = piece.levels[0].terms[0][0].shape[1]
        if mode == "final":
            groups = [((), [(len(outs), slice(0, count))])]
            outs.append([count, names])
            returned.append(len(outs) - 1)
            kind = names
        elif mode == "all":
            groups = [((), [send_to(place, count) for place in places(names)])]
            kind = BF
        else:
            groups = [(place, [send_to(place, count)]) for place in places(names)]
            kind = BF
        if mode != "final":
            returned.append([out for unused, targets in groups for out in targets])
        gone = piece.gone | frozenset(split)
        for flip, targets in groups:
            task = {"kind": "sum", "flip": flip, "loads": [], "sum": [], "stage": len(stages)}
            stages.append(shape((count, width), kind))
            task["outs"] = targets
            copies += len(targets)
            for level in piece.levels:
                strides = level.owner.strides(level.gone)
                slots = []
                for t, (array, at) in enumerate(level.terms):
                    slots.append(len(loads))
                    alt, alt_at = None, at
                    if level.alt is not None:
                        buffer, alt_at = level.alt.terms[t]
                        alt = index_of(buffer)
                    task["loads"].append(
                        {
                            "in": index_of(array),
                            "alt": alt,
                            "alt_at": alt_at,
                            "alt_moving": level.alt.moving(gone) if level.alt is not None else (),
                            "choice": level.choice,
                            "at": at,
                            "moving": level.moving(gone),
                            "bases": [
                                sum(i * strides[name] for name, i in loop.items()) for loop in loops
                            ],
                            "post": post,
                            "slot": len(loads),
                        }
                    )
                    loads.append(shape((count, width), array.dtype))
                    copies += len(loops)
                task["sum"].append((level.rounded, slots))
            tasks.append(task)
    results = kernel_call(
        functools.partial(
            combine_kernel,
            links,
            tasks,
            len(ins),
            len(outs),
            len(loads),
            len(after),
        ),
        "combine",
        [shape((count, width), kind) for count, kind in outs],
        loads + stages,
        copies,
        mib=mib,
    )(*ins, *after)
    came = {out: links.swap(results[out], *where) for where, out in sends.items()}
    values = []
    for (piece, names, mode), back in zip(steps, returned):
        if mode == "final":
            values.append(results[back])
        elif mode == "raw":
            values.append((came[back[0]], back[1].start))
        elif mode == "vec":
            piece.kept = results[back["kept"]]
            piece.came = [(came[out], at.start) for out, at in back["outs"]]
        else:
            if mode == "split":
                piece.gone = piece.gone | frozenset(names)
            piece.levels.append(
                Level(
                    piece, [(came[out], at.start) for out, at in back], piece.gone, mode == "all"
                )
            )
    return [results[out] for out in sends.values()], values


def touch_kernel(count, *refs):
    copies = Copies(refs[-1])
    loads = [copies.start(refs[i].at[0:16, 0:128], refs[-2].at[i]) for i in range(count)]
    for copy in loads:
        copy.wait()
    total = refs[-2][0].astype(F32)
    for i in range(1, count):
        total = total + refs[-2][i].astype(F32)
    refs[-3][...] = total


def touch(after, *pieces):
    buffers = []
    for piece in pieces:
        buffer = piece.levels[-1].terms[0][0]
        if not any(buffer is other for other in buffers):
            buffers.append(buffer)
    count = len(buffers)
    return kernel_call(
        functools.partial(touch_kernel, count),
        "touch",
        (shape((16, 128), F32),),
        (shape((count, 16, 128), BF),),
        count,
        vmem_out=1,
    )(*buffers, *after)[0]


def shards(
    links,
    pixels,
    visible,
    kernels,
    class_token,
    norm1_gain,
    norm1_bias,
    norm2_gain,
    norm2_bias,
    attn_qkv,
    attn_out,
    mlp_up,
    mlp_down,
    cotangent,
):
    width = attn_out.shape[0]
    half = width // 2
    chips = cotangent.shape[0]
    group_chips, bands, patches, pix = pixels.shape
    slots = visible.shape[1]
    body = chips * slots
    depth = bands * pix
    block = width // 16
    flat = lambda a: a.reshape(-1, half)
    core_swap = lambda a: (links.swap(flat(a), 0), 0)

    pixel_rows = jnp.swapaxes(pixels, 2, 3).reshape(group_chips, depth, patches)
    kernels_own = kernels.reshape(depth, width)
    my_half, picked_far = pick_far(
        links, visible, pixel_rows, kernels_own.reshape(2, depth // 2, width)
    )
    far_half = links.swap(my_half, "band")
    picked_in = links.swap(picked_far, "band")
    picked_own, cot, gact = prepare(links, visible, pixel_rows, cotangent, mlp_down)
    far_half, cot = lax.optimization_barrier((far_half, cot))
    far_other = links.swap(far_half, 0)
    vecs = jnp.stack(
        [class_token, norm1_gain, norm1_bias, norm2_gain, norm2_bias] + [class_token] * 3
    )

    stream, n1, packed, probs, tprobs, att, mid, n2, act1, gpre1, *parts1 = forward(
        links,
        chips,
        vecs,
        picked_own,
        picked_in,
        kernels_own,
        far_half,
        far_other,
        attn_qkv,
        attn_out,
        cot,
        gact,
        mlp_up,
    )

    x, y, core, plane = (1,), ("band",), (0,), (1, "band")
    down_send, down_keep, up_send, up_keep = parts1
    down1 = Piece(
        (1, 0, "band", "h", 3, 2),
        (2,) * 6,
        block,
        [(down_keep, 0), (links.swap(down_send, 1), 0)],
        x,
    )
    up1 = Piece(
        (3, 1, 0, "band"), (2,) * 4, 4 * block, [(up_keep, 0), (links.swap(up_send, "band"), 0)], y
    )
    *sums_send, sums_keep, gmid, gatt, out_rows, vec2 = mlp_back(
        links, vecs, n2, gact, act1, gpre1, mlp_up, mlp_down, mid, cot, att, attn_out, ()
    )
    both = lambda i, at: [(sums_keep, at), (links.swap(sums_send[i], 0), 0)]
    middle, end = 2 * width, 2 * width + mlp_up.shape[1] // 2
    down2 = Piece((0, 1, "band", "h", 3, 2), (2,) * 6, block, both(0, 0), core)
    up2 = Piece((0, 3, 1, "band"), (2,) * 4, 4 * block, both(1, middle), core)
    names, sizes = (0, 1, "band", 3, 2), (2,) * 5
    outp = Piece(names, sizes, block, both(2, end), core)
    tie, unused = combine(links, [(down1, core, "split"), (up1, core, "split")], (vec2,))
    tie, unused = combine(
        links,
        [
            (down1, y, "split"),
            (up1, x, "split"),
            (down2, x, "split"),
            (up2, y, "split"),
            (outp, (2,), "split"),
        ],
        tie,
    )

    gpacked, qkv_send, qkv_keep = attention_back(links, chips, gatt, packed, probs, tprobs, n1, tie)
    qkv_in = links.swap(qkv_send, 0)
    qkv = [
        Piece(names, sizes, count, [(qkv_keep, at), (qkv_in, at)], core)
        for at, count in qkv_parts(width)
    ]
    older = touch((gpacked,), down1, up1, down2, up2, outp)
    tie, unused = combine(
        links,
        [
            (down2, y, "split"),
            (up2, x, "split"),
            (qkv[0], x, "split"),
            (qkv[1], y, "split"),
            (down1, (2,), "split"),
            (up1, (3,), "split"),
            (outp, (3,), "split"),
        ],
        (older,),
    )
    kg_send, kg_keep, pgrad_own, pgrad_far, vec_keep = embed_back(
        links,
        chips,
        vecs,
        vec2,
        gpacked,
        attn_qkv,
        stream,
        gmid,
        picked_own,
        picked_in,
        kernels_own,
        far_half,
        far_other,
        tie,
    )
    kg_in = links.swap(kg_send, 0)
    kg = Piece((0, "band", 1, "h"), (2,) * 4, depth // 4, [(kg_keep, 0), (kg_in, 0)], core)
    vec = Vec(vec_keep, (kg_in, 2 * depth))
    older = touch((vec_keep,), down2, up2, *qkv, down1, up1, outp)
    tie, unused = combine(
        links,
        [
            (kg, plane, "split"),
            (vec, plane, "vec"),
            (qkv[0], y, "split"),
            (qkv[1], x, "split"),
            (outp, x, "split"),
            (down2, (2,), "split"),
            (up2, (3,), "split"),
            (down1, (3,), "split"),
        ],
        (older,),
    )
    far_grads = links.swap(flat(pgrad_far), "band")
    partly = scatter(links, 0, flat(pgrad_own), depth, visible, patches)
    up = Piece.join(up1, up2, 2)
    tie, (down1_sum,) = combine(
        links,
        [
            (qkv[0], (2,), "split"),
            (qkv[1], (2,), "split"),
            (kg, (3,), "all"),
            (vec, (3,), "vec"),
            (down2, (3,), "split"),
            (outp, y, "split"),
            (down1, F32, "final"),
        ],
        (partly,),
    )
    tie, (out_sum, down2_sum) = combine(
        links,
        [
            (qkv[0], (3,), "split"),
            (qkv[1], (3,), "split"),
            (kg, (2,), "all"),
            (vec, (2,), "vec"),
            (up, (2,), "split"),
            (outp, F32, "final"),
            (down2, F32, "final"),
        ],
    )
    scattered = scatter(links, 1, far_grads, depth, visible, patches, partly)
    pixel_grads = jnp.swapaxes(scattered.reshape(group_chips, bands, pix, patches), 2, 3)
    tie, (kgrad, *qkv_sums, up_sum) = combine(
        links,
        [
            (kg, BF, "final"),
            (qkv[0], F32, "final"),
            (qkv[1], F32, "final"),
            (up, F32, "final"),
        ],
        (scattered,),
    )
    vecs = links.total(vec.value()).reshape(8, width)
    kgrad = links.total(kgrad.astype(F32)).astype(BF)
    near = [kgrad, links.swap(kgrad, 1), links.swap(kgrad, 0), links.swap(kgrad, 0, 1)]
    turn = lambda bit, a, b: [jnp.where(bit == 0, a, b), jnp.where(bit == 0, b, a)]
    rows_of = [turn(links.bit(1), *near[:2]), turn(links.bit(1), *near[2:])]
    rows_of = [turn(links.bit(0), rows_of[0][i], rows_of[1][i]) for i in range(2)]
    kgrad = jnp.stack([rows_of[i][c] for c in range(2) for i in range(2)])
    kgrad = kgrad.reshape(4, 2, depth // 4, half).astype(F32)
    kernel_grads = jnp.transpose(kgrad, (0, 2, 1, 3)).reshape(bands, pix, width)
    block_output = jnp.concatenate(
        [
            out_rows[body : body + chips][:, None, :],
            out_rows[:body].reshape(chips, slots, width),
        ],
        axis=1,
    )
    weight = lambda part: jnp.swapaxes(links.last(part), 0, 1)
    down_sum = jnp.concatenate(
        [down1_sum.reshape(2, block, half), down2_sum.reshape(2, block, half)], axis=0
    )
    return (
        block_output,
        pixel_grads,
        kernel_grads,
        vecs[2],
        vecs[0],
        vecs[1],
        vecs[3],
        vecs[4],
        weight(jnp.concatenate(qkv_sums, axis=0)),
        weight(out_sum),
        weight(up_sum),
        weight(jnp.swapaxes(down_sum, 0, 1).reshape(block, 4 * half)),
    )


def solution(mesh):
    placed = (
        P("dp", "band", None, None),
        P("dp", None),
        P("band", None, None),
        P(),
        P(),
        P(),
        P(),
        P(),
        P(),
        P(),
        P(),
        P(),
        P(("dp", "band"), None, None),
    )
    return jax.shard_map(
        functools.partial(shards, Links(mesh)),
        mesh=mesh,
        in_specs=placed,
        out_specs=(
            P(("dp", "band"), None, None),
            P("dp", "band", None, None),
            P("band", None, None),
            P(),
            P(),
            P(),
            P(),
            P(),
            P("band", "dp"),
            P("band", "dp"),
            P("band", "dp"),
            P("band", "dp"),
        ),
        check_vma=False,
    )
```

```python
import functools

import jax
import jax.numpy as jnp
from jax import lax
from jax.experimental import pallas as pl
from jax.experimental.pallas import tpu as pltpu
from jax.sharding import PartitionSpec as P

HEADS = 12
HEAD = 64
BF = jnp.bfloat16
F32 = jnp.float32
TAIL = 16
BLOCK = 112
KEYS = 80
SCALE = HEAD ** (-0.5)
VMEM = pl.BlockSpec(memory_space=pltpu.VMEM)
HBM = pl.BlockSpec(memory_space=pl.ANY)
shape = jax.ShapeDtypeStruct
MICROSECONDS = {
    "pick_far": 5,
    "prepare": 11,
    "encoder_forward": 31,
    "mlp_back": 32,
    "attention_back": 18,
    "embed_back": 14,
    "combine": 12,
    "touch": 20,
    "assemble": 0.5,
    "finish": 0.5,
    "scatter": 4,
}


def dot(a, b):
    return jnp.dot(a, b, preferred_element_type=F32)


def dot_nt(a, b):
    return lax.dot_general(a, b, (((1,), (1,)), ((), ())), preferred_element_type=F32)


def dot_tn(a, b):
    return lax.dot_general(a, b, (((0,), (0,)), ((), ())), preferred_element_type=F32)


def kernel_call(body, name, outs, scratch, copies, vmem_in=0, vmem_out=0, mib=62, **more):
    def call(*operands):
        return pl.pallas_call(
            body,
            out_shape=tuple(outs),
            in_specs=[VMEM] * vmem_in + [HBM] * (len(operands) - vmem_in),
            out_specs=(HBM,) * (len(outs) - vmem_out) + (VMEM,) * vmem_out,
            scratch_shapes=[
                a if hasattr(a, "get_ref_aval") else pltpu.VMEM(a.shape, a.dtype) for a in scratch
            ]
            + [pltpu.SemaphoreType.DMA((copies,))],
            compiler_params=pltpu.CompilerParams(vmem_limit_bytes=mib * 1024 * 1024),
            cost_estimate=pl.CostEstimate(
                flops=int(MICROSECONDS[name] * 1.15e9), bytes_accessed=1, transcendentals=0
            ),
            name=name,
            **more,
        )(*operands)

    return call


def tiles(count, body, looped=False, base=0, tile=256):
    if not looped:
        for j in range(0, count, tile):
            body(slice(base + j, base + j + tile))
        return

    def step(j, carry):
        body(pl.ds(pl.multiple_of(base + j * tile, tile), tile))
        return carry

    lax.fori_loop(0, count // tile, step, 0)


LOOP = (True, False, True, True, False)


class Copies:
    def __init__(self, sems):
        self.sems, self.count, self.open = sems, 0, []

    def start(self, source, target):
        copy = pltpu.make_async_copy(source, target, self.sems.at[self.count])
        self.count += 1
        copy.start()
        return copy

    def out(self, source, target):
        self.open.append(self.start(source, target))

    def finish(self):
        for copy in self.open:
            copy.wait()


def chosen(seen_ref, chip, patches):
    first = seen_ref[pl.ds(chip, 1), :]
    second = seen_ref[pl.ds(chip + 1, 1), :]
    slots = first.shape[1]
    seen = jnp.concatenate([first, second], axis=1)
    ids = lax.broadcasted_iota(jnp.int32, (patches, 2 * slots), 0)
    lane = lax.broadcasted_iota(jnp.int32, (patches, 2 * slots), 1)
    hit = ids == seen
    return (
        jnp.where(hit & (lane < slots), 1.0, 0.0).astype(BF),
        jnp.where(hit & (lane >= slots), 1.0, 0.0).astype(BF),
    )


def load_pixels(copies, pixel_hbm, pixel_ref, base, pairs):
    return [
        copies.start(pixel_hbm.at[pl.ds(base + 2 * i, 2)], pixel_ref.at[2 * i : 2 * i + 2])
        for i in range(pairs)
    ]


def pick_pixels(arrive, seen_ref, pixel_ref, out_ref, base):
    for i, copy in enumerate(arrive):
        first, second = chosen(seen_ref, base + 2 * i, pixel_ref.shape[2])
        wide = first.shape[1]
        copy.wait()
        out_ref[:, i * wide : (i + 1) * wide] = (
            dot(pixel_ref[2 * i], first) + dot(pixel_ref[2 * i + 1], second)
        ).astype(BF)


def pick_far_kernel(
    links, pairs, seen_ref, pixel_hbm, halves_hbm, half_hbm, out_hbm, pixel_ref, out_ref, half_ref, sems
):
    copies = Copies(sems)
    base = (1 - links.bit("band")) * 2 * pairs
    half_in = copies.start(halves_hbm.at[links.bit(0)], half_ref)
    arrive = load_pixels(copies, pixel_hbm, pixel_ref, base, pairs)
    half_in.wait()
    copies.out(half_ref, half_hbm)
    pick_pixels(arrive, seen_ref, pixel_ref, out_ref, base)
    copies.out(out_ref, out_hbm)
    copies.finish()


def pick_far(links, seen, pixel_rows, halves):
    chips, depth, patches = pixel_rows.shape
    pairs = chips // 4
    outs = (shape(halves.shape[1:], BF), shape((depth, chips // 2 * seen.shape[1]), BF))
    return kernel_call(
        functools.partial(pick_far_kernel, links, pairs),
        "pick_far",
        outs,
        (shape((2 * pairs, depth, patches), BF), outs[1], outs[0]),
        pairs + 4,
        vmem_in=1,
    )(seen, pixel_rows, halves)


def prepare_kernel(
    links,
    pairs,
    seen_ref,
    pixel_hbm,
    cot_hbm,
    down_hbm,
    picked_hbm,
    rows_hbm,
    gact_hbm,
    pixel_ref,
    cot_ref,
    down_ref,
    picked_ref,
    rows_ref,
    gact_ref,
    tail_ref,
    sems,
):
    copies = Copies(sems)
    chips = cot_ref.shape[0]
    slots = cot_ref.shape[1] - 1
    rows, width = rows_ref.shape
    base = links.bit("band") * 2 * pairs
    cot_in = copies.start(cot_hbm, cot_ref)
    arrive = load_pixels(copies, pixel_hbm, pixel_ref, base, pairs)
    chunk = down_hbm.shape[0] // 4
    parts = [slice(i * chunk, (i + 1) * chunk) for i in range(4)]
    downs = [copies.start(down_hbm.at[part, :], down_ref.at[part, :]) for part in parts]
    cot_in.wait()
    tail_ref[...] = jnp.zeros_like(tail_ref)
    for c in range(chips):
        chip = cot_ref[c].astype(F32)
        rows_ref[c * slots : (c + 1) * slots, :] = chip[1:, :].astype(BF)
        tail_ref[c : c + 1, :] = chip[0:1, :]
    rows_ref[rows - TAIL : rows, :] = tail_ref[...].astype(BF)
    copies.out(rows_ref, rows_hbm)
    pick_pixels(arrive, seen_ref, pixel_ref, picked_ref, base)
    copies.out(picked_ref, picked_hbm)
    for part, copy in zip(parts, downs):
        copy.wait()
        gact_ref[:, part] = dot_nt(rows_ref[...], down_ref[part, :]).astype(BF)
        copies.out(gact_ref.at[:, part], gact_hbm.at[:, part])
    copies.finish()


def prepare(links, seen, pixel_rows, cot, down):
    group, depth, patches = pixel_rows.shape
    pairs = group // 4
    hidden, width = down.shape
    body = cot.shape[0] * seen.shape[1]
    rows = body + TAIL
    outs = (shape((depth, body), BF), shape((rows, width), BF), shape((rows, hidden), BF))
    return kernel_call(
        functools.partial(prepare_kernel, links, pairs),
        "prepare",
        outs,
        (shape((2 * pairs, depth, patches), BF), cot, down) + outs + (shape((TAIL, width), F32),),
        pairs + 12,
        vmem_in=1,
    )(seen, pixel_rows, cot, down)


def row_stats(values):
    average = jnp.mean(values, axis=-1, keepdims=True)
    centred = values - average
    spread = jnp.mean(centred * centred, axis=-1, keepdims=True)
    root = lax.rsqrt(spread + 1e-06)
    return centred * root, root


def norm_back(xhat, root, grad_out, gain):
    scaled = grad_out * gain
    mean_scaled = jnp.mean(scaled, axis=-1, keepdims=True)
    mean_along = jnp.mean(scaled * xhat, axis=-1, keepdims=True)
    return root * (scaled - mean_scaled - xhat * mean_along)


def head_rows(width):
    row = lax.broadcasted_iota(jnp.int32, (TAIL, width), 0)
    lane = lax.broadcasted_iota(jnp.int32, (TAIL, width), 1)
    return (lane // HEAD) == row


def two_heads(pair):
    low = lax.broadcasted_iota(jnp.int32, pair.shape, 1) < HEAD
    zero = jnp.zeros_like(pair)
    return jnp.concatenate([jnp.where(low, pair, zero), jnp.where(low, zero, pair)], axis=0)


def own_heads(stacked):
    rows = stacked.shape[0] // 2
    low = lax.broadcasted_iota(jnp.int32, (rows, stacked.shape[1]), 1) < HEAD
    return jnp.where(low, stacked[:rows], stacked[rows:])


def softmax_keys(scores, count):
    key = lax.broadcasted_iota(jnp.int32, scores.shape, 0)
    scores = jnp.where(key < count, scores * SCALE, -1e30)
    raised = jnp.exp(scores - jnp.max(scores, axis=0, keepdims=True))
    return raised * (1.0 / jnp.sum(raised, axis=0, keepdims=True))


def load_far(links, copies, half_hbm, other_hbm, target):
    count = half_hbm.shape[0]
    core = links.bit(0)
    return [
        copies.start(half_hbm, target.at[pl.ds(pl.multiple_of(core * count, 16), count), :]),
        copies.start(other_hbm, target.at[pl.ds(pl.multiple_of((1 - core) * count, 16), count), :]),
    ]


def forward_kernel(
    links,
    chips,
    vecs_ref,
    xo_hbm,
    xr_hbm,
    ko_hbm,
    half_hbm,
    other_hbm,
    wqkv_hbm,
    wout_hbm,
    cot_hbm,
    gact_hbm,
    up_hbm,
    stream_hbm,
    n1_hbm,
    packed_hbm,
    probs_hbm,
    tprobs_hbm,
    att_hbm,
    mid_hbm,
    n2_hbm,
    act_hbm,
    gpre_hbm,
    down_send_hbm,
    down_keep_hbm,
    up_send_hbm,
    up_keep_hbm,
    stream_ref,
    n1_ref,
    packed_ref,
    probs_ref,
    tprobs_ref,
    att_ref,
    mid_ref,
    n2_ref,
    xo_ref,
    xr_ref,
    ko_ref,
    kr_ref,
    tatt_ref,
    wqkv_ref,
    wout_ref,
    *half_refs,
):
    copies = Copies(half_refs[-1])
    rows, width = n1_ref.shape
    body = rows - TAIL
    slots = body // chips
    token, gain1, bias1, gain2, bias2 = (vecs_ref[i : i + 1, :] for i in range(5))
    first = [
        copies.start(source, target)
        for source, target in ((xo_hbm, xo_ref), (ko_hbm, ko_ref), (xr_hbm, xr_ref))
    ] + load_far(links, copies, half_hbm, other_hbm, kr_ref)
    for copy in first:
        copy.wait()
    wqkv_in = copies.start(wqkv_hbm, wqkv_ref)
    wout_in = copies.start(wout_hbm, wout_ref)
    half = MlpHalf(links, 0, copies, half_refs[:-1])

    def embed(at):
        stream_ref[at, :] = dot_tn(xo_ref[:, at], ko_ref[...]) + dot_tn(xr_ref[:, at], kr_ref[...])

    tiles(body, embed)
    tail_row = lax.broadcasted_iota(jnp.int32, (TAIL, width), 0)
    stream_ref[body:rows, :] = jnp.where(tail_row < chips, token, 0.0)

    def first_norm(i, carry):
        at = pl.ds(pl.multiple_of(i * BLOCK, BLOCK), BLOCK)
        xhat, unused = row_stats(stream_ref[at, :])
        n1_ref[at, :] = (xhat * gain1 + bias1).astype(BF)
        return carry

    lax.fori_loop(0, rows // BLOCK, first_norm, 0)
    wqkv_in.wait()
    half.load(cot_hbm, gact_hbm, up_hbm)
    copies.out(stream_ref, stream_hbm)
    copies.out(n1_ref, n1_hbm)


    def project(at):
        packed_ref[:, at] = dot(n1_ref[...], wqkv_ref[:, at]).astype(BF)

    tiles(3 * width, project)
    copies.out(packed_ref, packed_hbm)
    tail = packed_ref[body:rows, :]
    heads = head_rows(width)
    tquery = jnp.where(heads, jnp.broadcast_to(tail[0:1, 0:width], (TAIL, width)), 0).astype(BF)
    tatt_ref[...] = jnp.zeros_like(tatt_ref)

    def chip(c, carry):
        at = pl.ds(pl.multiple_of(c * slots, slots), slots)
        key = jnp.concatenate(
            [packed_ref[at, width : 2 * width], tail[:, width : 2 * width]], axis=0
        )
        val = jnp.concatenate([packed_ref[at, 2 * width :], tail[:, 2 * width :]], axis=0)
        tiles = [slice(128 * p, 128 * p + 128) for p in range(width // 128)]
        scores = [dot_nt(key[:, here], two_heads(packed_ref[at, here])) for here in tiles]
        scores.append(dot_nt(key, tquery))
        probs = [softmax_keys(s, slots + 1).astype(BF) for s in scores]
        mixed = [dot_tn(probs[p], val[:, tiles[p]]) for p in range(len(tiles))]
        mixed.append(dot_tn(probs[-1], val))
        for p in range(len(tiles)):
            probs_ref[c, p] = probs[p]
            att_ref[at, tiles[p]] = own_heads(mixed[p]).astype(BF)
        tprobs_ref[c] = probs[-1]
        tatt_ref[pl.ds(c, 1), :] = jnp.sum(jnp.where(heads, mixed[-1], 0.0), axis=0, keepdims=True)
        return carry

    lax.fori_loop(0, chips, chip, 0, unroll=2)
    att_ref[body:rows, :] = tatt_ref[...].astype(BF)
    copies.out(probs_ref, probs_hbm)
    copies.out(tprobs_ref, tprobs_hbm)
    copies.out(att_ref, att_hbm)
    wout_in.wait()


    def out_project(at):
        mid_ref[:, at] = stream_ref[:, at] + dot(att_ref[...], wout_ref[:, at])

    tiles(width, out_project)
    copies.out(mid_ref, mid_hbm)

    def second_norm(i, carry):
        at = pl.ds(pl.multiple_of(i * BLOCK, BLOCK), BLOCK)
        xhat, unused = row_stats(mid_ref[at, :])
        n2_ref[at, :] = (xhat * gain2 + bias2).astype(BF)
        return carry

    lax.fori_loop(0, rows // BLOCK, second_norm, 0)
    copies.out(n2_ref, n2_hbm)
    half.run(n2_ref, (down_send_hbm, down_keep_hbm), (up_send_hbm, up_keep_hbm))
    copies.out(half.act, act_hbm)
    copies.out(half.gpre, gpre_hbm)
    copies.finish()


class MlpHalf:
    def __init__(self, links, third, copies, refs):
        self.links, self.third, self.copies = links, third, copies
        self.looped = (False, False) if third == 0 else LOOP[:2]
        self.cot, self.gact, self.up, self.act, self.gpre, self.grads = refs

    @staticmethod
    def scratch(rows, width, hidden):
        return (
            shape((rows, width), BF),
            shape((rows, hidden // 2), BF),
            shape((width, hidden // 2), BF),
            shape((rows, hidden // 2), BF),
            shape((rows, hidden // 2), BF),
            shape((4, max(width, hidden // 4), width), BF),
        )

    def load(self, cot_hbm, gact_hbm, up_hbm):
        chunk = up_hbm.shape[1] // 4
        start = self.copies.start
        far = lambda i: slice((2 * i + self.third) * chunk, (2 * i + self.third + 1) * chunk)
        near = lambda i: slice(i * chunk, (i + 1) * chunk)
        self.first = [
            (
                start(up_hbm.at[:, far(i)], self.up.at[:, near(i)]),
                start(gact_hbm.at[:, far(i)], self.gact.at[:, near(i)]),
            )
            for i in range(2)
        ]
        self.cot_in = start(cot_hbm, self.cot)

    def run(self, n2_ref, down_out, up_out, then=None):
        copies, links = self.copies, self.links
        rows, width = n2_ref.shape
        chunk = self.up.shape[1] // 2
        half = width // 2
        block = width // 16
        for i in range(2):
            for copy in self.first[i]:
                copy.wait()
            if i == 1 and then is not None:
                then()

            def activate(cols):
                pre = dot(n2_ref[...], self.up[:, cols])
                phi = 0.5 + 0.5 * lax.erf(pre * (0.5**0.5))
                bell = jnp.exp(-0.5 * pre * pre) * 0.3989422804014327
                self.act[:, cols] = (pre * phi).astype(BF)
                gact = self.gact[:, cols].astype(F32)
                self.gpre[:, cols] = (gact * (phi + pre * bell)).astype(BF)

            tiles(chunk, activate, self.looped[0], i * chunk)
        where = (1, "band") if self.third == 0 else (0, 0)
        bits = [links.bit(w) for w in where]
        self.cot_in.wait()
        for i in range(2):

            def down_rows(at):
                self.grads[i, at, :] = dot_tn(
                    self.cot[:, at], self.act[:, i * chunk : (i + 1) * chunk]
                ).astype(BF)

            tiles(width, down_rows, self.looped[1])
            for side, bit in ((0, 1 - bits[0]), (1, bits[0])):
                for other in range(2):
                    x, c = (bit, other) if where[0] == 1 else (other, bit)
                    for z in range(4):
                        at = pl.multiple_of(((z * 2 + x) * 2 + c) * block, 16)
                        for h in range(2):
                            to = (((other * 2 + i) * 2 + h) * 4 + z) * block
                            copies.out(
                                self.grads.at[i, pl.ds(at, block), h * half : (h + 1) * half],
                                down_out[side].at[to : to + block, :],
                            )
        part = chunk // 4
        for i in range(2):

            def up_rows(at):
                self.grads[2 + i, at, :] = dot_tn(
                    self.gpre.at[:, i * chunk : (i + 1) * chunk][:, at], n2_ref[...]
                ).astype(BF)

            tiles(chunk, up_rows, self.looped[1])
            for side, bit in ((0, 1 - bits[1]), (1, bits[1])):
                for x in range(2):
                    for other in range(2):
                        if where[1] == "band":
                            at = (2 * x + other) * part
                            cols = pl.ds(pl.multiple_of(bit * half, 128), half)
                        else:
                            at = pl.multiple_of((2 * x + bit) * part, 16)
                            cols = slice(other * half, (other + 1) * half)
                        to = ((i * 2 + x) * 2 + other) * part
                        copies.out(
                            self.grads.at[2 + i, pl.ds(at, part), cols],
                            up_out[side].at[to : to + part, :],
                        )


def forward(links, chips, vecs, xo, xr, ko, half, other, wqkv, wout, cot, gact, up):
    width, hidden = up.shape
    body = xo.shape[1]
    rows = body + TAIL
    saved = (
        shape((rows, width), F32),
        shape((rows, width), BF),
        shape((rows, 3 * width), BF),
        shape((chips, width // 128, KEYS, 128), BF),
        shape((chips, KEYS, TAIL), BF),
        shape((rows, width), BF),
        shape((rows, width), F32),
        shape((rows, width), BF),
    )
    return kernel_call(
        functools.partial(forward_kernel, links, chips),
        "encoder_forward",
        saved
        + (shape((rows, hidden // 2), BF),) * 2
        + (shape((2 * width, width // 2), BF),) * 2
        + (shape((hidden // 2, width // 2), BF),) * 2,
        saved
        + (xo, xr, ko, ko, shape((TAIL, width), F32), wqkv, wout)
        + MlpHalf.scratch(rows, width, hidden),
        112,
        vmem_in=1,
    )(vecs, xo, xr, ko, half, other, wqkv, wout, cot, gact, up)


def spread_blocks(links, copies, full_ref, outs):
    core = links.bit(0)
    cols = full_ref.shape[1] // 2
    block = full_ref.shape[0] // 16
    for z in range(4):
        for x in range(2):
            for side, c in ((0, 1 - core), (1, core)):
                start = ((z * 2 + x) * 2 + c) * block
                for count, pair in outs:
                    rows = pl.ds(pl.multiple_of(start, 16), count)
                    start = start + count
                    for b in range(2):
                        to = ((x * 2 + b) * 4 + z) * count
                        copies.out(
                            full_ref.at[rows, b * cols : (b + 1) * cols],
                            pair[side].at[to : to + count, :],
                        )


def mlp_back_kernel(
    links,
    after,
    vecs_ref,
    n2_hbm,
    gact_hbm,
    act1_hbm,
    gpre1_hbm,
    up_hbm,
    down_hbm,
    mid_hbm,
    cot_hbm,
    att_hbm,
    wout_hbm,
    *rest,
):
    rest = rest[after:]
    sends, (keep_hbm, branch_hbm, gatt_hbm, out_hbm, vec_ref) = rest[:3], rest[3:8]
    (
        n2_ref,
        gatt_ref,
        out_ref,
        act_ref,
        gpre_ref,
        up_ref,
        down_ref,
        mid_ref,
        att_ref,
        wout_ref,
        back_ref,
        branch_ref,
        full_ref,
    ) = rest[8:21]
    half_refs, sems = rest[21:-1], rest[-1]
    copies = Copies(sems)
    rows, width = mid_ref.shape
    quarter = up_hbm.shape[1] // 4
    at = lambda i: slice(i * quarter, (i + 1) * quarter)
    n2_in = copies.start(n2_hbm, n2_ref)
    half = MlpHalf(links, 1, copies, half_refs)
    half.load(cot_hbm, gact_hbm, up_hbm)
    cot_ref = half.cot
    n2_in.wait()
    first_in = []

    def more():
        first_in.append(copies.start(gpre1_hbm, gpre_ref))
        for i in range(2):
            first_in.append(copies.start(up_hbm.at[:, at(2 * i)], up_ref.at[:, at(i)]))
        for source, target in ((mid_hbm, mid_ref), (att_hbm, att_ref), (wout_hbm, wout_ref)):
            first_in.append(copies.start(source, target))

    middle = 2 * width
    end = middle + up_hbm.shape[1] // 2
    half.run(
        n2_ref,
        (sends[0], keep_hbm.at[0:middle, :]),
        (sends[1], keep_hbm.at[middle:end, :]),
        more,
    )
    late = [copies.start(act1_hbm, act_ref)] + [
        copies.start(down_hbm.at[at(2 * i + third), :], down_ref.at[at(2 * third + i), :])
        for third in range(2)
        for i in range(2)
    ]
    for copy in first_in:
        copy.wait()

    def backward(cols):
        back_ref[:, cols] = dot_nt(gpre_ref[...], up_ref[cols, :]) + dot_nt(
            half.gpre[...], half.up[cols, :]
        )

    tiles(width, backward, LOOP[2])
    gain = vecs_ref[3:4, :]

    def norm(i, carry):
        at = pl.ds(pl.multiple_of(i * BLOCK, BLOCK), BLOCK)
        xhat, root = row_stats(mid_ref[at, :])
        grad = back_ref[at, :]
        total = cot_ref[at, :].astype(F32) + norm_back(xhat, root, grad, gain)
        branch_ref[at, :] = total.astype(BF)
        return (
            carry[0] + jnp.sum(grad * xhat, axis=0, keepdims=True),
            carry[1] + jnp.sum(grad, axis=0, keepdims=True),
        )

    zero = jnp.zeros((1, width), F32)
    gain_sum, bias_sum = lax.fori_loop(0, rows // BLOCK, norm, (zero, zero))
    vec_ref[0:1, :] = gain_sum
    vec_ref[1:2, :] = bias_sum
    copies.out(branch_ref, branch_hbm)

    def out_grad(at):
        full_ref[at, :] = dot_tn(branch_ref[:, at], att_ref[...]).astype(BF)

    tiles(width, out_grad, LOOP[4])
    spread_blocks(
        links, copies, full_ref, [(width // 16, (sends[2], keep_hbm.at[end : end + width, :]))]
    )

    def attended_grad(at):
        gatt_ref[:, at] = dot_nt(branch_ref[...], wout_ref[at, :]).astype(BF)

    tiles(width, attended_grad, LOOP[4])
    copies.out(gatt_ref, gatt_hbm)
    for copy in late:
        copy.wait()

    def outward(cols):
        out_ref[:, cols] = (
            mid_ref[:, cols]
            + dot(act_ref[...], down_ref[: 2 * quarter, cols])
            + dot(half.act[...], down_ref[2 * quarter :, cols])
        ).astype(BF)

    tiles(width, outward, LOOP[3])
    copies.out(out_ref, out_hbm)
    copies.finish()


def mlp_back(links, vecs, n2, gact, act1, gpre1, up, down, mid, cot, att, wout, after):
    rows, width = mid.shape
    hidden = up.shape[1]
    sums = shape((3 * width + hidden // 2, width // 2), BF)
    return kernel_call(
        functools.partial(mlp_back_kernel, links, len(after)),
        "mlp_back",
        tuple(shape((count, width // 2), BF) for count in (2 * width, hidden // 2, width))
        + (sums, cot, cot, cot, shape((2, width), F32)),
        (n2, cot, cot, act1, gpre1)
        + (shape((width, hidden // 2), BF), down, mid, att, wout, mid, cot, wout)
        + MlpHalf.scratch(rows, width, hidden),
        140,
        vmem_in=1,
        vmem_out=1,
    )(vecs, n2, gact, act1, gpre1, up, down, mid, cot, att, wout, *after)


def split_vec(vec):
    high = vec.astype(BF)
    return high, (vec - high.astype(F32)).astype(BF)


def attention_back_kernel(
    links, chips, after, gatt_hbm, packed_hbm, probs_hbm, tprobs_hbm, n1_hbm, *rest
):
    gpacked_hbm, send_hbm, keep_hbm = rest[after : after + 3]
    (
        gpacked_ref,
        gatt_ref,
        packed_ref,
        probs_ref,
        tprobs_ref,
        n1_ref,
        tgrad_ref,
        tout_ref,
        full_ref,
        chip_sems,
        sems,
    ) = rest[after + 3 :]
    rows, width = n1_ref.shape
    body = rows - TAIL
    slots = body // chips
    copies = Copies(sems)

    def arriving(c):
        at = pl.ds(pl.multiple_of(c * slots, slots), slots)
        return [
            pltpu.make_async_copy(source.at[where], target.at[where], chip_sems.at[k, c])
            for k, (source, target, where) in enumerate(
                (
                    (packed_hbm, packed_ref, (at, slice(None))),
                    (gatt_hbm, gatt_ref, (at, slice(None))),
                    (probs_hbm, probs_ref, c),
                )
            )
        ]

    tails = slice(body, rows)
    arrive = [
        copies.start(packed_hbm.at[tails, :], packed_ref.at[tails, :]),
        copies.start(gatt_hbm.at[tails, :], gatt_ref.at[tails, :]),
        copies.start(tprobs_hbm, tprobs_ref),
    ]
    for c in range(chips):
        for copy in arriving(c):
            copy.start()
    tout_ref[...] = jnp.zeros_like(tout_ref)
    heads = head_rows(width)
    for copy in arrive:
        copy.wait()
    n1_in = copies.start(n1_hbm, n1_ref)
    tgrad_ref[...] = gatt_ref[body:rows, :].astype(F32)
    tail = packed_ref[body:rows, :]
    tquery = jnp.where(heads, jnp.broadcast_to(tail[0:1, 0:width], (TAIL, width)), 0).astype(BF)

    def chip(c):
        at = pl.ds(pl.multiple_of(c * slots, slots), slots)
        key_all = jnp.concatenate(
            [packed_ref[at, width : 2 * width], tail[:, width : 2 * width]], axis=0
        )
        val_all = jnp.concatenate([packed_ref[at, 2 * width :], tail[:, 2 * width :]], axis=0)
        tgrad = jnp.where(
            heads, jnp.broadcast_to(tgrad_ref[pl.ds(c, 1), :], (TAIL, width)), 0.0
        ).astype(BF)
        tiles = [slice(128 * p, 128 * p + 128) for p in range(width // 128)]
        probs = [probs_ref[c, p] for p in range(len(tiles))] + [tprobs_ref[c]]
        gouts = [two_heads(gatt_ref[at, here]) for here in tiles]
        queries = [two_heads(packed_ref[at, here]) for here in tiles]
        gprobs = [dot_nt(val_all[:, tiles[p]], gouts[p]) for p in range(len(tiles))]
        gprobs.append(dot_nt(val_all, tgrad))
        gscores = []
        for prob, gprob in zip(probs, gprobs):
            wide = prob.astype(F32)
            inner = jnp.sum(gprob * wide, axis=0, keepdims=True)
            gscores.append((wide * (gprob - inner) * SCALE).astype(BF))
        gval_tail = dot(probs[-1], tgrad)
        gkey_tail = dot(gscores[-1], tquery)
        mixed = jnp.where(heads, dot_tn(gscores[-1], key_all), 0.0)
        gvals = [dot(probs[p], gouts[p]) + gval_tail[:, tiles[p]] for p in range(len(tiles))]
        gkeys = [dot(gscores[p], queries[p]) + gkey_tail[:, tiles[p]] for p in range(len(tiles))]
        gqueries = [own_heads(dot_tn(gscores[p], key_all[:, tiles[p]])) for p in range(len(tiles))]
        for p in range(len(tiles)):
            gpacked_ref[at, 128 * p : 128 * p + 128] = gqueries[p].astype(BF)
            base = width + 128 * p
            gpacked_ref[at, base : base + 128] = gkeys[p][:slots].astype(BF)
            gpacked_ref[at, width + base : width + base + 128] = gvals[p][:slots].astype(BF)
        tout_ref[pl.ds(c, 1), :] = jnp.concatenate(
            [jnp.sum(mixed, axis=0, keepdims=True)]
            + [g[slots : slots + 1] for g in gkeys + gvals],
            axis=1,
        )

    def two_chips(i, carry):
        for c in (2 * i, 2 * i + 1):
            for copy in arriving(c):
                copy.wait()
        chip(2 * i)
        chip(2 * i + 1)
        return carry

    lax.fori_loop(0, chips // 2, two_chips, 0)
    gpacked_ref[body:rows, :] = tout_ref[...].astype(BF)
    copies.out(gpacked_ref, gpacked_hbm)
    n1_in.wait()

    def qkv_rows(at):
        full_ref[at, :] = dot_tn(gpacked_ref[:, at], n1_ref[...]).astype(BF)

    tiles(3 * width, qkv_rows)
    outs = []
    for at, count in qkv_parts(width):
        here = slice(at, at + 16 * count)
        outs.append((count, (send_hbm.at[here, :], keep_hbm.at[here, :])))
    spread_blocks(links, copies, full_ref, outs)
    copies.finish()


def qkv_parts(width):
    block = 3 * width // 16
    count = -(-block // 32) * 16
    return [(0, count), (16 * count, block - count)]


def attention_back(links, chips, gatt, packed, probs, tprobs, n1, after):
    rows, width = n1.shape
    sums = shape((3 * width, width // 2), BF)
    return kernel_call(
        functools.partial(attention_back_kernel, links, chips, len(after)),
        "attention_back",
        (packed, sums, sums),
        (packed, gatt, packed, probs, tprobs, n1)
        + (
            shape((TAIL, width), F32),
            shape((TAIL, 3 * width), F32),
            shape((3 * width, width), BF),
            pltpu.SemaphoreType.DMA((3, chips)),
        ),
        80,
    )(gatt, packed, probs, tprobs, n1, *after)


def embed_back_kernel(
    links,
    chips,
    after,
    vecs_ref,
    vec2_ref,
    gpacked_hbm,
    wqkv_hbm,
    stream_hbm,
    branch_hbm,
    xo_hbm,
    xr_hbm,
    ko_hbm,
    half_hbm,
    other_hbm,
    *rest,
):
    send_hbm, keep_hbm, own_hbm, far_hbm, vec_ref = rest[after : after + 5]
    (
        gpacked_ref,
        wqkv_ref,
        stream_ref,
        branch_ref,
        xo_ref,
        xr_ref,
        ko_ref,
        kr_ref,
        send_ref,
        keep_ref,
        pgrad_ref,
        back_ref,
        embed_ref,
        kfull_ref,
        sems,
    ) = rest[after + 5 :]
    rows, width = stream_ref.shape
    body = rows - TAIL
    half = width // 2
    copies = Copies(sems)
    thirds = [slice(i * width, (i + 1) * width) for i in range(3)]
    arrive = [
        (
            copies.start(gpacked_hbm.at[:, part], gpacked_ref.at[:, part]),
            copies.start(wqkv_hbm.at[:, part], wqkv_ref.at[:, part]),
        )
        for part in thirds
    ]
    for i, part in enumerate(thirds):
        for copy in arrive[i]:
            copy.wait()
        if i == 0:
            late = [copies.start(stream_hbm, stream_ref), copies.start(branch_hbm, branch_ref)]
        if i == 1:
            last = [
                copies.start(source, target)
                for source, target in ((xo_hbm, xo_ref), (xr_hbm, xr_ref), (ko_hbm, ko_ref))
            ] + load_far(links, copies, half_hbm, other_hbm, kr_ref)
        grad = dot_nt(gpacked_ref[:, part], wqkv_ref[:, part])
        back_ref[...] = grad if i == 0 else back_ref[...] + grad
    for copy in late:
        copy.wait()
    gain = vecs_ref[1:2, :]

    def norm(i, carry):
        at = pl.ds(pl.multiple_of(i * BLOCK, BLOCK), BLOCK)
        xhat, root = row_stats(stream_ref[at, :])
        grad = back_ref[at, :]
        total = branch_ref[at, :].astype(F32) + norm_back(xhat, root, grad, gain)
        back_ref[at, :] = total
        embed_ref[at, :] = total.astype(BF)
        return (
            carry[0] + jnp.sum(grad * xhat, axis=0, keepdims=True),
            carry[1] + jnp.sum(grad, axis=0, keepdims=True),
        )

    zero = jnp.zeros((1, width), F32)
    gain_sum, bias_sum = lax.fori_loop(0, rows // BLOCK, norm, (zero, zero))
    token_sum = jnp.sum(back_ref[body:rows, :], axis=0, keepdims=True)
    vec_ref[...] = jnp.zeros_like(vec_ref)
    for i, v in enumerate((gain_sum, bias_sum, token_sum, vec2_ref[0:1, :], vec2_ref[1:2, :])):
        vec_ref[2 * i : 2 * i + 1, :] = v[:, :half]
        vec_ref[2 * i + 1 : 2 * i + 2, :] = v[:, half:]
    for copy in last:
        copy.wait()
    grad = embed_ref[0:body, :]
    depth = xo_ref.shape[0]
    core, band = links.bit(0), links.bit("band")
    kfull_ref[0] = dot(xo_ref[...], grad).astype(BF)
    kfull_ref[1] = dot(xr_ref[...], grad).astype(BF)
    piece = depth // 4
    for c, ref in ((1 - core, send_ref), (core, keep_ref)):
        for far in range(2):
            for x in range(2):
                start = pl.multiple_of(c * (depth // 2) + x * piece, 16)
                block = kfull_ref[far, pl.ds(start, piece), :]
                for h in range(2):
                    slot = ((far + band - 2 * far * band) * 2 + x) * 2 + h
                    to = pl.ds(pl.multiple_of(slot * piece, 16), piece)
                    ref[to, :] = block[:, h * half : (h + 1) * half]
    high, low = split_vec(vec_ref[...])
    send_ref[2 * depth : 2 * depth + 16, :] = high
    send_ref[2 * depth + 16 : 2 * depth + 32, :] = low
    vec_ref[...] = high.astype(F32) + low.astype(F32)
    copies.out(send_ref, send_hbm)
    copies.out(keep_ref, keep_hbm)
    middle = body // 2
    for side, kernel, target in ((0, kr_ref, far_hbm), (1, ko_ref, own_hbm)):
        for h in range(2):
            part = grad[h * middle : (h + 1) * middle]
            pgrad_ref[side, h] = dot_nt(kernel[...], part).astype(BF)
        copies.out(pgrad_ref.at[side], target)
    copies.finish()


def embed_back(
    links, chips, vecs, vec2, gpacked, wqkv, stream, branch, xo, xr, ko, half, other, after
):
    rows, width = stream.shape
    depth, body = xo.shape
    cols = width // 2
    send, keep = shape((2 * depth + 32, cols), BF), shape((2 * depth, cols), BF)
    pgrad = shape((2, depth, body // 2), BF)
    return kernel_call(
        functools.partial(embed_back_kernel, links, chips, len(after)),
        "embed_back",
        (send, keep, pgrad, pgrad, shape((16, cols), F32)),
        (gpacked, wqkv, stream, branch, xo, xr, ko, ko, send, keep)
        + (
            shape((2,) + pgrad.shape, BF),
            stream,
            shape((rows, width), BF),
            shape((2, depth, width), BF),
        ),
        24,
        vmem_in=2,
        vmem_out=1,
    )(vecs, vec2, gpacked, wqkv, stream, branch, xo, xr, ko, half, other, *after)


def scatter_kernel(links, side, pairs, depth, seen_ref, grad_hbm, *rest):
    out_hbm, grad_ref, out_ref, sems = rest[-4:]
    patches = out_ref.shape[2]
    copies = Copies(sems)
    copies.start(grad_hbm.at[0 : 2 * depth, :], grad_ref).wait()
    band = links.bit("band")
    base = (band if side == 0 else 1 - band) * 2 * pairs
    for i in range(pairs):
        first, second = chosen(seen_ref, base + 2 * i, patches)
        wide = first.shape[1]
        h, at = divmod(i * wide, grad_ref.shape[1])
        grad = grad_ref[h * depth : (h + 1) * depth, at : at + wide]
        out_ref[2 * i] = dot_nt(grad, first)
        out_ref[2 * i + 1] = dot_nt(grad, second)
        copies.out(out_ref.at[2 * i : 2 * i + 2], out_hbm.at[pl.ds(base + 2 * i, 2)])
    copies.finish()


def scatter(links, side, grads, depth, seen, patches, *earlier):
    chips = seen.shape[0]
    pairs = chips // 4
    return kernel_call(
        functools.partial(scatter_kernel, links, side, pairs, depth),
        "scatter",
        (shape((chips, depth, patches), F32),),
        (shape((2 * depth, grads.shape[1]), BF), shape((2 * pairs, depth, patches), F32)),
        pairs + 1,
        vmem_in=1,
        input_output_aliases={2: 0} if earlier else {},
    )(seen, grads, *earlier)[0]


class Links:
    def __init__(self, mesh):
        self.count = mesh.shape["dp"]
        self.extra = self.count // 16

    def swap(self, array, *where):
        flip = sum((1 << w) * self.extra for w in where if w != "band")
        if "band" not in where:
            return lax.ppermute(array, "dp", [(d, d ^ flip) for d in range(self.count)])
        if flip == 0:
            return lax.ppermute(array, "band", [(0, 1), (1, 0)])
        pairs = [
            (2 * d + b, 2 * (d ^ flip) + 1 - b) for d in range(self.count) for b in range(2)
        ]
        return lax.ppermute(array, ("dp", "band"), pairs)

    def bring(self, array, *where):
        return pltpu.with_memory_space_constraint(self.swap(array, *where), pltpu.HBM)

    def bit(self, where):
        if where == "band":
            return lax.axis_index("band")
        return lax.rem(lax.div(lax.axis_index("dp"), self.extra << where), 2)

    def groups(self):
        return [[block * self.extra + i for i in range(self.extra)] for block in range(16)]

    def last(self, array):
        if self.extra == 1:
            return array
        return lax.psum_scatter(
            array, "dp", scatter_dimension=0, tiled=True, axis_index_groups=self.groups()
        )

    def total(self, array):
        if self.extra == 1:
            return array
        return lax.psum(array, "dp", axis_index_groups=self.groups())


class Level:
    def __init__(self, owner, terms, gone=frozenset(), rounded=False, alt=None, choice=None):
        self.owner, self.terms, self.gone, self.rounded = owner, list(terms), frozenset(gone), rounded
        self.alt, self.choice = alt, choice

    def moving(self, gone):
        strides = self.owner.strides(self.gone)
        return [(name, strides[name]) for name in self.owner.names if name in gone and name in strides]


class Piece:
    def __init__(self, names, sizes, unit, terms, gone=()):
        self.names, self.sizes, self.unit = list(names), list(sizes), unit
        self.gone = frozenset(gone)
        self.levels = [Level(self, terms, self.gone)]

    @staticmethod
    def join(first, second, choice):
        joined = Piece(first.names, first.sizes, first.unit, (), first.gone)
        joined.levels = [
            Level(a.owner, a.terms, a.gone, a.rounded, b, choice)
            for a, b in zip(first.levels, second.levels)
        ]
        return joined

    def strides(self, gone):
        found, stride = {}, self.unit
        for name, size in reversed(list(zip(self.names, self.sizes))):
            if name not in gone:
                found[name] = stride
                stride = stride * size
        return found

    def layout(self, names):
        gone = self.gone | frozenset(names)
        last = max([i for i, name in enumerate(self.names) if name in gone], default=-1)
        post = self.unit
        for size in self.sizes[last + 1 :]:
            post = post * size
        loops = [{}]
        for name, size in list(zip(self.names, self.sizes))[: last + 1]:
            if name not in gone:
                loops = [{**at, name: i} for at in loops for i in range(size)]
        return post * len(loops), post, loops


class Vec:
    def __init__(self, kept, came):
        self.kept, self.came = kept, [came]

    def value(self):
        parts = [
            buffer[at : at + 16].astype(F32) + buffer[at + 16 : at + 32].astype(F32)
            for buffer, at in self.came
        ]
        return pairwise([self.kept] + parts)


def pairwise(parts):
    while len(parts) > 1:
        parts = [
            parts[i] + parts[i + 1] if i + 1 < len(parts) else parts[i]
            for i in range(0, len(parts), 2)
        ]
    return parts[0]


def combine_kernel(links, tasks, n_in, n_out, n_load, after, *refs):
    ins, refs = refs[:n_in], refs[n_in + after :]
    out_hbm, refs = refs[:n_out], refs[n_out:]
    loads, refs = refs[:n_load], refs[n_load:]
    staged, sems = refs[:-1], refs[-1]
    copies = Copies(sems)
    bits = {where: links.bit(where) for where in (0, 1, 2, 3, "band")}
    waits = []
    for task in tasks:
        mine = []
        waits.append(mine)
        if task["kind"] == "raw":
            mine.append(copies.start(ins[task["from"]], loads[task["slot"]]))
            continue
        if task["kind"] == "vec":
            mine += [
                copies.start(ins[i].at[at : at + count, :], loads[slot])
                for i, at, count, slot in task["loads"]
            ]
            continue
        index = {
            name: (1 - bits[name]) if name in task["flip"] else bits[name] for name in bits
        }
        for load in task["loads"]:
            moving = sum((index[name] * stride for name, stride in load["moving"]), load["at"])
            alt_moving = sum(
                (index[name] * stride for name, stride in load["alt_moving"]), load["alt_at"]
            )
            for p, base in enumerate(load["bases"]):
                rows = pl.ds(pl.multiple_of(moving + base, 16), load["post"])
                target = loads[load["slot"]].at[p * load["post"] : (p + 1) * load["post"], :]
                sem = copies.sems.at[copies.count]
                copies.count += 1
                if load["alt"] is None:
                    copy = pltpu.make_async_copy(ins[load["in"]].at[rows, :], target, sem)
                    copy.start()
                else:
                    chosen_bit = index[load["choice"]]
                    copy = pltpu.make_async_copy(ins[load["in"]].at[rows, :], target, sem)
                    rows = pl.ds(pl.multiple_of(alt_moving + base, 16), load["post"])
                    other = pltpu.make_async_copy(ins[load["alt"]].at[rows, :], target, sem)
                    pl.when(chosen_bit == 0)(copy.start)
                    pl.when(chosen_bit == 1)(other.start)
                mine.append(copy)
    for task, mine in zip(tasks, waits):
        for copy in mine:
            copy.wait()
        if task["kind"] == "raw":
            copies.out(loads[task["slot"]], out_hbm[task["out"]].at[task["at"], :])
            continue
        if task["kind"] == "vec":
            parts = [loads[task["loads"][0][3]][...]]
            for unused, also, count, slot in task["loads"][1:]:
                parts.append(loads[slot][0:16, :].astype(F32) + loads[slot][16:32, :].astype(F32))
            high, low = split_vec(pairwise(parts))
            sent, kept = staged[task["stage"]], staged[task["stage"] + 1]
            sent[0:16, :] = high
            sent[16:32, :] = low
            kept[...] = high.astype(F32) + low.astype(F32)
            for out, at in task["outs"]:
                copies.out(sent, out_hbm[out].at[at, :])
            copies.out(kept, out_hbm[task["kept"]])
            continue
        total = None
        for rounded, slots in task["sum"]:
            parts = [loads[slot][...].astype(F32) for slot in slots]
            if total is not None:
                parts = [total.astype(BF).astype(F32) if rounded else total] + parts
            total = pairwise(parts)
        result = staged[task["stage"]]
        result[...] = total.astype(result.dtype)
        for i, (out, at) in enumerate(task["outs"]):
            if isinstance(at, tuple):
                part = at[0].stop
                copies.out(result.at[i * part : (i + 1) * part, :], out_hbm[out].at[at])
            else:
                copies.out(result, out_hbm[out].at[at, :])
    copies.finish()


def combine(links, steps, after=(), name="combine"):
    ins, tasks, loads, stages, sends, outs = [], [], [], [], {}, []
    copies, finals, beside = 0, {}, {}
    returned = []

    def index_of(array):
        for i, other in enumerate(ins):
            if other is array:
                return i
        ins.append(array)
        return len(ins) - 1

    def send_to(where, count):
        if where not in sends:
            sends[where] = len(outs)
            outs.append([0, BF])
        at = outs[sends[where]][0]
        outs[sends[where]][0] += count
        return sends[where], slice(at, at + count)

    def places(names):
        return [
            tuple(name for k, name in enumerate(names) if mask >> k & 1)
            for mask in range(1, 1 << len(names))
        ]

    for piece, names, mode in steps:
        if mode == "raw":
            out, at = send_to(names, piece.shape[0])
            tasks.append(
                {"kind": "raw", "from": index_of(piece), "out": out, "at": at, "slot": len(loads)}
            )
            loads.append(piece)
            returned.append((out, at))
            copies += 2
            continue
        if mode == "vec":
            task = {"kind": "vec", "loads": [], "stage": len(stages)}
            width = piece.kept.shape[1]
            for array, at, count in [(piece.kept, 0, 16)] + [(b, at, 32) for b, at in piece.came]:
                task["loads"].append((index_of(array), at, count, len(loads)))
                loads.append(shape((count, width), array.dtype))
            stages += [shape((32, width), BF), shape((16, width), F32)]
            task["outs"] = [send_to(place, 32) for place in places(names)]
            task["kept"] = len(outs)
            outs.append([16, F32])
            copies += len(task["loads"]) + len(task["outs"]) + 1
            tasks.append(task)
            returned.append(task)
            continue
        split = names if mode == "split" else ()
        count, post, loops = piece.layout(split)
        width = piece.levels[0].terms[0][0].shape[1]
        if mode == "final":
            kind, key, across = (*names, 1)[:3] if isinstance(names, tuple) else (names, len(outs), 1)
            if key not in finals:
                finals[key] = len(outs)
                outs.append([0, kind])
            out = finals[key]
            at = outs[out][0]
            if across == 1:
                groups = [((), [(out, slice(at, at + count))])]
                outs[out][0] += count
            else:
                part = count // across
                places_at = [slice((at + i) * width, (at + i + 1) * width) for i in range(across)]
                groups = [((), [(out, (slice(0, part), where)) for where in places_at])]
                outs[out][0] += across
                beside[out] = part
            returned.append(out)
        elif mode == "all":
            groups = [((), [send_to(place, count) for place in places(names)])]
            kind = BF
        else:
            groups = [(place, [send_to(place, count)]) for place in places(names)]
            kind = BF
        if mode != "final":
            returned.append([out for unused, targets in groups for out in targets])
        gone = piece.gone | frozenset(split)
        for flip, targets in groups:
            task = {"kind": "sum", "flip": flip, "loads": [], "sum": [], "stage": len(stages)}
            stages.append(shape((count, width), kind))
            task["outs"] = targets
            copies += len(targets)
            for level in piece.levels:
                strides = level.owner.strides(level.gone)
                slots = []
                for t, (array, at) in enumerate(level.terms):
                    slots.append(len(loads))
                    alt, alt_at = None, at
                    if level.alt is not None:
                        buffer, alt_at = level.alt.terms[t]
                        alt = index_of(buffer)
                    task["loads"].append(
                        {
                            "in": index_of(array),
                            "alt": alt,
                            "alt_at": alt_at,
                            "alt_moving": level.alt.moving(gone) if level.alt is not None else (),
                            "choice": level.choice,
                            "at": at,
                            "moving": level.moving(gone),
                            "bases": [
                                sum(i * strides[name] for name, i in loop.items()) for loop in loops
                            ],
                            "post": post,
                            "slot": len(loads),
                        }
                    )
                    loads.append(shape((count, width), array.dtype))
                    copies += len(loops)
                task["sum"].append((level.rounded, slots))
            tasks.append(task)
    results = kernel_call(
        functools.partial(
            combine_kernel,
            links,
            tasks,
            len(ins),
            len(outs),
            len(loads),
            len(after),
        ),
        name,
        [
            shape((beside[i], count * width) if i in beside else (count, width), kind)
            for i, (count, kind) in enumerate(outs)
        ],
        loads + stages,
        copies,
    )(*ins, *after)
    came = {out: links.bring(results[out], *where) for where, out in sends.items()}
    values = []
    for (piece, names, mode), back in zip(steps, returned):
        if mode == "final":
            values.append(results[back])
        elif mode == "raw":
            values.append((came[back[0]], back[1].start))
        elif mode == "vec":
            piece.kept = results[back["kept"]]
            piece.came = [(came[out], at.start) for out, at in back["outs"]]
        else:
            if mode == "split":
                piece.gone = piece.gone | frozenset(names)
            piece.levels.append(
                Level(
                    piece, [(came[out], at.start) for out, at in back], piece.gone, mode == "all"
                )
            )
    return [results[out] for out in sends.values()], values


def touch_kernel(count, *refs):
    copies = Copies(refs[-1])
    loads = [copies.start(refs[i].at[0:16, 0:128], refs[-2].at[i]) for i in range(count)]
    for copy in loads:
        copy.wait()
    total = refs[-2][0].astype(F32)
    for i in range(1, count):
        total = total + refs[-2][i].astype(F32)
    refs[-3][...] = total


def touch(after, *pieces):
    buffers = []
    for piece in pieces:
        buffer = piece.levels[-1].terms[0][0]
        if not any(buffer is other for other in buffers):
            buffers.append(buffer)
    count = len(buffers)
    return kernel_call(
        functools.partial(touch_kernel, count),
        "touch",
        (shape((16, 128), F32),),
        (shape((count, 16, 128), BF),),
        count,
        vmem_out=1,
    )(*buffers, *after)[0]


def assemble_kernel(links, vec_ref, own_ref, x_ref, core_ref, both_ref, after_hbm, *outs):
    full_ref = outs[-2]
    piece = own_ref.shape[0] // 2
    half = own_ref.shape[1]
    x, c = links.bit(1), links.bit(0)
    for ref, dx, dc in ((own_ref, 0, 0), (x_ref, 1, 0), (core_ref, 0, 1), (both_ref, 1, 1)):
        at = ((1 - c if dc else c) * 2 + (1 - x if dx else x)) * piece
        rows = pl.ds(pl.multiple_of(at, 16), piece)
        for h in range(2):
            part = ref[h * piece : (h + 1) * piece, :]
            full_ref[rows, h * half : (h + 1) * half] = part.astype(F32)
    for i, out in enumerate(outs[:5]):
        row = jnp.concatenate([vec_ref[2 * i : 2 * i + 1, :], vec_ref[2 * i + 1 : 2 * i + 2, :]], axis=1)
        out[...] = row.reshape(out.shape)


def assemble(links, vec, near, after):
    rows, half = near[0].shape
    return kernel_call(
        functools.partial(assemble_kernel, links),
        "assemble",
        (shape((2 * half,), F32),) * 5 + (shape((2 * rows, 2 * half), F32),),
        (),
        1,
        vmem_in=5,
        vmem_out=6,
    )(vec, *near, after)


def shards(
    links,
    pixels,
    visible,
    kernels,
    class_token,
    norm1_gain,
    norm1_bias,
    norm2_gain,
    norm2_bias,
    attn_qkv,
    attn_out,
    mlp_up,
    mlp_down,
    cotangent,
):
    width = attn_out.shape[0]
    half = width // 2
    chips = cotangent.shape[0]
    group_chips, bands, patches, pix = pixels.shape
    slots = visible.shape[1]
    body = chips * slots
    depth = bands * pix
    block = width // 16
    flat = lambda a: a.reshape(-1, half)
    core_swap = lambda a: (links.swap(flat(a), 0), 0)

    pixel_rows = jnp.swapaxes(pixels, 2, 3).reshape(group_chips, depth, patches)
    kernels_own = kernels.reshape(depth, width)
    my_half, picked_far = pick_far(
        links, visible, pixel_rows, kernels_own.reshape(2, depth // 2, width)
    )
    far_half = links.swap(my_half, "band")
    picked_in = links.swap(picked_far, "band")
    picked_own, cot, gact = prepare(links, visible, pixel_rows, cotangent, mlp_down)
    far_half, cot = lax.optimization_barrier((far_half, cot))
    far_other = links.swap(far_half, 0)
    vecs = jnp.stack(
        [class_token, norm1_gain, norm1_bias, norm2_gain, norm2_bias] + [class_token] * 3
    )

    stream, n1, packed, probs, tprobs, att, mid, n2, act1, gpre1, *parts1 = forward(
        links,
        chips,
        vecs,
        picked_own,
        picked_in,
        kernels_own,
        far_half,
        far_other,
        attn_qkv,
        attn_out,
        cot,
        gact,
        mlp_up,
    )

    x, y, core, plane = (1,), ("band",), (0,), (1, "band")
    down_send, down_keep, up_send, up_keep = parts1
    down1 = Piece(
        (1, 0, "band", "h", 3, 2),
        (2,) * 6,
        block,
        [(down_keep, 0), (links.bring(down_send, 1), 0)],
        x,
    )
    up1 = Piece(
        (3, 1, 0, "band"), (2,) * 4, 4 * block, [(up_keep, 0), (links.bring(up_send, "band"), 0)], y
    )
    *sums_send, sums_keep, branch, gatt, out_rows, vec2 = mlp_back(
        links, vecs, n2, gact, act1, gpre1, mlp_up, mlp_down, mid, cot, att, attn_out, ()
    )
    both = lambda i, at: [(sums_keep, at), (links.bring(sums_send[i], 0), 0)]
    middle, end = 2 * width, 2 * width + mlp_up.shape[1] // 2
    down2 = Piece((0, 1, "band", "h", 3, 2), (2,) * 6, block, both(0, 0), core)
    up2 = Piece((0, 3, 1, "band"), (2,) * 4, 4 * block, both(1, middle), core)
    names, sizes = (0, 1, "band", 3, 2), (2,) * 5
    outp = Piece(names, sizes, block, both(2, end), core)
    block_output = jnp.concatenate(
        [
            out_rows[body : body + chips][:, None, :],
            out_rows[:body].reshape(chips, slots, width),
        ],
        axis=1,
    )
    tie, unused = combine(links, [(down1, core, "split"), (up1, core, "split")], (vec2,))
    tie, unused = combine(
        links,
        [
            (down1, y, "split"),
            (up1, x, "split"),
            (down2, x, "split"),
            (up2, y, "split"),
            (outp, (2,), "split"),
        ],
        (*tie, block_output),
    )

    gpacked, qkv_send, qkv_keep = attention_back(links, chips, gatt, packed, probs, tprobs, n1, tie)
    qkv_in = links.bring(qkv_send, 0)
    qkv = [
        Piece(names, sizes, count, [(qkv_keep, at), (qkv_in, at)], core)
        for at, count in qkv_parts(width)
    ]
    older = touch((gpacked,), down1, up1, down2, up2, outp)
    tie, unused = combine(
        links,
        [
            (down2, y, "split"),
            (up2, x, "split"),
            (qkv[0], x, "split"),
            (qkv[1], y, "split"),
            (down1, (2,), "split"),
            (up1, (3,), "split"),
            (outp, (3,), "split"),
        ],
        (older,),
    )
    kg_send, kg_keep, pgrad_own, pgrad_far, vec_keep = embed_back(
        links,
        chips,
        vecs,
        vec2,
        gpacked,
        attn_qkv,
        stream,
        branch,
        picked_own,
        picked_in,
        kernels_own,
        far_half,
        far_other,
        tie,
    )
    kg_in = links.bring(kg_send, 0)
    kg = Piece((0, "band", 1, "h"), (2,) * 4, depth // 4, [(kg_keep, 0), (kg_in, 0)], core)
    vec = Vec(vec_keep, (kg_in, 2 * depth))
    older = touch((vec_keep,), down2, up2, *qkv, down1, up1, outp)
    tie, unused = combine(
        links,
        [
            (kg, plane, "split"),
            (vec, plane, "vec"),
            (qkv[0], y, "split"),
            (qkv[1], x, "split"),
            (outp, plane, "split"),
            (down2, (2,), "split"),
            (up2, (3,), "split"),
            (down1, (3,), "split"),
        ],
        (older,),
    )
    far_grads = links.bring(flat(pgrad_far), "band")
    partly = scatter(links, 0, flat(pgrad_own), depth, visible, patches)
    up = Piece.join(up1, up2, 2)
    tie, (out_sum,) = combine(
        links,
        [
            (qkv[0], (2,), "split"),
            (qkv[1], (2,), "split"),
            (kg, (2, 3), "all"),
            (vec, (2, 3), "vec"),
            (outp, F32, "final"),
        ],
        (partly,),
    )
    scattered = scatter(links, 1, far_grads, depth, visible, patches, partly)
    pixel_grads = jnp.swapaxes(scattered.reshape(group_chips, bands, pix, patches), 2, 3)
    tie, unused = combine(
        links,
        [
            (qkv[0], (3,), "split"),
            (qkv[1], (3,), "split"),
            (up, (2,), "split"),
            (down2, (3,), "split"),
        ],
        (scattered,),
    )
    tie, (kgrad,) = combine(links, [(kg, BF, "final"), (vec, (), "vec")], tie, "finish")
    vec_sum = links.total(vec.value())
    kgrad = links.total(kgrad.astype(F32)).astype(BF)
    near = [kgrad, links.swap(kgrad, 1), links.swap(kgrad, 0), links.swap(kgrad, 0, 1)]
    tie, (*qkv_sums, up_sum, down_sum, unused) = combine(
        links,
        [
            (qkv[0], (F32, "qkv"), "final"),
            (qkv[1], (F32, "qkv"), "final"),
            (up, F32, "final"),
            (down1, (F32, "down", 2), "final"),
            (down2, (F32, "down", 2), "final"),
        ],
        (scattered,),
    )
    *vecs, kernel_grads = assemble(links, vec_sum, near, qkv_sums[0])

    weight = lambda part: jnp.swapaxes(links.last(part), 0, 1)
    return (
        block_output,
        pixel_grads,
        kernel_grads.reshape(bands, pix, width),
        vecs[2],
        vecs[0],
        vecs[1],
        vecs[3],
        vecs[4],
        weight(qkv_sums[0]),
        weight(out_sum),
        weight(up_sum),
        weight(down_sum),
    )


def solution(mesh):
    placed = (
        P("dp", "band", None, None),
        P("dp", None),
        P("band", None, None),
        P(),
        P(),
        P(),
        P(),
        P(),
        P(),
        P(),
        P(),
        P(),
        P(("dp", "band"), None, None),
    )
    return jax.shard_map(
        functools.partial(shards, Links(mesh)),
        mesh=mesh,
        in_specs=placed,
        out_specs=(
            P(("dp", "band"), None, None),
            P("dp", "band", None, None),
            P("band", None, None),
            P(),
            P(),
            P(),
            P(),
            P(),
            P("band", "dp"),
            P("band", "dp"),
            P("band", "dp"),
            P("band", "dp"),
        ),
        check_vma=False,
    )
```

```python
import functools

import jax
import jax.numpy as jnp
from jax import lax
from jax.experimental import pallas as pl
from jax.experimental.pallas import tpu as pltpu
from jax.sharding import PartitionSpec as P

HEADS = 12
HEAD = 64
BF = jnp.bfloat16
F32 = jnp.float32
TAIL = 16
BLOCK = 112
KEYS = 80
SCALE = HEAD ** (-0.5)
VMEM = pl.BlockSpec(memory_space=pltpu.VMEM)
HBM = pl.BlockSpec(memory_space=pl.ANY)
shape = jax.ShapeDtypeStruct
MICROSECONDS = {
    "pick_far": 5,
    "prepare": 11,
    "encoder_forward": 31,
    "mlp_back": 32,
    "attention_back": 18,
    "embed_back": 14,
    "combine": 12,
    "touch": 20,
    "assemble": 0.5,
    "finish": 0.5,
    "scatter": 4,
}


def dot(a, b):
    return jnp.dot(a, b, preferred_element_type=F32)


def dot_nt(a, b):
    return lax.dot_general(a, b, (((1,), (1,)), ((), ())), preferred_element_type=F32)


def dot_tn(a, b):
    return lax.dot_general(a, b, (((0,), (0,)), ((), ())), preferred_element_type=F32)


def kernel_call(body, name, outs, scratch, copies, vmem_in=0, vmem_out=0, mib=62, **more):
    def call(*operands):
        return pl.pallas_call(
            body,
            out_shape=tuple(outs),
            in_specs=[VMEM] * vmem_in + [HBM] * (len(operands) - vmem_in),
            out_specs=(HBM,) * (len(outs) - vmem_out) + (VMEM,) * vmem_out,
            scratch_shapes=[
                a if hasattr(a, "get_ref_aval") else pltpu.VMEM(a.shape, a.dtype) for a in scratch
            ]
            + [pltpu.SemaphoreType.DMA((copies,))],
            compiler_params=pltpu.CompilerParams(vmem_limit_bytes=mib * 1024 * 1024),
            cost_estimate=pl.CostEstimate(
                flops=int(MICROSECONDS[name] * 1.15e9), bytes_accessed=1, transcendentals=0
            ),
            name=name,
            **more,
        )(*operands)

    return call


def tiles(count, body, looped=False, base=0, tile=256):
    if not looped:
        for j in range(0, count, tile):
            body(slice(base + j, base + j + tile))
        return

    def step(j, carry):
        body(pl.ds(pl.multiple_of(base + j * tile, tile), tile))
        return carry

    lax.fori_loop(0, count // tile, step, 0)


LOOP = (True, False, True, True, False)


class Copies:
    def __init__(self, sems):
        self.sems, self.count, self.open = sems, 0, []

    def start(self, source, target):
        copy = pltpu.make_async_copy(source, target, self.sems.at[self.count])
        self.count += 1
        copy.start()
        return copy

    def out(self, source, target):
        self.open.append(self.start(source, target))

    def finish(self):
        for copy in self.open:
            copy.wait()


def chosen(seen_ref, chip, patches):
    first = seen_ref[pl.ds(chip, 1), :]
    second = seen_ref[pl.ds(chip + 1, 1), :]
    slots = first.shape[1]
    seen = jnp.concatenate([first, second], axis=1)
    ids = lax.broadcasted_iota(jnp.int32, (patches, 2 * slots), 0)
    lane = lax.broadcasted_iota(jnp.int32, (patches, 2 * slots), 1)
    hit = ids == seen
    return (
        jnp.where(hit & (lane < slots), 1.0, 0.0).astype(BF),
        jnp.where(hit & (lane >= slots), 1.0, 0.0).astype(BF),
    )


class Pixels:
    def __init__(self, pixel_hbm, pixel_ref, base, pairs, sems):
        self.hbm, self.ref, self.base, self.pairs, self.sems = pixel_hbm, pixel_ref, base, pairs, sems
        for i in range(pairs):
            self.copy(i).start()

    def copy(self, i):
        there, here = pl.ds(self.base + 2 * i, 2), pl.ds(2 * i, 2)
        return pltpu.make_async_copy(self.hbm.at[there], self.ref.at[here], self.sems.at[i])

    def pick(self, seen_ref, out_ref):
        wide = 2 * seen_ref.shape[1]

        def pair(i, carry):
            first, second = chosen(seen_ref, self.base + 2 * i, self.ref.shape[2])
            self.copy(i).wait()
            out_ref[:, pl.ds(pl.multiple_of(i * wide, wide), wide)] = (
                dot(self.ref[2 * i], first) + dot(self.ref[2 * i + 1], second)
            ).astype(BF)
            return carry

        lax.fori_loop(0, self.pairs, pair, 0)


def pick_far_kernel(
    links, pairs, seen_ref, pixel_hbm, halves_hbm, half_hbm, out_hbm, pixel_ref, out_ref, half_ref, pixel_sems, sems
):
    copies = Copies(sems)
    base = (1 - links.bit("band")) * 2 * pairs
    half_in = copies.start(halves_hbm.at[links.bit(0)], half_ref)
    pixels = Pixels(pixel_hbm, pixel_ref, base, pairs, pixel_sems)
    half_in.wait()
    copies.out(half_ref, half_hbm)
    pixels.pick(seen_ref, out_ref)
    copies.out(out_ref, out_hbm)
    copies.finish()


def pick_far(links, seen, pixel_rows, halves):
    chips, depth, patches = pixel_rows.shape
    pairs = chips // 4
    outs = (shape(halves.shape[1:], BF), shape((depth, chips // 2 * seen.shape[1]), BF))
    return kernel_call(
        functools.partial(pick_far_kernel, links, pairs),
        "pick_far",
        outs,
        (
            shape((2 * pairs, depth, patches), BF),
            outs[1],
            outs[0],
            pltpu.SemaphoreType.DMA((pairs,)),
        ),
        4,
        vmem_in=1,
    )(seen, pixel_rows, halves)


def prepare_kernel(
    links,
    pairs,
    seen_ref,
    pixel_hbm,
    cot_hbm,
    down_hbm,
    picked_hbm,
    rows_hbm,
    gact_hbm,
    pixel_ref,
    cot_ref,
    down_ref,
    picked_ref,
    rows_ref,
    gact_ref,
    tail_ref,
    pixel_sems,
    sems,
):
    copies = Copies(sems)
    chips = cot_ref.shape[0]
    slots = cot_ref.shape[1] - 1
    rows, width = rows_ref.shape
    base = links.bit("band") * 2 * pairs
    cot_in = copies.start(cot_hbm, cot_ref)
    pixels = Pixels(pixel_hbm, pixel_ref, base, pairs, pixel_sems)
    chunk = down_hbm.shape[0] // 4
    parts = [slice(i * chunk, (i + 1) * chunk) for i in range(4)]
    downs = [copies.start(down_hbm.at[part, :], down_ref.at[part, :]) for part in parts]
    cot_in.wait()
    tail_ref[...] = jnp.zeros_like(tail_ref)

    def lay(c, carry):
        chip = cot_ref[c].astype(F32)
        rows_ref[pl.ds(pl.multiple_of(c * slots, slots), slots), :] = chip[1:, :].astype(BF)
        tail_ref[pl.ds(c, 1), :] = chip[0:1, :]
        return carry

    lax.fori_loop(0, chips, lay, 0)
    rows_ref[rows - TAIL : rows, :] = tail_ref[...].astype(BF)
    copies.out(rows_ref, rows_hbm)
    pixels.pick(seen_ref, picked_ref)
    copies.out(picked_ref, picked_hbm)
    for part, copy in zip(parts, downs):
        copy.wait()

        def act_grad(at):
            gact_ref[:, at] = dot_nt(rows_ref[...], down_ref[at, :]).astype(BF)

        tiles(chunk, act_grad, True, part.start)
        copies.out(gact_ref.at[:, part], gact_hbm.at[:, part])
    copies.finish()


def prepare(links, seen, pixel_rows, cot, down):
    group, depth, patches = pixel_rows.shape
    pairs = group // 4
    hidden, width = down.shape
    body = cot.shape[0] * seen.shape[1]
    rows = body + TAIL
    outs = (shape((depth, body), BF), shape((rows, width), BF), shape((rows, hidden), BF))
    return kernel_call(
        functools.partial(prepare_kernel, links, pairs),
        "prepare",
        outs,
        (shape((2 * pairs, depth, patches), BF), cot, down)
        + outs
        + (shape((TAIL, width), F32), pltpu.SemaphoreType.DMA((pairs,))),
        12,
        vmem_in=1,
    )(seen, pixel_rows, cot, down)


def row_stats(values):
    average = jnp.mean(values, axis=-1, keepdims=True)
    centred = values - average
    spread = jnp.mean(centred * centred, axis=-1, keepdims=True)
    root = lax.rsqrt(spread + 1e-06)
    return centred * root, root


def norm_back(xhat, root, grad_out, gain):
    scaled = grad_out * gain
    mean_scaled = jnp.mean(scaled, axis=-1, keepdims=True)
    mean_along = jnp.mean(scaled * xhat, axis=-1, keepdims=True)
    return root * (scaled - mean_scaled - xhat * mean_along)


def head_rows(width):
    row = lax.broadcasted_iota(jnp.int32, (TAIL, width), 0)
    lane = lax.broadcasted_iota(jnp.int32, (TAIL, width), 1)
    return (lane // HEAD) == row


def two_heads(pair):
    low = lax.broadcasted_iota(jnp.int32, pair.shape, 1) < HEAD
    zero = jnp.zeros_like(pair)
    return jnp.concatenate([jnp.where(low, pair, zero), jnp.where(low, zero, pair)], axis=0)


def own_heads(stacked):
    rows = stacked.shape[0] // 2
    low = lax.broadcasted_iota(jnp.int32, (rows, stacked.shape[1]), 1) < HEAD
    return jnp.where(low, stacked[:rows], stacked[rows:])


def softmax_keys(scores, count):
    key = lax.broadcasted_iota(jnp.int32, scores.shape, 0)
    scores = jnp.where(key < count, scores * SCALE, -1e30)
    raised = jnp.exp(scores - jnp.max(scores, axis=0, keepdims=True))
    return raised * (1.0 / jnp.sum(raised, axis=0, keepdims=True))


def load_far(links, copies, half_hbm, other_hbm, target):
    count = half_hbm.shape[0]
    core = links.bit(0)
    return [
        copies.start(half_hbm, target.at[pl.ds(pl.multiple_of(core * count, 16), count), :]),
        copies.start(other_hbm, target.at[pl.ds(pl.multiple_of((1 - core) * count, 16), count), :]),
    ]


def forward_kernel(
    links,
    chips,
    vecs_ref,
    xo_hbm,
    xr_hbm,
    ko_hbm,
    half_hbm,
    other_hbm,
    wqkv_hbm,
    wout_hbm,
    cot_hbm,
    gact_hbm,
    up_hbm,
    stream_hbm,
    n1_hbm,
    packed_hbm,
    probs_hbm,
    tprobs_hbm,
    att_hbm,
    mid_hbm,
    n2_hbm,
    act_hbm,
    gpre_hbm,
    down_send_hbm,
    down_keep_hbm,
    up_send_hbm,
    up_keep_hbm,
    stream_ref,
    n1_ref,
    packed_ref,
    probs_ref,
    tprobs_ref,
    att_ref,
    mid_ref,
    n2_ref,
    xo_ref,
    xr_ref,
    ko_ref,
    kr_ref,
    tatt_ref,
    wqkv_ref,
    wout_ref,
    *half_refs,
):
    copies = Copies(half_refs[-1])
    rows, width = n1_ref.shape
    body = rows - TAIL
    slots = body // chips
    token, gain1, bias1, gain2, bias2 = (vecs_ref[i : i + 1, :] for i in range(5))
    first = [
        copies.start(source, target)
        for source, target in ((xo_hbm, xo_ref), (ko_hbm, ko_ref), (xr_hbm, xr_ref))
    ] + load_far(links, copies, half_hbm, other_hbm, kr_ref)
    for copy in first:
        copy.wait()
    wqkv_in = copies.start(wqkv_hbm, wqkv_ref)
    wout_in = copies.start(wout_hbm, wout_ref)
    half = MlpHalf(links, 0, copies, half_refs[:-1])

    def embed(at):
        stream_ref[at, :] = dot_tn(xo_ref[:, at], ko_ref[...]) + dot_tn(xr_ref[:, at], kr_ref[...])

    tiles(body, embed, True)
    tail_row = lax.broadcasted_iota(jnp.int32, (TAIL, width), 0)
    stream_ref[body:rows, :] = jnp.where(tail_row < chips, token, 0.0)

    def first_norm(i, carry):
        at = pl.ds(pl.multiple_of(i * BLOCK, BLOCK), BLOCK)
        xhat, unused = row_stats(stream_ref[at, :])
        n1_ref[at, :] = (xhat * gain1 + bias1).astype(BF)
        return carry

    lax.fori_loop(0, rows // BLOCK, first_norm, 0)
    wqkv_in.wait()
    half.load(cot_hbm, gact_hbm, up_hbm)
    copies.out(stream_ref, stream_hbm)
    copies.out(n1_ref, n1_hbm)


    def project(at):
        packed_ref[:, at] = dot(n1_ref[...], wqkv_ref[:, at]).astype(BF)

    tiles(3 * width, project, True)
    copies.out(packed_ref, packed_hbm)
    tail = packed_ref[body:rows, :]
    heads = head_rows(width)
    tquery = jnp.where(heads, jnp.broadcast_to(tail[0:1, 0:width], (TAIL, width)), 0).astype(BF)
    tatt_ref[...] = jnp.zeros_like(tatt_ref)

    def chip(c, carry):
        at = pl.ds(pl.multiple_of(c * slots, slots), slots)
        key = jnp.concatenate(
            [packed_ref[at, width : 2 * width], tail[:, width : 2 * width]], axis=0
        )
        val = jnp.concatenate([packed_ref[at, 2 * width :], tail[:, 2 * width :]], axis=0)
        tiles = [slice(128 * p, 128 * p + 128) for p in range(width // 128)]
        scores = [dot_nt(key[:, here], two_heads(packed_ref[at, here])) for here in tiles]
        scores.append(dot_nt(key, tquery))
        probs = [softmax_keys(s, slots + 1).astype(BF) for s in scores]
        mixed = [dot_tn(probs[p], val[:, tiles[p]]) for p in range(len(tiles))]
        mixed.append(dot_tn(probs[-1], val))
        for p in range(len(tiles)):
            probs_ref[c, p] = probs[p]
            att_ref[at, tiles[p]] = own_heads(mixed[p]).astype(BF)
        tprobs_ref[c] = probs[-1]
        tatt_ref[pl.ds(c, 1), :] = jnp.sum(jnp.where(heads, mixed[-1], 0.0), axis=0, keepdims=True)
        return carry

    lax.fori_loop(0, chips, chip, 0, unroll=2)
    att_ref[body:rows, :] = tatt_ref[...].astype(BF)
    copies.out(probs_ref, probs_hbm)
    copies.out(tprobs_ref, tprobs_hbm)
    copies.out(att_ref, att_hbm)
    wout_in.wait()


    def out_project(at):
        mid_ref[:, at] = stream_ref[:, at] + dot(att_ref[...], wout_ref[:, at])

    tiles(width, out_project, True)
    copies.out(mid_ref, mid_hbm)

    def second_norm(i, carry):
        at = pl.ds(pl.multiple_of(i * BLOCK, BLOCK), BLOCK)
        xhat, unused = row_stats(mid_ref[at, :])
        n2_ref[at, :] = (xhat * gain2 + bias2).astype(BF)
        return carry

    lax.fori_loop(0, rows // BLOCK, second_norm, 0)
    copies.out(n2_ref, n2_hbm)
    half.run(n2_ref, (down_send_hbm, down_keep_hbm), (up_send_hbm, up_keep_hbm))
    copies.out(half.act, act_hbm)
    copies.out(half.gpre, gpre_hbm)
    copies.finish()


class MlpHalf:
    def __init__(self, links, third, copies, refs):
        self.links, self.third, self.copies = links, third, copies
        self.looped = (True, False)
        self.cot, self.gact, self.up, self.act, self.gpre, self.grads = refs

    @staticmethod
    def scratch(rows, width, hidden):
        return (
            shape((rows, width), BF),
            shape((rows, hidden // 2), BF),
            shape((width, hidden // 2), BF),
            shape((rows, hidden // 2), BF),
            shape((rows, hidden // 2), BF),
            shape((4, max(width, hidden // 4), width), BF),
        )

    def load(self, cot_hbm, gact_hbm, up_hbm):
        chunk = up_hbm.shape[1] // 4
        start = self.copies.start
        far = lambda i: slice((2 * i + self.third) * chunk, (2 * i + self.third + 1) * chunk)
        near = lambda i: slice(i * chunk, (i + 1) * chunk)
        self.first = [
            (
                start(up_hbm.at[:, far(i)], self.up.at[:, near(i)]),
                start(gact_hbm.at[:, far(i)], self.gact.at[:, near(i)]),
            )
            for i in range(2)
        ]
        self.cot_in = start(cot_hbm, self.cot)

    def run(self, n2_ref, down_out, up_out, then=None):
        copies, links = self.copies, self.links
        rows, width = n2_ref.shape
        chunk = self.up.shape[1] // 2
        half = width // 2
        block = width // 16
        for i in range(2):
            for copy in self.first[i]:
                copy.wait()
            if i == 1 and then is not None:
                then()

            def activate(cols):
                pre = dot(n2_ref[...], self.up[:, cols])
                phi = 0.5 + 0.5 * lax.erf(pre * (0.5**0.5))
                bell = jnp.exp(-0.5 * pre * pre) * 0.3989422804014327
                self.act[:, cols] = (pre * phi).astype(BF)
                gact = self.gact[:, cols].astype(F32)
                self.gpre[:, cols] = (gact * (phi + pre * bell)).astype(BF)

            tiles(chunk, activate, self.looped[0], i * chunk)
        where = (1, "band") if self.third == 0 else (0, 0)
        bits = [links.bit(w) for w in where]
        self.cot_in.wait()
        for i in range(2):

            def down_rows(at):
                self.grads[i, at, :] = dot_tn(
                    self.cot[:, at], self.act[:, i * chunk : (i + 1) * chunk]
                ).astype(BF)

            tiles(width, down_rows, self.looped[1])
            for side, bit in ((0, 1 - bits[0]), (1, bits[0])):
                for other in range(2):
                    x, c = (bit, other) if where[0] == 1 else (other, bit)
                    for z in range(4):
                        at = pl.multiple_of(((z * 2 + x) * 2 + c) * block, 16)
                        for h in range(2):
                            to = (((other * 2 + i) * 2 + h) * 4 + z) * block
                            copies.out(
                                self.grads.at[i, pl.ds(at, block), h * half : (h + 1) * half],
                                down_out[side].at[to : to + block, :],
                            )
        part = chunk // 4
        for i in range(2):

            def up_rows(at):
                self.grads[2 + i, at, :] = dot_tn(
                    self.gpre.at[:, i * chunk : (i + 1) * chunk][:, at], n2_ref[...]
                ).astype(BF)

            tiles(chunk, up_rows, self.looped[1])
            for side, bit in ((0, 1 - bits[1]), (1, bits[1])):
                for x in range(2):
                    for other in range(2):
                        if where[1] == "band":
                            at = (2 * x + other) * part
                            cols = pl.ds(pl.multiple_of(bit * half, 128), half)
                        else:
                            at = pl.multiple_of((2 * x + bit) * part, 16)
                            cols = slice(other * half, (other + 1) * half)
                        to = ((i * 2 + x) * 2 + other) * part
                        copies.out(
                            self.grads.at[2 + i, pl.ds(at, part), cols],
                            up_out[side].at[to : to + part, :],
                        )


def forward(links, chips, vecs, xo, xr, ko, half, other, wqkv, wout, cot, gact, up):
    width, hidden = up.shape
    body = xo.shape[1]
    rows = body + TAIL
    saved = (
        shape((rows, width), F32),
        shape((rows, width), BF),
        shape((rows, 3 * width), BF),
        shape((chips, width // 128, KEYS, 128), BF),
        shape((chips, KEYS, TAIL), BF),
        shape((rows, width), BF),
        shape((rows, width), F32),
        shape((rows, width), BF),
    )
    return kernel_call(
        functools.partial(forward_kernel, links, chips),
        "encoder_forward",
        saved
        + (shape((rows, hidden // 2), BF),) * 2
        + (shape((2 * width, width // 2), BF),) * 2
        + (shape((hidden // 2, width // 2), BF),) * 2,
        saved
        + (xo, xr, ko, ko, shape((TAIL, width), F32), wqkv, wout)
        + MlpHalf.scratch(rows, width, hidden),
        112,
        vmem_in=1,
    )(vecs, xo, xr, ko, half, other, wqkv, wout, cot, gact, up)


def spread_blocks(links, copies, full_ref, outs):
    core = links.bit(0)
    cols = full_ref.shape[1] // 2
    block = full_ref.shape[0] // 16
    for z in range(4):
        for x in range(2):
            for side, c in ((0, 1 - core), (1, core)):
                start = ((z * 2 + x) * 2 + c) * block
                for count, pair in outs:
                    rows = pl.ds(pl.multiple_of(start, 16), count)
                    start = start + count
                    for b in range(2):
                        to = ((x * 2 + b) * 4 + z) * count
                        copies.out(
                            full_ref.at[rows, b * cols : (b + 1) * cols],
                            pair[side].at[to : to + count, :],
                        )


def mlp_back_kernel(
    links,
    after,
    vecs_ref,
    n2_hbm,
    gact_hbm,
    act1_hbm,
    gpre1_hbm,
    up_hbm,
    down_hbm,
    mid_hbm,
    cot_hbm,
    att_hbm,
    wout_hbm,
    *rest,
):
    rest = rest[after:]
    sends, (keep_hbm, branch_hbm, gatt_hbm, out_hbm, vec_ref) = rest[:3], rest[3:8]
    (
        n2_ref,
        gatt_ref,
        out_ref,
        act_ref,
        gpre_ref,
        up_ref,
        down_ref,
        mid_ref,
        att_ref,
        wout_ref,
        back_ref,
        branch_ref,
        full_ref,
    ) = rest[8:21]
    half_refs, sems = rest[21:-1], rest[-1]
    copies = Copies(sems)
    rows, width = mid_ref.shape
    quarter = up_hbm.shape[1] // 4
    at = lambda i: slice(i * quarter, (i + 1) * quarter)
    n2_in = copies.start(n2_hbm, n2_ref)
    half = MlpHalf(links, 1, copies, half_refs)
    half.load(cot_hbm, gact_hbm, up_hbm)
    cot_ref = half.cot
    n2_in.wait()
    first_in = []

    def more():
        first_in.append(copies.start(gpre1_hbm, gpre_ref))
        for i in range(2):
            first_in.append(copies.start(up_hbm.at[:, at(2 * i)], up_ref.at[:, at(i)]))
        for source, target in ((mid_hbm, mid_ref), (att_hbm, att_ref), (wout_hbm, wout_ref)):
            first_in.append(copies.start(source, target))

    middle = 2 * width
    end = middle + up_hbm.shape[1] // 2
    half.run(
        n2_ref,
        (sends[0], keep_hbm.at[0:middle, :]),
        (sends[1], keep_hbm.at[middle:end, :]),
        more,
    )
    late = [copies.start(act1_hbm, act_ref)] + [
        copies.start(down_hbm.at[at(2 * i + third), :], down_ref.at[at(2 * third + i), :])
        for third in range(2)
        for i in range(2)
    ]
    for copy in first_in:
        copy.wait()

    def backward(cols):
        back_ref[:, cols] = dot_nt(gpre_ref[...], up_ref[cols, :]) + dot_nt(
            half.gpre[...], half.up[cols, :]
        )

    tiles(width, backward, LOOP[2])
    gain = vecs_ref[3:4, :]

    def norm(i, carry):
        at = pl.ds(pl.multiple_of(i * BLOCK, BLOCK), BLOCK)
        xhat, root = row_stats(mid_ref[at, :])
        grad = back_ref[at, :]
        total = cot_ref[at, :].astype(F32) + norm_back(xhat, root, grad, gain)
        branch_ref[at, :] = total.astype(BF)
        return (
            carry[0] + jnp.sum(grad * xhat, axis=0, keepdims=True),
            carry[1] + jnp.sum(grad, axis=0, keepdims=True),
        )

    zero = jnp.zeros((1, width), F32)
    gain_sum, bias_sum = lax.fori_loop(0, rows // BLOCK, norm, (zero, zero))
    vec_ref[0:1, :] = gain_sum
    vec_ref[1:2, :] = bias_sum
    copies.out(branch_ref, branch_hbm)

    def out_grad(at):
        full_ref[at, :] = dot_tn(branch_ref[:, at], att_ref[...]).astype(BF)

    tiles(width, out_grad, LOOP[4])
    spread_blocks(
        links, copies, full_ref, [(width // 16, (sends[2], keep_hbm.at[end : end + width, :]))]
    )

    def attended_grad(at):
        gatt_ref[:, at] = dot_nt(branch_ref[...], wout_ref[at, :]).astype(BF)

    tiles(width, attended_grad, LOOP[4])
    copies.out(gatt_ref, gatt_hbm)
    for copy in late:
        copy.wait()

    def outward(cols):
        out_ref[:, cols] = (
            mid_ref[:, cols]
            + dot(act_ref[...], down_ref[: 2 * quarter, cols])
            + dot(half.act[...], down_ref[2 * quarter :, cols])
        ).astype(BF)

    tiles(width, outward, LOOP[3])
    copies.out(out_ref, out_hbm)
    copies.finish()


def mlp_back(links, vecs, n2, gact, act1, gpre1, up, down, mid, cot, att, wout, after):
    rows, width = mid.shape
    hidden = up.shape[1]
    sums = shape((3 * width + hidden // 2, width // 2), BF)
    return kernel_call(
        functools.partial(mlp_back_kernel, links, len(after)),
        "mlp_back",
        tuple(shape((count, width // 2), BF) for count in (2 * width, hidden // 2, width))
        + (sums, cot, cot, cot, shape((2, width), F32)),
        (n2, cot, cot, act1, gpre1)
        + (shape((width, hidden // 2), BF), down, mid, att, wout, mid, cot, wout)
        + MlpHalf.scratch(rows, width, hidden),
        140,
        vmem_in=1,
        vmem_out=1,
    )(vecs, n2, gact, act1, gpre1, up, down, mid, cot, att, wout, *after)


def split_vec(vec):
    high = vec.astype(BF)
    return high, (vec - high.astype(F32)).astype(BF)


def attention_back_kernel(
    links, chips, after, gatt_hbm, packed_hbm, probs_hbm, tprobs_hbm, n1_hbm, *rest
):
    gpacked_hbm, send_hbm, keep_hbm = rest[after : after + 3]
    (
        gpacked_ref,
        gatt_ref,
        packed_ref,
        probs_ref,
        tprobs_ref,
        n1_ref,
        tgrad_ref,
        tout_ref,
        full_ref,
        chip_sems,
        sems,
    ) = rest[after + 3 :]
    rows, width = n1_ref.shape
    body = rows - TAIL
    slots = body // chips
    copies = Copies(sems)

    def arriving(c):
        at = pl.ds(pl.multiple_of(c * slots, slots), slots)
        return [
            pltpu.make_async_copy(source.at[where], target.at[where], chip_sems.at[k, c])
            for k, (source, target, where) in enumerate(
                (
                    (packed_hbm, packed_ref, (at, slice(None))),
                    (gatt_hbm, gatt_ref, (at, slice(None))),
                    (probs_hbm, probs_ref, c),
                )
            )
        ]

    tails = slice(body, rows)
    arrive = [
        copies.start(packed_hbm.at[tails, :], packed_ref.at[tails, :]),
        copies.start(gatt_hbm.at[tails, :], gatt_ref.at[tails, :]),
        copies.start(tprobs_hbm, tprobs_ref),
    ]
    for c in range(chips):
        for copy in arriving(c):
            copy.start()
    tout_ref[...] = jnp.zeros_like(tout_ref)
    heads = head_rows(width)
    for copy in arrive:
        copy.wait()
    n1_in = copies.start(n1_hbm, n1_ref)
    tgrad_ref[...] = gatt_ref[body:rows, :].astype(F32)
    tail = packed_ref[body:rows, :]
    tquery = jnp.where(heads, jnp.broadcast_to(tail[0:1, 0:width], (TAIL, width)), 0).astype(BF)

    def chip(c):
        at = pl.ds(pl.multiple_of(c * slots, slots), slots)
        key_all = jnp.concatenate(
            [packed_ref[at, width : 2 * width], tail[:, width : 2 * width]], axis=0
        )
        val_all = jnp.concatenate([packed_ref[at, 2 * width :], tail[:, 2 * width :]], axis=0)
        tgrad = jnp.where(
            heads, jnp.broadcast_to(tgrad_ref[pl.ds(c, 1), :], (TAIL, width)), 0.0
        ).astype(BF)
        tiles = [slice(128 * p, 128 * p + 128) for p in range(width // 128)]
        probs = [probs_ref[c, p] for p in range(len(tiles))] + [tprobs_ref[c]]
        gouts = [two_heads(gatt_ref[at, here]) for here in tiles]
        queries = [two_heads(packed_ref[at, here]) for here in tiles]
        gprobs = [dot_nt(val_all[:, tiles[p]], gouts[p]) for p in range(len(tiles))]
        gprobs.append(dot_nt(val_all, tgrad))
        gscores = []
        for prob, gprob in zip(probs, gprobs):
            wide = prob.astype(F32)
            inner = jnp.sum(gprob * wide, axis=0, keepdims=True)
            gscores.append((wide * (gprob - inner) * SCALE).astype(BF))
        gval_tail = dot(probs[-1], tgrad)
        gkey_tail = dot(gscores[-1], tquery)
        mixed = jnp.where(heads, dot_tn(gscores[-1], key_all), 0.0)
        gvals = [dot(probs[p], gouts[p]) + gval_tail[:, tiles[p]] for p in range(len(tiles))]
        gkeys = [dot(gscores[p], queries[p]) + gkey_tail[:, tiles[p]] for p in range(len(tiles))]
        gqueries = [own_heads(dot_tn(gscores[p], key_all[:, tiles[p]])) for p in range(len(tiles))]
        for p in range(len(tiles)):
            gpacked_ref[at, 128 * p : 128 * p + 128] = gqueries[p].astype(BF)
            base = width + 128 * p
            gpacked_ref[at, base : base + 128] = gkeys[p][:slots].astype(BF)
            gpacked_ref[at, width + base : width + base + 128] = gvals[p][:slots].astype(BF)
        tout_ref[pl.ds(c, 1), :] = jnp.concatenate(
            [jnp.sum(mixed, axis=0, keepdims=True)]
            + [g[slots : slots + 1] for g in gkeys + gvals],
            axis=1,
        )

    def two_chips(i, carry):
        for c in (2 * i, 2 * i + 1):
            for copy in arriving(c):
                copy.wait()
        chip(2 * i)
        chip(2 * i + 1)
        return carry

    lax.fori_loop(0, chips // 2, two_chips, 0)
    gpacked_ref[body:rows, :] = tout_ref[...].astype(BF)
    copies.out(gpacked_ref, gpacked_hbm)
    n1_in.wait()

    def qkv_rows(at):
        full_ref[at, :] = dot_tn(gpacked_ref[:, at], n1_ref[...]).astype(BF)

    tiles(3 * width, qkv_rows)
    outs = []
    for at, count in qkv_parts(width):
        here = slice(at, at + 16 * count)
        outs.append((count, (send_hbm.at[here, :], keep_hbm.at[here, :])))
    spread_blocks(links, copies, full_ref, outs)
    copies.finish()


def qkv_parts(width):
    block = 3 * width // 16
    count = -(-block // 32) * 16
    return [(0, count), (16 * count, block - count)]


def attention_back(links, chips, gatt, packed, probs, tprobs, n1, after):
    rows, width = n1.shape
    sums = shape((3 * width, width // 2), BF)
    return kernel_call(
        functools.partial(attention_back_kernel, links, chips, len(after)),
        "attention_back",
        (packed, sums, sums),
        (packed, gatt, packed, probs, tprobs, n1)
        + (
            shape((TAIL, width), F32),
            shape((TAIL, 3 * width), F32),
            shape((3 * width, width), BF),
            pltpu.SemaphoreType.DMA((3, chips)),
        ),
        80,
    )(gatt, packed, probs, tprobs, n1, *after)


def embed_back_kernel(
    links,
    chips,
    after,
    vecs_ref,
    vec2_ref,
    gpacked_hbm,
    wqkv_hbm,
    stream_hbm,
    branch_hbm,
    xo_hbm,
    xr_hbm,
    ko_hbm,
    half_hbm,
    other_hbm,
    *rest,
):
    send_hbm, keep_hbm, own_hbm, far_hbm, vec_ref = rest[after : after + 5]
    (
        gpacked_ref,
        wqkv_ref,
        stream_ref,
        branch_ref,
        xo_ref,
        xr_ref,
        ko_ref,
        kr_ref,
        send_ref,
        keep_ref,
        pgrad_ref,
        back_ref,
        embed_ref,
        kfull_ref,
        sems,
    ) = rest[after + 5 :]
    rows, width = stream_ref.shape
    body = rows - TAIL
    half = width // 2
    copies = Copies(sems)
    thirds = [slice(i * width, (i + 1) * width) for i in range(3)]
    arrive = [
        (
            copies.start(gpacked_hbm.at[:, part], gpacked_ref.at[:, part]),
            copies.start(wqkv_hbm.at[:, part], wqkv_ref.at[:, part]),
        )
        for part in thirds
    ]
    for i, part in enumerate(thirds):
        for copy in arrive[i]:
            copy.wait()
        if i == 0:
            late = [copies.start(stream_hbm, stream_ref), copies.start(branch_hbm, branch_ref)]
        if i == 1:
            last = [
                copies.start(source, target)
                for source, target in ((xo_hbm, xo_ref), (xr_hbm, xr_ref), (ko_hbm, ko_ref))
            ] + load_far(links, copies, half_hbm, other_hbm, kr_ref)

        def backward(cols):
            grad = dot_nt(gpacked_ref[:, part], wqkv_ref[cols, part])
            back_ref[:, cols] = grad if i == 0 else back_ref[:, cols] + grad

        tiles(width, backward, True)
    for copy in late:
        copy.wait()
    gain = vecs_ref[1:2, :]

    def norm(i, carry):
        at = pl.ds(pl.multiple_of(i * BLOCK, BLOCK), BLOCK)
        xhat, root = row_stats(stream_ref[at, :])
        grad = back_ref[at, :]
        total = branch_ref[at, :].astype(F32) + norm_back(xhat, root, grad, gain)
        back_ref[at, :] = total
        embed_ref[at, :] = total.astype(BF)
        return (
            carry[0] + jnp.sum(grad * xhat, axis=0, keepdims=True),
            carry[1] + jnp.sum(grad, axis=0, keepdims=True),
        )

    zero = jnp.zeros((1, width), F32)
    gain_sum, bias_sum = lax.fori_loop(0, rows // BLOCK, norm, (zero, zero))
    token_sum = jnp.sum(back_ref[body:rows, :], axis=0, keepdims=True)
    vec_ref[...] = jnp.zeros_like(vec_ref)
    for i, v in enumerate((gain_sum, bias_sum, token_sum, vec2_ref[0:1, :], vec2_ref[1:2, :])):
        vec_ref[2 * i : 2 * i + 1, :] = v[:, :half]
        vec_ref[2 * i + 1 : 2 * i + 2, :] = v[:, half:]
    for copy in last:
        copy.wait()
    grad = embed_ref[0:body, :]
    depth = xo_ref.shape[0]
    core, band = links.bit(0), links.bit("band")
    kfull_ref[0] = dot(xo_ref[...], grad).astype(BF)
    kfull_ref[1] = dot(xr_ref[...], grad).astype(BF)
    piece = depth // 4
    for c, ref in ((1 - core, send_ref), (core, keep_ref)):
        for far in range(2):
            for x in range(2):
                start = pl.multiple_of(c * (depth // 2) + x * piece, 16)
                block = kfull_ref[far, pl.ds(start, piece), :]
                for h in range(2):
                    slot = ((far + band - 2 * far * band) * 2 + x) * 2 + h
                    to = pl.ds(pl.multiple_of(slot * piece, 16), piece)
                    ref[to, :] = block[:, h * half : (h + 1) * half]
    high, low = split_vec(vec_ref[...])
    send_ref[2 * depth : 2 * depth + 16, :] = high
    send_ref[2 * depth + 16 : 2 * depth + 32, :] = low
    vec_ref[...] = high.astype(F32) + low.astype(F32)
    copies.out(send_ref, send_hbm)
    copies.out(keep_ref, keep_hbm)
    middle = body // 2
    for side, kernel, target in ((0, kr_ref, far_hbm), (1, ko_ref, own_hbm)):
        for h in range(2):
            part = grad[h * middle : (h + 1) * middle]
            pgrad_ref[side, h] = dot_nt(kernel[...], part).astype(BF)
        copies.out(pgrad_ref.at[side], target)
    copies.finish()


def embed_back(
    links, chips, vecs, vec2, gpacked, wqkv, stream, branch, xo, xr, ko, half, other, after
):
    rows, width = stream.shape
    depth, body = xo.shape
    cols = width // 2
    send, keep = shape((2 * depth + 32, cols), BF), shape((2 * depth, cols), BF)
    pgrad = shape((2, depth, body // 2), BF)
    return kernel_call(
        functools.partial(embed_back_kernel, links, chips, len(after)),
        "embed_back",
        (send, keep, pgrad, pgrad, shape((16, cols), F32)),
        (gpacked, wqkv, stream, branch, xo, xr, ko, ko, send, keep)
        + (
            shape((2,) + pgrad.shape, BF),
            stream,
            shape((rows, width), BF),
            shape((2, depth, width), BF),
        ),
        24,
        vmem_in=2,
        vmem_out=1,
    )(vecs, vec2, gpacked, wqkv, stream, branch, xo, xr, ko, half, other, *after)


def scatter_kernel(links, side, pairs, depth, seen_ref, grad_hbm, *rest):
    out_hbm, grad_ref, out_ref, sems = rest[-4:]
    patches = out_ref.shape[2]
    copies = Copies(sems)
    copies.start(grad_hbm.at[0 : 2 * depth, :], grad_ref).wait()
    band = links.bit("band")
    base = (band if side == 0 else 1 - band) * 2 * pairs
    wide = 2 * seen_ref.shape[1]
    half = grad_ref.shape[1] // wide

    def written(i):
        two = pl.ds(2 * i, 2)
        there = pl.ds(base + 2 * i, 2)
        return pltpu.make_async_copy(out_ref.at[two], out_hbm.at[there], sems.at[1 + i])

    def pair(i, carry):
        first, second = chosen(seen_ref, base + 2 * i, patches)
        row = pl.multiple_of(lax.div(i, half) * depth, 16)
        col = pl.multiple_of(lax.rem(i, half) * wide, 128)
        grad = grad_ref[pl.ds(row, depth), pl.ds(col, wide)]
        out_ref[2 * i] = dot_nt(grad, first)
        out_ref[2 * i + 1] = dot_nt(grad, second)
        written(i).start()
        return carry

    def landed(i, carry):
        written(i).wait()
        return carry

    lax.fori_loop(0, pairs, pair, 0)
    lax.fori_loop(0, pairs, landed, 0)


def scatter(links, side, grads, depth, seen, patches, *earlier):
    chips = seen.shape[0]
    pairs = chips // 4
    return kernel_call(
        functools.partial(scatter_kernel, links, side, pairs, depth),
        "scatter",
        (shape((chips, depth, patches), F32),),
        (shape((2 * depth, grads.shape[1]), BF), shape((2 * pairs, depth, patches), F32)),
        pairs + 1,
        vmem_in=1,
        input_output_aliases={2: 0} if earlier else {},
    )(seen, grads, *earlier)[0]


class Links:
    def __init__(self, mesh):
        self.count = mesh.shape["dp"]
        self.extra = self.count // 16

    def swap(self, array, *where):
        flip = sum((1 << w) * self.extra for w in where if w != "band")
        if "band" not in where:
            return lax.ppermute(array, "dp", [(d, d ^ flip) for d in range(self.count)])
        if flip == 0:
            return lax.ppermute(array, "band", [(0, 1), (1, 0)])
        pairs = [
            (2 * d + b, 2 * (d ^ flip) + 1 - b) for d in range(self.count) for b in range(2)
        ]
        return lax.ppermute(array, ("dp", "band"), pairs)

    def bring(self, array, *where):
        return pltpu.with_memory_space_constraint(self.swap(array, *where), pltpu.HBM)

    def bit(self, where):
        if where == "band":
            return lax.axis_index("band")
        return lax.rem(lax.div(lax.axis_index("dp"), self.extra << where), 2)

    def groups(self):
        return [[block * self.extra + i for i in range(self.extra)] for block in range(16)]

    def last(self, array):
        if self.extra == 1:
            return array
        return lax.psum_scatter(
            array, "dp", scatter_dimension=0, tiled=True, axis_index_groups=self.groups()
        )

    def total(self, array):
        if self.extra == 1:
            return array
        return lax.psum(array, "dp", axis_index_groups=self.groups())


class Level:
    def __init__(self, owner, terms, gone=frozenset(), rounded=False, alt=None, choice=None):
        self.owner, self.terms, self.gone, self.rounded = owner, list(terms), frozenset(gone), rounded
        self.alt, self.choice = alt, choice

    def moving(self, gone):
        strides = self.owner.strides(self.gone)
        return [(name, strides[name]) for name in self.owner.names if name in gone and name in strides]


class Piece:
    def __init__(self, names, sizes, unit, terms, gone=()):
        self.names, self.sizes, self.unit = list(names), list(sizes), unit
        self.gone = frozenset(gone)
        self.levels = [Level(self, terms, self.gone)]

    @staticmethod
    def join(first, second, choice):
        joined = Piece(first.names, first.sizes, first.unit, (), first.gone)
        joined.levels = [
            Level(a.owner, a.terms, a.gone, a.rounded, b, choice)
            for a, b in zip(first.levels, second.levels)
        ]
        return joined

    def strides(self, gone):
        found, stride = {}, self.unit
        for name, size in reversed(list(zip(self.names, self.sizes))):
            if name not in gone:
                found[name] = stride
                stride = stride * size
        return found

    def layout(self, names):
        gone = self.gone | frozenset(names)
        last = max([i for i, name in enumerate(self.names) if name in gone], default=-1)
        post = self.unit
        for size in self.sizes[last + 1 :]:
            post = post * size
        loops = [{}]
        for name, size in list(zip(self.names, self.sizes))[: last + 1]:
            if name not in gone:
                loops = [{**at, name: i} for at in loops for i in range(size)]
        return post * len(loops), post, loops


class Vec:
    def __init__(self, kept, came):
        self.kept, self.came = kept, [came]

    def value(self):
        parts = [
            buffer[at : at + 16].astype(F32) + buffer[at + 16 : at + 32].astype(F32)
            for buffer, at in self.came
        ]
        return pairwise([self.kept] + parts)


def pairwise(parts):
    while len(parts) > 1:
        parts = [
            parts[i] + parts[i + 1] if i + 1 < len(parts) else parts[i]
            for i in range(0, len(parts), 2)
        ]
    return parts[0]


def combine_kernel(links, tasks, n_in, n_out, n_load, after, *refs):
    ins, refs = refs[:n_in], refs[n_in + after :]
    out_hbm, refs = refs[:n_out], refs[n_out:]
    loads, refs = refs[:n_load], refs[n_load:]
    staged, sems = refs[:-1], refs[-1]
    copies = Copies(sems)
    bits = {where: links.bit(where) for where in (0, 1, 2, 3, "band")}
    waits = []
    for task in tasks:
        mine = []
        waits.append(mine)
        if task["kind"] == "raw":
            mine.append(copies.start(ins[task["from"]], loads[task["slot"]]))
            continue
        if task["kind"] == "vec":
            mine += [
                copies.start(ins[i].at[at : at + count, :], loads[slot])
                for i, at, count, slot in task["loads"]
            ]
            continue
        index = {
            name: (1 - bits[name]) if name in task["flip"] else bits[name] for name in bits
        }
        for load in task["loads"]:
            moving = sum((index[name] * stride for name, stride in load["moving"]), load["at"])
            alt_moving = sum(
                (index[name] * stride for name, stride in load["alt_moving"]), load["alt_at"]
            )
            for p, base in enumerate(load["bases"]):
                rows = pl.ds(pl.multiple_of(moving + base, 16), load["post"])
                target = loads[load["slot"]].at[p * load["post"] : (p + 1) * load["post"], :]
                sem = copies.sems.at[copies.count]
                copies.count += 1
                if load["alt"] is None:
                    copy = pltpu.make_async_copy(ins[load["in"]].at[rows, :], target, sem)
                    copy.start()
                else:
                    chosen_bit = index[load["choice"]]
                    copy = pltpu.make_async_copy(ins[load["in"]].at[rows, :], target, sem)
                    rows = pl.ds(pl.multiple_of(alt_moving + base, 16), load["post"])
                    other = pltpu.make_async_copy(ins[load["alt"]].at[rows, :], target, sem)
                    pl.when(chosen_bit == 0)(copy.start)
                    pl.when(chosen_bit == 1)(other.start)
                mine.append(copy)
    for task, mine in zip(tasks, waits):
        for copy in mine:
            copy.wait()
        if task["kind"] == "raw":
            copies.out(loads[task["slot"]], out_hbm[task["out"]].at[task["at"], :])
            continue
        if task["kind"] == "vec":
            parts = [loads[task["loads"][0][3]][...]]
            for unused, also, count, slot in task["loads"][1:]:
                parts.append(loads[slot][0:16, :].astype(F32) + loads[slot][16:32, :].astype(F32))
            high, low = split_vec(pairwise(parts))
            sent, kept = staged[task["stage"]], staged[task["stage"] + 1]
            sent[0:16, :] = high
            sent[16:32, :] = low
            kept[...] = high.astype(F32) + low.astype(F32)
            for out, at in task["outs"]:
                copies.out(sent, out_hbm[out].at[at, :])
            copies.out(kept, out_hbm[task["kept"]])
            continue
        result = staged[task["stage"]]
        count = result.shape[0]
        tile = max(t for t in (16, 32, 48, 64, 80, 96) if count % t == 0)

        def add(i, carry, task=task, result=result, tile=tile):
            at = pl.ds(pl.multiple_of(i * tile, 16), tile)
            total = None
            for rounded, slots in task["sum"]:
                parts = [loads[slot][at, :].astype(F32) for slot in slots]
                if total is not None:
                    parts = [total.astype(BF).astype(F32) if rounded else total] + parts
                total = pairwise(parts)
            result[at, :] = total.astype(result.dtype)
            return carry

        lax.fori_loop(0, count // tile, add, 0)
        for i, (out, at) in enumerate(task["outs"]):
            if isinstance(at, tuple):
                part = at[0].stop
                copies.out(result.at[i * part : (i + 1) * part, :], out_hbm[out].at[at])
            else:
                copies.out(result, out_hbm[out].at[at, :])
    copies.finish()


def combine(links, steps, after=(), name="combine"):
    ins, tasks, loads, stages, sends, outs = [], [], [], [], {}, []
    copies, finals, beside = 0, {}, {}
    returned = []

    def index_of(array):
        for i, other in enumerate(ins):
            if other is array:
                return i
        ins.append(array)
        return len(ins) - 1

    def send_to(where, count):
        if where not in sends:
            sends[where] = len(outs)
            outs.append([0, BF])
        at = outs[sends[where]][0]
        outs[sends[where]][0] += count
        return sends[where], slice(at, at + count)

    def places(names):
        return [
            tuple(name for k, name in enumerate(names) if mask >> k & 1)
            for mask in range(1, 1 << len(names))
        ]

    for piece, names, mode in steps:
        if mode == "raw":
            out, at = send_to(names, piece.shape[0])
            tasks.append(
                {"kind": "raw", "from": index_of(piece), "out": out, "at": at, "slot": len(loads)}
            )
            loads.append(piece)
            returned.append((out, at))
            copies += 2
            continue
        if mode == "vec":
            task = {"kind": "vec", "loads": [], "stage": len(stages)}
            width = piece.kept.shape[1]
            for array, at, count in [(piece.kept, 0, 16)] + [(b, at, 32) for b, at in piece.came]:
                task["loads"].append((index_of(array), at, count, len(loads)))
                loads.append(shape((count, width), array.dtype))
            stages += [shape((32, width), BF), shape((16, width), F32)]
            task["outs"] = [send_to(place, 32) for place in places(names)]
            task["kept"] = len(outs)
            outs.append([16, F32])
            copies += len(task["loads"]) + len(task["outs"]) + 1
            tasks.append(task)
            returned.append(task)
            continue
        split = names if mode == "split" else ()
        count, post, loops = piece.layout(split)
        width = piece.levels[0].terms[0][0].shape[1]
        if mode == "final":
            kind, key, across = (*names, 1)[:3] if isinstance(names, tuple) else (names, len(outs), 1)
            if key not in finals:
                finals[key] = len(outs)
                outs.append([0, kind])
            out = finals[key]
            at = outs[out][0]
            if across == 1:
                groups = [((), [(out, slice(at, at + count))])]
                outs[out][0] += count
            else:
                part = count // across
                places_at = [slice((at + i) * width, (at + i + 1) * width) for i in range(across)]
                groups = [((), [(out, (slice(0, part), where)) for where in places_at])]
                outs[out][0] += across
                beside[out] = part
            returned.append(out)
        elif mode == "all":
            groups = [((), [send_to(place, count) for place in places(names)])]
            kind = BF
        else:
            groups = [(place, [send_to(place, count)]) for place in places(names)]
            kind = BF
        if mode != "final":
            returned.append([out for unused, targets in groups for out in targets])
        gone = piece.gone | frozenset(split)
        for flip, targets in groups:
            task = {"kind": "sum", "flip": flip, "loads": [], "sum": [], "stage": len(stages)}
            stages.append(shape((count, width), kind))
            task["outs"] = targets
            copies += len(targets)
            for level in piece.levels:
                strides = level.owner.strides(level.gone)
                slots = []
                for t, (array, at) in enumerate(level.terms):
                    slots.append(len(loads))
                    alt, alt_at = None, at
                    if level.alt is not None:
                        buffer, alt_at = level.alt.terms[t]
                        alt = index_of(buffer)
                    task["loads"].append(
                        {
                            "in": index_of(array),
                            "alt": alt,
                            "alt_at": alt_at,
                            "alt_moving": level.alt.moving(gone) if level.alt is not None else (),
                            "choice": level.choice,
                            "at": at,
                            "moving": level.moving(gone),
                            "bases": [
                                sum(i * strides[name] for name, i in loop.items()) for loop in loops
                            ],
                            "post": post,
                            "slot": len(loads),
                        }
                    )
                    loads.append(shape((count, width), array.dtype))
                    copies += len(loops)
                task["sum"].append((level.rounded, slots))
            tasks.append(task)
    results = kernel_call(
        functools.partial(
            combine_kernel,
            links,
            tasks,
            len(ins),
            len(outs),
            len(loads),
            len(after),
        ),
        name,
        [
            shape((beside[i], count * width) if i in beside else (count, width), kind)
            for i, (count, kind) in enumerate(outs)
        ],
        loads + stages,
        copies,
    )(*ins, *after)
    came = {out: links.bring(results[out], *where) for where, out in sends.items()}
    values = []
    for (piece, names, mode), back in zip(steps, returned):
        if mode == "final":
            values.append(results[back])
        elif mode == "raw":
            values.append((came[back[0]], back[1].start))
        elif mode == "vec":
            piece.kept = results[back["kept"]]
            piece.came = [(came[out], at.start) for out, at in back["outs"]]
        else:
            if mode == "split":
                piece.gone = piece.gone | frozenset(names)
            piece.levels.append(
                Level(
                    piece, [(came[out], at.start) for out, at in back], piece.gone, mode == "all"
                )
            )
    return [results[out] for out in sends.values()], values


def touch_kernel(count, *refs):
    copies = Copies(refs[-1])
    loads = [copies.start(refs[i].at[0:16, 0:128], refs[-2].at[i]) for i in range(count)]
    for copy in loads:
        copy.wait()
    total = refs[-2][0].astype(F32)
    for i in range(1, count):
        total = total + refs[-2][i].astype(F32)
    refs[-3][...] = total


def touch(after, *pieces):
    buffers = []
    for piece in pieces:
        buffer = piece.levels[-1].terms[0][0]
        if not any(buffer is other for other in buffers):
            buffers.append(buffer)
    count = len(buffers)
    return kernel_call(
        functools.partial(touch_kernel, count),
        "touch",
        (shape((16, 128), F32),),
        (shape((count, 16, 128), BF),),
        count,
        vmem_out=1,
    )(*buffers, *after)[0]


def assemble_kernel(links, vec_ref, own_ref, x_ref, core_ref, both_ref, after_hbm, *outs):
    full_ref = outs[-2]
    piece = own_ref.shape[0] // 2
    half = own_ref.shape[1]
    x, c = links.bit(1), links.bit(0)
    for ref, dx, dc in ((own_ref, 0, 0), (x_ref, 1, 0), (core_ref, 0, 1), (both_ref, 1, 1)):
        at = ((1 - c if dc else c) * 2 + (1 - x if dx else x)) * piece
        rows = pl.ds(pl.multiple_of(at, 16), piece)
        for h in range(2):
            part = ref[h * piece : (h + 1) * piece, :]
            full_ref[rows, h * half : (h + 1) * half] = part.astype(F32)
    for i, out in enumerate(outs[:5]):
        row = jnp.concatenate([vec_ref[2 * i : 2 * i + 1, :], vec_ref[2 * i + 1 : 2 * i + 2, :]], axis=1)
        out[...] = row.reshape(out.shape)


def assemble(links, vec, near, after):
    rows, half = near[0].shape
    return kernel_call(
        functools.partial(assemble_kernel, links),
        "assemble",
        (shape((2 * half,), F32),) * 5 + (shape((2 * rows, 2 * half), F32),),
        (),
        1,
        vmem_in=5,
        vmem_out=6,
    )(vec, *near, after)


def shards(
    links,
    pixels,
    visible,
    kernels,
    class_token,
    norm1_gain,
    norm1_bias,
    norm2_gain,
    norm2_bias,
    attn_qkv,
    attn_out,
    mlp_up,
    mlp_down,
    cotangent,
):
    width = attn_out.shape[0]
    half = width // 2
    chips = cotangent.shape[0]
    group_chips, bands, patches, pix = pixels.shape
    slots = visible.shape[1]
    body = chips * slots
    depth = bands * pix
    block = width // 16
    flat = lambda a: a.reshape(-1, half)
    core_swap = lambda a: (links.swap(flat(a), 0), 0)

    pixel_rows = jnp.swapaxes(pixels, 2, 3).reshape(group_chips, depth, patches)
    kernels_own = kernels.reshape(depth, width)
    my_half, picked_far = pick_far(
        links, visible, pixel_rows, kernels_own.reshape(2, depth // 2, width)
    )
    far_half = links.swap(my_half, "band")
    picked_in = links.swap(picked_far, "band")
    picked_own, cot, gact = prepare(links, visible, pixel_rows, cotangent, mlp_down)
    far_half, cot = lax.optimization_barrier((far_half, cot))
    far_other = links.swap(far_half, 0)
    vecs = jnp.stack(
        [class_token, norm1_gain, norm1_bias, norm2_gain, norm2_bias] + [class_token] * 3
    )

    stream, n1, packed, probs, tprobs, att, mid, n2, act1, gpre1, *parts1 = forward(
        links,
        chips,
        vecs,
        picked_own,
        picked_in,
        kernels_own,
        far_half,
        far_other,
        attn_qkv,
        attn_out,
        cot,
        gact,
        mlp_up,
    )

    x, y, core, plane = (1,), ("band",), (0,), (1, "band")
    down_send, down_keep, up_send, up_keep = parts1
    down1 = Piece(
        (1, 0, "band", "h", 3, 2),
        (2,) * 6,
        block,
        [(down_keep, 0), (links.bring(down_send, 1), 0)],
        x,
    )
    up1 = Piece(
        (3, 1, 0, "band"), (2,) * 4, 4 * block, [(up_keep, 0), (links.bring(up_send, "band"), 0)], y
    )
    *sums_send, sums_keep, branch, gatt, out_rows, vec2 = mlp_back(
        links, vecs, n2, gact, act1, gpre1, mlp_up, mlp_down, mid, cot, att, attn_out, ()
    )
    both = lambda i, at: [(sums_keep, at), (links.bring(sums_send[i], 0), 0)]
    middle, end = 2 * width, 2 * width + mlp_up.shape[1] // 2
    down2 = Piece((0, 1, "band", "h", 3, 2), (2,) * 6, block, both(0, 0), core)
    up2 = Piece((0, 3, 1, "band"), (2,) * 4, 4 * block, both(1, middle), core)
    names, sizes = (0, 1, "band", 3, 2), (2,) * 5
    outp = Piece(names, sizes, block, both(2, end), core)
    block_output = jnp.concatenate(
        [
            out_rows[body : body + chips][:, None, :],
            out_rows[:body].reshape(chips, slots, width),
        ],
        axis=1,
    )
    tie, unused = combine(links, [(down1, core, "split"), (up1, core, "split")], (vec2,))
    tie, unused = combine(
        links,
        [
            (down1, y, "split"),
            (up1, x, "split"),
            (down2, x, "split"),
            (up2, y, "split"),
            (outp, (2,), "split"),
        ],
        (*tie, block_output),
    )

    gpacked, qkv_send, qkv_keep = attention_back(links, chips, gatt, packed, probs, tprobs, n1, tie)
    qkv_in = links.bring(qkv_send, 0)
    qkv = [
        Piece(names, sizes, count, [(qkv_keep, at), (qkv_in, at)], core)
        for at, count in qkv_parts(width)
    ]
    older = touch((gpacked,), down1, up1, down2, up2, outp)
    tie, unused = combine(
        links,
        [
            (down2, y, "split"),
            (up2, x, "split"),
            (qkv[0], x, "split"),
            (qkv[1], y, "split"),
            (down1, (2,), "split"),
            (up1, (3,), "split"),
            (outp, (3,), "split"),
        ],
        (older,),
    )
    kg_send, kg_keep, pgrad_own, pgrad_far, vec_keep = embed_back(
        links,
        chips,
        vecs,
        vec2,
        gpacked,
        attn_qkv,
        stream,
        branch,
        picked_own,
        picked_in,
        kernels_own,
        far_half,
        far_other,
        tie,
    )
    kg_in = links.bring(kg_send, 0)
    kg = Piece((0, "band", 1, "h"), (2,) * 4, depth // 4, [(kg_keep, 0), (kg_in, 0)], core)
    vec = Vec(vec_keep, (kg_in, 2 * depth))
    older = touch((vec_keep,), down2, up2, *qkv, down1, up1, outp)
    tie, unused = combine(
        links,
        [
            (kg, plane, "split"),
            (vec, plane, "vec"),
            (qkv[0], y, "split"),
            (qkv[1], x, "split"),
            (outp, plane, "split"),
            (down2, (2,), "split"),
            (up2, (3,), "split"),
            (down1, (3,), "split"),
        ],
        (older,),
    )
    far_grads = links.bring(flat(pgrad_far), "band")
    partly = scatter(links, 0, flat(pgrad_own), depth, visible, patches)
    up = Piece.join(up1, up2, 2)
    tie, (out_sum,) = combine(
        links,
        [
            (qkv[0], (2,), "split"),
            (qkv[1], (2,), "split"),
            (kg, (2, 3), "all"),
            (vec, (2, 3), "vec"),
            (outp, F32, "final"),
        ],
        (partly,),
    )
    scattered = scatter(links, 1, far_grads, depth, visible, patches, partly)
    pixel_grads = jnp.swapaxes(scattered.reshape(group_chips, bands, pix, patches), 2, 3)
    tie, unused = combine(
        links,
        [
            (qkv[0], (3,), "split"),
            (qkv[1], (3,), "split"),
            (up, (2,), "split"),
            (down2, (3,), "split"),
        ],
        (scattered,),
    )
    tie, (kgrad,) = combine(links, [(kg, BF, "final"), (vec, (), "vec")], tie, "finish")
    vec_sum = links.total(vec.value())
    kgrad = links.total(kgrad.astype(F32)).astype(BF)
    near = [kgrad, links.swap(kgrad, 1), links.swap(kgrad, 0), links.swap(kgrad, 0, 1)]
    tie, (*qkv_sums, up_sum, down_sum, unused) = combine(
        links,
        [
            (qkv[0], (F32, "qkv"), "final"),
            (qkv[1], (F32, "qkv"), "final"),
            (up, F32, "final"),
            (down1, (F32, "down", 2), "final"),
            (down2, (F32, "down", 2), "final"),
        ],
        (scattered,),
    )
    *vecs, kernel_grads = assemble(links, vec_sum, near, qkv_sums[0])

    weight = lambda part: jnp.swapaxes(links.last(part), 0, 1)
    return (
        block_output,
        pixel_grads,
        kernel_grads.reshape(bands, pix, width),
        vecs[2],
        vecs[0],
        vecs[1],
        vecs[3],
        vecs[4],
        weight(qkv_sums[0]),
        weight(out_sum),
        weight(up_sum),
        weight(down_sum),
    )


def solution(mesh):
    placed = (
        P("dp", "band", None, None),
        P("dp", None),
        P("band", None, None),
        P(),
        P(),
        P(),
        P(),
        P(),
        P(),
        P(),
        P(),
        P(),
        P(("dp", "band"), None, None),
    )
    return jax.shard_map(
        functools.partial(shards, Links(mesh)),
        mesh=mesh,
        in_specs=placed,
        out_specs=(
            P(("dp", "band"), None, None),
            P("dp", "band", None, None),
            P("band", None, None),
            P(),
            P(),
            P(),
            P(),
            P(),
            P("band", "dp"),
            P("band", "dp"),
            P("band", "dp"),
            P("band", "dp"),
        ),
        check_vma=False,
    )
```

```python
import functools

import jax
import jax.numpy as jnp
from jax import lax
from jax.experimental import pallas as pl
from jax.experimental.pallas import tpu as pltpu
from jax.sharding import PartitionSpec as P

HEADS = 12
HEAD = 64
BF = jnp.bfloat16
F32 = jnp.float32
TAIL = 16
BLOCK = 112
KEYS = 80
SCALE = HEAD ** (-0.5)
VMEM = pl.BlockSpec(memory_space=pltpu.VMEM)
HBM = pl.BlockSpec(memory_space=pl.ANY)
shape = jax.ShapeDtypeStruct
MICROSECONDS = {
    "pick_far": 5,
    "prepare": 11,
    "encoder_forward": 31,
    "mlp_back": 32,
    "attention_back": 18,
    "embed_back": 14,
    "combine": 12,
    "mlp_out": 8,
    "touch": 20,
    "assemble": 0.5,
    "finish": 0.5,
    "scatter": 4,
}


def dot(a, b):
    return jnp.dot(a, b, preferred_element_type=F32)


def dot_nt(a, b):
    return lax.dot_general(a, b, (((1,), (1,)), ((), ())), preferred_element_type=F32)


def dot_tn(a, b):
    return lax.dot_general(a, b, (((0,), (0,)), ((), ())), preferred_element_type=F32)


def kernel_call(body, name, outs, scratch, copies, vmem_in=0, vmem_out=0, mib=62, **more):
    def call(*operands):
        return pl.pallas_call(
            body,
            out_shape=tuple(outs),
            in_specs=[VMEM] * vmem_in + [HBM] * (len(operands) - vmem_in),
            out_specs=(HBM,) * (len(outs) - vmem_out) + (VMEM,) * vmem_out,
            scratch_shapes=[
                a if hasattr(a, "get_ref_aval") else pltpu.VMEM(a.shape, a.dtype) for a in scratch
            ]
            + [pltpu.SemaphoreType.DMA((copies,))],
            compiler_params=pltpu.CompilerParams(vmem_limit_bytes=mib * 1024 * 1024),
            cost_estimate=pl.CostEstimate(
                flops=int(MICROSECONDS[name] * 1.15e9), bytes_accessed=1, transcendentals=0
            ),
            name=name,
            **more,
        )(*operands)

    return call


def tiles(count, body, looped=False, base=0, tile=256):
    if not looped:
        for j in range(0, count, tile):
            body(slice(base + j, base + j + tile))
        return

    def step(j, carry):
        body(pl.ds(pl.multiple_of(base + j * tile, tile), tile))
        return carry

    lax.fori_loop(0, count // tile, step, 0)


LOOP = (True, False, True, True, False)


class Copies:
    def __init__(self, sems):
        self.sems, self.count, self.open = sems, 0, []

    def start(self, source, target):
        copy = pltpu.make_async_copy(source, target, self.sems.at[self.count])
        self.count += 1
        copy.start()
        return copy

    def out(self, source, target):
        self.open.append(self.start(source, target))

    def finish(self):
        for copy in self.open:
            copy.wait()


def chosen(seen_ref, chip, patches):
    first = seen_ref[pl.ds(chip, 1), :]
    second = seen_ref[pl.ds(chip + 1, 1), :]
    slots = first.shape[1]
    seen = jnp.concatenate([first, second], axis=1)
    ids = lax.broadcasted_iota(jnp.int32, (patches, 2 * slots), 0)
    lane = lax.broadcasted_iota(jnp.int32, (patches, 2 * slots), 1)
    hit = ids == seen
    return (
        jnp.where(hit & (lane < slots), 1.0, 0.0).astype(BF),
        jnp.where(hit & (lane >= slots), 1.0, 0.0).astype(BF),
    )


class Pixels:
    def __init__(self, pixel_hbm, pixel_ref, base, pairs, sems):
        self.hbm, self.ref, self.base, self.pairs, self.sems = pixel_hbm, pixel_ref, base, pairs, sems
        for i in range(pairs):
            self.copy(i).start()

    def copy(self, i):
        there, here = pl.ds(self.base + 2 * i, 2), pl.ds(2 * i, 2)
        return pltpu.make_async_copy(self.hbm.at[there], self.ref.at[here], self.sems.at[i])

    def pick(self, seen_ref, out_ref, looped=True):
        wide = 2 * seen_ref.shape[1]

        def pair(i, carry):
            first, second = chosen(seen_ref, self.base + 2 * i, self.ref.shape[2])
            self.copy(i).wait()
            out_ref[:, pl.ds(pl.multiple_of(i * wide, wide), wide)] = (
                dot(self.ref[2 * i], first) + dot(self.ref[2 * i + 1], second)
            ).astype(BF)
            return carry

        if looped:
            lax.fori_loop(0, self.pairs, pair, 0)
        else:
            for i in range(self.pairs):
                pair(i, 0)


def pick_far_kernel(links, pairs, seen_ref, pixel_hbm, out_hbm, pixel_ref, out_ref, pixel_sems, sems):
    base = (1 - links.bit("band")) * 2 * pairs
    Pixels(pixel_hbm, pixel_ref, base, pairs, pixel_sems).pick(seen_ref, out_ref, False)
    copies = Copies(sems)
    copies.out(out_ref, out_hbm)
    copies.finish()


def pick_far(links, seen, pixel_rows):
    chips, depth, patches = pixel_rows.shape
    pairs = chips // 4
    out = shape((depth, chips // 2 * seen.shape[1]), BF)
    return kernel_call(
        functools.partial(pick_far_kernel, links, pairs),
        "pick_far",
        (out,),
        (shape((2 * pairs, depth, patches), BF), out, pltpu.SemaphoreType.DMA((pairs,))),
        1,
        vmem_in=1,
    )(seen, pixel_rows)[0]


def prepare_kernel(
    links,
    pairs,
    seen_ref,
    pixel_hbm,
    cot_hbm,
    down_hbm,
    picked_hbm,
    rows_hbm,
    gact_hbm,
    pixel_ref,
    cot_ref,
    down_ref,
    picked_ref,
    rows_ref,
    gact_ref,
    tail_ref,
    pixel_sems,
    sems,
):
    copies = Copies(sems)
    chips = cot_ref.shape[0]
    slots = cot_ref.shape[1] - 1
    rows, width = rows_ref.shape
    base = links.bit("band") * 2 * pairs
    cot_in = copies.start(cot_hbm, cot_ref)
    pixels = Pixels(pixel_hbm, pixel_ref, base, pairs, pixel_sems)
    chunk = down_hbm.shape[0] // 4
    parts = [slice(i * chunk, (i + 1) * chunk) for i in range(4)]
    downs = [copies.start(down_hbm.at[part, :], down_ref.at[part, :]) for part in parts]
    cot_in.wait()
    tail_ref[...] = jnp.zeros_like(tail_ref)

    def lay(c, carry):
        chip = cot_ref[c].astype(F32)
        rows_ref[pl.ds(pl.multiple_of(c * slots, slots), slots), :] = chip[1:, :].astype(BF)
        tail_ref[pl.ds(c, 1), :] = chip[0:1, :]
        return carry

    lax.fori_loop(0, chips, lay, 0)
    rows_ref[rows - TAIL : rows, :] = tail_ref[...].astype(BF)
    copies.out(rows_ref, rows_hbm)
    pixels.pick(seen_ref, picked_ref)
    copies.out(picked_ref, picked_hbm)
    for part, copy in zip(parts, downs):
        copy.wait()

        def act_grad(at):
            gact_ref[:, at] = dot_nt(rows_ref[...], down_ref[at, :]).astype(BF)

        tiles(chunk, act_grad, True, part.start)
        copies.out(gact_ref.at[:, part], gact_hbm.at[:, part])
    copies.finish()


def prepare(links, seen, pixel_rows, cot, down):
    group, depth, patches = pixel_rows.shape
    pairs = group // 4
    hidden, width = down.shape
    body = cot.shape[0] * seen.shape[1]
    rows = body + TAIL
    outs = (shape((depth, body), BF), shape((rows, width), BF), shape((rows, hidden), BF))
    return kernel_call(
        functools.partial(prepare_kernel, links, pairs),
        "prepare",
        outs,
        (shape((2 * pairs, depth, patches), BF), cot, down)
        + outs
        + (shape((TAIL, width), F32), pltpu.SemaphoreType.DMA((pairs,))),
        12,
        vmem_in=1,
    )(seen, pixel_rows, cot, down)


def row_stats(values):
    average = jnp.mean(values, axis=-1, keepdims=True)
    centred = values - average
    spread = jnp.mean(centred * centred, axis=-1, keepdims=True)
    root = lax.rsqrt(spread + 1e-06)
    return centred * root, root


def norm_back(xhat, root, grad_out, gain):
    scaled = grad_out * gain
    mean_scaled = jnp.mean(scaled, axis=-1, keepdims=True)
    mean_along = jnp.mean(scaled * xhat, axis=-1, keepdims=True)
    return root * (scaled - mean_scaled - xhat * mean_along)


def head_rows(width):
    row = lax.broadcasted_iota(jnp.int32, (TAIL, width), 0)
    lane = lax.broadcasted_iota(jnp.int32, (TAIL, width), 1)
    return (lane // HEAD) == row


def two_heads(pair):
    low = lax.broadcasted_iota(jnp.int32, pair.shape, 1) < HEAD
    zero = jnp.zeros_like(pair)
    return jnp.concatenate([jnp.where(low, pair, zero), jnp.where(low, zero, pair)], axis=0)


def own_heads(stacked):
    rows = stacked.shape[0] // 2
    low = lax.broadcasted_iota(jnp.int32, (rows, stacked.shape[1]), 1) < HEAD
    return jnp.where(low, stacked[:rows], stacked[rows:])


def softmax_keys(scores, count):
    key = lax.broadcasted_iota(jnp.int32, scores.shape, 0)
    scores = jnp.where(key < count, scores * SCALE, -1e30)
    raised = jnp.exp(scores - jnp.max(scores, axis=0, keepdims=True))
    return raised * (1.0 / jnp.sum(raised, axis=0, keepdims=True))


def load_far(links, copies, half_hbm, other_hbm, target):
    count = half_hbm.shape[0]
    core = links.bit(0)
    return [
        copies.start(half_hbm, target.at[pl.ds(pl.multiple_of(core * count, 16), count), :]),
        copies.start(other_hbm, target.at[pl.ds(pl.multiple_of((1 - core) * count, 16), count), :]),
    ]


def forward_kernel(
    links,
    chips,
    vecs_ref,
    xo_hbm,
    xr_hbm,
    ko_hbm,
    half_hbm,
    other_hbm,
    wqkv_hbm,
    wout_hbm,
    cot_hbm,
    gact_hbm,
    up_hbm,
    stream_hbm,
    n1_hbm,
    packed_hbm,
    probs_hbm,
    tprobs_hbm,
    att_hbm,
    mid_hbm,
    n2_hbm,
    act_hbm,
    gpre_hbm,
    down_send_hbm,
    down_keep_hbm,
    up_send_hbm,
    up_keep_hbm,
    stream_ref,
    n1_ref,
    packed_ref,
    probs_ref,
    tprobs_ref,
    att_ref,
    mid_ref,
    n2_ref,
    xo_ref,
    xr_ref,
    ko_ref,
    kr_ref,
    tatt_ref,
    wqkv_ref,
    wout_ref,
    *half_refs,
):
    copies = Copies(half_refs[-1])
    rows, width = n1_ref.shape
    body = rows - TAIL
    slots = body // chips
    token, gain1, bias1, gain2, bias2 = (vecs_ref[i : i + 1, :] for i in range(5))
    first = [
        copies.start(source, target)
        for source, target in ((xo_hbm, xo_ref), (ko_hbm, ko_ref), (xr_hbm, xr_ref))
    ] + load_far(links, copies, half_hbm, other_hbm, kr_ref)
    for copy in first:
        copy.wait()
    wqkv_in = copies.start(wqkv_hbm, wqkv_ref)
    wout_in = copies.start(wout_hbm, wout_ref)
    half = MlpHalf(links, 0, copies, half_refs[:-1])

    def embed(at):
        stream_ref[at, :] = dot_tn(xo_ref[:, at], ko_ref[...]) + dot_tn(xr_ref[:, at], kr_ref[...])

    tiles(body, embed, True)
    tail_row = lax.broadcasted_iota(jnp.int32, (TAIL, width), 0)
    stream_ref[body:rows, :] = jnp.where(tail_row < chips, token, 0.0)

    def first_norm(i, carry):
        at = pl.ds(pl.multiple_of(i * BLOCK, BLOCK), BLOCK)
        xhat, unused = row_stats(stream_ref[at, :])
        n1_ref[at, :] = (xhat * gain1 + bias1).astype(BF)
        return carry

    lax.fori_loop(0, rows // BLOCK, first_norm, 0)
    wqkv_in.wait()
    half.load(cot_hbm, gact_hbm, up_hbm)
    copies.out(stream_ref, stream_hbm)
    copies.out(n1_ref, n1_hbm)


    def project(at):
        packed_ref[:, at] = dot(n1_ref[...], wqkv_ref[:, at]).astype(BF)

    tiles(3 * width, project, True)
    copies.out(packed_ref, packed_hbm)
    tail = packed_ref[body:rows, :]
    heads = head_rows(width)
    tquery = jnp.where(heads, jnp.broadcast_to(tail[0:1, 0:width], (TAIL, width)), 0).astype(BF)
    tatt_ref[...] = jnp.zeros_like(tatt_ref)

    def chip(c, carry):
        at = pl.ds(pl.multiple_of(c * slots, slots), slots)
        key = jnp.concatenate(
            [packed_ref[at, width : 2 * width], tail[:, width : 2 * width]], axis=0
        )
        val = jnp.concatenate([packed_ref[at, 2 * width :], tail[:, 2 * width :]], axis=0)
        tiles = [slice(128 * p, 128 * p + 128) for p in range(width // 128)]
        scores = [dot_nt(key[:, here], two_heads(packed_ref[at, here])) for here in tiles]
        scores.append(dot_nt(key, tquery))
        probs = [softmax_keys(s, slots + 1).astype(BF) for s in scores]
        mixed = [dot_tn(probs[p], val[:, tiles[p]]) for p in range(len(tiles))]
        mixed.append(dot_tn(probs[-1], val))
        for p in range(len(tiles)):
            probs_ref[c, p] = probs[p]
            att_ref[at, tiles[p]] = own_heads(mixed[p]).astype(BF)
        tprobs_ref[c] = probs[-1]
        tatt_ref[pl.ds(c, 1), :] = jnp.sum(jnp.where(heads, mixed[-1], 0.0), axis=0, keepdims=True)
        return carry

    lax.fori_loop(0, chips, chip, 0, unroll=2)
    att_ref[body:rows, :] = tatt_ref[...].astype(BF)
    copies.out(probs_ref, probs_hbm)
    copies.out(tprobs_ref, tprobs_hbm)
    copies.out(att_ref, att_hbm)
    wout_in.wait()


    def out_project(at):
        mid_ref[:, at] = stream_ref[:, at] + dot(att_ref[...], wout_ref[:, at])

    tiles(width, out_project, True)
    copies.out(mid_ref, mid_hbm)

    def second_norm(i, carry):
        at = pl.ds(pl.multiple_of(i * BLOCK, BLOCK), BLOCK)
        xhat, unused = row_stats(mid_ref[at, :])
        n2_ref[at, :] = (xhat * gain2 + bias2).astype(BF)
        return carry

    lax.fori_loop(0, rows // BLOCK, second_norm, 0)
    copies.out(n2_ref, n2_hbm)
    half.run(n2_ref, (down_send_hbm, down_keep_hbm), (up_send_hbm, up_keep_hbm))
    copies.out(half.act, act_hbm)
    copies.out(half.gpre, gpre_hbm)
    copies.finish()


class MlpHalf:
    def __init__(self, links, third, copies, refs):
        self.links, self.third, self.copies = links, third, copies
        self.looped = (True, False)
        self.cot, self.gact, self.up, self.act, self.gpre, self.grads = refs

    @staticmethod
    def scratch(rows, width, hidden):
        return (
            shape((rows, width), BF),
            shape((rows, hidden // 2), BF),
            shape((width, hidden // 2), BF),
            shape((rows, hidden // 2), BF),
            shape((rows, hidden // 2), BF),
            shape((4, max(width, hidden // 4), width), BF),
        )

    def load(self, cot_hbm, gact_hbm, up_hbm):
        chunk = up_hbm.shape[1] // 4
        start = self.copies.start
        far = lambda i: slice((2 * i + self.third) * chunk, (2 * i + self.third + 1) * chunk)
        near = lambda i: slice(i * chunk, (i + 1) * chunk)
        self.first = [
            (
                start(up_hbm.at[:, far(i)], self.up.at[:, near(i)]),
                start(gact_hbm.at[:, far(i)], self.gact.at[:, near(i)]),
            )
            for i in range(2)
        ]
        self.cot_in = start(cot_hbm, self.cot)

    def run(self, n2_ref, down_out, up_out, then=None):
        copies, links = self.copies, self.links
        rows, width = n2_ref.shape
        chunk = self.up.shape[1] // 2
        half = width // 2
        block = width // 16
        for i in range(2):
            for copy in self.first[i]:
                copy.wait()
            if i == 1 and then is not None:
                then()

            def activate(cols):
                pre = dot(n2_ref[...], self.up[:, cols])
                phi = 0.5 + 0.5 * lax.erf(pre * (0.5**0.5))
                bell = jnp.exp(-0.5 * pre * pre) * 0.3989422804014327
                self.act[:, cols] = (pre * phi).astype(BF)
                gact = self.gact[:, cols].astype(F32)
                self.gpre[:, cols] = (gact * (phi + pre * bell)).astype(BF)

            tiles(chunk, activate, self.looped[0], i * chunk)
        where = (1, "band") if self.third == 0 else (0, 0)
        bits = [links.bit(w) for w in where]
        self.cot_in.wait()
        for i in range(2):

            def down_rows(at):
                self.grads[i, at, :] = dot_tn(
                    self.cot[:, at], self.act[:, i * chunk : (i + 1) * chunk]
                ).astype(BF)

            tiles(width, down_rows, self.looped[1])
            for side, bit in ((0, 1 - bits[0]), (1, bits[0])):
                for other in range(2):
                    x, c = (bit, other) if where[0] == 1 else (other, bit)
                    for z in range(4):
                        at = pl.multiple_of(((z * 2 + x) * 2 + c) * block, 16)
                        for h in range(2):
                            to = (((other * 2 + i) * 2 + h) * 4 + z) * block
                            copies.out(
                                self.grads.at[i, pl.ds(at, block), h * half : (h + 1) * half],
                                down_out[side].at[to : to + block, :],
                            )
        part = chunk // 4
        for i in range(2):

            def up_rows(at):
                self.grads[2 + i, at, :] = dot_tn(
                    self.gpre.at[:, i * chunk : (i + 1) * chunk][:, at], n2_ref[...]
                ).astype(BF)

            tiles(chunk, up_rows, self.looped[1])
            for side, bit in ((0, 1 - bits[1]), (1, bits[1])):
                for x in range(2):
                    for other in range(2):
                        if where[1] == "band":
                            at = (2 * x + other) * part
                            cols = pl.ds(pl.multiple_of(bit * half, 128), half)
                        else:
                            at = pl.multiple_of((2 * x + bit) * part, 16)
                            cols = slice(other * half, (other + 1) * half)
                        to = ((i * 2 + x) * 2 + other) * part
                        copies.out(
                            self.grads.at[2 + i, pl.ds(at, part), cols],
                            up_out[side].at[to : to + part, :],
                        )


def forward(links, chips, vecs, xo, xr, ko, half, other, wqkv, wout, cot, gact, up):
    width, hidden = up.shape
    body = xo.shape[1]
    rows = body + TAIL
    saved = (
        shape((rows, width), F32),
        shape((rows, width), BF),
        shape((rows, 3 * width), BF),
        shape((chips, width // 128, KEYS, 128), BF),
        shape((chips, KEYS, TAIL), BF),
        shape((rows, width), BF),
        shape((rows, width), F32),
        shape((rows, width), BF),
    )
    return kernel_call(
        functools.partial(forward_kernel, links, chips),
        "encoder_forward",
        saved
        + (shape((rows, hidden // 2), BF),) * 2
        + (shape((2 * width, width // 2), BF),) * 2
        + (shape((hidden // 2, width // 2), BF),) * 2,
        saved
        + (xo, xr, ko, ko, shape((TAIL, width), F32), wqkv, wout)
        + MlpHalf.scratch(rows, width, hidden),
        112,
        vmem_in=1,
    )(vecs, xo, xr, ko, half, other, wqkv, wout, cot, gact, up)


def spread_blocks(links, copies, full_ref, outs):
    core = links.bit(0)
    cols = full_ref.shape[1] // 2
    block = full_ref.shape[0] // 16
    for z in range(4):
        for x in range(2):
            for side, c in ((0, 1 - core), (1, core)):
                start = ((z * 2 + x) * 2 + c) * block
                for count, pair in outs:
                    rows = pl.ds(pl.multiple_of(start, 16), count)
                    start = start + count
                    for b in range(2):
                        to = ((x * 2 + b) * 4 + z) * count
                        copies.out(
                            full_ref.at[rows, b * cols : (b + 1) * cols],
                            pair[side].at[to : to + count, :],
                        )


def mlp_back_kernel(
    links,
    after,
    vecs_ref,
    n2_hbm,
    gact_hbm,
    gpre1_hbm,
    up_hbm,
    mid_hbm,
    cot_hbm,
    att_hbm,
    wout_hbm,
    *rest,
):
    rest = rest[after:]
    sends, (keep_hbm, branch_hbm, gatt_hbm, act2_hbm, vec_ref) = rest[:3], rest[3:8]
    (
        n2_ref,
        gatt_ref,
        gpre_ref,
        up_ref,
        mid_ref,
        att_ref,
        wout_ref,
        back_ref,
        branch_ref,
        full_ref,
    ) = rest[8:18]
    half_refs, sems = rest[18:-1], rest[-1]
    copies = Copies(sems)
    rows, width = mid_ref.shape
    quarter = up_hbm.shape[1] // 4
    at = lambda i: slice(i * quarter, (i + 1) * quarter)
    n2_in = copies.start(n2_hbm, n2_ref)
    half = MlpHalf(links, 1, copies, half_refs)
    half.load(cot_hbm, gact_hbm, up_hbm)
    cot_ref = half.cot
    n2_in.wait()
    first_in = []

    def more():
        first_in.append(copies.start(gpre1_hbm, gpre_ref))
        for i in range(2):
            first_in.append(copies.start(up_hbm.at[:, at(2 * i)], up_ref.at[:, at(i)]))
        for source, target in ((mid_hbm, mid_ref), (att_hbm, att_ref), (wout_hbm, wout_ref)):
            first_in.append(copies.start(source, target))

    middle = 2 * width
    end = middle + up_hbm.shape[1] // 2
    half.run(
        n2_ref,
        (sends[0], keep_hbm.at[0:middle, :]),
        (sends[1], keep_hbm.at[middle:end, :]),
        more,
    )
    copies.out(half.act, act2_hbm)
    for copy in first_in:
        copy.wait()

    def backward(cols):
        back_ref[:, cols] = dot_nt(gpre_ref[...], up_ref[cols, :]) + dot_nt(
            half.gpre[...], half.up[cols, :]
        )

    tiles(width, backward, LOOP[2])
    gain = vecs_ref[3:4, :]

    def norm(i, carry):
        at = pl.ds(pl.multiple_of(i * BLOCK, BLOCK), BLOCK)
        xhat, root = row_stats(mid_ref[at, :])
        grad = back_ref[at, :]
        total = cot_ref[at, :].astype(F32) + norm_back(xhat, root, grad, gain)
        branch_ref[at, :] = total.astype(BF)
        return (
            carry[0] + jnp.sum(grad * xhat, axis=0, keepdims=True),
            carry[1] + jnp.sum(grad, axis=0, keepdims=True),
        )

    zero = jnp.zeros((1, width), F32)
    gain_sum, bias_sum = lax.fori_loop(0, rows // BLOCK, norm, (zero, zero))
    vec_ref[0:1, :] = gain_sum
    vec_ref[1:2, :] = bias_sum
    copies.out(branch_ref, branch_hbm)

    def out_grad(at):
        full_ref[at, :] = dot_tn(branch_ref[:, at], att_ref[...]).astype(BF)

    tiles(width, out_grad, LOOP[4])
    spread_blocks(
        links, copies, full_ref, [(width // 16, (sends[2], keep_hbm.at[end : end + width, :]))]
    )

    def attended_grad(at):
        gatt_ref[:, at] = dot_nt(branch_ref[...], wout_ref[at, :]).astype(BF)

    tiles(width, attended_grad, LOOP[4])
    copies.out(gatt_ref, gatt_hbm)
    copies.finish()


def mlp_back(links, vecs, n2, gact, gpre1, up, mid, cot, att, wout, after):
    rows, width = mid.shape
    hidden = up.shape[1]
    sums = shape((3 * width + hidden // 2, width // 2), BF)
    return kernel_call(
        functools.partial(mlp_back_kernel, links, len(after)),
        "mlp_back",
        tuple(shape((count, width // 2), BF) for count in (2 * width, hidden // 2, width))
        + (sums, cot, cot, gpre1, shape((2, width), F32)),
        (n2, cot, gpre1)
        + (shape((width, hidden // 2), BF), mid, att, wout, mid, cot, wout)
        + MlpHalf.scratch(rows, width, hidden),
        140,
        vmem_in=1,
        vmem_out=1,
    )(vecs, n2, gact, gpre1, up, mid, cot, att, wout, *after)


def mlp_out_kernel(chips, after, act1_hbm, act2_hbm, down_hbm, mid_hbm, *rest):
    out_hbm = rest[after]
    act1_ref, act2_ref, down_ref, mid_ref, rows_ref, out_ref, sems = rest[after + 1 :]
    copies = Copies(sems)
    rows, width = mid_ref.shape
    slots = (rows - TAIL) // chips
    quarter = down_hbm.shape[0] // 4
    at = lambda i: slice(i * quarter, (i + 1) * quarter)
    arrive = []
    for third, source, target in ((0, act1_hbm, act1_ref), (1, act2_hbm, act2_ref)):
        arrive.append(copies.start(source, target))
        for i in range(2):
            arrive.append(
                copies.start(down_hbm.at[at(2 * i + third), :], down_ref.at[at(2 * third + i), :])
            )
    arrive.append(copies.start(mid_hbm, mid_ref))
    for copy in arrive:
        copy.wait()

    def outward(cols):
        rows_ref[:, cols] = (
            mid_ref[:, cols]
            + dot(act1_ref[...], down_ref[: 2 * quarter, cols])
            + dot(act2_ref[...], down_ref[2 * quarter :, cols])
        )

    tiles(width, outward, True)

    def chip(c, carry):
        first = rows_ref[pl.ds(rows - TAIL + c, 1), :]
        others = rows_ref[pl.ds(pl.multiple_of(c * slots, slots), slots), :]
        out_ref[c] = jnp.concatenate([first, others], axis=0).astype(BF)
        return carry

    lax.fori_loop(0, chips, chip, 0)
    copies.out(out_ref, out_hbm)
    copies.finish()


def mlp_out(chips, act1, act2, down, mid, after):
    rows, width = mid.shape
    out = shape((chips, (rows - TAIL) // chips + 1, width), BF)
    return kernel_call(
        functools.partial(mlp_out_kernel, chips, len(after)),
        "mlp_out",
        (out,),
        (act1, act2, down, mid, mid, out),
        8,
    )(act1, act2, down, mid, *after)[0]


def split_vec(vec):
    high = vec.astype(BF)
    return high, (vec - high.astype(F32)).astype(BF)


def attention_back_kernel(
    links, chips, after, gatt_hbm, packed_hbm, probs_hbm, tprobs_hbm, n1_hbm, *rest
):
    gpacked_hbm, send_hbm, keep_hbm = rest[after : after + 3]
    (
        gpacked_ref,
        gatt_ref,
        packed_ref,
        probs_ref,
        tprobs_ref,
        n1_ref,
        tgrad_ref,
        tout_ref,
        full_ref,
        chip_sems,
        sems,
    ) = rest[after + 3 :]
    rows, width = n1_ref.shape
    body = rows - TAIL
    slots = body // chips
    copies = Copies(sems)

    def arriving(c):
        at = pl.ds(pl.multiple_of(c * slots, slots), slots)
        return [
            pltpu.make_async_copy(source.at[where], target.at[where], chip_sems.at[k, c])
            for k, (source, target, where) in enumerate(
                (
                    (packed_hbm, packed_ref, (at, slice(None))),
                    (gatt_hbm, gatt_ref, (at, slice(None))),
                    (probs_hbm, probs_ref, c),
                )
            )
        ]

    tails = slice(body, rows)
    arrive = [
        copies.start(packed_hbm.at[tails, :], packed_ref.at[tails, :]),
        copies.start(gatt_hbm.at[tails, :], gatt_ref.at[tails, :]),
        copies.start(tprobs_hbm, tprobs_ref),
    ]
    for c in range(chips):
        for copy in arriving(c):
            copy.start()
    tout_ref[...] = jnp.zeros_like(tout_ref)
    heads = head_rows(width)
    for copy in arrive:
        copy.wait()
    n1_in = copies.start(n1_hbm, n1_ref)
    tgrad_ref[...] = gatt_ref[body:rows, :].astype(F32)
    tail = packed_ref[body:rows, :]
    tquery = jnp.where(heads, jnp.broadcast_to(tail[0:1, 0:width], (TAIL, width)), 0).astype(BF)

    def chip(c):
        at = pl.ds(pl.multiple_of(c * slots, slots), slots)
        key_all = jnp.concatenate(
            [packed_ref[at, width : 2 * width], tail[:, width : 2 * width]], axis=0
        )
        val_all = jnp.concatenate([packed_ref[at, 2 * width :], tail[:, 2 * width :]], axis=0)
        tgrad = jnp.where(
            heads, jnp.broadcast_to(tgrad_ref[pl.ds(c, 1), :], (TAIL, width)), 0.0
        ).astype(BF)
        tiles = [slice(128 * p, 128 * p + 128) for p in range(width // 128)]
        probs = [probs_ref[c, p] for p in range(len(tiles))] + [tprobs_ref[c]]
        gouts = [two_heads(gatt_ref[at, here]) for here in tiles]
        queries = [two_heads(packed_ref[at, here]) for here in tiles]
        gprobs = [dot_nt(val_all[:, tiles[p]], gouts[p]) for p in range(len(tiles))]
        gprobs.append(dot_nt(val_all, tgrad))
        gscores = []
        for prob, gprob in zip(probs, gprobs):
            wide = prob.astype(F32)
            inner = jnp.sum(gprob * wide, axis=0, keepdims=True)
            gscores.append((wide * (gprob - inner) * SCALE).astype(BF))
        gval_tail = dot(probs[-1], tgrad)
        gkey_tail = dot(gscores[-1], tquery)
        mixed = jnp.where(heads, dot_tn(gscores[-1], key_all), 0.0)
        gvals = [dot(probs[p], gouts[p]) + gval_tail[:, tiles[p]] for p in range(len(tiles))]
        gkeys = [dot(gscores[p], queries[p]) + gkey_tail[:, tiles[p]] for p in range(len(tiles))]
        gqueries = [own_heads(dot_tn(gscores[p], key_all[:, tiles[p]])) for p in range(len(tiles))]
        for p in range(len(tiles)):
            gpacked_ref[at, 128 * p : 128 * p + 128] = gqueries[p].astype(BF)
            base = width + 128 * p
            gpacked_ref[at, base : base + 128] = gkeys[p][:slots].astype(BF)
            gpacked_ref[at, width + base : width + base + 128] = gvals[p][:slots].astype(BF)
        tout_ref[pl.ds(c, 1), :] = jnp.concatenate(
            [jnp.sum(mixed, axis=0, keepdims=True)]
            + [g[slots : slots + 1] for g in gkeys + gvals],
            axis=1,
        )

    def two_chips(i, carry):
        for c in (2 * i, 2 * i + 1):
            for copy in arriving(c):
                copy.wait()
        chip(2 * i)
        chip(2 * i + 1)
        return carry

    lax.fori_loop(0, chips // 2, two_chips, 0)
    gpacked_ref[body:rows, :] = tout_ref[...].astype(BF)
    copies.out(gpacked_ref, gpacked_hbm)
    n1_in.wait()

    def qkv_rows(at):
        full_ref[at, :] = dot_tn(gpacked_ref[:, at], n1_ref[...]).astype(BF)

    tiles(3 * width, qkv_rows)
    outs = []
    for at, count in qkv_parts(width):
        here = slice(at, at + 16 * count)
        outs.append((count, (send_hbm.at[here, :], keep_hbm.at[here, :])))
    spread_blocks(links, copies, full_ref, outs)
    copies.finish()


def qkv_parts(width):
    block = 3 * width // 16
    count = -(-block // 32) * 16
    return [(0, count), (16 * count, block - count)]


def attention_back(links, chips, gatt, packed, probs, tprobs, n1, after):
    rows, width = n1.shape
    sums = shape((3 * width, width // 2), BF)
    return kernel_call(
        functools.partial(attention_back_kernel, links, chips, len(after)),
        "attention_back",
        (packed, sums, sums),
        (packed, gatt, packed, probs, tprobs, n1)
        + (
            shape((TAIL, width), F32),
            shape((TAIL, 3 * width), F32),
            shape((3 * width, width), BF),
            pltpu.SemaphoreType.DMA((3, chips)),
        ),
        80,
    )(gatt, packed, probs, tprobs, n1, *after)


def embed_back_kernel(
    links,
    chips,
    after,
    vecs_ref,
    vec2_ref,
    gpacked_hbm,
    wqkv_hbm,
    stream_hbm,
    branch_hbm,
    xo_hbm,
    xr_hbm,
    ko_hbm,
    half_hbm,
    other_hbm,
    *rest,
):
    send_hbm, keep_hbm, own_hbm, far_hbm, vec_ref = rest[after : after + 5]
    (
        gpacked_ref,
        wqkv_ref,
        stream_ref,
        branch_ref,
        xo_ref,
        xr_ref,
        ko_ref,
        kr_ref,
        send_ref,
        keep_ref,
        pgrad_ref,
        back_ref,
        embed_ref,
        kfull_ref,
        sems,
    ) = rest[after + 5 :]
    rows, width = stream_ref.shape
    body = rows - TAIL
    half = width // 2
    copies = Copies(sems)
    thirds = [slice(i * width, (i + 1) * width) for i in range(3)]
    arrive = [
        (
            copies.start(gpacked_hbm.at[:, part], gpacked_ref.at[:, part]),
            copies.start(wqkv_hbm.at[:, part], wqkv_ref.at[:, part]),
        )
        for part in thirds
    ]
    for i, part in enumerate(thirds):
        for copy in arrive[i]:
            copy.wait()
        if i == 0:
            late = [copies.start(stream_hbm, stream_ref), copies.start(branch_hbm, branch_ref)]
        if i == 1:
            last = [
                copies.start(source, target)
                for source, target in ((xo_hbm, xo_ref), (xr_hbm, xr_ref), (ko_hbm, ko_ref))
            ] + load_far(links, copies, half_hbm, other_hbm, kr_ref)

        def backward(cols):
            grad = dot_nt(gpacked_ref[:, part], wqkv_ref[cols, part])
            back_ref[:, cols] = grad if i == 0 else back_ref[:, cols] + grad

        tiles(width, backward, True)
    for copy in late:
        copy.wait()
    gain = vecs_ref[1:2, :]

    def norm(i, carry):
        at = pl.ds(pl.multiple_of(i * BLOCK, BLOCK), BLOCK)
        xhat, root = row_stats(stream_ref[at, :])
        grad = back_ref[at, :]
        total = branch_ref[at, :].astype(F32) + norm_back(xhat, root, grad, gain)
        back_ref[at, :] = total
        embed_ref[at, :] = total.astype(BF)
        return (
            carry[0] + jnp.sum(grad * xhat, axis=0, keepdims=True),
            carry[1] + jnp.sum(grad, axis=0, keepdims=True),
        )

    zero = jnp.zeros((1, width), F32)
    gain_sum, bias_sum = lax.fori_loop(0, rows // BLOCK, norm, (zero, zero))
    token_sum = jnp.sum(back_ref[body:rows, :], axis=0, keepdims=True)
    vec_ref[...] = jnp.zeros_like(vec_ref)
    for i, v in enumerate((gain_sum, bias_sum, token_sum, vec2_ref[0:1, :], vec2_ref[1:2, :])):
        vec_ref[2 * i : 2 * i + 1, :] = v[:, :half]
        vec_ref[2 * i + 1 : 2 * i + 2, :] = v[:, half:]
    for copy in last:
        copy.wait()
    grad = embed_ref[0:body, :]
    depth = xo_ref.shape[0]
    core, band = links.bit(0), links.bit("band")
    kfull_ref[0] = dot(xo_ref[...], grad).astype(BF)
    kfull_ref[1] = dot(xr_ref[...], grad).astype(BF)
    piece = depth // 4
    for c, ref in ((1 - core, send_ref), (core, keep_ref)):
        for far in range(2):
            for x in range(2):
                start = pl.multiple_of(c * (depth // 2) + x * piece, 16)
                block = kfull_ref[far, pl.ds(start, piece), :]
                for h in range(2):
                    slot = ((far + band - 2 * far * band) * 2 + x) * 2 + h
                    to = pl.ds(pl.multiple_of(slot * piece, 16), piece)
                    ref[to, :] = block[:, h * half : (h + 1) * half]
    high, low = split_vec(vec_ref[...])
    send_ref[2 * depth : 2 * depth + 16, :] = high
    send_ref[2 * depth + 16 : 2 * depth + 32, :] = low
    vec_ref[...] = high.astype(F32) + low.astype(F32)
    copies.out(send_ref, send_hbm)
    copies.out(keep_ref, keep_hbm)
    middle = body // 2
    for side, kernel, target in ((0, kr_ref, far_hbm), (1, ko_ref, own_hbm)):
        for h in range(2):
            part = grad[h * middle : (h + 1) * middle]
            pgrad_ref[side, h] = dot_nt(kernel[...], part).astype(BF)
        copies.out(pgrad_ref.at[side], target)
    copies.finish()


def embed_back(
    links, chips, vecs, vec2, gpacked, wqkv, stream, branch, xo, xr, ko, half, other, after
):
    rows, width = stream.shape
    depth, body = xo.shape
    cols = width // 2
    send, keep = shape((2 * depth + 32, cols), BF), shape((2 * depth, cols), BF)
    pgrad = shape((2, depth, body // 2), BF)
    return kernel_call(
        functools.partial(embed_back_kernel, links, chips, len(after)),
        "embed_back",
        (send, keep, pgrad, pgrad, shape((16, cols), F32)),
        (gpacked, wqkv, stream, branch, xo, xr, ko, ko, send, keep)
        + (
            shape((2,) + pgrad.shape, BF),
            stream,
            shape((rows, width), BF),
            shape((2, depth, width), BF),
        ),
        24,
        vmem_in=2,
        vmem_out=1,
    )(vecs, vec2, gpacked, wqkv, stream, branch, xo, xr, ko, half, other, *after)


def scatter_kernel(links, side, pairs, depth, seen_ref, grad_hbm, *rest):
    out_hbm, grad_ref, out_ref, sems = rest[-4:]
    patches = out_ref.shape[2]
    copies = Copies(sems)
    copies.start(grad_hbm.at[0 : 2 * depth, :], grad_ref).wait()
    band = links.bit("band")
    base = (band if side == 0 else 1 - band) * 2 * pairs
    wide = 2 * seen_ref.shape[1]
    half = grad_ref.shape[1] // wide

    def written(i):
        two = pl.ds(2 * i, 2)
        there = pl.ds(base + 2 * i, 2)
        return pltpu.make_async_copy(out_ref.at[two], out_hbm.at[there], sems.at[1 + i])

    def pair(i, carry):
        first, second = chosen(seen_ref, base + 2 * i, patches)
        row = pl.multiple_of(lax.div(i, half) * depth, 16)
        col = pl.multiple_of(lax.rem(i, half) * wide, 128)
        grad = grad_ref[pl.ds(row, depth), pl.ds(col, wide)]
        out_ref[2 * i] = dot_nt(grad, first)
        out_ref[2 * i + 1] = dot_nt(grad, second)
        written(i).start()
        return carry

    def landed(i, carry):
        written(i).wait()
        return carry

    lax.fori_loop(0, pairs, pair, 0)
    lax.fori_loop(0, pairs, landed, 0)


def scatter(links, side, grads, depth, seen, patches, *earlier):
    chips = seen.shape[0]
    pairs = chips // 4
    return kernel_call(
        functools.partial(scatter_kernel, links, side, pairs, depth),
        "scatter",
        (shape((chips, depth, patches), F32),),
        (shape((2 * depth, grads.shape[1]), BF), shape((2 * pairs, depth, patches), F32)),
        pairs + 1,
        vmem_in=1,
        input_output_aliases={2: 0} if earlier else {},
    )(seen, grads, *earlier)[0]


class Links:
    def __init__(self, mesh):
        self.count = mesh.shape["dp"]
        self.extra = self.count // 16

    def swap(self, array, *where):
        flip = sum((1 << w) * self.extra for w in where if w != "band")
        if "band" not in where:
            return lax.ppermute(array, "dp", [(d, d ^ flip) for d in range(self.count)])
        if flip == 0:
            return lax.ppermute(array, "band", [(0, 1), (1, 0)])
        pairs = [
            (2 * d + b, 2 * (d ^ flip) + 1 - b) for d in range(self.count) for b in range(2)
        ]
        return lax.ppermute(array, ("dp", "band"), pairs)

    def bring(self, array, *where):
        return pltpu.with_memory_space_constraint(self.swap(array, *where), pltpu.HBM)

    def bit(self, where):
        if where == "band":
            return lax.axis_index("band")
        return lax.rem(lax.div(lax.axis_index("dp"), self.extra << where), 2)

    def groups(self):
        return [[block * self.extra + i for i in range(self.extra)] for block in range(16)]

    def last(self, array):
        if self.extra == 1:
            return array
        return lax.psum_scatter(
            array, "dp", scatter_dimension=0, tiled=True, axis_index_groups=self.groups()
        )

    def total(self, array):
        if self.extra == 1:
            return array
        return lax.psum(array, "dp", axis_index_groups=self.groups())


class Level:
    def __init__(self, owner, terms, gone=frozenset(), rounded=False, alt=None, choice=None):
        self.owner, self.terms, self.gone, self.rounded = owner, list(terms), frozenset(gone), rounded
        self.alt, self.choice = alt, choice

    def moving(self, gone):
        strides = self.owner.strides(self.gone)
        return [(name, strides[name]) for name in self.owner.names if name in gone and name in strides]


class Piece:
    def __init__(self, names, sizes, unit, terms, gone=()):
        self.names, self.sizes, self.unit = list(names), list(sizes), unit
        self.gone = frozenset(gone)
        self.levels = [Level(self, terms, self.gone)]

    @staticmethod
    def join(first, second, choice):
        joined = Piece(first.names, first.sizes, first.unit, (), first.gone)
        joined.levels = [
            Level(a.owner, a.terms, a.gone, a.rounded, b, choice)
            for a, b in zip(first.levels, second.levels)
        ]
        return joined

    def strides(self, gone):
        found, stride = {}, self.unit
        for name, size in reversed(list(zip(self.names, self.sizes))):
            if name not in gone:
                found[name] = stride
                stride = stride * size
        return found

    def layout(self, names):
        gone = self.gone | frozenset(names)
        last = max([i for i, name in enumerate(self.names) if name in gone], default=-1)
        post = self.unit
        for size in self.sizes[last + 1 :]:
            post = post * size
        loops = [{}]
        for name, size in list(zip(self.names, self.sizes))[: last + 1]:
            if name not in gone:
                loops = [{**at, name: i} for at in loops for i in range(size)]
        return post * len(loops), post, loops


class Vec:
    def __init__(self, kept, came):
        self.kept, self.came = kept, [came]

    def value(self):
        parts = [
            buffer[at : at + 16].astype(F32) + buffer[at + 16 : at + 32].astype(F32)
            for buffer, at in self.came
        ]
        return pairwise([self.kept] + parts)


def pairwise(parts):
    while len(parts) > 1:
        parts = [
            parts[i] + parts[i + 1] if i + 1 < len(parts) else parts[i]
            for i in range(0, len(parts), 2)
        ]
    return parts[0]


def combine_kernel(links, tasks, n_in, n_out, n_load, after, *refs):
    ins, refs = refs[:n_in], refs[n_in + after :]
    out_hbm, refs = refs[:n_out], refs[n_out:]
    loads, refs = refs[:n_load], refs[n_load:]
    staged, sems = refs[:-1], refs[-1]
    copies = Copies(sems)
    bits = {where: links.bit(where) for where in (0, 1, 2, 3, "band")}
    waits = []
    for task in tasks:
        mine = []
        waits.append(mine)
        if task["kind"] == "raw":
            mine.append(copies.start(ins[task["from"]], loads[task["slot"]]))
            continue
        if task["kind"] == "vec":
            mine += [
                copies.start(ins[i].at[at : at + count, :], loads[slot])
                for i, at, count, slot in task["loads"]
            ]
            continue
        index = {
            name: (1 - bits[name]) if name in task["flip"] else bits[name] for name in bits
        }
        for load in task["loads"]:
            moving = sum((index[name] * stride for name, stride in load["moving"]), load["at"])
            alt_moving = sum(
                (index[name] * stride for name, stride in load["alt_moving"]), load["alt_at"]
            )
            for p, base in enumerate(load["bases"]):
                rows = pl.ds(pl.multiple_of(moving + base, 16), load["post"])
                target = loads[load["slot"]].at[p * load["post"] : (p + 1) * load["post"], :]
                sem = copies.sems.at[copies.count]
                copies.count += 1
                if load["alt"] is None:
                    copy = pltpu.make_async_copy(ins[load["in"]].at[rows, :], target, sem)
                    copy.start()
                else:
                    chosen_bit = index[load["choice"]]
                    copy = pltpu.make_async_copy(ins[load["in"]].at[rows, :], target, sem)
                    rows = pl.ds(pl.multiple_of(alt_moving + base, 16), load["post"])
                    other = pltpu.make_async_copy(ins[load["alt"]].at[rows, :], target, sem)
                    pl.when(chosen_bit == 0)(copy.start)
                    pl.when(chosen_bit == 1)(other.start)
                mine.append(copy)
    for task, mine in zip(tasks, waits):
        for copy in mine:
            copy.wait()
        if task["kind"] == "raw":
            copies.out(loads[task["slot"]], out_hbm[task["out"]].at[task["at"], :])
            continue
        if task["kind"] == "vec":
            parts = [loads[task["loads"][0][3]][...]]
            for unused, also, count, slot in task["loads"][1:]:
                parts.append(loads[slot][0:16, :].astype(F32) + loads[slot][16:32, :].astype(F32))
            high, low = split_vec(pairwise(parts))
            sent, kept = staged[task["stage"]], staged[task["stage"] + 1]
            sent[0:16, :] = high
            sent[16:32, :] = low
            kept[...] = high.astype(F32) + low.astype(F32)
            for out, at in task["outs"]:
                copies.out(sent, out_hbm[out].at[at, :])
            copies.out(kept, out_hbm[task["kept"]])
            continue
        result = staged[task["stage"]]
        count = result.shape[0]
        tile = max(t for t in (16, 32, 48, 64, 80, 96) if count % t == 0)

        def add(i, carry, task=task, result=result, tile=tile):
            at = pl.ds(pl.multiple_of(i * tile, 16), tile)
            total = None
            for rounded, slots in task["sum"]:
                parts = [loads[slot][at, :].astype(F32) for slot in slots]
                if total is not None:
                    parts = [total.astype(BF).astype(F32) if rounded else total] + parts
                total = pairwise(parts)
            result[at, :] = total.astype(result.dtype)
            return carry

        lax.fori_loop(0, count // tile, add, 0)
        for i, (out, at) in enumerate(task["outs"]):
            if isinstance(at, tuple):
                part = at[0].stop
                copies.out(result.at[i * part : (i + 1) * part, :], out_hbm[out].at[at])
            else:
                copies.out(result, out_hbm[out].at[at, :])
    copies.finish()


def combine(links, steps, after=(), name="combine"):
    ins, tasks, loads, stages, sends, outs = [], [], [], [], {}, []
    copies, finals, beside = 0, {}, {}
    returned = []

    def index_of(array):
        for i, other in enumerate(ins):
            if other is array:
                return i
        ins.append(array)
        return len(ins) - 1

    def send_to(where, count):
        if where not in sends:
            sends[where] = len(outs)
            outs.append([0, BF])
        at = outs[sends[where]][0]
        outs[sends[where]][0] += count
        return sends[where], slice(at, at + count)

    def places(names):
        return [
            tuple(name for k, name in enumerate(names) if mask >> k & 1)
            for mask in range(1, 1 << len(names))
        ]

    for piece, names, mode in steps:
        if mode == "raw":
            out, at = send_to(names, piece.shape[0])
            tasks.append(
                {"kind": "raw", "from": index_of(piece), "out": out, "at": at, "slot": len(loads)}
            )
            loads.append(piece)
            returned.append((out, at))
            copies += 2
            continue
        if mode == "vec":
            task = {"kind": "vec", "loads": [], "stage": len(stages)}
            width = piece.kept.shape[1]
            for array, at, count in [(piece.kept, 0, 16)] + [(b, at, 32) for b, at in piece.came]:
                task["loads"].append((index_of(array), at, count, len(loads)))
                loads.append(shape((count, width), array.dtype))
            stages += [shape((32, width), BF), shape((16, width), F32)]
            task["outs"] = [send_to(place, 32) for place in places(names)]
            task["kept"] = len(outs)
            outs.append([16, F32])
            copies += len(task["loads"]) + len(task["outs"]) + 1
            tasks.append(task)
            returned.append(task)
            continue
        split = names if mode == "split" else ()
        count, post, loops = piece.layout(split)
        width = piece.levels[0].terms[0][0].shape[1]
        if mode == "final":
            kind, key, across = (*names, 1)[:3] if isinstance(names, tuple) else (names, len(outs), 1)
            if key not in finals:
                finals[key] = len(outs)
                outs.append([0, kind])
            out = finals[key]
            at = outs[out][0]
            if across == 1:
                groups = [((), [(out, slice(at, at + count))])]
                outs[out][0] += count
            else:
                part = count // across
                places_at = [slice((at + i) * width, (at + i + 1) * width) for i in range(across)]
                groups = [((), [(out, (slice(0, part), where)) for where in places_at])]
                outs[out][0] += across
                beside[out] = part
            returned.append(out)
        elif mode == "all":
            groups = [((), [send_to(place, count) for place in places(names)])]
            kind = BF
        else:
            groups = [(place, [send_to(place, count)]) for place in places(names)]
            kind = BF
        if mode != "final":
            returned.append([out for unused, targets in groups for out in targets])
        gone = piece.gone | frozenset(split)
        for flip, targets in groups:
            task = {"kind": "sum", "flip": flip, "loads": [], "sum": [], "stage": len(stages)}
            stages.append(shape((count, width), kind))
            task["outs"] = targets
            copies += len(targets)
            for level in piece.levels:
                strides = level.owner.strides(level.gone)
                slots = []
                for t, (array, at) in enumerate(level.terms):
                    slots.append(len(loads))
                    alt, alt_at = None, at
                    if level.alt is not None:
                        buffer, alt_at = level.alt.terms[t]
                        alt = index_of(buffer)
                    task["loads"].append(
                        {
                            "in": index_of(array),
                            "alt": alt,
                            "alt_at": alt_at,
                            "alt_moving": level.alt.moving(gone) if level.alt is not None else (),
                            "choice": level.choice,
                            "at": at,
                            "moving": level.moving(gone),
                            "bases": [
                                sum(i * strides[name] for name, i in loop.items()) for loop in loops
                            ],
                            "post": post,
                            "slot": len(loads),
                        }
                    )
                    loads.append(shape((count, width), array.dtype))
                    copies += len(loops)
                task["sum"].append((level.rounded, slots))
            tasks.append(task)
    results = kernel_call(
        functools.partial(
            combine_kernel,
            links,
            tasks,
            len(ins),
            len(outs),
            len(loads),
            len(after),
        ),
        name,
        [
            shape((beside[i], count * width) if i in beside else (count, width), kind)
            for i, (count, kind) in enumerate(outs)
        ],
        loads + stages,
        copies,
    )(*ins, *after)
    came = {out: links.bring(results[out], *where) for where, out in sends.items()}
    values = []
    for (piece, names, mode), back in zip(steps, returned):
        if mode == "final":
            values.append(results[back])
        elif mode == "raw":
            values.append((came[back[0]], back[1].start))
        elif mode == "vec":
            piece.kept = results[back["kept"]]
            piece.came = [(came[out], at.start) for out, at in back["outs"]]
        else:
            if mode == "split":
                piece.gone = piece.gone | frozenset(names)
            piece.levels.append(
                Level(
                    piece, [(came[out], at.start) for out, at in back], piece.gone, mode == "all"
                )
            )
    return [results[out] for out in sends.values()], values


def touch_kernel(count, *refs):
    copies = Copies(refs[-1])
    loads = [copies.start(refs[i].at[0:16, 0:128], refs[-2].at[i]) for i in range(count)]
    for copy in loads:
        copy.wait()
    total = refs[-2][0].astype(F32)
    for i in range(1, count):
        total = total + refs[-2][i].astype(F32)
    refs[-3][...] = total


def touch(after, *pieces):
    buffers = []
    for piece in pieces:
        buffer = piece.levels[-1].terms[0][0]
        if not any(buffer is other for other in buffers):
            buffers.append(buffer)
    count = len(buffers)
    return kernel_call(
        functools.partial(touch_kernel, count),
        "touch",
        (shape((16, 128), F32),),
        (shape((count, 16, 128), BF),),
        count,
        vmem_out=1,
    )(*buffers, *after)[0]


def assemble_kernel(links, vec_ref, own_ref, x_ref, core_ref, both_ref, after_hbm, *outs):
    full_ref = outs[-2]
    piece = own_ref.shape[0] // 2
    half = own_ref.shape[1]
    x, c = links.bit(1), links.bit(0)
    for ref, dx, dc in ((own_ref, 0, 0), (x_ref, 1, 0), (core_ref, 0, 1), (both_ref, 1, 1)):
        at = ((1 - c if dc else c) * 2 + (1 - x if dx else x)) * piece
        rows = pl.ds(pl.multiple_of(at, 16), piece)
        for h in range(2):
            part = ref[h * piece : (h + 1) * piece, :]
            full_ref[rows, h * half : (h + 1) * half] = part.astype(F32)
    for i, out in enumerate(outs[:5]):
        row = jnp.concatenate([vec_ref[2 * i : 2 * i + 1, :], vec_ref[2 * i + 1 : 2 * i + 2, :]], axis=1)
        out[...] = row.reshape(out.shape)


def assemble(links, vec, near, after):
    rows, half = near[0].shape
    return kernel_call(
        functools.partial(assemble_kernel, links),
        "assemble",
        (shape((2 * half,), F32),) * 5 + (shape((2 * rows, 2 * half), F32),),
        (),
        1,
        vmem_in=5,
        vmem_out=6,
    )(vec, *near, after)


def shards(
    links,
    pixels,
    visible,
    kernels,
    class_token,
    norm1_gain,
    norm1_bias,
    norm2_gain,
    norm2_bias,
    attn_qkv,
    attn_out,
    mlp_up,
    mlp_down,
    cotangent,
):
    width = attn_out.shape[0]
    half = width // 2
    chips = cotangent.shape[0]
    group_chips, bands, patches, pix = pixels.shape
    slots = visible.shape[1]
    body = chips * slots
    depth = bands * pix
    block = width // 16
    flat = lambda a: a.reshape(-1, half)
    core_swap = lambda a: (links.swap(flat(a), 0), 0)

    pixel_rows = jnp.swapaxes(pixels, 2, 3).reshape(group_chips, depth, patches)
    kernels_own = kernels.reshape(depth, width)
    my_half = lax.dynamic_slice_in_dim(kernels_own, links.bit(0) * (depth // 2), depth // 2, 0)
    far_half = links.swap(my_half, "band")
    picked_in = links.swap(pick_far(links, visible, pixel_rows), "band")
    far_half, cotangent = lax.optimization_barrier((far_half, cotangent))
    picked_own, cot, gact = prepare(links, visible, pixel_rows, cotangent, mlp_down)
    far_other = links.swap(far_half, 0)
    vecs = jnp.stack(
        [class_token, norm1_gain, norm1_bias, norm2_gain, norm2_bias] + [class_token] * 3
    )

    stream, n1, packed, probs, tprobs, att, mid, n2, act1, gpre1, *parts1 = forward(
        links,
        chips,
        vecs,
        picked_own,
        picked_in,
        kernels_own,
        far_half,
        far_other,
        attn_qkv,
        attn_out,
        cot,
        gact,
        mlp_up,
    )

    x, y, core, plane = (1,), ("band",), (0,), (1, "band")
    down_send, down_keep, up_send, up_keep = parts1
    down1 = Piece(
        (1, 0, "band", "h", 3, 2),
        (2,) * 6,
        block,
        [(down_keep, 0), (links.bring(down_send, 1), 0)],
        x,
    )
    up1 = Piece(
        (3, 1, 0, "band"), (2,) * 4, 4 * block, [(up_keep, 0), (links.bring(up_send, "band"), 0)], y
    )
    *sums_send, sums_keep, branch, gatt, act2, vec2 = mlp_back(
        links, vecs, n2, gact, gpre1, mlp_up, mid, cot, att, attn_out, ()
    )
    both = lambda i, at: [(sums_keep, at), (links.bring(sums_send[i], 0), 0)]
    middle, end = 2 * width, 2 * width + mlp_up.shape[1] // 2
    down2 = Piece((0, 1, "band", "h", 3, 2), (2,) * 6, block, both(0, 0), core)
    up2 = Piece((0, 3, 1, "band"), (2,) * 4, 4 * block, both(1, middle), core)
    names, sizes = (0, 1, "band", 3, 2), (2,) * 5
    outp = Piece(names, sizes, block, both(2, end), core)
    tie, unused = combine(links, [(down1, core, "split"), (up1, core, "split")], (vec2,))
    tie, unused = combine(
        links,
        [
            (down1, y, "split"),
            (up1, x, "split"),
            (down2, x, "split"),
            (up2, y, "split"),
            (outp, (2,), "split"),
        ],
        tie,
    )

    gpacked, qkv_send, qkv_keep = attention_back(links, chips, gatt, packed, probs, tprobs, n1, tie)
    qkv_in = links.bring(qkv_send, 0)
    qkv = [
        Piece(names, sizes, count, [(qkv_keep, at), (qkv_in, at)], core)
        for at, count in qkv_parts(width)
    ]
    older = touch((gpacked,), down1, up1, down2, up2, outp)
    tie, unused = combine(
        links,
        [
            (down2, y, "split"),
            (up2, x, "split"),
            (qkv[0], x, "split"),
            (qkv[1], y, "split"),
            (down1, (2,), "split"),
            (up1, (3,), "split"),
            (outp, (3,), "split"),
        ],
        (older,),
    )
    kg_send, kg_keep, pgrad_own, pgrad_far, vec_keep = embed_back(
        links,
        chips,
        vecs,
        vec2,
        gpacked,
        attn_qkv,
        stream,
        branch,
        picked_own,
        picked_in,
        kernels_own,
        far_half,
        far_other,
        tie,
    )
    kg_in = links.bring(kg_send, 0)
    kg = Piece((0, "band", 1, "h"), (2,) * 4, depth // 4, [(kg_keep, 0), (kg_in, 0)], core)
    vec = Vec(vec_keep, (kg_in, 2 * depth))
    older = touch((vec_keep,), down2, up2, *qkv, down1, up1, outp)
    tie, unused = combine(
        links,
        [
            (kg, plane, "split"),
            (vec, plane, "vec"),
            (qkv[0], y, "split"),
            (qkv[1], x, "split"),
            (outp, plane, "split"),
            (down2, (2,), "split"),
            (up2, (3,), "split"),
            (down1, (3,), "split"),
        ],
        (older,),
    )
    far_grads = links.bring(flat(pgrad_far), "band")
    partly = scatter(links, 0, flat(pgrad_own), depth, visible, patches)
    up = Piece.join(up1, up2, 2)
    tie, (out_sum,) = combine(
        links,
        [
            (qkv[0], (2,), "split"),
            (qkv[1], (2,), "split"),
            (kg, (2, 3), "all"),
            (vec, (2, 3), "vec"),
            (outp, F32, "final"),
        ],
        (partly,),
    )
    block_output = mlp_out(chips, act1, act2, mlp_down, mid, tie)
    scattered = scatter(links, 1, far_grads, depth, visible, patches, partly)
    pixel_grads = jnp.swapaxes(scattered.reshape(group_chips, bands, pix, patches), 2, 3)
    tie, unused = combine(
        links,
        [
            (qkv[0], (3,), "split"),
            (qkv[1], (3,), "split"),
            (up, (2,), "split"),
            (down2, (3,), "split"),
        ],
        (scattered, block_output),
    )
    tie, (kgrad,) = combine(links, [(kg, BF, "final"), (vec, (), "vec")], tie, "finish")
    vec_sum = links.total(vec.value())
    kgrad = links.total(kgrad.astype(F32)).astype(BF)
    near = [kgrad, links.swap(kgrad, 1), links.swap(kgrad, 0), links.swap(kgrad, 0, 1)]
    tie, (*qkv_sums, up_sum, down_sum, unused) = combine(
        links,
        [
            (qkv[0], (F32, "qkv"), "final"),
            (qkv[1], (F32, "qkv"), "final"),
            (up, F32, "final"),
            (down1, (F32, "down", 2), "final"),
            (down2, (F32, "down", 2), "final"),
        ],
        (scattered,),
    )
    *vecs, kernel_grads = assemble(links, vec_sum, near, qkv_sums[0])

    weight = lambda part: jnp.swapaxes(links.last(part), 0, 1)
    return (
        block_output,
        pixel_grads,
        kernel_grads.reshape(bands, pix, width),
        vecs[2],
        vecs[0],
        vecs[1],
        vecs[3],
        vecs[4],
        weight(qkv_sums[0]),
        weight(out_sum),
        weight(up_sum),
        weight(down_sum),
    )


def solution(mesh):
    placed = (
        P("dp", "band", None, None),
        P("dp", None),
        P("band", None, None),
        P(),
        P(),
        P(),
        P(),
        P(),
        P(),
        P(),
        P(),
        P(),
        P(("dp", "band"), None, None),
    )
    return jax.shard_map(
        functools.partial(shards, Links(mesh)),
        mesh=mesh,
        in_specs=placed,
        out_specs=(
            P(("dp", "band"), None, None),
            P("dp", "band", None, None),
            P("band", None, None),
            P(),
            P(),
            P(),
            P(),
            P(),
            P("band", "dp"),
            P("band", "dp"),
            P("band", "dp"),
            P("band", "dp"),
        ),
        check_vma=False,
    )
```

```python
import functools

import jax
import jax.numpy as jnp
from jax import lax
from jax.experimental import pallas as pl
from jax.experimental.pallas import tpu as pltpu
from jax.sharding import PartitionSpec as P

HEADS = 12
HEAD = 64
BF = jnp.bfloat16
F32 = jnp.float32
TAIL = 16
BLOCK = 112
KEYS = 80
SCALE = HEAD ** (-0.5)
VMEM = pl.BlockSpec(memory_space=pltpu.VMEM)
HBM = pl.BlockSpec(memory_space=pl.ANY)
shape = jax.ShapeDtypeStruct
MICROSECONDS = {
    "pick_far": 5,
    "prepare": 11,
    "encoder_forward": 31,
    "mlp_back": 32,
    "attention_back": 18,
    "embed_back": 14,
    "combine": 12,
    "mlp_out": 8,
    "touch": 20,
    "assemble": 0.5,
    "finish": 0.5,
    "scatter": 4,
}


def dot(a, b):
    return jnp.dot(a, b, preferred_element_type=F32)


def dot_nt(a, b):
    return lax.dot_general(a, b, (((1,), (1,)), ((), ())), preferred_element_type=F32)


def dot_tn(a, b):
    return lax.dot_general(a, b, (((0,), (0,)), ((), ())), preferred_element_type=F32)


def kernel_call(body, name, outs, scratch, copies, vmem_in=0, vmem_out=0, mib=62, **more):
    def call(*operands):
        return pl.pallas_call(
            body,
            out_shape=tuple(outs),
            in_specs=[VMEM] * vmem_in + [HBM] * (len(operands) - vmem_in),
            out_specs=(HBM,) * (len(outs) - vmem_out) + (VMEM,) * vmem_out,
            scratch_shapes=[
                a if hasattr(a, "get_ref_aval") else pltpu.VMEM(a.shape, a.dtype) for a in scratch
            ]
            + [pltpu.SemaphoreType.DMA((copies,))],
            compiler_params=pltpu.CompilerParams(vmem_limit_bytes=mib * 1024 * 1024),
            cost_estimate=pl.CostEstimate(
                flops=int(MICROSECONDS[name] * 1.15e9), bytes_accessed=1, transcendentals=0
            ),
            name=name,
            **more,
        )(*operands)

    return call


def tiles(count, body, looped=False, base=0, tile=256):
    if not looped:
        for j in range(0, count, tile):
            body(slice(base + j, base + j + tile))
        return

    def step(j, carry):
        body(pl.ds(pl.multiple_of(base + j * tile, tile), tile))
        return carry

    lax.fori_loop(0, count // tile, step, 0)


LOOP = (True, False, True, True, False)


class Copies:
    def __init__(self, sems):
        self.sems, self.count, self.open = sems, 0, []

    def start(self, source, target):
        copy = pltpu.make_async_copy(source, target, self.sems.at[self.count])
        self.count += 1
        copy.start()
        return copy

    def out(self, source, target):
        self.open.append(self.start(source, target))

    def finish(self):
        for copy in self.open:
            copy.wait()


def chosen(seen_ref, chip, patches):
    first = seen_ref[pl.ds(chip, 1), :]
    second = seen_ref[pl.ds(chip + 1, 1), :]
    slots = first.shape[1]
    seen = jnp.concatenate([first, second], axis=1)
    ids = lax.broadcasted_iota(jnp.int32, (patches, 2 * slots), 0)
    lane = lax.broadcasted_iota(jnp.int32, (patches, 2 * slots), 1)
    hit = ids == seen
    return (
        jnp.where(hit & (lane < slots), 1.0, 0.0).astype(BF),
        jnp.where(hit & (lane >= slots), 1.0, 0.0).astype(BF),
    )


class Pixels:
    def __init__(self, pixel_hbm, pixel_ref, base, pairs, sems):
        self.hbm, self.ref, self.base, self.pairs, self.sems = pixel_hbm, pixel_ref, base, pairs, sems
        for i in range(pairs):
            self.copy(i).start()

    def copy(self, i):
        there, here = pl.ds(self.base + 2 * i, 2), pl.ds(2 * i, 2)
        return pltpu.make_async_copy(self.hbm.at[there], self.ref.at[here], self.sems.at[i])

    def pick(self, seen_ref, out_ref, looped=True):
        wide = 2 * seen_ref.shape[1]

        def pair(i, carry):
            first, second = chosen(seen_ref, self.base + 2 * i, self.ref.shape[2])
            self.copy(i).wait()
            out_ref[:, pl.ds(pl.multiple_of(i * wide, wide), wide)] = (
                dot(self.ref[2 * i], first) + dot(self.ref[2 * i + 1], second)
            ).astype(BF)
            return carry

        if looped:
            lax.fori_loop(0, self.pairs, pair, 0)
        else:
            for i in range(self.pairs):
                pair(i, 0)


def pick_far_kernel(links, pairs, seen_ref, pixel_hbm, out_hbm, pixel_ref, out_ref, pixel_sems, sems):
    base = (1 - links.bit("band")) * 2 * pairs
    Pixels(pixel_hbm, pixel_ref, base, pairs, pixel_sems).pick(seen_ref, out_ref, False)
    copies = Copies(sems)
    copies.out(out_ref, out_hbm)
    copies.finish()


def pick_far(links, seen, pixel_rows):
    chips, depth, patches = pixel_rows.shape
    pairs = chips // 4
    out = shape((depth, chips // 2 * seen.shape[1]), BF)
    return kernel_call(
        functools.partial(pick_far_kernel, links, pairs),
        "pick_far",
        (out,),
        (shape((2 * pairs, depth, patches), BF), out, pltpu.SemaphoreType.DMA((pairs,))),
        1,
        vmem_in=1,
    )(seen, pixel_rows)[0]


def prepare_kernel(
    links,
    pairs,
    seen_ref,
    pixel_hbm,
    cot_hbm,
    down_hbm,
    picked_hbm,
    rows_hbm,
    gact_hbm,
    pixel_ref,
    cot_ref,
    down_ref,
    picked_ref,
    rows_ref,
    gact_ref,
    tail_ref,
    pixel_sems,
    sems,
):
    copies = Copies(sems)
    chips = cot_ref.shape[0]
    slots = cot_ref.shape[1] - 1
    rows, width = rows_ref.shape
    base = links.bit("band") * 2 * pairs
    cot_in = copies.start(cot_hbm, cot_ref)
    pixels = Pixels(pixel_hbm, pixel_ref, base, pairs, pixel_sems)
    chunk = down_hbm.shape[0] // 4
    parts = [slice(i * chunk, (i + 1) * chunk) for i in range(4)]
    downs = [copies.start(down_hbm.at[part, :], down_ref.at[part, :]) for part in parts]
    cot_in.wait()
    tail_ref[...] = jnp.zeros_like(tail_ref)

    def lay(c, carry):
        chip = cot_ref[c].astype(F32)
        rows_ref[pl.ds(pl.multiple_of(c * slots, slots), slots), :] = chip[1:, :].astype(BF)
        tail_ref[pl.ds(c, 1), :] = chip[0:1, :]
        return carry

    lax.fori_loop(0, chips, lay, 0)
    rows_ref[rows - TAIL : rows, :] = tail_ref[...].astype(BF)
    copies.out(rows_ref, rows_hbm)
    pixels.pick(seen_ref, picked_ref)
    copies.out(picked_ref, picked_hbm)
    for part, copy in zip(parts, downs):
        copy.wait()

        def act_grad(at):
            gact_ref[:, at] = dot_nt(rows_ref[...], down_ref[at, :]).astype(BF)

        tiles(chunk, act_grad, True, part.start)
        copies.out(gact_ref.at[:, part], gact_hbm.at[:, part])
    copies.finish()


def prepare(links, seen, pixel_rows, cot, down):
    group, depth, patches = pixel_rows.shape
    pairs = group // 4
    hidden, width = down.shape
    body = cot.shape[0] * seen.shape[1]
    rows = body + TAIL
    outs = (shape((depth, body), BF), shape((rows, width), BF), shape((rows, hidden), BF))
    return kernel_call(
        functools.partial(prepare_kernel, links, pairs),
        "prepare",
        outs,
        (shape((2 * pairs, depth, patches), BF), cot, down)
        + outs
        + (shape((TAIL, width), F32), pltpu.SemaphoreType.DMA((pairs,))),
        12,
        vmem_in=1,
    )(seen, pixel_rows, cot, down)


def row_stats(values):
    average = jnp.mean(values, axis=-1, keepdims=True)
    centred = values - average
    spread = jnp.mean(centred * centred, axis=-1, keepdims=True)
    root = lax.rsqrt(spread + 1e-06)
    return centred * root, root


def norm_back(xhat, root, grad_out, gain):
    scaled = grad_out * gain
    mean_scaled = jnp.mean(scaled, axis=-1, keepdims=True)
    mean_along = jnp.mean(scaled * xhat, axis=-1, keepdims=True)
    return root * (scaled - mean_scaled - xhat * mean_along)


def head_rows(width):
    row = lax.broadcasted_iota(jnp.int32, (TAIL, width), 0)
    lane = lax.broadcasted_iota(jnp.int32, (TAIL, width), 1)
    return (lane // HEAD) == row


def two_heads(pair):
    low = lax.broadcasted_iota(jnp.int32, pair.shape, 1) < HEAD
    zero = jnp.zeros_like(pair)
    return jnp.concatenate([jnp.where(low, pair, zero), jnp.where(low, zero, pair)], axis=0)


def own_heads(stacked):
    rows = stacked.shape[0] // 2
    low = lax.broadcasted_iota(jnp.int32, (rows, stacked.shape[1]), 1) < HEAD
    return jnp.where(low, stacked[:rows], stacked[rows:])


def softmax_keys(scores, count):
    key = lax.broadcasted_iota(jnp.int32, scores.shape, 0)
    scores = jnp.where(key < count, scores * SCALE, -1e30)
    raised = jnp.exp(scores - jnp.max(scores, axis=0, keepdims=True))
    return raised * (1.0 / jnp.sum(raised, axis=0, keepdims=True))


def load_far(links, copies, half_hbm, other_hbm, target):
    count = half_hbm.shape[0]
    core = links.bit(0)
    return [
        copies.start(half_hbm, target.at[pl.ds(pl.multiple_of(core * count, 16), count), :]),
        copies.start(other_hbm, target.at[pl.ds(pl.multiple_of((1 - core) * count, 16), count), :]),
    ]


def forward_kernel(
    links,
    chips,
    vecs_ref,
    xo_hbm,
    xr_hbm,
    ko_hbm,
    half_hbm,
    other_hbm,
    wqkv_hbm,
    wout_hbm,
    cot_hbm,
    gact_hbm,
    up_hbm,
    stream_hbm,
    n1_hbm,
    packed_hbm,
    probs_hbm,
    tprobs_hbm,
    att_hbm,
    mid_hbm,
    n2_hbm,
    act_hbm,
    gpre_hbm,
    down_send_hbm,
    down_keep_hbm,
    up_send_hbm,
    up_keep_hbm,
    stream_ref,
    n1_ref,
    packed_ref,
    probs_ref,
    tprobs_ref,
    att_ref,
    mid_ref,
    n2_ref,
    xo_ref,
    xr_ref,
    ko_ref,
    kr_ref,
    tatt_ref,
    wqkv_ref,
    wout_ref,
    *half_refs,
):
    copies = Copies(half_refs[-1])
    rows, width = n1_ref.shape
    body = rows - TAIL
    slots = body // chips
    token, gain1, bias1, gain2, bias2 = (vecs_ref[i : i + 1, :] for i in range(5))
    first = [
        copies.start(source, target)
        for source, target in ((xo_hbm, xo_ref), (ko_hbm, ko_ref), (xr_hbm, xr_ref))
    ] + load_far(links, copies, half_hbm, other_hbm, kr_ref)
    for copy in first:
        copy.wait()
    wqkv_in = copies.start(wqkv_hbm, wqkv_ref)
    wout_in = copies.start(wout_hbm, wout_ref)
    half = MlpHalf(links, 0, copies, half_refs[:-1])

    def embed(at):
        stream_ref[at, :] = dot_tn(xo_ref[:, at], ko_ref[...]) + dot_tn(xr_ref[:, at], kr_ref[...])

    tiles(body, embed, True)
    tail_row = lax.broadcasted_iota(jnp.int32, (TAIL, width), 0)
    stream_ref[body:rows, :] = jnp.where(tail_row < chips, token, 0.0)

    def first_norm(i, carry):
        at = pl.ds(pl.multiple_of(i * BLOCK, BLOCK), BLOCK)
        xhat, unused = row_stats(stream_ref[at, :])
        n1_ref[at, :] = (xhat * gain1 + bias1).astype(BF)
        return carry

    lax.fori_loop(0, rows // BLOCK, first_norm, 0)
    wqkv_in.wait()
    half.load(cot_hbm, gact_hbm, up_hbm)
    copies.out(stream_ref, stream_hbm)
    copies.out(n1_ref, n1_hbm)


    def project(at):
        packed_ref[:, at] = dot(n1_ref[...], wqkv_ref[:, at]).astype(BF)

    tiles(3 * width, project)
    copies.out(packed_ref, packed_hbm)
    tail = packed_ref[body:rows, :]
    heads = head_rows(width)
    tquery = jnp.where(heads, jnp.broadcast_to(tail[0:1, 0:width], (TAIL, width)), 0).astype(BF)
    tatt_ref[...] = jnp.zeros_like(tatt_ref)

    def chip(c, carry):
        at = pl.ds(pl.multiple_of(c * slots, slots), slots)
        key = jnp.concatenate(
            [packed_ref[at, width : 2 * width], tail[:, width : 2 * width]], axis=0
        )
        val = jnp.concatenate([packed_ref[at, 2 * width :], tail[:, 2 * width :]], axis=0)
        tiles = [slice(128 * p, 128 * p + 128) for p in range(width // 128)]
        scores = [dot_nt(key[:, here], two_heads(packed_ref[at, here])) for here in tiles]
        scores.append(dot_nt(key, tquery))
        probs = [softmax_keys(s, slots + 1).astype(BF) for s in scores]
        mixed = [dot_tn(probs[p], val[:, tiles[p]]) for p in range(len(tiles))]
        mixed.append(dot_tn(probs[-1], val))
        for p in range(len(tiles)):
            probs_ref[c, p] = probs[p]
            att_ref[at, tiles[p]] = own_heads(mixed[p]).astype(BF)
        tprobs_ref[c] = probs[-1]
        tatt_ref[pl.ds(c, 1), :] = jnp.sum(jnp.where(heads, mixed[-1], 0.0), axis=0, keepdims=True)
        return carry

    lax.fori_loop(0, chips, chip, 0, unroll=2)
    att_ref[body:rows, :] = tatt_ref[...].astype(BF)
    copies.out(probs_ref, probs_hbm)
    copies.out(tprobs_ref, tprobs_hbm)
    copies.out(att_ref, att_hbm)
    wout_in.wait()


    def out_project(at):
        mid_ref[:, at] = stream_ref[:, at] + dot(att_ref[...], wout_ref[:, at])

    tiles(width, out_project, True)
    copies.out(mid_ref, mid_hbm)

    def second_norm(i, carry):
        at = pl.ds(pl.multiple_of(i * BLOCK, BLOCK), BLOCK)
        xhat, unused = row_stats(mid_ref[at, :])
        n2_ref[at, :] = (xhat * gain2 + bias2).astype(BF)
        return carry

    lax.fori_loop(0, rows // BLOCK, second_norm, 0)
    copies.out(n2_ref, n2_hbm)
    half.run(n2_ref, (down_send_hbm, down_keep_hbm), (up_send_hbm, up_keep_hbm))
    copies.out(half.act, act_hbm)
    copies.out(half.gpre, gpre_hbm)
    copies.finish()


class MlpHalf:
    def __init__(self, links, third, copies, refs):
        self.links, self.third, self.copies = links, third, copies
        self.looped = (True, False)
        self.cot, self.gact, self.up, self.act, self.gpre, self.grads = refs

    @staticmethod
    def scratch(rows, width, hidden):
        return (
            shape((rows, width), BF),
            shape((rows, hidden // 2), BF),
            shape((width, hidden // 2), BF),
            shape((rows, hidden // 2), BF),
            shape((rows, hidden // 2), BF),
            shape((4, max(width, hidden // 4), width), BF),
        )

    def load(self, cot_hbm, gact_hbm, up_hbm):
        chunk = up_hbm.shape[1] // 4
        start = self.copies.start
        far = lambda i: slice((2 * i + self.third) * chunk, (2 * i + self.third + 1) * chunk)
        near = lambda i: slice(i * chunk, (i + 1) * chunk)
        self.first = [
            (
                start(up_hbm.at[:, far(i)], self.up.at[:, near(i)]),
                start(gact_hbm.at[:, far(i)], self.gact.at[:, near(i)]),
            )
            for i in range(2)
        ]
        self.cot_in = start(cot_hbm, self.cot)

    def run(self, n2_ref, down_out, up_out, then=None):
        copies, links = self.copies, self.links
        rows, width = n2_ref.shape
        chunk = self.up.shape[1] // 2
        half = width // 2
        block = width // 16
        for i in range(2):
            for copy in self.first[i]:
                copy.wait()
            if i == 1 and then is not None:
                then()

            def activate(cols):
                pre = dot(n2_ref[...], self.up[:, cols])
                phi = 0.5 + 0.5 * lax.erf(pre * (0.5**0.5))
                bell = jnp.exp(-0.5 * pre * pre) * 0.3989422804014327
                self.act[:, cols] = (pre * phi).astype(BF)
                gact = self.gact[:, cols].astype(F32)
                self.gpre[:, cols] = (gact * (phi + pre * bell)).astype(BF)

            tiles(chunk, activate, self.looped[0], i * chunk)
        where = (1, "band") if self.third == 0 else (0, 0)
        bits = [links.bit(w) for w in where]
        self.cot_in.wait()
        for i in range(2):

            def down_rows(at):
                self.grads[i, at, :] = dot_tn(
                    self.cot[:, at], self.act[:, i * chunk : (i + 1) * chunk]
                ).astype(BF)

            tiles(width, down_rows, self.looped[1])
            for side, bit in ((0, 1 - bits[0]), (1, bits[0])):
                for other in range(2):
                    x, c = (bit, other) if where[0] == 1 else (other, bit)
                    for z in range(4):
                        at = pl.multiple_of(((z * 2 + x) * 2 + c) * block, 16)
                        for h in range(2):
                            to = (((other * 2 + i) * 2 + h) * 4 + z) * block
                            copies.out(
                                self.grads.at[i, pl.ds(at, block), h * half : (h + 1) * half],
                                down_out[side].at[to : to + block, :],
                            )
        part = chunk // 4
        for i in range(2):

            def up_rows(at):
                self.grads[2 + i, at, :] = dot_tn(
                    self.gpre.at[:, i * chunk : (i + 1) * chunk][:, at], n2_ref[...]
                ).astype(BF)

            tiles(chunk, up_rows, self.looped[1])
            for side, bit in ((0, 1 - bits[1]), (1, bits[1])):
                for x in range(2):
                    for other in range(2):
                        if where[1] == "band":
                            at = (2 * x + other) * part
                            cols = pl.ds(pl.multiple_of(bit * half, 128), half)
                        else:
                            at = pl.multiple_of((2 * x + bit) * part, 16)
                            cols = slice(other * half, (other + 1) * half)
                        to = ((i * 2 + x) * 2 + other) * part
                        copies.out(
                            self.grads.at[2 + i, pl.ds(at, part), cols],
                            up_out[side].at[to : to + part, :],
                        )


def forward(links, chips, vecs, xo, xr, ko, half, other, wqkv, wout, cot, gact, up):
    width, hidden = up.shape
    body = xo.shape[1]
    rows = body + TAIL
    saved = (
        shape((rows, width), F32),
        shape((rows, width), BF),
        shape((rows, 3 * width), BF),
        shape((chips, width // 128, KEYS, 128), BF),
        shape((chips, KEYS, TAIL), BF),
        shape((rows, width), BF),
        shape((rows, width), F32),
        shape((rows, width), BF),
    )
    return kernel_call(
        functools.partial(forward_kernel, links, chips),
        "encoder_forward",
        saved
        + (shape((rows, hidden // 2), BF),) * 2
        + (shape((2 * width, width // 2), BF),) * 2
        + (shape((hidden // 2, width // 2), BF),) * 2,
        saved
        + (xo, xr, ko, ko, shape((TAIL, width), F32), wqkv, wout)
        + MlpHalf.scratch(rows, width, hidden),
        112,
        vmem_in=1,
    )(vecs, xo, xr, ko, half, other, wqkv, wout, cot, gact, up)


def spread_blocks(links, copies, full_ref, outs):
    core = links.bit(0)
    cols = full_ref.shape[1] // 2
    block = full_ref.shape[0] // 16
    for z in range(4):
        for x in range(2):
            for side, c in ((0, 1 - core), (1, core)):
                start = ((z * 2 + x) * 2 + c) * block
                for count, pair in outs:
                    rows = pl.ds(pl.multiple_of(start, 16), count)
                    start = start + count
                    for b in range(2):
                        to = ((x * 2 + b) * 4 + z) * count
                        copies.out(
                            full_ref.at[rows, b * cols : (b + 1) * cols],
                            pair[side].at[to : to + count, :],
                        )


def mlp_back_kernel(
    links,
    after,
    vecs_ref,
    n2_hbm,
    gact_hbm,
    gpre1_hbm,
    up_hbm,
    mid_hbm,
    cot_hbm,
    att_hbm,
    wout_hbm,
    *rest,
):
    rest = rest[after:]
    sends, (keep_hbm, branch_hbm, gatt_hbm, act2_hbm, vec_ref) = rest[:3], rest[3:8]
    (
        n2_ref,
        gatt_ref,
        gpre_ref,
        up_ref,
        mid_ref,
        att_ref,
        wout_ref,
        back_ref,
        branch_ref,
        full_ref,
    ) = rest[8:18]
    half_refs, sems = rest[18:-1], rest[-1]
    copies = Copies(sems)
    rows, width = mid_ref.shape
    quarter = up_hbm.shape[1] // 4
    at = lambda i: slice(i * quarter, (i + 1) * quarter)
    n2_in = copies.start(n2_hbm, n2_ref)
    half = MlpHalf(links, 1, copies, half_refs)
    half.load(cot_hbm, gact_hbm, up_hbm)
    cot_ref = half.cot
    n2_in.wait()
    first_in = []

    def more():
        first_in.append(copies.start(gpre1_hbm, gpre_ref))
        for i in range(2):
            first_in.append(copies.start(up_hbm.at[:, at(2 * i)], up_ref.at[:, at(i)]))
        for source, target in ((mid_hbm, mid_ref), (att_hbm, att_ref), (wout_hbm, wout_ref)):
            first_in.append(copies.start(source, target))

    middle = 2 * width
    end = middle + up_hbm.shape[1] // 2
    half.run(
        n2_ref,
        (sends[0], keep_hbm.at[0:middle, :]),
        (sends[1], keep_hbm.at[middle:end, :]),
        more,
    )
    copies.out(half.act, act2_hbm)
    for copy in first_in:
        copy.wait()

    def backward(cols):
        back_ref[:, cols] = dot_nt(gpre_ref[...], up_ref[cols, :]) + dot_nt(
            half.gpre[...], half.up[cols, :]
        )

    tiles(width, backward, LOOP[2])
    gain = vecs_ref[3:4, :]

    def norm(i, carry):
        at = pl.ds(pl.multiple_of(i * BLOCK, BLOCK), BLOCK)
        xhat, root = row_stats(mid_ref[at, :])
        grad = back_ref[at, :]
        total = cot_ref[at, :].astype(F32) + norm_back(xhat, root, grad, gain)
        branch_ref[at, :] = total.astype(BF)
        return (
            carry[0] + jnp.sum(grad * xhat, axis=0, keepdims=True),
            carry[1] + jnp.sum(grad, axis=0, keepdims=True),
        )

    zero = jnp.zeros((1, width), F32)
    gain_sum, bias_sum = lax.fori_loop(0, rows // BLOCK, norm, (zero, zero))
    vec_ref[0:1, :] = gain_sum
    vec_ref[1:2, :] = bias_sum
    copies.out(branch_ref, branch_hbm)

    def out_grad(at):
        full_ref[at, :] = dot_tn(branch_ref[:, at], att_ref[...]).astype(BF)

    tiles(width, out_grad, LOOP[4])
    spread_blocks(
        links, copies, full_ref, [(width // 16, (sends[2], keep_hbm.at[end : end + width, :]))]
    )

    def attended_grad(at):
        gatt_ref[:, at] = dot_nt(branch_ref[...], wout_ref[at, :]).astype(BF)

    tiles(width, attended_grad, LOOP[4])
    copies.out(gatt_ref, gatt_hbm)
    copies.finish()


def mlp_back(links, vecs, n2, gact, gpre1, up, mid, cot, att, wout, after):
    rows, width = mid.shape
    hidden = up.shape[1]
    sums = shape((3 * width + hidden // 2, width // 2), BF)
    return kernel_call(
        functools.partial(mlp_back_kernel, links, len(after)),
        "mlp_back",
        tuple(shape((count, width // 2), BF) for count in (2 * width, hidden // 2, width))
        + (sums, cot, cot, gpre1, shape((2, width), F32)),
        (n2, cot, gpre1)
        + (shape((width, hidden // 2), BF), mid, att, wout, mid, cot, wout)
        + MlpHalf.scratch(rows, width, hidden),
        140,
        vmem_in=1,
        vmem_out=1,
    )(vecs, n2, gact, gpre1, up, mid, cot, att, wout, *after)


def mlp_out_kernel(chips, after, act1_hbm, act2_hbm, down_hbm, mid_hbm, *rest):
    out_hbm = rest[after]
    act1_ref, act2_ref, down_ref, mid_ref, rows_ref, out_ref, sems = rest[after + 1 :]
    copies = Copies(sems)
    rows, width = mid_ref.shape
    slots = (rows - TAIL) // chips
    quarter = down_hbm.shape[0] // 4
    at = lambda i: slice(i * quarter, (i + 1) * quarter)
    arrive = []
    for third, source, target in ((0, act1_hbm, act1_ref), (1, act2_hbm, act2_ref)):
        arrive.append(copies.start(source, target))
        for i in range(2):
            arrive.append(
                copies.start(down_hbm.at[at(2 * i + third), :], down_ref.at[at(2 * third + i), :])
            )
    arrive.append(copies.start(mid_hbm, mid_ref))
    for copy in arrive:
        copy.wait()

    def outward(cols):
        rows_ref[:, cols] = (
            mid_ref[:, cols]
            + dot(act1_ref[...], down_ref[: 2 * quarter, cols])
            + dot(act2_ref[...], down_ref[2 * quarter :, cols])
        )

    tiles(width, outward, True)

    def chip(c, carry):
        first = rows_ref[pl.ds(rows - TAIL + c, 1), :]
        others = rows_ref[pl.ds(pl.multiple_of(c * slots, slots), slots), :]
        out_ref[c] = jnp.concatenate([first, others], axis=0).astype(BF)
        return carry

    lax.fori_loop(0, chips, chip, 0)
    copies.out(out_ref, out_hbm)
    copies.finish()


def mlp_out(chips, act1, act2, down, mid, after):
    rows, width = mid.shape
    out = shape((chips, (rows - TAIL) // chips + 1, width), BF)
    return kernel_call(
        functools.partial(mlp_out_kernel, chips, len(after)),
        "mlp_out",
        (out,),
        (act1, act2, down, mid, mid, out),
        8,
    )(act1, act2, down, mid, *after)[0]


def split_vec(vec):
    high = vec.astype(BF)
    return high, (vec - high.astype(F32)).astype(BF)


def attention_back_kernel(
    links, chips, after, gatt_hbm, packed_hbm, probs_hbm, tprobs_hbm, n1_hbm, *rest
):
    gpacked_hbm, send_hbm, keep_hbm = rest[after : after + 3]
    (
        gpacked_ref,
        gatt_ref,
        packed_ref,
        probs_ref,
        tprobs_ref,
        n1_ref,
        tgrad_ref,
        tout_ref,
        full_ref,
        chip_sems,
        sems,
    ) = rest[after + 3 :]
    rows, width = n1_ref.shape
    body = rows - TAIL
    slots = body // chips
    copies = Copies(sems)

    def arriving(c):
        at = pl.ds(pl.multiple_of(c * slots, slots), slots)
        return [
            pltpu.make_async_copy(source.at[where], target.at[where], chip_sems.at[k, c])
            for k, (source, target, where) in enumerate(
                (
                    (packed_hbm, packed_ref, (at, slice(None))),
                    (gatt_hbm, gatt_ref, (at, slice(None))),
                    (probs_hbm, probs_ref, c),
                )
            )
        ]

    tails = slice(body, rows)
    arrive = [
        copies.start(packed_hbm.at[tails, :], packed_ref.at[tails, :]),
        copies.start(gatt_hbm.at[tails, :], gatt_ref.at[tails, :]),
        copies.start(tprobs_hbm, tprobs_ref),
    ]
    for c in range(chips):
        for copy in arriving(c):
            copy.start()
    tout_ref[...] = jnp.zeros_like(tout_ref)
    heads = head_rows(width)
    for copy in arrive:
        copy.wait()
    n1_in = copies.start(n1_hbm, n1_ref)
    tgrad_ref[...] = gatt_ref[body:rows, :].astype(F32)
    tail = packed_ref[body:rows, :]
    tquery = jnp.where(heads, jnp.broadcast_to(tail[0:1, 0:width], (TAIL, width)), 0).astype(BF)

    def chip(c):
        at = pl.ds(pl.multiple_of(c * slots, slots), slots)
        key_all = jnp.concatenate(
            [packed_ref[at, width : 2 * width], tail[:, width : 2 * width]], axis=0
        )
        val_all = jnp.concatenate([packed_ref[at, 2 * width :], tail[:, 2 * width :]], axis=0)
        tgrad = jnp.where(
            heads, jnp.broadcast_to(tgrad_ref[pl.ds(c, 1), :], (TAIL, width)), 0.0
        ).astype(BF)
        tiles = [slice(128 * p, 128 * p + 128) for p in range(width // 128)]
        probs = [probs_ref[c, p] for p in range(len(tiles))] + [tprobs_ref[c]]
        gouts = [two_heads(gatt_ref[at, here]) for here in tiles]
        queries = [two_heads(packed_ref[at, here]) for here in tiles]
        gprobs = [dot_nt(val_all[:, tiles[p]], gouts[p]) for p in range(len(tiles))]
        gprobs.append(dot_nt(val_all, tgrad))
        gscores = []
        for prob, gprob in zip(probs, gprobs):
            wide = prob.astype(F32)
            inner = jnp.sum(gprob * wide, axis=0, keepdims=True)
            gscores.append((wide * (gprob - inner) * SCALE).astype(BF))
        gval_tail = dot(probs[-1], tgrad)
        gkey_tail = dot(gscores[-1], tquery)
        mixed = jnp.where(heads, dot_tn(gscores[-1], key_all), 0.0)
        gvals = [dot(probs[p], gouts[p]) + gval_tail[:, tiles[p]] for p in range(len(tiles))]
        gkeys = [dot(gscores[p], queries[p]) + gkey_tail[:, tiles[p]] for p in range(len(tiles))]
        gqueries = [own_heads(dot_tn(gscores[p], key_all[:, tiles[p]])) for p in range(len(tiles))]
        for p in range(len(tiles)):
            gpacked_ref[at, 128 * p : 128 * p + 128] = gqueries[p].astype(BF)
            base = width + 128 * p
            gpacked_ref[at, base : base + 128] = gkeys[p][:slots].astype(BF)
            gpacked_ref[at, width + base : width + base + 128] = gvals[p][:slots].astype(BF)
        tout_ref[pl.ds(c, 1), :] = jnp.concatenate(
            [jnp.sum(mixed, axis=0, keepdims=True)]
            + [g[slots : slots + 1] for g in gkeys + gvals],
            axis=1,
        )

    def two_chips(i, carry):
        for c in (2 * i, 2 * i + 1):
            for copy in arriving(c):
                copy.wait()
        chip(2 * i)
        chip(2 * i + 1)
        return carry

    lax.fori_loop(0, chips // 2, two_chips, 0)
    gpacked_ref[body:rows, :] = tout_ref[...].astype(BF)
    copies.out(gpacked_ref, gpacked_hbm)
    n1_in.wait()

    def qkv_rows(at):
        full_ref[at, :] = dot_tn(gpacked_ref[:, at], n1_ref[...]).astype(BF)

    tiles(3 * width, qkv_rows)
    outs = []
    for at, count in qkv_parts(width):
        here = slice(at, at + 16 * count)
        outs.append((count, (send_hbm.at[here, :], keep_hbm.at[here, :])))
    spread_blocks(links, copies, full_ref, outs)
    copies.finish()


def qkv_parts(width):
    block = 3 * width // 16
    count = -(-block // 32) * 16
    return [(0, count), (16 * count, block - count)]


def attention_back(links, chips, gatt, packed, probs, tprobs, n1, after):
    rows, width = n1.shape
    sums = shape((3 * width, width // 2), BF)
    return kernel_call(
        functools.partial(attention_back_kernel, links, chips, len(after)),
        "attention_back",
        (packed, sums, sums),
        (packed, gatt, packed, probs, tprobs, n1)
        + (
            shape((TAIL, width), F32),
            shape((TAIL, 3 * width), F32),
            shape((3 * width, width), BF),
            pltpu.SemaphoreType.DMA((3, chips)),
        ),
        80,
    )(gatt, packed, probs, tprobs, n1, *after)


def embed_back_kernel(
    links,
    chips,
    after,
    vecs_ref,
    vec2_ref,
    gpacked_hbm,
    wqkv_hbm,
    stream_hbm,
    branch_hbm,
    xo_hbm,
    xr_hbm,
    ko_hbm,
    half_hbm,
    other_hbm,
    *rest,
):
    send_hbm, keep_hbm, own_hbm, far_hbm, vec_ref = rest[after : after + 5]
    (
        gpacked_ref,
        wqkv_ref,
        stream_ref,
        branch_ref,
        xo_ref,
        xr_ref,
        ko_ref,
        kr_ref,
        send_ref,
        keep_ref,
        pgrad_ref,
        back_ref,
        embed_ref,
        kfull_ref,
        sems,
    ) = rest[after + 5 :]
    rows, width = stream_ref.shape
    body = rows - TAIL
    half = width // 2
    copies = Copies(sems)
    thirds = [slice(i * width, (i + 1) * width) for i in range(3)]
    arrive = [
        (
            copies.start(gpacked_hbm.at[:, part], gpacked_ref.at[:, part]),
            copies.start(wqkv_hbm.at[:, part], wqkv_ref.at[:, part]),
        )
        for part in thirds
    ]
    for i, part in enumerate(thirds):
        for copy in arrive[i]:
            copy.wait()
        if i == 0:
            late = [copies.start(stream_hbm, stream_ref), copies.start(branch_hbm, branch_ref)]
        if i == 1:
            last = [
                copies.start(source, target)
                for source, target in ((xo_hbm, xo_ref), (xr_hbm, xr_ref), (ko_hbm, ko_ref))
            ] + load_far(links, copies, half_hbm, other_hbm, kr_ref)

        def backward(cols):
            grad = dot_nt(gpacked_ref[:, part], wqkv_ref[cols, part])
            back_ref[:, cols] = grad if i == 0 else back_ref[:, cols] + grad

        tiles(width, backward, True)
    for copy in late:
        copy.wait()
    gain = vecs_ref[1:2, :]

    def norm(i, carry):
        at = pl.ds(pl.multiple_of(i * BLOCK, BLOCK), BLOCK)
        xhat, root = row_stats(stream_ref[at, :])
        grad = back_ref[at, :]
        total = branch_ref[at, :].astype(F32) + norm_back(xhat, root, grad, gain)
        back_ref[at, :] = total
        embed_ref[at, :] = total.astype(BF)
        return (
            carry[0] + jnp.sum(grad * xhat, axis=0, keepdims=True),
            carry[1] + jnp.sum(grad, axis=0, keepdims=True),
        )

    zero = jnp.zeros((1, width), F32)
    gain_sum, bias_sum = lax.fori_loop(0, rows // BLOCK, norm, (zero, zero))
    token_sum = jnp.sum(back_ref[body:rows, :], axis=0, keepdims=True)
    vec_ref[...] = jnp.zeros_like(vec_ref)
    for i, v in enumerate((gain_sum, bias_sum, token_sum, vec2_ref[0:1, :], vec2_ref[1:2, :])):
        vec_ref[2 * i : 2 * i + 1, :] = v[:, :half]
        vec_ref[2 * i + 1 : 2 * i + 2, :] = v[:, half:]
    for copy in last:
        copy.wait()
    grad = embed_ref[0:body, :]
    depth = xo_ref.shape[0]
    core, band = links.bit(0), links.bit("band")
    kfull_ref[0] = dot(xo_ref[...], grad).astype(BF)
    kfull_ref[1] = dot(xr_ref[...], grad).astype(BF)
    piece = depth // 4
    for c, ref in ((1 - core, send_ref), (core, keep_ref)):
        for far in range(2):
            for x in range(2):
                start = pl.multiple_of(c * (depth // 2) + x * piece, 16)
                block = kfull_ref[far, pl.ds(start, piece), :]
                for h in range(2):
                    slot = ((far + band - 2 * far * band) * 2 + x) * 2 + h
                    to = pl.ds(pl.multiple_of(slot * piece, 16), piece)
                    ref[to, :] = block[:, h * half : (h + 1) * half]
    high, low = split_vec(vec_ref[...])
    send_ref[2 * depth : 2 * depth + 16, :] = high
    send_ref[2 * depth + 16 : 2 * depth + 32, :] = low
    vec_ref[...] = high.astype(F32) + low.astype(F32)
    copies.out(send_ref, send_hbm)
    copies.out(keep_ref, keep_hbm)
    middle = body // 2
    for side, kernel, target in ((0, kr_ref, far_hbm), (1, ko_ref, own_hbm)):
        for h in range(2):
            part = grad[h * middle : (h + 1) * middle]
            pgrad_ref[side, h] = dot_nt(kernel[...], part).astype(BF)
        copies.out(pgrad_ref.at[side], target)
    copies.finish()


def embed_back(
    links, chips, vecs, vec2, gpacked, wqkv, stream, branch, xo, xr, ko, half, other, after
):
    rows, width = stream.shape
    depth, body = xo.shape
    cols = width // 2
    send, keep = shape((2 * depth + 32, cols), BF), shape((2 * depth, cols), BF)
    pgrad = shape((2, depth, body // 2), BF)
    return kernel_call(
        functools.partial(embed_back_kernel, links, chips, len(after)),
        "embed_back",
        (send, keep, pgrad, pgrad, shape((16, cols), F32)),
        (gpacked, wqkv, stream, branch, xo, xr, ko, ko, send, keep)
        + (
            shape((2,) + pgrad.shape, BF),
            stream,
            shape((rows, width), BF),
            shape((2, depth, width), BF),
        ),
        24,
        vmem_in=2,
        vmem_out=1,
    )(vecs, vec2, gpacked, wqkv, stream, branch, xo, xr, ko, half, other, *after)


def scatter_kernel(links, side, pairs, depth, seen_ref, grad_hbm, *rest):
    out_hbm, grad_ref, out_ref, sems = rest[-4:]
    patches = out_ref.shape[2]
    copies = Copies(sems)
    copies.start(grad_hbm.at[0 : 2 * depth, :], grad_ref).wait()
    band = links.bit("band")
    base = (band if side == 0 else 1 - band) * 2 * pairs
    wide = 2 * seen_ref.shape[1]
    half = grad_ref.shape[1] // wide

    def written(i):
        two = pl.ds(2 * i, 2)
        there = pl.ds(base + 2 * i, 2)
        return pltpu.make_async_copy(out_ref.at[two], out_hbm.at[there], sems.at[1 + i])

    def pair(i, carry):
        first, second = chosen(seen_ref, base + 2 * i, patches)
        row = pl.multiple_of(lax.div(i, half) * depth, 16)
        col = pl.multiple_of(lax.rem(i, half) * wide, 128)
        grad = grad_ref[pl.ds(row, depth), pl.ds(col, wide)]
        out_ref[2 * i] = dot_nt(grad, first)
        out_ref[2 * i + 1] = dot_nt(grad, second)
        written(i).start()
        return carry

    def landed(i, carry):
        written(i).wait()
        return carry

    lax.fori_loop(0, pairs, pair, 0)
    lax.fori_loop(0, pairs, landed, 0)


def scatter(links, side, grads, depth, seen, patches, *earlier):
    chips = seen.shape[0]
    pairs = chips // 4
    return kernel_call(
        functools.partial(scatter_kernel, links, side, pairs, depth),
        "scatter",
        (shape((chips, depth, patches), F32),),
        (shape((2 * depth, grads.shape[1]), BF), shape((2 * pairs, depth, patches), F32)),
        pairs + 1,
        vmem_in=1,
        input_output_aliases={2: 0} if earlier else {},
    )(seen, grads, *earlier)[0]


class Links:
    def __init__(self, mesh):
        self.count = mesh.shape["dp"]
        self.extra = self.count // 16

    def swap(self, array, *where):
        flip = sum((1 << w) * self.extra for w in where if w != "band")
        if "band" not in where:
            return lax.ppermute(array, "dp", [(d, d ^ flip) for d in range(self.count)])
        if flip == 0:
            return lax.ppermute(array, "band", [(0, 1), (1, 0)])
        pairs = [
            (2 * d + b, 2 * (d ^ flip) + 1 - b) for d in range(self.count) for b in range(2)
        ]
        return lax.ppermute(array, ("dp", "band"), pairs)

    def bring(self, array, *where):
        return pltpu.with_memory_space_constraint(self.swap(array, *where), pltpu.HBM)

    def bit(self, where):
        if where == "band":
            return lax.axis_index("band")
        return lax.rem(lax.div(lax.axis_index("dp"), self.extra << where), 2)

    def groups(self):
        return [[block * self.extra + i for i in range(self.extra)] for block in range(16)]

    def last(self, array):
        if self.extra == 1:
            return array
        return lax.psum_scatter(
            array, "dp", scatter_dimension=0, tiled=True, axis_index_groups=self.groups()
        )

    def total(self, array):
        if self.extra == 1:
            return array
        return lax.psum(array, "dp", axis_index_groups=self.groups())


class Level:
    def __init__(self, owner, terms, gone=frozenset(), rounded=False, alt=None, choice=None):
        self.owner, self.terms, self.gone, self.rounded = owner, list(terms), frozenset(gone), rounded
        self.alt, self.choice = alt, choice

    def moving(self, gone):
        strides = self.owner.strides(self.gone)
        return [(name, strides[name]) for name in self.owner.names if name in gone and name in strides]


class Piece:
    def __init__(self, names, sizes, unit, terms, gone=()):
        self.names, self.sizes, self.unit = list(names), list(sizes), unit
        self.gone = frozenset(gone)
        self.levels = [Level(self, terms, self.gone)]

    @staticmethod
    def join(first, second, choice):
        joined = Piece(first.names, first.sizes, first.unit, (), first.gone)
        joined.levels = [
            Level(a.owner, a.terms, a.gone, a.rounded, b, choice)
            for a, b in zip(first.levels, second.levels)
        ]
        return joined

    def strides(self, gone):
        found, stride = {}, self.unit
        for name, size in reversed(list(zip(self.names, self.sizes))):
            if name not in gone:
                found[name] = stride
                stride = stride * size
        return found

    def layout(self, names):
        gone = self.gone | frozenset(names)
        last = max([i for i, name in enumerate(self.names) if name in gone], default=-1)
        post = self.unit
        for size in self.sizes[last + 1 :]:
            post = post * size
        loops = [{}]
        for name, size in list(zip(self.names, self.sizes))[: last + 1]:
            if name not in gone:
                loops = [{**at, name: i} for at in loops for i in range(size)]
        return post * len(loops), post, loops


class Vec:
    def __init__(self, kept, came):
        self.kept, self.came = kept, [came]

    def value(self):
        parts = [
            buffer[at : at + 16].astype(F32) + buffer[at + 16 : at + 32].astype(F32)
            for buffer, at in self.came
        ]
        return pairwise([self.kept] + parts)


def pairwise(parts):
    while len(parts) > 1:
        parts = [
            parts[i] + parts[i + 1] if i + 1 < len(parts) else parts[i]
            for i in range(0, len(parts), 2)
        ]
    return parts[0]


def combine_kernel(links, tasks, n_in, n_out, n_load, after, *refs):
    ins, refs = refs[:n_in], refs[n_in + after :]
    out_hbm, refs = refs[:n_out], refs[n_out:]
    loads, refs = refs[:n_load], refs[n_load:]
    staged, sems = refs[:-1], refs[-1]
    copies = Copies(sems)
    bits = {where: links.bit(where) for where in (0, 1, 2, 3, "band")}
    waits = []
    for task in tasks:
        mine = []
        waits.append(mine)
        if task["kind"] == "raw":
            mine.append(copies.start(ins[task["from"]], loads[task["slot"]]))
            continue
        if task["kind"] == "vec":
            mine += [
                copies.start(ins[i].at[at : at + count, :], loads[slot])
                for i, at, count, slot in task["loads"]
            ]
            continue
        index = {
            name: (1 - bits[name]) if name in task["flip"] else bits[name] for name in bits
        }
        for load in task["loads"]:
            moving = sum((index[name] * stride for name, stride in load["moving"]), load["at"])
            alt_moving = sum(
                (index[name] * stride for name, stride in load["alt_moving"]), load["alt_at"]
            )
            for p, base in enumerate(load["bases"]):
                rows = pl.ds(pl.multiple_of(moving + base, 16), load["post"])
                target = loads[load["slot"]].at[p * load["post"] : (p + 1) * load["post"], :]
                sem = copies.sems.at[copies.count]
                copies.count += 1
                if load["alt"] is None:
                    copy = pltpu.make_async_copy(ins[load["in"]].at[rows, :], target, sem)
                    copy.start()
                else:
                    chosen_bit = index[load["choice"]]
                    copy = pltpu.make_async_copy(ins[load["in"]].at[rows, :], target, sem)
                    rows = pl.ds(pl.multiple_of(alt_moving + base, 16), load["post"])
                    other = pltpu.make_async_copy(ins[load["alt"]].at[rows, :], target, sem)
                    pl.when(chosen_bit == 0)(copy.start)
                    pl.when(chosen_bit == 1)(other.start)
                mine.append(copy)
    for task, mine in zip(tasks, waits):
        for copy in mine:
            copy.wait()
        if task["kind"] == "raw":
            copies.out(loads[task["slot"]], out_hbm[task["out"]].at[task["at"], :])
            continue
        if task["kind"] == "vec":
            parts = [loads[task["loads"][0][3]][...]]
            for unused, also, count, slot in task["loads"][1:]:
                parts.append(loads[slot][0:16, :].astype(F32) + loads[slot][16:32, :].astype(F32))
            high, low = split_vec(pairwise(parts))
            sent, kept = staged[task["stage"]], staged[task["stage"] + 1]
            sent[0:16, :] = high
            sent[16:32, :] = low
            kept[...] = high.astype(F32) + low.astype(F32)
            for out, at in task["outs"]:
                copies.out(sent, out_hbm[out].at[at, :])
            copies.out(kept, out_hbm[task["kept"]])
            continue
        result = staged[task["stage"]]
        count = result.shape[0]
        tile = max(t for t in (16, 32, 48, 64, 80, 96) if count % t == 0)

        def add(i, carry, task=task, result=result, tile=tile):
            at = pl.ds(pl.multiple_of(i * tile, 16), tile)
            total = None
            for rounded, slots in task["sum"]:
                parts = [loads[slot][at, :].astype(F32) for slot in slots]
                if total is not None:
                    parts = [total.astype(BF).astype(F32) if rounded else total] + parts
                total = pairwise(parts)
            result[at, :] = total.astype(result.dtype)
            return carry

        lax.fori_loop(0, count // tile, add, 0)
        for i, (out, at) in enumerate(task["outs"]):
            if isinstance(at, tuple):
                part = at[0].stop
                copies.out(result.at[i * part : (i + 1) * part, :], out_hbm[out].at[at])
            else:
                copies.out(result, out_hbm[out].at[at, :])
    copies.finish()


def combine(links, steps, after=(), name="combine"):
    ins, tasks, loads, stages, sends, outs = [], [], [], [], {}, []
    copies, finals, beside = 0, {}, {}
    returned = []

    def index_of(array):
        for i, other in enumerate(ins):
            if other is array:
                return i
        ins.append(array)
        return len(ins) - 1

    def send_to(where, count):
        if where not in sends:
            sends[where] = len(outs)
            outs.append([0, BF])
        at = outs[sends[where]][0]
        outs[sends[where]][0] += count
        return sends[where], slice(at, at + count)

    def places(names):
        return [
            tuple(name for k, name in enumerate(names) if mask >> k & 1)
            for mask in range(1, 1 << len(names))
        ]

    for piece, names, mode in steps:
        if mode == "raw":
            out, at = send_to(names, piece.shape[0])
            tasks.append(
                {"kind": "raw", "from": index_of(piece), "out": out, "at": at, "slot": len(loads)}
            )
            loads.append(piece)
            returned.append((out, at))
            copies += 2
            continue
        if mode == "vec":
            task = {"kind": "vec", "loads": [], "stage": len(stages)}
            width = piece.kept.shape[1]
            for array, at, count in [(piece.kept, 0, 16)] + [(b, at, 32) for b, at in piece.came]:
                task["loads"].append((index_of(array), at, count, len(loads)))
                loads.append(shape((count, width), array.dtype))
            stages += [shape((32, width), BF), shape((16, width), F32)]
            task["outs"] = [send_to(place, 32) for place in places(names)]
            task["kept"] = len(outs)
            outs.append([16, F32])
            copies += len(task["loads"]) + len(task["outs"]) + 1
            tasks.append(task)
            returned.append(task)
            continue
        split = names if mode == "split" else ()
        count, post, loops = piece.layout(split)
        width = piece.levels[0].terms[0][0].shape[1]
        if mode == "final":
            kind, key, across = (*names, 1)[:3] if isinstance(names, tuple) else (names, len(outs), 1)
            if key not in finals:
                finals[key] = len(outs)
                outs.append([0, kind])
            out = finals[key]
            at = outs[out][0]
            if across == 1:
                groups = [((), [(out, slice(at, at + count))])]
                outs[out][0] += count
            else:
                part = count // across
                places_at = [slice((at + i) * width, (at + i + 1) * width) for i in range(across)]
                groups = [((), [(out, (slice(0, part), where)) for where in places_at])]
                outs[out][0] += across
                beside[out] = part
            returned.append(out)
        elif mode == "all":
            groups = [((), [send_to(place, count) for place in places(names)])]
            kind = BF
        else:
            groups = [(place, [send_to(place, count)]) for place in places(names)]
            kind = BF
        if mode != "final":
            returned.append([out for unused, targets in groups for out in targets])
        gone = piece.gone | frozenset(split)
        for flip, targets in groups:
            task = {"kind": "sum", "flip": flip, "loads": [], "sum": [], "stage": len(stages)}
            stages.append(shape((count, width), kind))
            task["outs"] = targets
            copies += len(targets)
            for level in piece.levels:
                strides = level.owner.strides(level.gone)
                slots = []
                for t, (array, at) in enumerate(level.terms):
                    slots.append(len(loads))
                    alt, alt_at = None, at
                    if level.alt is not None:
                        buffer, alt_at = level.alt.terms[t]
                        alt = index_of(buffer)
                    task["loads"].append(
                        {
                            "in": index_of(array),
                            "alt": alt,
                            "alt_at": alt_at,
                            "alt_moving": level.alt.moving(gone) if level.alt is not None else (),
                            "choice": level.choice,
                            "at": at,
                            "moving": level.moving(gone),
                            "bases": [
                                sum(i * strides[name] for name, i in loop.items()) for loop in loops
                            ],
                            "post": post,
                            "slot": len(loads),
                        }
                    )
                    loads.append(shape((count, width), array.dtype))
                    copies += len(loops)
                task["sum"].append((level.rounded, slots))
            tasks.append(task)
    results = kernel_call(
        functools.partial(
            combine_kernel,
            links,
            tasks,
            len(ins),
            len(outs),
            len(loads),
            len(after),
        ),
        name,
        [
            shape((beside[i], count * width) if i in beside else (count, width), kind)
            for i, (count, kind) in enumerate(outs)
        ],
        loads + stages,
        copies,
    )(*ins, *after)
    came = {out: links.bring(results[out], *where) for where, out in sends.items()}
    values = []
    for (piece, names, mode), back in zip(steps, returned):
        if mode == "final":
            values.append(results[back])
        elif mode == "raw":
            values.append((came[back[0]], back[1].start))
        elif mode == "vec":
            piece.kept = results[back["kept"]]
            piece.came = [(came[out], at.start) for out, at in back["outs"]]
        else:
            if mode == "split":
                piece.gone = piece.gone | frozenset(names)
            piece.levels.append(
                Level(
                    piece, [(came[out], at.start) for out, at in back], piece.gone, mode == "all"
                )
            )
    return [results[out] for out in sends.values()], values


def touch_kernel(count, *refs):
    copies = Copies(refs[-1])
    loads = [copies.start(refs[i].at[0:16, 0:128], refs[-2].at[i]) for i in range(count)]
    for copy in loads:
        copy.wait()
    total = refs[-2][0].astype(F32)
    for i in range(1, count):
        total = total + refs[-2][i].astype(F32)
    refs[-3][...] = total


def touch(after, *pieces):
    buffers = []
    for piece in pieces:
        buffer = piece.levels[-1].terms[0][0]
        if not any(buffer is other for other in buffers):
            buffers.append(buffer)
    count = len(buffers)
    return kernel_call(
        functools.partial(touch_kernel, count),
        "touch",
        (shape((16, 128), F32),),
        (shape((count, 16, 128), BF),),
        count,
        vmem_out=1,
    )(*buffers, *after)[0]


def assemble_kernel(links, vec_ref, own_ref, x_ref, core_ref, both_ref, after_hbm, *outs):
    full_ref = outs[-2]
    piece = own_ref.shape[0] // 2
    half = own_ref.shape[1]
    x, c = links.bit(1), links.bit(0)
    for ref, dx, dc in ((own_ref, 0, 0), (x_ref, 1, 0), (core_ref, 0, 1), (both_ref, 1, 1)):
        at = ((1 - c if dc else c) * 2 + (1 - x if dx else x)) * piece
        rows = pl.ds(pl.multiple_of(at, 16), piece)
        for h in range(2):
            part = ref[h * piece : (h + 1) * piece, :]
            full_ref[rows, h * half : (h + 1) * half] = part.astype(F32)
    for i, out in enumerate(outs[:5]):
        row = jnp.concatenate([vec_ref[2 * i : 2 * i + 1, :], vec_ref[2 * i + 1 : 2 * i + 2, :]], axis=1)
        out[...] = row.reshape(out.shape)


def assemble(links, vec, near, after):
    rows, half = near[0].shape
    return kernel_call(
        functools.partial(assemble_kernel, links),
        "assemble",
        (shape((2 * half,), F32),) * 5 + (shape((2 * rows, 2 * half), F32),),
        (),
        1,
        vmem_in=5,
        vmem_out=6,
    )(vec, *near, after)


def shards(
    links,
    pixels,
    visible,
    kernels,
    class_token,
    norm1_gain,
    norm1_bias,
    norm2_gain,
    norm2_bias,
    attn_qkv,
    attn_out,
    mlp_up,
    mlp_down,
    cotangent,
):
    width = attn_out.shape[0]
    half = width // 2
    chips = cotangent.shape[0]
    group_chips, bands, patches, pix = pixels.shape
    slots = visible.shape[1]
    body = chips * slots
    depth = bands * pix
    block = width // 16
    flat = lambda a: a.reshape(-1, half)
    core_swap = lambda a: (links.swap(flat(a), 0), 0)

    pixel_rows = jnp.swapaxes(pixels, 2, 3).reshape(group_chips, depth, patches)
    kernels_own = kernels.reshape(depth, width)
    my_half = lax.dynamic_slice_in_dim(kernels_own, links.bit(0) * (depth // 2), depth // 2, 0)
    far_half = links.swap(my_half, "band")
    picked_in = links.swap(pick_far(links, visible, pixel_rows), "band")
    far_half, cotangent = lax.optimization_barrier((far_half, cotangent))
    picked_own, cot, gact = prepare(links, visible, pixel_rows, cotangent, mlp_down)
    far_other = links.swap(far_half, 0)
    vecs = jnp.stack(
        [class_token, norm1_gain, norm1_bias, norm2_gain, norm2_bias] + [class_token] * 3
    )

    stream, n1, packed, probs, tprobs, att, mid, n2, act1, gpre1, *parts1 = forward(
        links,
        chips,
        vecs,
        picked_own,
        picked_in,
        kernels_own,
        far_half,
        far_other,
        attn_qkv,
        attn_out,
        cot,
        gact,
        mlp_up,
    )

    x, y, core, plane = (1,), ("band",), (0,), (1, "band")
    down_send, down_keep, up_send, up_keep = parts1
    down1 = Piece(
        (1, 0, "band", "h", 3, 2),
        (2,) * 6,
        block,
        [(down_keep, 0), (links.bring(down_send, 1), 0)],
        x,
    )
    up1 = Piece(
        (3, 1, 0, "band"), (2,) * 4, 4 * block, [(up_keep, 0), (links.bring(up_send, "band"), 0)], y
    )
    *sums_send, sums_keep, branch, gatt, act2, vec2 = mlp_back(
        links, vecs, n2, gact, gpre1, mlp_up, mid, cot, att, attn_out, ()
    )
    both = lambda i, at: [(sums_keep, at), (links.bring(sums_send[i], 0), 0)]
    middle, end = 2 * width, 2 * width + mlp_up.shape[1] // 2
    down2 = Piece((0, 1, "band", "h", 3, 2), (2,) * 6, block, both(0, 0), core)
    up2 = Piece((0, 3, 1, "band"), (2,) * 4, 4 * block, both(1, middle), core)
    names, sizes = (0, 1, "band", 3, 2), (2,) * 5
    outp = Piece(names, sizes, block, both(2, end), core)
    tie, unused = combine(links, [(down1, core, "split"), (up1, core, "split")], (vec2,))
    tie, unused = combine(
        links,
        [
            (down1, y, "split"),
            (up1, x, "split"),
            (down2, x, "split"),
            (up2, y, "split"),
            (outp, (2,), "split"),
        ],
        tie,
    )

    gpacked, qkv_send, qkv_keep = attention_back(links, chips, gatt, packed, probs, tprobs, n1, tie)
    qkv_in = links.bring(qkv_send, 0)
    qkv = [
        Piece(names, sizes, count, [(qkv_keep, at), (qkv_in, at)], core)
        for at, count in qkv_parts(width)
    ]
    older = touch((gpacked,), down1, up1, down2, up2, outp)
    tie, unused = combine(
        links,
        [
            (down2, y, "split"),
            (up2, x, "split"),
            (qkv[0], x, "split"),
            (qkv[1], y, "split"),
            (down1, (2,), "split"),
            (up1, (3,), "split"),
            (outp, (3,), "split"),
        ],
        (older,),
    )
    kg_send, kg_keep, pgrad_own, pgrad_far, vec_keep = embed_back(
        links,
        chips,
        vecs,
        vec2,
        gpacked,
        attn_qkv,
        stream,
        branch,
        picked_own,
        picked_in,
        kernels_own,
        far_half,
        far_other,
        tie,
    )
    kg_in = links.bring(kg_send, 0)
    kg = Piece((0, "band", 1, "h"), (2,) * 4, depth // 4, [(kg_keep, 0), (kg_in, 0)], core)
    vec = Vec(vec_keep, (kg_in, 2 * depth))
    older = touch((vec_keep,), down2, up2, *qkv, down1, up1, outp)
    tie, unused = combine(
        links,
        [
            (kg, plane, "split"),
            (vec, plane, "vec"),
            (qkv[0], y, "split"),
            (qkv[1], x, "split"),
            (outp, plane, "split"),
            (down2, (2,), "split"),
            (up2, (3,), "split"),
            (down1, (3,), "split"),
        ],
        (older,),
    )
    far_grads = links.bring(flat(pgrad_far), "band")
    partly = scatter(links, 0, flat(pgrad_own), depth, visible, patches)
    up = Piece.join(up1, up2, 2)
    tie, (out_sum,) = combine(
        links,
        [
            (qkv[0], (2,), "split"),
            (qkv[1], (2,), "split"),
            (kg, (2, 3), "all"),
            (vec, (2, 3), "vec"),
            (outp, F32, "final"),
        ],
        (partly,),
    )
    block_output = mlp_out(chips, act1, act2, mlp_down, mid, tie)
    scattered = scatter(links, 1, far_grads, depth, visible, patches, partly)
    pixel_grads = jnp.swapaxes(scattered.reshape(group_chips, bands, pix, patches), 2, 3)
    tie, unused = combine(
        links,
        [
            (qkv[0], (3,), "split"),
            (qkv[1], (3,), "split"),
            (up, (2,), "split"),
            (down2, (3,), "split"),
        ],
        (scattered, block_output),
    )
    tie, (kgrad,) = combine(links, [(kg, BF, "final"), (vec, (), "vec")], tie, "finish")
    vec_sum = links.total(vec.value())
    kgrad = links.total(kgrad.astype(F32)).astype(BF)
    near = [kgrad, links.swap(kgrad, 1), links.swap(kgrad, 0), links.swap(kgrad, 0, 1)]
    tie, (*qkv_sums, up_sum, down_sum, unused) = combine(
        links,
        [
            (qkv[0], (F32, "qkv"), "final"),
            (qkv[1], (F32, "qkv"), "final"),
            (up, F32, "final"),
            (down1, (F32, "down", 2), "final"),
            (down2, (F32, "down", 2), "final"),
        ],
        (scattered,),
    )
    *vecs, kernel_grads = assemble(links, vec_sum, near, qkv_sums[0])

    weight = lambda part: jnp.swapaxes(links.last(part), 0, 1)
    return (
        block_output,
        pixel_grads,
        kernel_grads.reshape(bands, pix, width),
        vecs[2],
        vecs[0],
        vecs[1],
        vecs[3],
        vecs[4],
        weight(qkv_sums[0]),
        weight(out_sum),
        weight(up_sum),
        weight(down_sum),
    )


def solution(mesh):
    placed = (
        P("dp", "band", None, None),
        P("dp", None),
        P("band", None, None),
        P(),
        P(),
        P(),
        P(),
        P(),
        P(),
        P(),
        P(),
        P(),
        P(("dp", "band"), None, None),
    )
    return jax.shard_map(
        functools.partial(shards, Links(mesh)),
        mesh=mesh,
        in_specs=placed,
        out_specs=(
            P(("dp", "band"), None, None),
            P("dp", "band", None, None),
            P("band", None, None),
            P(),
            P(),
            P(),
            P(),
            P(),
            P("band", "dp"),
            P("band", "dp"),
            P("band", "dp"),
            P("band", "dp"),
        ),
        check_vma=False,
    )
```
